32 devices in a mesh: grid: 8 (over z, y), spec: 4 (over x, core).
Axes of the slice: x: 2, y: 2, z: 4, core: 2. Of those that a mesh axis runs over, the one named last changes fastest.
Arguments:
- energy: float32 [36, 36, 32, 128], P('spec', None, 'grid'), may hold values from 0.05 to 1
- nest_energy: float32 [36, 36, 32, 128], P('spec', None, 'grid'), may hold values from 0.05 to 1
- ocean_mask: int32 [32, 128], P('grid'), may hold values 0 or 1
- wind_field: float32 [2, 32, 128], P(None, 'grid'), may hold values from -6 to 6
- rim_cell: int32 [1024, 2], P('grid'), may hold values from 0 to 126, as said below
- rim_dest: int32 [1024, 1], P('grid'), may hold values from 0 to 7; in each aligned block of 128 rows (0 to 127, 128 to 255, ...) at most 32 rows name the same one
- rim_target: int32 [1024], P('grid'), may hold values from 0 to 511
- rim_weight: float32 [1024, 3], P('grid'), may hold values from 0.1 to 0.9
Outputs:
- global_next: float32 [36, 36, 32, 128], P('spec', None, 'grid')
- nest_next: float32 [36, 36, 32, 128], P('spec', None, 'grid')
The draws below stay inside these ranges and needn't reach their ends.
Inputs may be any that keep to these rules, and one draw needn't show every extreme that they name: `rim_cell`: rows of device g of the grid axis have column 0 between g * 4 and (g + 1) * 4 - 1; column 1 is at most 126. `rim_dest`: the 128 rows of one device name any one nest device at most 32 times, and some device's rows name one exactly 32 times.
All inputs are finite; a program needn't handle non-finite values. No bound on the sum of `ocean_mask` on one device may be relied on, other than what follows from the above.
Results may differ from the reference program's by a relative error of at most 0.003.
Values may be sent and summed in bfloat16 or wider, within the bound.
No kernel may reach another device: no remote copies, remote signals or barrier semaphores. Data moves between devices by JAX's collectives and lax.ppermute only.
A program may use at most 64 MiB of HBM per device.

```python
import math
import jax
import jax.numpy as jnp
import numpy as np
from jax import lax

FREQS = 36
ANGLES = 36
LON_DEV = 4
LAT_ROWS = 128
RIM_DEV = 128
LON_ALL = 32
CELL_DEV = 512
RIM_ALL = 1024
SLOT_CAP = 32
N_GRID = 8


def draw_rim_cell(key, part):
    key_lon = jax.random.fold_in(key, 11)
    key_lat = jax.random.fold_in(key, 12)
    row_ids = jnp.arange(RIM_ALL, dtype=jnp.int32)
    local_rank = row_ids % RIM_DEV
    local_col = jnp.minimum(jax.random.randint(key_lon, (RIM_ALL,), 0, 2 * LON_DEV, dtype=jnp.int32), LON_DEV - 1)
    local_col = jnp.where(local_rank == RIM_DEV - 1, LON_DEV - 1, local_col)
    local_col = jnp.where(row_ids == 0, 0, local_col)
    rim_lon = row_ids // RIM_DEV * LON_DEV + local_col
    rim_lat = jax.random.randint(key_lat, (RIM_ALL,), 0, LAT_ROWS - 1, dtype=jnp.int32)
    rim_lat = jnp.where(local_rank == 0, LAT_ROWS - 2, rim_lat)
    return jnp.stack([rim_lon, rim_lat], axis=1).astype(jnp.int32)


def set_ends(entries, key, low, top_value):
    place = [jax.random.randint(jax.random.fold_in(key, axis), (), 0, length) for axis, length in enumerate(entries.shape)]
    longest = entries.shape.index(max(entries.shape))
    neighbour = place[:longest] + [(place[longest] + 1) % entries.shape[longest]] + place[longest + 1:]
    return entries.at[tuple(place)].set(low).at[tuple(neighbour)].set(top_value)


def shard_levels(key, extent, shards, low, largest):
    gain = 1.0
    for dim, blocks in shards:
        steps = jax.random.uniform(jax.random.fold_in(jax.random.fold_in(key, 6), dim), (blocks,), jnp.float32, low / len(shards), largest / len(shards))
        gain = gain * jnp.repeat(jnp.exp(steps), extent[dim] // blocks).reshape((-1,) + (1,) * (len(extent) - 1 - dim))
    return gain


def routed_block(key, own, number, rows, count, top, limit, skew):
    sequence = jax.random.permutation(key, count)
    packed, ordinary = portions_of(count, rows * top, limit, skew, True), portions_of(count, rows * top, limit, skew, False)
    places = jnp.arange(count)

    def named(lengths, turn):
        used = int((lengths > 0).sum())
        fixed = max(1, used // 4)
        moved = fixed + (places - fixed + turn * (used - fixed)) % max(1, count - fixed)
        return jnp.zeros((count,), jnp.int32).at[sequence[jnp.where(places < fixed, places, moved)]].set(jnp.asarray(lengths, jnp.int32))

    lengths = jnp.where(number % 4 == 0, named(packed, number // 4), named(ordinary, number - number // 4 - 1))
    mixed = jax.random.permutation(jax.random.fold_in(own, 3), count)
    donor, receiver = mixed[0:count // 2 * 2:2], mixed[1:count // 2 * 2:2]
    room = jnp.minimum(lengths[donor] - 1, limit - lengths[receiver]) // 2
    room = jnp.where((donor == sequence[0]) | (receiver == sequence[0]) | (lengths[receiver] == 0), 0, jnp.maximum(room, 0))
    moved = jax.random.randint(jax.random.fold_in(own, 4), (count // 2,), 0, 1 << 20) % (room + 1)
    lengths = lengths.at[donor].add(-moved).at[receiver].add(moved)
    members = jnp.searchsorted(jnp.cumsum(lengths), jnp.arange(rows * top), side="right").astype(jnp.int32)
    grid = members.reshape(top, rows).T
    grid = grid[jax.random.permutation(jax.random.fold_in(own, 1), rows)]
    turn = jax.random.randint(jax.random.fold_in(own, 2), (rows, 1), 0, top)
    return jnp.take_along_axis(grid, (jnp.arange(top)[None, :] + turn) % top, axis=1)


def portions_of(count, total, most, slope, full):
    loads = [(1 << 20) // math.isqrt(grade ** slope) + 1 for grade in range(1, count + 1)]
    largest = most if full else min(most, max(-(-total // count), total * loads[0] // sum(loads)))
    least = 1 if total - largest >= count - 1 else 0
    counts, spare = [largest] + [least] * (count - 1), total - largest - least * (count - 1)
    while spare > 0:
        free = [i for i in range(1, count) if counts[i] < largest] or [i for i in range(1, count) if counts[i] < most]
        whole, remaining = sum([loads[i] for i in free]), spare
        for i in free:
            more = min(most - counts[i], max(1, remaining * loads[i] // whole), spare)
            counts[i] = counts[i] + more
            spare = spare - more
    return np.array(counts)


def scatter_about(stream_key, dims, deviation, most, pieces=(), kind=jnp.bfloat16):
    entries = jax.random.normal(stream_key, dims, jnp.float32) * deviation
    if len(pieces) > 0:
        entries = shard_levels(stream_key, dims, pieces, -0.22, 0.18) * entries
    return jnp.clip(entries, min=-most, max=most).astype(kind)


def setup_inputs(seed: int = 0) -> dict:
    streams_of = jax.random.split(jax.random.key(seed), 9)
    energy = jnp.clip(jnp.exp(math.log(1.0) - 2.9957323 * jax.random.uniform(streams_of[0], (FREQS, ANGLES, LON_ALL, LAT_ROWS), jnp.float32) ** shard_levels(streams_of[0], (FREQS, ANGLES, LON_ALL, LAT_ROWS), ((0, 4), (2, 8)), -0.2, 0.2)), 0.05, 1.0)
    nest_energy = jnp.clip(jnp.exp(math.log(1.0) - 2.9957323 * jax.random.uniform(streams_of[1], (FREQS, ANGLES, LON_ALL, LAT_ROWS), jnp.float32) ** shard_levels(streams_of[1], (FREQS, ANGLES, LON_ALL, LAT_ROWS), ((0, 4), (2, 8)), -0.2, 0.2)), 0.05, 1.0)
    ocean_mask = set_ends((jax.random.randint(streams_of[2], (LON_ALL, LAT_ROWS), 0, 4) < 3).astype(jnp.int32), jax.random.fold_in(streams_of[2], 1), 0, 1)
    wind_field = scatter_about(streams_of[3], (2, LON_ALL, LAT_ROWS), 1.0, 6.0, ((1, 8),), jnp.float32)
    rim_cell = draw_rim_cell(jax.random.fold_in(streams_of[8], 71), 0)
    rim_dest_keys = jax.random.split(jax.random.fold_in(streams_of[5], 1), RIM_ALL // RIM_DEV)
    rim_dest_turns = jax.random.permutation(jax.random.fold_in(streams_of[5], 3), RIM_ALL // RIM_DEV)
    rim_dest = jax.vmap(lambda own, number: routed_block(jax.random.fold_in(streams_of[5], 2), own, number, RIM_DEV, N_GRID, 1, SLOT_CAP, 2))(rim_dest_keys, rim_dest_turns).reshape((RIM_ALL, 1))
    rim_target = set_ends(jax.random.randint(streams_of[6], (RIM_ALL,), 0, CELL_DEV), jax.random.fold_in(streams_of[6], 1), 0, CELL_DEV - 1).astype(jnp.int32)
    rim_weight = jnp.clip(0.1 + 0.79999997 * jax.random.uniform(streams_of[7], (RIM_ALL, 3), jnp.float32) ** shard_levels(streams_of[7], (RIM_ALL, 3), ((0, 8),), -0.2, 0.2), 0.1, 0.9)
    return {"energy": energy, "nest_energy": nest_energy, "ocean_mask": ocean_mask, "wind_field": wind_field, "rim_cell": rim_cell, "rim_dest": rim_dest, "rim_target": rim_target, "rim_weight": rim_weight}


ratio_step = 1.1
speed_coef = 0.054
wind_coef = 0.05
dissip_coef = 0.2
nonlin_coef = 0.12
nest_speedup = 2.0
band_reach = 5


def freq_ratio(first_band, band_count):
    band_ranks = jnp.asarray(first_band).astype(jnp.float32) + jnp.arange(band_count).astype(jnp.float32)
    return jnp.power(jnp.float32(ratio_step), band_ranks - FREQS // 2)


def lat_secant(lat_rows):
    lat_degrees = -60.0 + 120.0 * (jnp.arange(lat_rows).astype(jnp.float32) + 0.5) / lat_rows
    return 1.0 / jnp.cos(lat_degrees * (jnp.pi / 180.0))


def headings():
    return 2.0 * jnp.pi * jnp.arange(ANGLES).astype(jnp.float32) / ANGLES


def courant_pair(ratios, lat_scale, speedup):
    group_speed = speedup * speed_coef / ratios
    heading = headings()
    along_lon = group_speed[:, None, None, None] * jnp.cos(heading)[None, :, None, None] * lat_scale[None, None, None, :]
    along_lat = group_speed[:, None, None, None] * jnp.sin(heading)[None, :, None, None]
    return along_lon, along_lat


def advect(padded, along_lon, along_lat):
    center = padded[:, :, 1:-1]
    west_cells = padded[:, :, :-2]
    east_cells = padded[:, :, 2:]
    zeros_row = jnp.zeros_like(center[..., :1])
    south_cells = jnp.concatenate([zeros_row, center[..., :-1]], axis=3)
    north_cells = jnp.concatenate([center[..., 1:], zeros_row], axis=3)
    flux_lon = jnp.maximum(along_lon, 0.0) * (center - west_cells) + jnp.minimum(along_lon, 0.0) * (east_cells - center)
    flux_lat = jnp.maximum(along_lat, 0.0) * (center - south_cells) + jnp.minimum(along_lat, 0.0) * (north_cells - center)
    return center - flux_lon - flux_lat


def nonlinear(banded, ratios_padded):
    band_count = banded.shape[0] - 2 * band_reach
    centre = banded[3:band_count + 8]
    strength = nonlin_coef * ratios_padded[3:band_count + 8][:, None, None, None]
    result = jnp.zeros_like(banded[band_reach:band_reach + band_count])
    for mirror in (1, -1):
        upper_pair = jnp.roll(banded[5:band_count + 10], -3 * mirror, axis=1)
        lower_pair = jnp.roll(banded[0:band_count + 5], mirror, axis=1)
        transfer = strength * (centre * centre * (upper_pair + lower_pair) - 2.0 * centre * upper_pair * lower_pair)
        result = result - 2.0 * transfer[2:band_count + 2] + jnp.roll(transfer[0:band_count], 3 * mirror, axis=1) + jnp.roll(transfer[5:band_count + 5], -mirror, axis=1)
    return result


def step_sources(advected, banded, ratios, ratios_padded, wind_block, mean_energy):
    heading = headings()
    along_wind = jnp.maximum(wind_block[0][None, None] * jnp.cos(heading)[None, :, None, None] + wind_block[1][None, None] * jnp.sin(heading)[None, :, None, None], 0.0)
    wind_gain = wind_coef * ratios[:, None, None, None] * along_wind * advected
    transfer = nonlinear(banded, ratios_padded)
    return (advected + wind_gain + transfer) / (1.0 + dissip_coef * (ratios * ratios)[:, None, None, None] * mean_energy[None, None])


def interpolate(spectra_flat, base_cell, east_cell, rim_weight):
    east_share = rim_weight[:, 0]
    north_share = rim_weight[:, 1]
    corner_sw = jnp.take(spectra_flat, base_cell, axis=1)
    corner_nw = jnp.take(spectra_flat, base_cell + 1, axis=1)
    corner_se = jnp.take(spectra_flat, east_cell, axis=1)
    corner_ne = jnp.take(spectra_flat, east_cell + 1, axis=1)
    mixed = (1.0 - east_share) * (1.0 - north_share) * corner_sw + (1.0 - east_share) * north_share * corner_nw
    mixed = mixed + east_share * (1.0 - north_share) * corner_se + east_share * north_share * corner_ne
    return mixed.astype(jnp.bfloat16)


def global_tile(tile_block, mask_block, wind_block):
    ratios = freq_ratio(0, FREQS)
    along_lon, along_lat = courant_pair(ratios, lat_secant(LAT_ROWS), 1.0)
    advected = advect(tile_block, along_lon, along_lat) * mask_block.astype(jnp.float32)
    band_weight = 0.1 * ratios
    partial_value = jnp.sum(band_weight[:, None, None, None] * advected, axis=(0, 1))
    mean_energy = partial_value / (ANGLES * (0.1 * jnp.sum(freq_ratio(0, FREQS))))
    banded = jnp.pad(advected, ((band_reach, band_reach), (0, 0), (0, 0), (0, 0)))
    ratios_padded = freq_ratio(-band_reach, FREQS + 2 * band_reach)
    return step_sources(advected, banded, ratios, ratios_padded, wind_block, mean_energy)


def reference(energy, nest_energy, ocean_mask, wind_field, rim_cell, rim_dest, rim_target, rim_weight):
    padded = jnp.concatenate([energy[:, :, -1:], energy, energy[:, :, :1]], axis=2)

    def one_tile(tile_index):
        offset = tile_index * LON_DEV
        tile_block = lax.dynamic_slice_in_dim(padded, offset, LON_DEV + 2, 2)
        mask_block = lax.dynamic_slice_in_dim(ocean_mask, offset, LON_DEV, 0)
        wind_block = lax.dynamic_slice_in_dim(wind_field, offset, LON_DEV, 1)
        return global_tile(tile_block, mask_block, wind_block)

    tile_stack = lax.map(one_tile, jnp.arange(N_GRID, dtype=jnp.int32))
    global_next = jnp.moveaxis(tile_stack, 0, 2).reshape(FREQS, ANGLES, LON_ALL, LAT_ROWS)

    spectra_flat = global_next.reshape(FREQS * ANGLES, LON_ALL * LAT_ROWS)
    rim_lon = rim_cell[:, 0]
    rim_lat = rim_cell[:, 1]
    base_cell = rim_lon * LAT_ROWS + rim_lat
    east_cell = ((rim_lon + 1) % LON_ALL) * LAT_ROWS + rim_lat
    boundary = interpolate(spectra_flat, base_cell, east_cell, rim_weight)

    ratios = freq_ratio(0, FREQS)
    nest_lon, nest_lat = courant_pair(ratios, jnp.ones((LAT_ROWS,), jnp.float32), nest_speedup)
    half_cols = LON_ALL // 2
    quarter_cols = LON_ALL // 4
    rolled = jnp.roll(nest_energy, -quarter_cols, axis=2)
    halves = []
    for half_index in range(2):
        piece_cols = rolled[:, :, half_index * half_cols:(half_index + 1) * half_cols]
        piece_padded = jnp.pad(piece_cols, ((0, 0), (0, 0), (1, 1), (0, 0)))
        halves.append(advect(piece_padded, nest_lon, nest_lat))
    nest_cols = jnp.roll(jnp.concatenate(halves, axis=2), quarter_cols, axis=2)
    nest_flat = nest_cols.reshape(FREQS * ANGLES, LON_ALL * LAT_ROWS)
    nest_cell = rim_dest[:, 0] * CELL_DEV + rim_target
    picked = jnp.take(nest_flat, nest_cell, axis=1)
    increment = rim_weight[:, 2][None, :] * (boundary.astype(jnp.float32) - picked)
    nest_next = nest_flat.at[:, nest_cell].add(increment).reshape(FREQS, ANGLES, LON_ALL, LAT_ROWS)
    return global_next, nest_next
```

```python
import functools

import jax
import jax.numpy as jnp
import numpy as np
from jax import lax
from jax.experimental import pallas as pl
from jax.experimental.pallas import tpu as pltpu
from jax.sharding import PartitionSpec as P

ratio_step = 1.1
speed_coef = 0.054
wind_coef = 0.05
dissip_coef = 0.2
nonlin_coef = 0.12
nest_speedup = 2.0
reach = 5

VREG = 8
BF16 = jnp.bfloat16
F32 = jnp.float32


class Sizes:
    def __init__(self, mesh, energy, rim_rows):
        self.grid = mesh.shape["grid"]
        self.spec = mesh.shape["spec"]
        self.bands, self.angles, self.cols, self.lat = energy.shape
        self.freqs = self.bands * self.spec
        self.bins = self.bands * self.angles
        self.ring = self.angles * self.cols
        self.rows = self.bins * self.cols
        self.vregs = self.ring // VREG
        self.rim = rim_rows
        self.cap = max(2, (2 * rim_rows + self.grid - 1) // self.grid)
        self.slots = self.grid * self.cap
        self.lanes = (self.bins + 4 + 127) // 128 * 128
        self.msg_rows = (self.bins + 8 + 15) // 16 * 16
        self.edge_rows = reach * self.ring
        self.band_rows = self.edge_rows + 16
        self.half = self.angles // 2
        self.quarter = self.angles // 4


def ratio_table(sz):
    ranks = np.arange(-reach, sz.freqs + reach, dtype=np.float64) - sz.freqs // 2
    return (ratio_step**ranks).astype(np.float32)


def angle_table(sz):
    heading = 2.0 * np.pi * np.arange(sz.angles) / sz.angles
    table = np.zeros((sz.ring + VREG, sz.lat), np.float32)
    table[: sz.ring, 0] = np.repeat(np.cos(heading), sz.cols)
    table[: sz.ring, 1] = np.repeat(np.sin(heading), sz.cols)
    degrees = -60.0 + 120.0 * (np.arange(sz.lat) + 0.5) / sz.lat
    table[sz.ring :] = 1.0 / np.cos(degrees * (np.pi / 180.0))
    return table


def from_west(sz, angle):
    return angle < sz.quarter or angle >= 3 * sz.quarter


def split2(x):
    high = x.astype(BF16).astype(F32)
    return high, x - high


def pack_kernel(sz, energy, nest, cell, dest, weight, east_msg, west_msg, tmp):
    q = sz.quarter
    for msg, col, mine in ((east_msg, sz.cols - 1, True), (west_msg, 0, False)):
        for k in range(sz.bands):
            for part in range(4):
                own = (part in (0, 3)) == mine
                src = energy if own else nest
                angle = part * q if own else ((part + 2) % 4) * q
                row = (k * sz.angles + angle) * sz.cols + col
                tmp[pl.ds(k * sz.angles + part * q, q), :] = src[pl.ds(row, q, stride=sz.cols), :]
        if mine:
            last = cell[0:1, :] - lax.axis_index("grid") * sz.cols == sz.cols - 1
            lat = jnp.where(last, cell[1:2, :], -1).astype(F32)
            ex, ny = weight[0:1, :], weight[1:2, :]
            south, north = split2(ex * (1.0 - ny)), split2(ex * ny)
            info = [dest[...].astype(F32), lat, south[0], south[1], north[0], north[1]]
            for i, line in enumerate(info):
                tmp[pl.ds(sz.bins + i, 1), :] = line
            rest = sz.msg_rows - sz.bins - len(info)
            tmp[pl.ds(sz.bins + len(info), rest), :] = jnp.zeros((rest, sz.lat), F32)
        else:
            rest = sz.msg_rows - sz.bins
            tmp[pl.ds(sz.bins, rest), :] = jnp.zeros((rest, sz.lat), F32)
        msg[...] = tmp[...].astype(BF16)


def spread_halo(sz, from_w, from_e, halo):
    halo[pl.ds(0, sz.msg_rows, stride=sz.cols), :] = from_w[...].astype(F32)
    halo[pl.ds(sz.cols - 1, sz.msg_rows, stride=sz.cols), :] = from_e[...].astype(F32)


def fill_coefficients(sz, table, secant, centre, lon, lat):
    lane = lax.broadcasted_iota(jnp.int32, (VREG, sz.lat), 1)
    sec = table[pl.ds(sz.ring, VREG), :]
    for v in range(sz.vregs):
        rows = table[pl.ds(v * VREG, VREG), :]
        along = jnp.broadcast_to(jnp.abs(rows[:, 0:1]), (VREG, sz.lat))
        across = jnp.broadcast_to(jnp.abs(rows[:, 1:2]), (VREG, sz.lat))
        if secant:
            along = along * sec
        edge = 0 if v * VREG < sz.half * sz.cols else sz.lat - 1
        centre[pl.ds(v * VREG, VREG), :] = along + across
        lon[pl.ds(v * VREG, VREG), :] = along
        lat[pl.ds(v * VREG, VREG), :] = jnp.where(lane == edge, 0.0, across)


def transported(sz, field, halo, k, v, coefficients, speed, shift, keep=None):
    sub = lax.broadcasted_iota(jnp.int32, (VREG, sz.lat), 0)
    base = pl.multiple_of(k * sz.ring, VREG)
    x = field[pl.ds(base + v * VREG, VREG), :]
    edge = halo[pl.ds(base + (v * VREG + shift) % sz.ring, VREG), :]
    first = v * VREG // sz.cols
    per = VREG // sz.cols
    wests = [from_west(sz, first + i) for i in range(per)]
    col = sub % sz.cols
    if all(wests):
        near, at_edge = pltpu.roll(x, 1, 0), col == 0
    elif not any(wests):
        near, at_edge = pltpu.roll(x, VREG - 1, 0), col == sz.cols - 1
    else:
        west = sub < 0
        for i in range(per):
            if wests[i]:
                west = west | ((sub >= i * sz.cols) & (sub < (i + 1) * sz.cols))
        near = jnp.where(west, pltpu.roll(x, 1, 0), pltpu.roll(x, VREG - 1, 0))
        at_edge = jnp.where(west, col, sz.cols - 1 - col) == 0
    if keep is not None:
        edge = edge * jnp.where(col == 0, keep[0], keep[1])
    near = jnp.where(at_edge, edge, near)
    beside = pltpu.roll(x, 1 if v * VREG < sz.half * sz.cols else sz.lat - 1, 1)
    centre, lon, lat = (c[pl.ds(v * VREG, VREG), :] for c in coefficients)
    return x - speed * (centre * x - lon * near - lat * beside)


def advect_kernel(
    sz, table, ratios, energy, from_w, from_e, mask, adv, msg_a, msg_b, part, halo, centre, lon, lat
):
    spec_rank = lax.axis_index("spec")
    spread_halo(sz, from_w, from_e, halo)
    fill_coefficients(sz, table, True, centre, lon, lat)
    sea4 = mask[...].astype(F32)
    sea = jnp.concatenate([sea4] * (VREG // sz.cols), axis=0)

    def band(k, total):
        ratio = ratios[spec_rank * sz.bands + reach + k]
        speed = ratios[sz.freqs + 2 * reach + spec_rank * sz.bands + reach + k]
        base = pl.multiple_of(k * sz.ring, VREG)
        line = jnp.zeros((VREG, sz.lat), F32)
        for v in range(sz.vregs):
            out = sea * transported(sz, energy, halo, k, v, (centre, lon, lat), speed, 0)
            adv[pl.ds(base + v * VREG, VREG), :] = out
            line = line + out
        return total + line * (0.1 * ratio)

    total = lax.fori_loop(0, sz.bands, band, jnp.zeros((VREG, sz.lat), F32))
    mine = total[0 : sz.cols]
    for i in range(1, VREG // sz.cols):
        mine = mine + total[i * sz.cols : (i + 1) * sz.cols]
    part[...] = mine
    even = lax.rem(spec_rank, 2) == 0
    top = (sz.bands - reach) * sz.ring
    first_a = pl.multiple_of(jnp.where(even, top, 0), VREG)
    first_b = pl.multiple_of(jnp.where(even, 0, top), VREG)
    msg_a[pl.ds(0, sz.edge_rows), :] = adv[pl.ds(first_a, sz.edge_rows), :].astype(BF16)
    msg_b[...] = adv[pl.ds(first_b, sz.edge_rows), :].astype(BF16)
    high, rest = split2(mine)
    middle, low = split2(rest)
    pieces = jnp.concatenate([high, middle, low, jnp.zeros_like(mine)], axis=0)
    msg_a[pl.ds(sz.edge_rows, 4 * sz.cols), :] = pieces.astype(BF16)


def slot_matrix(sz, dest):
    device = lax.broadcasted_iota(jnp.int32, (sz.grid, sz.rim), 0).astype(F32)
    hot = jnp.where(device == dest, 1.0, 0.0)
    before = lax.broadcasted_iota(jnp.int32, (sz.rim, sz.rim), 0)
    after = lax.broadcasted_iota(jnp.int32, (sz.rim, sz.rim), 1)
    earlier = jnp.dot(
        hot.astype(BF16), jnp.where(before < after, 1.0, 0.0).astype(BF16), preferred_element_type=F32
    )
    rank = jnp.sum(hot * earlier, axis=0, keepdims=True)
    place = dest * sz.cap + rank
    slot = lax.broadcasted_iota(jnp.int32, (sz.slots, sz.rim), 0).astype(F32)
    return jnp.where(slot == place, 1.0, 0.0).astype(BF16)


def dot_lanes(a, b):
    return lax.dot_general(a, b, (((1,), (1,)), ((), ())), preferred_element_type=F32)


def side_kernel(
    sz, table, ratios, nest, from_w, from_e, cell, dest, target, weight, nest_adv, mix, halo, centre, lon, lat
):
    spec_rank, grid_rank = lax.axis_index("spec"), lax.axis_index("grid")
    quarter = sz.grid // 4
    keep_w = jnp.where((grid_rank != quarter) & (grid_rank != 3 * quarter), 1.0, 0.0).astype(F32)
    keep_e = jnp.where((grid_rank != quarter - 1) & (grid_rank != 3 * quarter - 1), 1.0, 0.0).astype(F32)
    spread_halo(sz, from_w, from_e, halo)
    fill_coefficients(sz, table, False, centre, lon, lat)

    def band(k, carry):
        speed = nest_speedup * ratios[sz.freqs + 2 * reach + spec_rank * sz.bands + reach + k]
        base = pl.multiple_of(k * sz.ring, VREG)
        for v in range(sz.vregs):
            nest_adv[pl.ds(base + v * VREG, VREG), :] = transported(
                sz, nest, halo, k, v, (centre, lon, lat), speed, sz.half * sz.cols, (keep_w, keep_e)
            )
        return carry

    lax.fori_loop(0, sz.bands, band, 0)

    row = lax.broadcasted_iota(jnp.int32, (sz.lat, sz.rim), 0)
    hot = slot_matrix(sz, dest[...].astype(F32))
    col = cell[0:1, :] - grid_rank * sz.cols
    south_row = cell[1:2, :]
    ex, ny = weight[0:1, :], weight[1:2, :]
    for c in range(sz.cols):
        share = jnp.where(col == c, 1.0 - ex, 0.0) + jnp.where(col + 1 == c, ex, 0.0)
        south, north = share * (1.0 - ny), share * ny
        corner = jnp.where(row == south_row, south, 0.0) + jnp.where(row == south_row + 1, north, 0.0)
        mix[:, c * sz.lat : (c + 1) * sz.lat] = dot_lanes(hot, corner.astype(BF16)).astype(BF16)
    info = from_w[pl.ds(sz.bins // 16 * 16, 16), :].astype(F32)
    off = sz.bins % 16
    their_dest, their_row = info[off : off + 1], info[off + 1 : off + 2]
    south = info[off + 2 : off + 3] + info[off + 3 : off + 4]
    north = info[off + 4 : off + 5] + info[off + 5 : off + 6]
    their_hot = slot_matrix(sz, their_dest)
    valid = their_row >= 0.0
    rowf = row.astype(F32)
    corner = jnp.where(valid & (rowf == their_row), south, 0.0) + jnp.where(
        valid & (rowf == their_row + 1.0), north, 0.0
    )
    n = sz.cols * sz.lat
    mix[:, n : n + sz.lat] = dot_lanes(their_hot, corner.astype(BF16)).astype(BF16)
    at = sz.bins % 128
    line = lax.broadcasted_iota(jnp.int32, (128, sz.rim), 0)
    t = target[...]
    t_col = t // sz.lat
    about = jnp.where(line == at, t_col.astype(F32), 0.0)
    about = about + jnp.where(line == at + 1, (t - t_col * sz.lat).astype(F32), 0.0)
    rate, rest = split2(weight[2:3, :])
    about = about + jnp.where(line == at + 2, rate, 0.0) + jnp.where(line == at + 3, rest, 0.0)
    n = n + sz.lat
    mix[:, n : n + 128] = dot_lanes(hot, about.astype(BF16)).astype(BF16)


def source_kernel(
    sz, table, ratios, adv, recv_a, recv_b, pair, other, wind, mix, out, msg, plain, turned, plus, minus, wide
):
    spec_rank = lax.axis_index("spec")
    first = spec_rank * sz.bands
    nv = sz.vregs
    low = lax.broadcasted_iota(jnp.int32, (VREG, sz.lat), 0) < VREG // 2
    turn = VREG // 2

    def put(slot, load):
        vals = [load(v) for v in range(nv)]
        for v in range(nv):
            plain[slot, pl.ds(v * VREG, VREG), :] = vals[v]
            nxt = pltpu.roll(jnp.where(low, vals[(v + 1) % nv], vals[v]), turn, 0)
            turned[slot, pl.ds((v + 2) * VREG, VREG), :] = nxt
            if v >= nv - 2:
                turned[slot, pl.ds((v + 2 - nv) * VREG, VREG), :] = nxt
            if v == 0:
                turned[slot, pl.ds((nv + 2) * VREG, VREG), :] = nxt

    even = lax.rem(spec_rank, 2) == 0
    base_a = jnp.where(even, sz.bands + reach, 0)
    base_b = jnp.where(even, 0, sz.bands + reach)

    def own(k, carry):
        base = pl.multiple_of(k * sz.ring, VREG)
        put(k + reach, lambda v: adv[pl.ds(base + v * VREG, VREG), :])
        return carry

    def halo(k, carry):
        base = pl.multiple_of(k * sz.ring, 16)
        a = recv_a[pl.ds(base, sz.ring), :].astype(F32)
        put(base_a + k, lambda v: a[v * VREG : (v + 1) * VREG])
        b = recv_b[pl.ds(base, sz.ring), :].astype(F32)
        put(base_b + k, lambda v: b[v * VREG : (v + 1) * VREG])
        return carry

    lax.fori_loop(0, sz.bands, own, 0)
    lax.fori_loop(0, reach, halo, 0)

    def strengths(n, carry):
        strength = nonlin_coef * ratios[first + n + 3]
        for v in range(nv):
            c = plain[n + 3, pl.ds(v * VREG, VREG), :]
            sc = strength * c
            for ref, up_row, down_row in ((plus, v + 3, v + 1), (minus, v, v + 2)):
                up = turned[n + 5, pl.ds(up_row * VREG, VREG), :]
                down = turned[n, pl.ds(down_row * VREG, VREG), :]
                delta = sc * (c * (up + down) - 2.0 * (up * down))
                ref[n, pl.ds((v + 1) * VREG, VREG), :] = delta
                if v == nv - 1:
                    ref[n, pl.ds(0, VREG), :] = delta
                if v < 2:
                    ref[n, pl.ds((nv + 1 + v) * VREG, VREG), :] = delta
        return carry

    lax.fori_loop(0, sz.bands + reach, strengths, 0)

    per = VREG // sz.cols
    east = jnp.concatenate([wind[0]] * per, axis=0)
    north = jnp.concatenate([wind[1]] * per, axis=0)
    for v in range(nv):
        rows = table[pl.ds(v * VREG, VREG), :]
        along = rows[:, 0:1] * east + rows[:, 1:2] * north
        wide[pl.ds(v * VREG, VREG), :] = wind_coef * jnp.maximum(along, 0.0)
    total_weight = float(sz.angles * 0.1 * np.sum(ratio_table(sz)[reach:-reach].astype(np.float64)))
    mean4 = (pair[...] + other[...]) * (1.0 / total_weight)
    mean = jnp.concatenate([mean4] * per, axis=0)

    def result(k, carry):
        ratio = ratios[first + reach + k]
        scale = 1.0 / (1.0 + (dissip_coef * ratio * ratio) * mean)
        base = pl.multiple_of(k * sz.ring, VREG)

        def side(v):
            return (
                plus[k, pl.ds(v * VREG, VREG), :]
                + minus[k, pl.ds((v + 3) * VREG, VREG), :]
                + plus[k + 5, pl.ds((v + 2) * VREG, VREG), :]
                + minus[k + 5, pl.ds((v + 1) * VREG, VREG), :]
            )

        before = side(nv - 1)
        for v in range(nv):
            now = side(v)
            moved = pltpu.roll(jnp.where(low, now, before), turn, 0)
            before = now
            here = pl.ds((v + 1) * VREG, VREG)
            transfer = moved - 2.0 * (plus[k + 2, here, :] + minus[k + 2, here, :])
            a = adv[pl.ds(base + v * VREG, VREG), :]
            gain = ratio * wide[pl.ds(v * VREG, VREG), :]
            out[pl.ds(base + v * VREG, VREG), :] = (a + gain * a + transfer) * scale
        return carry

    lax.fori_loop(0, sz.bands, result, 0)

    pad = jnp.zeros((sz.lanes - sz.bins, sz.lat), BF16)
    columns = [
        jnp.concatenate([out[pl.ds(c, sz.bins, stride=sz.cols), :].astype(BF16), pad], axis=0)
        for c in range(sz.cols)
    ]
    n = sz.cols * sz.lat
    spectra = dot_lanes(mix[:, 0:n], jnp.concatenate(columns, axis=1))
    about = mix[:, n + sz.lat : n + sz.lat + 128].astype(F32)
    msg[:, 0 : sz.lanes - 128] = spectra[:, : sz.lanes - 128].astype(BF16)
    msg[:, sz.lanes - 128 : sz.lanes] = (spectra[:, sz.lanes - 128 :] + about).astype(BF16)
    msg[:, sz.lanes :] = dot_lanes(mix[:, n : n + sz.lat], columns[0]).astype(BF16)


def blend_kernel(sz, recv, nest_adv, out):
    east = recv[:, sz.lanes :].astype(F32)
    east = jnp.concatenate([east[sz.cap :], east[: sz.cap]], axis=0)
    own = recv[:, : sz.lanes].astype(F32)
    spectra = (own + east).astype(BF16)
    at = sz.bins - (sz.lanes - 128)
    about = own[:, sz.lanes - 128 :]
    t_col, t_row, rate = about[:, at : at + 1], about[:, at + 1 : at + 2], about[:, at + 2 : at + 3]
    lane = lax.broadcasted_iota(jnp.int32, (sz.slots, sz.lat), 1).astype(F32)
    hit = jnp.where(lane == t_row, rate, 0.0)
    for c in range(sz.cols):
        relax = jnp.where(t_col == float(c), hit, 0.0)
        kept = 1.0 - jnp.sum(relax, axis=0, keepdims=True)
        added = lax.dot_general(
            spectra, relax.astype(BF16), (((0,), (0,)), ((), ())), preferred_element_type=F32
        )
        here = pl.ds(c, sz.bins, stride=sz.cols)
        out[here, :] = nest_adv[here, :] * kept + added[: sz.bins]


def kernel_call(body, out_shape, n_in, smem=(), scratch=(), flops=0, moved=0, name=None):
    specs = [
        pl.BlockSpec(memory_space=pltpu.SMEM if i in smem else pltpu.VMEM) for i in range(n_in)
    ]
    return pl.pallas_call(
        body,
        out_shape=out_shape,
        in_specs=specs,
        out_specs=jax.tree.map(lambda _: pl.BlockSpec(memory_space=pltpu.VMEM), out_shape),
        scratch_shapes=list(scratch),
        compiler_params=pltpu.CompilerParams(vmem_limit_bytes=20 * 2**20),
        cost_estimate=pl.CostEstimate(flops=flops, bytes_accessed=moved, transcendentals=0),
        name=name,
    )


def per_device(
    mesh, energy, nest_energy, ocean_mask, wind_field, rim_cell, rim_dest, rim_target, rim_weight
):
    sz = Sizes(mesh, energy, rim_dest.shape[0])
    shape = jax.ShapeDtypeStruct
    field = shape((sz.rows, sz.lat), F32)
    vmem = pltpu.VMEM
    ratio = ratio_table(sz)
    ratios = jnp.asarray(np.concatenate([ratio, speed_coef / ratio]).astype(np.float32))
    table = jnp.asarray(angle_table(sz))
    energy = energy.reshape(sz.rows, sz.lat)
    nest = nest_energy.reshape(sz.rows, sz.lat)
    cell, dest, weight = rim_cell.T, rim_dest.T, rim_weight.T
    target = rim_target.reshape(1, sz.rim)

    edge = shape((sz.msg_rows, sz.lat), BF16)
    east_msg, west_msg = kernel_call(
        functools.partial(pack_kernel, sz),
        (edge, edge),
        5,
        scratch=[vmem((sz.msg_rows, sz.lat), F32)],
        name="pack",
    )(energy, nest, cell, dest, weight)
    up = [(i, (i + 1) % sz.grid) for i in range(sz.grid)]
    from_w = lax.ppermute(east_msg, "grid", up)
    from_e = lax.ppermute(west_msg, "grid", [(j, i) for i, j in up])

    coefficient = [vmem((sz.ring, sz.lat), F32)] * 3
    halo = vmem((sz.msg_rows * sz.cols, sz.lat), F32)
    adv, msg_a, msg_b, part = kernel_call(
        functools.partial(advect_kernel, sz),
        (
            field,
            shape((sz.band_rows, sz.lat), BF16),
            shape((sz.edge_rows, sz.lat), BF16),
            shape((sz.cols, sz.lat), F32),
        ),
        6,
        smem=(1,),
        scratch=[halo] + coefficient,
        name="advect",
    )(table, ratios, energy, from_w, from_e, ocean_mask)

    recv_a = lax.ppermute(msg_a, "spec", [(i, i ^ 1) for i in range(sz.spec)])
    across = [(i, i + 1) for i in range(1, sz.spec - 1, 2)]
    recv_b = lax.ppermute(msg_b, "spec", across + [(j, i) for i, j in across])
    pieces = recv_a[sz.edge_rows : sz.edge_rows + 3 * sz.cols].astype(F32)
    pair = part + pieces.reshape(3, sz.cols, sz.lat).sum(axis=0)
    other = jnp.zeros_like(pair)
    step = 2
    while step < sz.spec:
        pair = pair + other
        other = lax.ppermute(pair, "spec", [(i, i ^ step) for i in range(sz.spec)])
        step *= 2

    nest_adv, mix = kernel_call(
        functools.partial(side_kernel, sz),
        (field, shape((sz.slots, (sz.cols + 1) * sz.lat + 128), BF16)),
        9,
        smem=(1,),
        scratch=[halo] + coefficient,
        flops=10**9,
        moved=2 * 10**6,
        name="side",
    )(table, ratios, nest, from_w, from_e, cell, dest, target, weight)

    padded = sz.bands + 2 * reach
    global_next, msg = kernel_call(
        functools.partial(source_kernel, sz),
        (field, shape((sz.slots, 2 * sz.lanes), BF16)),
        9,
        smem=(1,),
        scratch=[
            vmem((padded, sz.ring, sz.lat), F32),
            vmem((padded, sz.ring + 3 * VREG, sz.lat), F32),
            vmem((sz.bands + reach, sz.ring + 3 * VREG, sz.lat), F32),
            vmem((sz.bands + reach, sz.ring + 3 * VREG, sz.lat), F32),
            vmem((sz.ring, sz.lat), F32),
        ],
        name="sources",
    )(table, ratios, adv, recv_a, recv_b, pair, other, wind_field, mix)

    recv = lax.all_to_all(msg, "grid", split_axis=0, concat_axis=0, tiled=True)
    nest_next = kernel_call(functools.partial(blend_kernel, sz), field, 2, name="blend")(recv, nest_adv)
    full = (sz.bands, sz.angles, sz.cols, sz.lat)
    return global_next.reshape(full), nest_next.reshape(full)


def solution(mesh):
    in_specs = (
        P("spec", None, "grid", None),
        P("spec", None, "grid", None),
        P("grid", None),
        P(None, "grid", None),
        P("grid", None),
        P("grid", None),
        P("grid"),
        P("grid", None),
    )
    out_specs = (P("spec", None, "grid", None), P("spec", None, "grid", None))
    return jax.shard_map(
        functools.partial(per_device, mesh),
        mesh=mesh,
        in_specs=in_specs,
        out_specs=out_specs,
        check_vma=False,
    )
```

```python
import functools

import jax
import jax.numpy as jnp
import numpy as np
from jax import lax
from jax.experimental import pallas as pl
from jax.experimental.pallas import tpu as pltpu
from jax.sharding import PartitionSpec as P

ratio_step = 1.1
speed_coef = 0.054
wind_coef = 0.05
dissip_coef = 0.2
nonlin_coef = 0.12
nest_speedup = 2.0
reach = 5

VREG = 8
BF16 = jnp.bfloat16
F32 = jnp.float32


class Sizes:
    def __init__(self, mesh, energy, rim_rows):
        self.grid = mesh.shape["grid"]
        self.spec = mesh.shape["spec"]
        self.bands, self.angles, self.cols, self.lat = energy.shape
        self.freqs = self.bands * self.spec
        self.bins = self.bands * self.angles
        self.ring = self.angles * self.cols
        self.rows = self.bins * self.cols
        self.vregs = self.ring // VREG
        self.rim = rim_rows
        self.cap = max(2, (2 * rim_rows + self.grid - 1) // self.grid)
        self.slots = self.grid * self.cap
        self.lanes = (self.bins + 3 + 127) // 128 * 128
        self.half = self.angles // 2
        self.quarter = self.angles // 4
        self.side = (self.angles + VREG - 1) // VREG * VREG
        self.frame = self.side + 2 * VREG
        self.thin = self.bands * self.half
        self.thin_rows = (2 * self.thin + 15) // 16 * 16
        self.thick = (self.angles + self.half + VREG - 1) // VREG * VREG
        self.info = self.bands * self.thick
        self.thick_nest = (self.info + 7 + VREG - 1) // VREG * VREG
        self.thick_rows = (self.thick_nest + self.thin + 15) // 16 * 16
        self.edge_rows = reach * self.ring
        self.rim_band = (2 * self.half + VREG - 1) // VREG * VREG
        self.far_band = self.rim_band + self.side
        self.sum_row = reach * self.far_band
        self.fix_rows = (self.sum_row + 3 * VREG + 15) // 16 * 16


def band_ratio(sz, band, inverse=False):
    rank = lax.axis_index("spec")
    ratio = F32(0.0)
    for s in range(sz.spec):
        power = ratio_step ** (s * sz.bands + band - sz.freqs // 2)
        ratio = jnp.where(rank == s, F32(1.0 / power if inverse else power), ratio)
    return ratio


def over_bands(count, ratio, body, inverse=False):
    step = F32(1.0 / ratio_step if inverse else ratio_step)

    def turn(i, r):
        body(i, r)
        return r * step

    lax.fori_loop(0, count, turn, ratio)


def angle_table(sz):
    heading = 2.0 * np.pi * np.arange(sz.angles) / sz.angles
    table = np.zeros((sz.ring + VREG + sz.side, sz.lat), np.float32)
    table[sz.ring + VREG :][: sz.angles, 0] = np.cos(heading)
    table[sz.ring + VREG :][: sz.angles, 1] = np.sin(heading)
    table[: sz.ring, 0] = np.repeat(np.cos(heading), sz.cols)
    table[: sz.ring, 1] = np.repeat(np.sin(heading), sz.cols)
    degrees = -60.0 + 120.0 * (np.arange(sz.lat) + 0.5) / sz.lat
    table[sz.ring : sz.ring + VREG] = 1.0 / np.cos(degrees * (np.pi / 180.0))
    return table


def from_west(sz, angle):
    return angle < sz.quarter or angle >= 3 * sz.quarter


def split3(x):
    high = x.astype(BF16).astype(F32)
    middle = (x - high).astype(BF16).astype(F32)
    return [high, middle, x - high - middle]


def upwind(sz, v):
    sub = lax.broadcasted_iota(jnp.int32, (VREG, sz.lat), 0)
    first, per = v * VREG // sz.cols, VREG // sz.cols
    wests = [from_west(sz, first + i) for i in range(per)]
    west = sub < 0
    for i in range(per):
        if wests[i]:
            west = west | ((sub >= i * sz.cols) & (sub < (i + 1) * sz.cols))
    return wests, west, sub % sz.cols


def west_half(sz):
    return ((3 * sz.quarter, sz.angles - 3 * sz.quarter), (0, sz.quarter))


def fetch(pairs, sems):
    copies = [pltpu.make_async_copy(a, b, sems.at[i]) for i, (a, b) in enumerate(pairs)]
    for c in copies:
        c.start()
    return copies


def far_band(sz):
    return jnp.where(lax.rem(lax.axis_index("spec"), 2) == 0, 0, sz.bands - reach)


def pack_kernel(
    sz, table, energy, nest, mask, wind,
    thin, thick, moves, nest_moves, s_moves, gain, sea,
    table_v, field, nest_field, mask_v, wind_v, tmp_thin, tmp_thick, sems,
):
    pairs = [(table, table_v), (mask, mask_v), (wind, wind_v)]
    for source, target in ((energy, field), (nest, nest_field)):
        for k in range(sz.bands):
            band = pl.ds(k * sz.ring, sz.ring)
            pairs.append((source.at[band], target.at[band]))
    copies = [pltpu.make_async_copy(a, b, sems.at[i]) for i, (a, b) in enumerate(pairs)]
    for copy in copies:
        copy.start()
    rest = sz.thin_rows - 2 * sz.thin
    if rest:
        tmp_thin[pl.ds(2 * sz.thin, rest), :] = jnp.zeros((rest, sz.lat), F32)
    tmp_thick[...] = jnp.zeros_like(tmp_thick)
    for copy in copies[:3]:
        copy.wait()
    info = [mask_v[0:1, :].astype(F32)] + split3(wind_v[0, 0:1, :]) + split3(wind_v[1, 0:1, :])
    for i, line in enumerate(info):
        tmp_thick[pl.ds(sz.info + i, 1), :] = line
    per = VREG // sz.cols
    sea[...] = jnp.concatenate([mask_v[...].astype(F32)] * per, axis=0)
    east_wind = jnp.concatenate([wind_v[0]] * per, axis=0)
    north_wind = jnp.concatenate([wind_v[1]] * per, axis=0)
    fill_moves(sz, 0, table_v, sz.cols, (moves, nest_moves))
    fill_moves(sz, sz.ring + VREG, table_v, 1, (s_moves, None))
    for v in range(sz.vregs):
        rows = table_v[pl.ds(v * VREG, VREG), :]
        along = rows[:, 0:1] * east_wind + rows[:, 1:2] * north_wind
        gain[pl.ds(v * VREG, VREG), :] = wind_coef * jnp.maximum(along, 0.0)
    for v in range(sz.side // VREG):
        rows = table_v[pl.ds(sz.ring + VREG + v * VREG, VREG), :]
        for i in range(2):
            s_moves[3 + i, pl.ds(v * VREG, VREG), :] = jnp.broadcast_to(rows[:, i : i + 1], (VREG, sz.lat))

    def west(source, row, at):
        for first, count in west_half(sz):
            start = row + first * sz.cols + sz.cols - 1
            tmp_thin[pl.ds(at, count), :] = source[pl.ds(start, count, stride=sz.cols), :]
            at += count

    def east(source, row, at):
        start = row + sz.quarter * sz.cols
        tmp_thick[pl.ds(at, sz.half), :] = source[pl.ds(start, sz.half, stride=sz.cols), :]

    for k in range(sz.bands):
        copies[k + 3].wait()
        row = k * sz.ring
        west(field, row, k * sz.half)
        at = k * sz.thick
        tmp_thick[pl.ds(at, sz.angles), :] = field[pl.ds(row, sz.angles, stride=sz.cols), :]
        east(field, row + 1, at + sz.angles)
    for k in range(sz.bands):
        copies[k + 3 + sz.bands].wait()
        row = k * sz.ring
        west(nest_field, row, sz.thin + k * sz.half)
        east(nest_field, row, sz.thick_nest + k * sz.half)
    thin[...] = tmp_thin[...].astype(BF16)
    thick[...] = tmp_thick[...].astype(BF16)


def raw_kernel(sz, energy, raw_a, raw_b):
    for raw, first in ((raw_a, sz.bands - reach - far_band(sz)), (raw_b, far_band(sz))):
        raw[...] = energy[pl.ds(pl.multiple_of(first * sz.ring, VREG), sz.edge_rows), :].astype(BF16)


def spread_halo(sz, wide_w, first_w, wide_e, stride_e, first_e, halo):
    for k in range(sz.bands):
        at = first_w + k * sz.half
        for first, count in west_half(sz):
            start = k * sz.ring + first * sz.cols
            halo[pl.ds(start, count, stride=sz.cols), :] = wide_w[pl.ds(at, count), :]
            at += count
        start = k * sz.ring + (sz.quarter + 1) * sz.cols - 1
        halo[pl.ds(start, sz.half, stride=sz.cols), :] = wide_e[pl.ds(k * stride_e + first_e, sz.half), :]


def fill_moves(sz, rows, table, cols, targets):
    lane = lax.broadcasted_iota(jnp.int32, (VREG, sz.lat), 1)
    sub = lax.broadcasted_iota(jnp.int32, (VREG, sz.lat), 0)
    sec = table[pl.ds(sz.ring, VREG), :]
    for v in range(targets[0].shape[1] // VREG):
        line = table[pl.ds(rows + v * VREG, VREG), :]
        along = jnp.broadcast_to(jnp.abs(line[:, 0:1]), (VREG, sz.lat))
        across = jnp.broadcast_to(jnp.abs(line[:, 1:2]), (VREG, sz.lat))
        edge = lane == jnp.where(sub < sz.half * cols - v * VREG, 0, sz.lat - 1)
        here = pl.ds(v * VREG, VREG)
        for target, by in zip(targets, (along * sec, along)):
            if target is not None:
                target[0, here, :] = by + across
                target[1, here, :] = by
                target[2, here, :] = jnp.where(edge, 0.0, across)


def beside(sz, x, turn):
    if turn >= VREG:
        return pltpu.roll(x, 1, 1)
    if turn <= 0:
        return pltpu.roll(x, sz.lat - 1, 1)
    sub = lax.broadcasted_iota(jnp.int32, (VREG, sz.lat), 0)
    return jnp.where(sub < turn, pltpu.roll(x, 1, 1), pltpu.roll(x, sz.lat - 1, 1))


def transported(sz, field, halo, base, v, moves, speed):
    here = pl.ds(v * VREG, VREG)
    x = field[pl.ds(base + v * VREG, VREG), :]
    wests, west, col = upwind(sz, v)
    if all(wests):
        near, at_edge = pltpu.roll(x, 1, 0), col == 0
    elif not any(wests):
        near, at_edge = pltpu.roll(x, VREG - 1, 0), col == sz.cols - 1
    else:
        near = jnp.where(west, pltpu.roll(x, 1, 0), pltpu.roll(x, VREG - 1, 0))
        at_edge = jnp.where(west, col, sz.cols - 1 - col) == 0
    edge = 0.0 if halo is None else halo[pl.ds(base + v * VREG, VREG), :]
    near = jnp.where(at_edge, edge, near)
    south = sz.half * sz.cols - v * VREG
    return x - speed * (moves[0, here, :] * x - moves[1, here, :] * near - moves[2, here, :] * beside(sz, x, south))


def advect_kernel(
    sz, energy, from_w, from_e, moves, s_moves, sea, adv, side, msg_a, msg_b, part,
    wide_w, wide_e, halo, s_near, totals, fix,
):
    wide_w[...] = from_w[...].astype(F32)
    wide_e[...] = from_e[...].astype(F32)
    spread_halo(sz, wide_w, 0, wide_e, sz.thick, sz.quarter, halo)
    for k in range(sz.bands):
        for first, count in west_half(sz):
            start = k * sz.ring + first * sz.cols + sz.cols - 1
            s_near[pl.ds(k * sz.side + first, count), :] = energy[pl.ds(start, count, stride=sz.cols), :]
        there = pl.ds(k * sz.thick + sz.angles, sz.half)
        s_near[pl.ds(k * sz.side + sz.quarter, sz.half), :] = wide_e[there, :]
        if sz.side > sz.angles:
            rest = sz.side - sz.angles
            s_near[pl.ds(k * sz.side + sz.angles, rest), :] = jnp.zeros((rest, sz.lat), F32)
    s_sea = wide_e[pl.ds(sz.info, 1), :]
    sub = lax.broadcasted_iota(jnp.int32, (VREG, sz.lat), 0)
    totals[...] = jnp.zeros_like(totals)

    def band(k, inverse):
        speed = speed_coef * inverse
        base = pl.multiple_of(k * sz.ring, VREG)
        line = jnp.zeros((VREG, sz.lat), F32)
        for v in range(sz.vregs):
            out = sea[...] * transported(sz, energy, halo, base, v, moves, speed)
            adv[pl.ds(base + v * VREG, VREG), :] = out
            line = line + out
        s_line = jnp.zeros((VREG, sz.lat), F32)
        s_base = pl.multiple_of(k * sz.side, VREG)
        from_base = pl.multiple_of(k * sz.thick, VREG)
        for v in range(sz.side // VREG):
            here = pl.ds(v * VREG, VREG)
            x = wide_e[pl.ds(from_base + v * VREG, VREG), :]
            near = s_near[pl.ds(s_base + v * VREG, VREG), :]
            move = s_moves[0, here, :] * x - s_moves[1, here, :] * near
            move = move - s_moves[2, here, :] * beside(sz, x, sz.half - v * VREG)
            out = s_sea * (x - speed * move)
            side[pl.ds(s_base + v * VREG, VREG), :] = out
            s_line = s_line + jnp.where(sub < sz.angles - v * VREG, out, 0.0)
        totals[0] = totals[0] * F32(1.0 / ratio_step) + line
        totals[1] = totals[1] * F32(1.0 / ratio_step) + s_line

    over_bands(sz.bands, band_ratio(sz, 0, True), band, True)
    weight = 0.1 * band_ratio(sz, sz.bands - 1)
    total, s_total = totals[0] * weight, totals[1] * weight
    sums = total[0 : sz.cols]
    for i in range(1, VREG // sz.cols):
        sums = sums + total[i * sz.cols : (i + 1) * sz.cols]
    s_sum = jnp.sum(s_total, axis=0, keepdims=True)
    sums = jnp.concatenate([sums, s_sum, jnp.zeros((VREG - sz.cols - 1, sz.lat), F32)], axis=0)
    part[...] = sums
    fix[...] = jnp.zeros_like(fix)
    fix[pl.ds(sz.sum_row, 3 * VREG), :] = jnp.concatenate(split3(sums), axis=0)
    for msg, start in ((msg_a, sz.bands - reach - far_band(sz)), (msg_b, far_band(sz))):
        for k in range(reach):
            band_row = pl.multiple_of((start + k) * sz.ring, VREG)
            at = k * sz.far_band
            for first, count in west_half(sz):
                fix[pl.ds(at, count), :] = adv[pl.ds(band_row + first * sz.cols, count, stride=sz.cols), :]
                at += count
            last = band_row + (sz.quarter + 1) * sz.cols - 1
            fix[pl.ds(at, sz.half), :] = adv[pl.ds(last, sz.half, stride=sz.cols), :]
            s_row = pl.multiple_of((start + k) * sz.side, VREG)
            fix[pl.ds(k * sz.far_band + sz.rim_band, sz.side), :] = side[pl.ds(s_row, sz.side), :]
        msg[...] = fix[...].astype(BF16) if msg is msg_a else jnp.concatenate([fix[...], fix[0:16, :]], axis=0).astype(BF16)


def nest_kernel(sz, nest, moves, out):
    def band(k, inverse):
        base = pl.multiple_of(k * sz.ring, VREG)
        for v in range(sz.vregs):
            moved = transported(sz, nest, None, base, v, moves, nest_speedup * speed_coef * inverse)
            out[pl.ds(base + v * VREG, VREG), :] = moved

    over_bands(sz.bands, band_ratio(sz, 0, True), band, True)


def nest_edge_kernel(sz, inner, from_w, from_e, moves, out, wide_w, wide_e):
    grid_rank = lax.axis_index("grid")
    quarter = sz.grid // 4
    keep_w = jnp.where((grid_rank != quarter) & (grid_rank != 3 * quarter), 1.0, 0.0).astype(F32)
    keep_e = jnp.where((grid_rank != quarter - 1) & (grid_rank != 3 * quarter - 1), 1.0, 0.0).astype(F32)
    wide_w[...] = from_w[...].astype(F32)
    wide_e[...] = from_e[...].astype(F32)
    for k in range(sz.bands):
        speed = nest_speedup * speed_coef * band_ratio(sz, k, True)

        def add(first, count, col, wide, at, keep):
            rows = pl.ds(k * sz.ring + first * sz.cols + col, count, stride=sz.cols)
            by = moves[1, pl.ds(first * sz.cols, count, stride=sz.cols), :] * (speed * keep)
            out[rows, :] = out[rows, :] + by * wide[pl.ds(at, count), :]

        at = sz.thin + k * sz.half
        for first, count in west_half(sz):
            add(first, count, 0, wide_w, at, keep_w)
            at += count
        add(sz.quarter, sz.half, sz.cols - 1, wide_e, sz.thick_nest + k * sz.half, keep_e)


def dot_lanes(a, b):
    return lax.dot_general(a, b, (((1,), (1,)), ((), ())), preferred_element_type=F32)


def rim_kernel(sz, cell, dest, target, weight, mix):
    device = lax.broadcasted_iota(jnp.int32, (sz.grid, sz.rim), 0)
    hot = jnp.where(device == dest[...], 1.0, 0.0)
    before = lax.broadcasted_iota(jnp.int32, (sz.rim, sz.rim), 0)
    after = lax.broadcasted_iota(jnp.int32, (sz.rim, sz.rim), 1)
    earlier = jnp.dot(
        hot.astype(BF16), jnp.where(before < after, 1.0, 0.0).astype(BF16), preferred_element_type=F32
    )
    rank = jnp.sum(hot * earlier, axis=0, keepdims=True)
    place = dest[...] * sz.cap + rank.astype(jnp.int32)
    slot = lax.broadcasted_iota(jnp.int32, (sz.slots, sz.rim), 0)
    takes = jnp.where(slot == place, 1.0, 0.0).astype(BF16)
    row = lax.broadcasted_iota(jnp.int32, (sz.lat, sz.rim), 0)
    col = cell[0:1, :] - lax.axis_index("grid") * sz.cols
    south_row = cell[1:2, :]
    ex, ny = weight[0:1, :], weight[1:2, :]
    for c in range(sz.cols + 1):
        share = jnp.where(col == c, 1.0 - ex, 0.0) + jnp.where(col + 1 == c, ex, 0.0)
        south, north = share * (1.0 - ny), share * ny
        corner = jnp.where(row == south_row, south, 0.0) + jnp.where(row == south_row + 1, north, 0.0)
        mix[:, c * sz.lat : (c + 1) * sz.lat] = dot_lanes(takes, corner.astype(BF16)).astype(BF16)
    at = sz.bins - (sz.lanes - 128)
    line = lax.broadcasted_iota(jnp.int32, (128, sz.rim), 0)
    t = target[...]
    t_col = t // sz.lat
    about = jnp.where(line == at, t_col.astype(F32), 0.0)
    about = about + jnp.where(line == at + 1, (t - t_col * sz.lat).astype(F32), 0.0)
    about = about + jnp.where(line == at + 2, weight[2:3, :], 0.0)
    n = (sz.cols + 1) * sz.lat
    mix[:, n : n + 128] = dot_lanes(takes, about.astype(BF16)).astype(BF16)


def low_rows(sz):
    return lax.broadcasted_iota(jnp.int32, (VREG, sz.lat), 0) < VREG // 2


def put(sz, plain, turned, slot, vals):
    nv, low = sz.vregs, low_rows(sz)
    for v in range(nv):
        if plain is not None:
            plain[slot, pl.ds(v * VREG, VREG), :] = vals[v]
        nxt = pltpu.roll(jnp.where(low, vals[(v + 1) % nv], vals[v]), VREG // 2, 0)
        turned[slot, pl.ds((v + 2) * VREG, VREG), :] = nxt
        if v >= nv - 2:
            turned[slot, pl.ds((v + 2 - nv) * VREG, VREG), :] = nxt
        if v == 0:
            turned[slot, pl.ds((nv + 2) * VREG, VREG), :] = nxt


def close(sz, ref, slot):
    ref[slot, pl.ds(VREG - 3, 3), :] = ref[slot, pl.ds(VREG + sz.angles - 3, 3), :]
    ref[slot, pl.ds(VREG + sz.angles, 3), :] = ref[slot, pl.ds(VREG, 3), :]


def s_put(sz, s_plain, slot, load):
    for v in range(sz.side // VREG):
        s_plain[slot, pl.ds((v + 1) * VREG, VREG), :] = load(v)
    close(sz, s_plain, slot)


def exchange(sc, c, up, down):
    return sc * (c * (up + down) - 2.0 * (up * down))


def strengths(sz, ratio, n, plain, turned, plus, minus, s_plain, s_plus, s_minus):
    nv = sz.vregs
    strength = nonlin_coef * ratio
    for v in range(nv):
        c = plain[n + 3, pl.ds(v * VREG, VREG), :]
        sc = strength * c
        for ref, up_row, down_row in ((plus, v + 3, v + 1), (minus, v, v + 2)):
            up = turned[n + 5, pl.ds(up_row * VREG, VREG), :]
            down = turned[n, pl.ds(down_row * VREG, VREG), :]
            delta = exchange(sc, c, up, down)
            ref[n, pl.ds((v + 1) * VREG, VREG), :] = delta
            if v == nv - 1:
                ref[n, pl.ds(0, VREG), :] = delta
            if v < 2:
                ref[n, pl.ds((nv + 1 + v) * VREG, VREG), :] = delta
    for v in range(sz.side // VREG):
        row = (v + 1) * VREG
        c = s_plain[n + 3, pl.ds(row, VREG), :]
        sc = strength * c
        for ref, s in ((s_plus, 1), (s_minus, -1)):
            up = s_plain[n + 5, pl.ds(row + 3 * s, VREG), :]
            down = s_plain[n, pl.ds(row - s, VREG), :]
            ref[n, pl.ds(row, VREG), :] = exchange(sc, c, up, down)
    close(sz, s_plus, n)
    close(sz, s_minus, n)


def is_even():
    return lax.rem(lax.axis_index("spec"), 2) == 0


def complete(sz, slot, fix, k, plain, turned, s_plain, real=None):
    at = k * sz.far_band
    for start, count in west_half(sz):
        plain[slot, pl.ds(start * sz.cols, count, stride=sz.cols), :] = fix[pl.ds(at, count), :]
        at += count
    last = (sz.quarter + 1) * sz.cols - 1
    plain[slot, pl.ds(last, sz.half, stride=sz.cols), :] = fix[pl.ds(at, sz.half), :]
    at = k * sz.far_band + sz.rim_band
    s_put(sz, s_plain, slot, lambda v: fix[pl.ds(at + v * VREG, VREG), :])


def turn_halo(sz, base, plain, turned, real=None):
    def halo(k, carry):
        vals = [plain[base + k, pl.ds(v * VREG, VREG), :] for v in range(sz.vregs)]
        put(sz, None if real is None else plain, turned, base + k, vals if real is None else [x * real for x in vals])
        return carry

    lax.fori_loop(0, reach, halo, 0)


def inner_kernel(
    sz, adv, side, recv_a, raw_a, raw_b, moves, sea, plain, turned, plus, minus, s_plain, s_plus, s_minus, wide, fix
):
    base_a = jnp.where(is_even(), sz.bands + reach, 0)
    base_b = sz.bands + reach - base_a
    below, above = band_ratio(sz, -reach, True), band_ratio(sz, sz.bands, True)

    def own(k, carry):
        base = pl.multiple_of(k * sz.ring, VREG)
        put(sz, plain, turned, k + reach, [adv[pl.ds(base + v * VREG, VREG), :] for v in range(sz.vregs)])
        s_base = pl.multiple_of(k * sz.side, VREG)
        s_put(sz, s_plain, k + reach, lambda v: side[pl.ds(s_base + v * VREG, VREG), :])
        return carry

    lax.fori_loop(0, sz.bands, own, 0)

    for raw, first, inverse in (
        (raw_a, base_a, jnp.where(is_even(), above, below)),
        (raw_b, base_b, jnp.where(is_even(), below, above)),
    ):
        wide[...] = raw[...].astype(F32)

        def transport(k, r, first=first):
            base = pl.multiple_of(k * sz.ring, VREG)
            for v in range(sz.vregs):
                moved = transported(sz, wide, None, base, v, moves, speed_coef * r)
                plain[first + k, pl.ds(v * VREG, VREG), :] = sea[...] * moved

        over_bands(reach, inverse, transport, True)

    fix[...] = recv_a[...].astype(F32)
    for k in range(reach):
        complete(sz, base_a + k, fix, k, plain, turned, s_plain)
    turn_halo(sz, base_a, plain, turned)

    arrays = (plain, turned, plus, minus, s_plain, s_plus, s_minus)
    start = jnp.where(is_even(), reach, 0)
    ratio = jnp.where(is_even(), band_ratio(sz, 3), band_ratio(sz, 3 - reach))
    over_bands(sz.bands, ratio, lambda i, r: strengths(sz, r, start + i, *arrays))


def source_kernel(
    sz, adv, side, recv_b, pair, other, gain, s_moves, from_e, mix,
    plain_in, turned_in, plus_in, minus_in, s_plain_in, s_plus_in, s_minus_in,
    out, msg, plain, turned, plus, minus, s_plain, s_plus, s_minus, s_out, fix,
):
    spec_rank = lax.axis_index("spec")
    nv, ns = sz.vregs, sz.side // VREG
    low, turn = low_rows(sz), VREG // 2
    base_b = jnp.where(is_even(), 0, sz.bands + reach)
    real_b = jnp.where((spec_rank == 0) | (spec_rank == sz.spec - 1), 0.0, 1.0).astype(F32)
    fix[...] = recv_b[...].astype(F32) * real_b
    for k in range(reach):
        complete(sz, base_b + k, fix, k, plain, turned, s_plain)
    turn_halo(sz, base_b, plain, turned, real_b)
    arrays = (plain, turned, plus, minus, s_plain, s_plus, s_minus)
    begin = jnp.where(is_even(), 0, sz.bands)
    ratio = jnp.where(is_even(), band_ratio(sz, 3 - reach), band_ratio(sz, sz.bands + 3 - reach))
    over_bands(reach, ratio, lambda i, r: strengths(sz, r, begin + i, *arrays))

    info = from_e[pl.ds(sz.info // 16 * 16, 32), :].astype(F32)
    at = sz.info % 16 + 1
    s_east = info[at : at + 1] + info[at + 1 : at + 2] + info[at + 2 : at + 3]
    s_north = info[at + 3 : at + 4] + info[at + 4 : at + 5] + info[at + 5 : at + 6]
    total_weight = sz.angles * 0.1 * sum(ratio_step ** (k - sz.freqs // 2) for k in range(sz.freqs))
    means = (pair[...] + other[...]) * (1.0 / total_weight)
    mean = jnp.concatenate([means[0 : sz.cols]] * (VREG // sz.cols), axis=0)
    s_mean = means[sz.cols : sz.cols + 1]

    def result(k, ratio):
        scale = 1.0 / (1.0 + (dissip_coef * ratio * ratio) * mean)
        base = pl.multiple_of(k * sz.ring, VREG)

        def moved_in(v):
            return (
                plus[k, pl.ds(v * VREG, VREG), :]
                + minus[k, pl.ds((v + 3) * VREG, VREG), :]
                + plus[k + 5, pl.ds((v + 2) * VREG, VREG), :]
                + minus[k + 5, pl.ds((v + 1) * VREG, VREG), :]
            )

        before = moved_in(nv - 1)
        for v in range(nv):
            now = moved_in(v)
            moved = pltpu.roll(jnp.where(low, now, before), turn, 0)
            before = now
            here = pl.ds((v + 1) * VREG, VREG)
            transfer = moved - 2.0 * (plus[k + 2, here, :] + minus[k + 2, here, :])
            a = adv[pl.ds(base + v * VREG, VREG), :]
            grown = ratio * gain[pl.ds(v * VREG, VREG), :]
            out[pl.ds(base + v * VREG, VREG), :] = (a + grown * a + transfer) * scale

    over_bands(sz.bands, band_ratio(sz, 0), result)

    s_gain = []
    for v in range(ns):
        here = pl.ds(v * VREG, VREG)
        along = s_moves[3, here, :] * s_east + s_moves[4, here, :] * s_north
        s_gain.append(wind_coef * jnp.maximum(along, 0.0))
    for k in range(sz.bands):
        ratio = band_ratio(sz, k)
        scale = 1.0 / (1.0 + (dissip_coef * ratio * ratio) * s_mean)
        for v in range(ns):
            row = (v + 1) * VREG
            here = pl.ds(row, VREG)
            transfer = (
                s_plus[k, pl.ds(row - 3, VREG), :]
                + s_minus[k, pl.ds(row + 3, VREG), :]
                + s_plus[k + 5, pl.ds(row + 1, VREG), :]
                + s_minus[k + 5, pl.ds(row - 1, VREG), :]
                - 2.0 * (s_plus[k + 2, here, :] + s_minus[k + 2, here, :])
            )
            a = side[pl.ds(k * sz.side + v * VREG, VREG), :]
            s_out[pl.ds(k * sz.angles + v * VREG, VREG), :] = (a + (ratio * s_gain[v]) * a + transfer) * scale

    pad = jnp.zeros((sz.lanes - sz.bins, sz.lat), BF16)
    columns = [out[pl.ds(c, sz.bins, stride=sz.cols), :] for c in range(sz.cols)]
    columns.append(s_out[pl.ds(0, sz.bins), :])
    columns = [jnp.concatenate([c.astype(BF16), pad], axis=0) for c in columns]
    n = (sz.cols + 1) * sz.lat
    spectra = dot_lanes(mix[:, 0:n], jnp.concatenate(columns, axis=1))
    about = mix[:, n : n + 128].astype(F32)
    msg[:, 0 : sz.lanes - 128] = spectra[:, : sz.lanes - 128].astype(BF16)
    msg[:, sz.lanes - 128 : sz.lanes] = (spectra[:, sz.lanes - 128 :] + about).astype(BF16)


def blend_kernel(sz, recv, nest_adv, out):
    spectra = recv[...]
    at = sz.bins - (sz.lanes - 128)
    about = spectra[:, sz.lanes - 128 :].astype(F32)
    t_col, t_row, rate = about[:, at : at + 1], about[:, at + 1 : at + 2], about[:, at + 2 : at + 3]
    lane = lax.broadcasted_iota(jnp.int32, (sz.slots, sz.lat), 1).astype(F32)
    hit = jnp.where(lane == t_row, rate, 0.0)
    for c in range(sz.cols):
        relax = jnp.where(t_col == float(c), hit, 0.0)
        kept = 1.0 - jnp.sum(relax, axis=0, keepdims=True)
        added = lax.dot_general(
            spectra, relax.astype(BF16), (((0,), (0,)), ((), ())), preferred_element_type=F32
        )
        here = pl.ds(c, sz.bins, stride=sz.cols)
        out[here, :] = nest_adv[here, :] * kept + added[: sz.bins]


def kernel_call(body, out_shape, n_in, hbm=(), scratch=(), aliases=None, flops=0, name=None):
    return pl.pallas_call(
        body,
        out_shape=out_shape,
        in_specs=[pl.BlockSpec(memory_space=pltpu.HBM if i in hbm else pltpu.VMEM) for i in range(n_in)],
        out_specs=jax.tree.map(lambda _: pl.BlockSpec(memory_space=pltpu.VMEM), out_shape),
        scratch_shapes=list(scratch),
        input_output_aliases=aliases or {},
        compiler_params=pltpu.CompilerParams(vmem_limit_bytes=20 * 2**20),
        cost_estimate=pl.CostEstimate(flops=flops, bytes_accessed=0, transcendentals=0) if flops else None,
        name=name,
    )


def per_device(
    mesh, energy, nest_energy, ocean_mask, wind_field, rim_cell, rim_dest, rim_target, rim_weight
):
    sz = Sizes(mesh, energy, rim_dest.shape[0])

    def array(*shape, dtype=F32):
        return jax.ShapeDtypeStruct(shape + (sz.lat,), dtype)

    def vmem(*shape):
        return pltpu.VMEM(shape + (sz.lat,), F32)

    def half(rows):
        return array(rows, dtype=BF16)

    field = array(sz.rows)
    table = jnp.asarray(angle_table(sz))
    energy = energy.reshape(sz.rows, sz.lat)
    nest = nest_energy.reshape(sz.rows, sz.lat)
    up = [(i, (i + 1) % sz.grid) for i in range(sz.grid)]
    down = [(j, i) for i, j in up]
    across = [(i, (i + 1 if i % 2 else i - 1) % sz.spec) for i in range(sz.spec)]
    near_rows = [vmem(sz.thin_rows), vmem(sz.thick_rows)]

    stay = functools.partial(pltpu.with_memory_space_constraint, memory_space=pltpu.HBM)
    thin, thick, moves, nest_moves, s_moves, gain, sea = kernel_call(
        functools.partial(pack_kernel, sz),
        (
            half(sz.thin_rows),
            half(sz.thick_rows),
            array(3, sz.ring),
            array(3, sz.ring),
            array(5, sz.side),
            array(sz.ring),
            array(VREG),
        ),
        5,
        hbm=range(5),
        scratch=[
            vmem(*table.shape[:1]),
            vmem(sz.rows),
            vmem(sz.rows),
            pltpu.VMEM(ocean_mask.shape, ocean_mask.dtype),
            pltpu.VMEM(wind_field.shape, F32),
        ]
        + near_rows
        + [pltpu.SemaphoreType.DMA((2 * sz.bands + 3,))],
        name="pack",
    )(stay(table), stay(energy), stay(nest), stay(ocean_mask), stay(wind_field))
    from_e = lax.ppermute(thick, "grid", down)
    from_w = lax.ppermute(thin, "grid", up)

    energy, sea = lax.optimization_barrier((energy, sea))
    raw_a, raw_b = kernel_call(
        functools.partial(raw_kernel, sz), (half(sz.edge_rows), half(sz.edge_rows)), 1, name="raw"
    )(energy)
    pairs = [(i, i ^ 1) for i in range(sz.spec)]
    recv_raw_b = lax.ppermute(raw_b, "spec", [(i, j) for i, j in across if abs(i - j) == 1])
    recv_raw_a = lax.ppermute(raw_a, "spec", pairs)
    rim = (rim_cell.T, rim_dest.T, rim_target.reshape(1, sz.rim), rim_weight.T)
    rim, raw_a = lax.optimization_barrier((rim, raw_a))
    mix = kernel_call(
        functools.partial(rim_kernel, sz),
        jax.ShapeDtypeStruct((sz.slots, (sz.cols + 1) * sz.lat + 128), BF16),
        4,
        name="rim",
    )(*rim)
    nest, raw_a = lax.optimization_barrier((nest, raw_a))
    nest_inner = kernel_call(functools.partial(nest_kernel, sz), field, 2, flops=3 * 10**10, name="nest")(nest, nest_moves)
    from_e, from_w, recv_raw_a, recv_raw_b, mix, nest_inner = lax.optimization_barrier(
        (from_e, from_w, recv_raw_a, recv_raw_b, mix, nest_inner)
    )

    adv, side, msg_a, msg_b, part = kernel_call(
        functools.partial(advect_kernel, sz),
        (field, array(sz.bands * sz.side), half(sz.fix_rows), half(sz.fix_rows + 16), array(VREG)),
        6,
        scratch=near_rows
        + [
            vmem(sz.rows),
            vmem(sz.bands * sz.side),
            vmem(2, VREG),
            vmem(sz.fix_rows),
        ],
        name="advect",
    )(energy, from_w, from_e, moves, s_moves, sea)

    recv_a = lax.ppermute(msg_a, "spec", pairs)
    recv_b = lax.ppermute(msg_b, "spec", across)
    pieces = recv_a[sz.sum_row : sz.sum_row + 3 * VREG].astype(F32)
    pair = part + pieces.reshape(3, VREG, sz.lat).sum(axis=0)
    other = jnp.zeros_like(pair)
    step = 2
    while step < sz.spec:
        pair = pair + other
        other = lax.ppermute(pair, "spec", [(i, i ^ step) for i in range(sz.spec)])
        step *= 2

    nest_adv = kernel_call(
        functools.partial(nest_edge_kernel, sz),
        field,
        4,
        scratch=near_rows,
        aliases={0: 0},
        name="nest_edge",
    )(nest_inner, from_w, from_e, nest_moves)

    padded, centres, turns = sz.bands + 2 * reach, sz.bands + reach, sz.ring + 3 * VREG
    arrays = (
        array(padded, sz.ring),
        array(padded, turns),
        array(centres, turns),
        array(centres, turns),
        array(padded, sz.frame),
        array(centres, sz.frame),
        array(centres, sz.frame),
    )
    inner = kernel_call(
        functools.partial(inner_kernel, sz),
        arrays,
        7,
        scratch=[vmem(sz.edge_rows), vmem(sz.fix_rows)],
        name="inner",
    )(adv, side, recv_a, recv_raw_a, recv_raw_b, moves, sea)
    nest_adv, recv_b = lax.optimization_barrier((nest_adv, recv_b))
    global_next, msg, *_ = kernel_call(
        functools.partial(source_kernel, sz),
        (field, jax.ShapeDtypeStruct((sz.slots, sz.lanes), BF16)) + arrays,
        9 + len(arrays),
        scratch=[vmem(sz.bins + VREG), vmem(sz.fix_rows + 16)],
        aliases={9 + i: 2 + i for i in range(len(arrays))},
        name="sources",
    )(adv, side, recv_b, pair, other, gain, s_moves, from_e, mix, *inner)

    recv = lax.all_to_all(msg, "grid", split_axis=0, concat_axis=0, tiled=True)
    nest_next = kernel_call(functools.partial(blend_kernel, sz), field, 2, name="blend")(recv, nest_adv)
    full = (sz.bands, sz.angles, sz.cols, sz.lat)
    return global_next.reshape(full), nest_next.reshape(full)


def solution(mesh):
    in_specs = (
        P("spec", None, "grid", None),
        P("spec", None, "grid", None),
        P("grid", None),
        P(None, "grid", None),
        P("grid", None),
        P("grid", None),
        P("grid"),
        P("grid", None),
    )
    out_specs = (P("spec", None, "grid", None), P("spec", None, "grid", None))
    return jax.shard_map(
        functools.partial(per_device, mesh),
        mesh=mesh,
        in_specs=in_specs,
        out_specs=out_specs,
        check_vma=False,
    )
```

```python
import functools

import jax
import jax.numpy as jnp
import numpy as np
from jax import lax
from jax.experimental import pallas as pl
from jax.experimental.pallas import tpu as pltpu
from jax.sharding import PartitionSpec as P

ratio_step = 1.1
speed_coef = 0.054
wind_coef = 0.05
dissip_coef = 0.2
nonlin_coef = 0.12
nest_speedup = 2.0
reach = 5

VREG = 8
BF16 = jnp.bfloat16
F32 = jnp.float32


class Sizes:
    def __init__(self, mesh, energy, rim_rows):
        self.grid = mesh.shape["grid"]
        self.spec = mesh.shape["spec"]
        self.bands, self.angles, self.cols, self.lat = energy.shape
        self.freqs = self.bands * self.spec
        self.bins = self.bands * self.angles
        self.ring = self.angles * self.cols
        self.rows = self.bins * self.cols
        self.vregs = self.ring // VREG
        self.rim = rim_rows
        self.cap = max(2, (2 * rim_rows + self.grid - 1) // self.grid)
        self.slots = self.grid * self.cap
        self.lanes = (self.bins + 3 + 127) // 128 * 128
        self.half = self.angles // 2
        self.quarter = self.angles // 4
        self.side = (self.angles + VREG - 1) // VREG * VREG
        self.frame = self.side + 2 * VREG
        self.thin = self.bands * self.half
        self.thin_rows = (2 * self.thin + 15) // 16 * 16
        self.thick = (self.angles + self.half + VREG - 1) // VREG * VREG
        self.info = self.bands * self.thick
        self.thick_nest = (self.info + 7 + VREG - 1) // VREG * VREG
        self.thick_rows = (self.thick_nest + self.thin + 15) // 16 * 16
        self.edge_rows = reach * self.ring
        self.rim_band = 2 * self.half
        self.far_band = self.rim_band + self.angles
        self.sum_row = (reach * self.far_band + VREG - 1) // VREG * VREG
        self.fix_rows = (self.sum_row + 3 * VREG + 15) // 16 * 16
        self.pass_thick = (reach * self.half + VREG - 1) // VREG * VREG
        self.pass_rows = max(self.fix_rows + 16, (self.pass_thick + reach * self.thick + 15) // 16 * 16)


def band_ratio(sz, band, inverse=False):
    rank = lax.axis_index("spec")
    ratio = F32(0.0)
    for s in range(sz.spec):
        power = ratio_step ** (s * sz.bands + band - sz.freqs // 2)
        ratio = jnp.where(rank == s, F32(1.0 / power if inverse else power), ratio)
    return ratio


def over_bands(count, ratio, body, inverse=False):
    step = F32(1.0 / ratio_step if inverse else ratio_step)

    def turn(i, r):
        body(i, r)
        return r * step

    lax.fori_loop(0, count, turn, ratio)


def angle_table(sz):
    heading = 2.0 * np.pi * np.arange(sz.angles) / sz.angles
    table = np.zeros((sz.ring + VREG + sz.side, sz.lat), np.float32)
    table[sz.ring + VREG :][: sz.angles, 0] = np.cos(heading)
    table[sz.ring + VREG :][: sz.angles, 1] = np.sin(heading)
    table[: sz.ring, 0] = np.repeat(np.cos(heading), sz.cols)
    table[: sz.ring, 1] = np.repeat(np.sin(heading), sz.cols)
    degrees = -60.0 + 120.0 * (np.arange(sz.lat) + 0.5) / sz.lat
    table[sz.ring : sz.ring + VREG] = 1.0 / np.cos(degrees * (np.pi / 180.0))
    return table


def from_west(sz, angle):
    return angle < sz.quarter or angle >= 3 * sz.quarter


def split3(x):
    high = x.astype(BF16).astype(F32)
    middle = (x - high).astype(BF16).astype(F32)
    return [high, middle, x - high - middle]


def upwind(sz, v):
    sub = lax.broadcasted_iota(jnp.int32, (VREG, sz.lat), 0)
    first, per = v * VREG // sz.cols, VREG // sz.cols
    wests = [from_west(sz, first + i) for i in range(per)]
    west = sub < 0
    for i in range(per):
        if wests[i]:
            west = west | ((sub >= i * sz.cols) & (sub < (i + 1) * sz.cols))
    return wests, west, sub % sz.cols


def west_half(sz):
    return ((3 * sz.quarter, sz.angles - 3 * sz.quarter), (0, sz.quarter))


def fetch(pairs, sems):
    copies = [pltpu.make_async_copy(a, b, sems.at[i]) for i, (a, b) in enumerate(pairs)]
    for c in copies:
        c.start()
    return copies


def far_band(sz):
    return jnp.where(lax.rem(lax.axis_index("spec"), 2) == 0, 0, sz.bands - reach)


def pack_kernel(
    sz, table, energy, nest, mask, wind,
    thin, thick, moves, nest_moves, s_moves, gain, sea,
    table_v, field, nest_field, mask_v, wind_v, tmp_thin, tmp_thick, sems,
):
    pairs = [(table, table_v), (mask, mask_v), (wind, wind_v), (energy, field), (nest, nest_field)]
    copies = [pltpu.make_async_copy(a, b, sems.at[i]) for i, (a, b) in enumerate(pairs)]
    for copy in copies:
        copy.start()
    rest = sz.thin_rows - 2 * sz.thin
    if rest:
        tmp_thin[pl.ds(2 * sz.thin, rest), :] = jnp.zeros((rest, sz.lat), F32)
    tmp_thick[...] = jnp.zeros_like(tmp_thick)
    for copy in copies[:3]:
        copy.wait()
    info = [mask_v[0:1, :].astype(F32)] + split3(wind_v[0, 0:1, :]) + split3(wind_v[1, 0:1, :])
    for i, line in enumerate(info):
        tmp_thick[pl.ds(sz.info + i, 1), :] = line
    per = VREG // sz.cols
    sea[...] = jnp.concatenate([mask_v[...].astype(F32)] * per, axis=0)
    east_wind = jnp.concatenate([wind_v[0]] * per, axis=0)
    north_wind = jnp.concatenate([wind_v[1]] * per, axis=0)
    fill_moves(sz, 0, table_v, sz.cols, (moves, nest_moves))
    fill_moves(sz, sz.ring + VREG, table_v, 1, (s_moves, None))
    for v in range(sz.vregs):
        rows = table_v[pl.ds(v * VREG, VREG), :]
        along = rows[:, 0:1] * east_wind + rows[:, 1:2] * north_wind
        gain[pl.ds(v * VREG, VREG), :] = wind_coef * jnp.maximum(along, 0.0)
    for v in range(sz.side // VREG):
        rows = table_v[pl.ds(sz.ring + VREG + v * VREG, VREG), :]
        for i in range(2):
            s_moves[3 + i, pl.ds(v * VREG, VREG), :] = jnp.broadcast_to(rows[:, i : i + 1], (VREG, sz.lat))

    def west(source, row, at):
        for first, count in west_half(sz):
            start = row + first * sz.cols + sz.cols - 1
            tmp_thin[pl.ds(at, count), :] = source[pl.ds(start, count, stride=sz.cols), :]
            at += count

    def east(source, row, at):
        start = row + sz.quarter * sz.cols
        tmp_thick[pl.ds(at, sz.half), :] = source[pl.ds(start, sz.half, stride=sz.cols), :]

    copies[3].wait()
    for k in range(sz.bands):
        row = k * sz.ring
        west(field, row, k * sz.half)
        at = k * sz.thick
        tmp_thick[pl.ds(at, sz.angles), :] = field[pl.ds(row, sz.angles, stride=sz.cols), :]
        east(field, row + 1, at + sz.angles)
    copies[4].wait()
    for k in range(sz.bands):
        row = k * sz.ring
        west(nest_field, row, sz.thin + k * sz.half)
        east(nest_field, row, sz.thick_nest + k * sz.half)
    thin[...] = tmp_thin[...].astype(BF16)
    thick[...] = tmp_thick[...].astype(BF16)


def raw_kernel(sz, energy, raw_a, raw_b):
    for raw, first in ((raw_a, sz.bands - reach - far_band(sz)), (raw_b, far_band(sz))):
        raw[...] = energy[pl.ds(pl.multiple_of(first * sz.ring, VREG), sz.edge_rows), :].astype(BF16)


def pass_kernel(sz, from_w, from_e, msg, wide_w, wide_e, tmp):
    wide_w[...] = from_w[...].astype(F32)
    wide_e[...] = from_e[...].astype(F32)
    tmp[...] = jnp.zeros_like(tmp)
    first = far_band(sz)
    count = reach * sz.half
    tmp[pl.ds(0, count), :] = wide_w[pl.ds(first * sz.half, count), :]
    start = pl.multiple_of(first * sz.thick, VREG)
    tmp[pl.ds(sz.pass_thick, reach * sz.thick), :] = wide_e[pl.ds(start, reach * sz.thick), :]
    msg[...] = tmp[...].astype(BF16)


def fill_moves(sz, rows, table, cols, targets):
    lane = lax.broadcasted_iota(jnp.int32, (VREG, sz.lat), 1)
    sub = lax.broadcasted_iota(jnp.int32, (VREG, sz.lat), 0)
    sec = table[pl.ds(sz.ring, VREG), :]
    for v in range(targets[0].shape[1] // VREG):
        line = table[pl.ds(rows + v * VREG, VREG), :]
        along = jnp.broadcast_to(jnp.abs(line[:, 0:1]), (VREG, sz.lat))
        across = jnp.broadcast_to(jnp.abs(line[:, 1:2]), (VREG, sz.lat))
        edge = lane == jnp.where(sub < sz.half * cols - v * VREG, 0, sz.lat - 1)
        here = pl.ds(v * VREG, VREG)
        for target, by in zip(targets, (along * sec, along)):
            if target is not None:
                target[0, here, :] = by + across
                target[1, here, :] = by
                target[2, here, :] = jnp.where(edge, 0.0, across)


def beside(sz, x, turn):
    if turn >= VREG:
        return pltpu.roll(x, 1, 1)
    if turn <= 0:
        return pltpu.roll(x, sz.lat - 1, 1)
    sub = lax.broadcasted_iota(jnp.int32, (VREG, sz.lat), 0)
    return jnp.where(sub < turn, pltpu.roll(x, 1, 1), pltpu.roll(x, sz.lat - 1, 1))


def transported(sz, field, base, v, moves, speed):
    here = pl.ds(v * VREG, VREG)
    x = field[pl.ds(base + v * VREG, VREG), :]
    wests, west, col = upwind(sz, v)
    if all(wests):
        near, at_edge = pltpu.roll(x, 1, 0), col == 0
    elif not any(wests):
        near, at_edge = pltpu.roll(x, VREG - 1, 0), col == sz.cols - 1
    else:
        near = jnp.where(west, pltpu.roll(x, 1, 0), pltpu.roll(x, VREG - 1, 0))
        at_edge = jnp.where(west, col, sz.cols - 1 - col) == 0
    near = jnp.where(at_edge, 0.0, near)
    south = sz.half * sz.cols - v * VREG
    return x - speed * (moves[0, here, :] * x - moves[1, here, :] * near - moves[2, here, :] * beside(sz, x, south))


def edge_parts(sz, moves, wide_w, at_w, wide_e, at_e):
    parts = []
    for first, count in west_half(sz):
        parts.append((first, count, 0, wide_w[pl.ds(at_w, count), :]))
        at_w += count
    parts.append((sz.quarter, sz.half, sz.cols - 1, wide_e[pl.ds(at_e, sz.half), :]))
    for first, count, col, cells in parts:
        yield first, count, col, moves[1, pl.ds(first * sz.cols, count, stride=sz.cols), :] * cells


def side_transported(sz, x, near, v, s_moves, speed):
    here = pl.ds(v * VREG, VREG)
    move = s_moves[0, here, :] * x - s_moves[1, here, :] * near
    return x - speed * (move - s_moves[2, here, :] * beside(sz, x, sz.half - v * VREG))


def local_kernel(sz, energy, moves, sea, adv, total):
    total[...] = jnp.zeros_like(total)

    def band(k, inverse):
        base = pl.multiple_of(k * sz.ring, VREG)
        line = jnp.zeros((VREG, sz.lat), F32)
        for v in range(sz.vregs):
            out = sea[...] * transported(sz, energy, base, v, moves, speed_coef * inverse)
            adv[pl.ds(base + v * VREG, VREG), :] = out
            line = line + out
        total[...] = total[...] * F32(1.0 / ratio_step) + line

    over_bands(sz.bands, band_ratio(sz, 0, True), band, True)
    total[...] = total[...] * (0.1 * band_ratio(sz, sz.bands - 1))


def edge_kernel(
    sz, adv_in, total, energy, from_w, from_e, moves, s_moves, sea, adv, side, msg_a, part,
    wide_w, wide_e, s_near, fix,
):
    wide_w[...] = from_w[...].astype(F32)
    wide_e[...] = from_e[...].astype(F32)
    s_sea = wide_e[pl.ds(sz.info, 1), :]
    sub = lax.broadcasted_iota(jnp.int32, (VREG, sz.lat), 0)
    s_total = jnp.zeros((VREG, sz.lat), F32)
    lines = {}
    for k in range(sz.bands):
        inverse = band_ratio(sz, k, True)
        weight = 0.1 * band_ratio(sz, k)
        speed = speed_coef * inverse
        at_e = k * sz.thick + sz.quarter
        for first, count, col, moved in edge_parts(sz, moves, wide_w, k * sz.half, wide_e, at_e):
            moved = moved * (speed * sea[col : col + 1, :])
            rows = pl.ds(k * sz.ring + first * sz.cols + col, count, stride=sz.cols)
            adv[rows, :] = adv[rows, :] + moved
            lines[first, col] = lines.get((first, col), 0.0) + moved * weight
        at = k * sz.side
        for first, count in west_half(sz):
            start = k * sz.ring + first * sz.cols + sz.cols - 1
            s_near[pl.ds(at + first, count), :] = energy[pl.ds(start, count, stride=sz.cols), :]
        s_near[pl.ds(at + sz.quarter, sz.half), :] = wide_e[pl.ds(k * sz.thick + sz.angles, sz.half), :]
        if sz.side > sz.angles:
            rest = sz.side - sz.angles
            s_near[pl.ds(at + sz.angles, rest), :] = jnp.zeros((rest, sz.lat), F32)
        s_line = jnp.zeros((VREG, sz.lat), F32)
        for v in range(sz.side // VREG):
            x = wide_e[pl.ds(k * sz.thick + v * VREG, VREG), :]
            near = s_near[pl.ds(at + v * VREG, VREG), :]
            out = s_sea * side_transported(sz, x, near, v, s_moves, speed)
            side[pl.ds(at + v * VREG, VREG), :] = out
            s_line = s_line + (out if (v + 1) * VREG <= sz.angles else jnp.where(sub < sz.angles - v * VREG, out, 0.0))
        s_total = s_total + s_line * weight
    mine = total[0 : sz.cols, :]
    for i in range(1, VREG // sz.cols):
        mine = mine + total[i * sz.cols : (i + 1) * sz.cols, :]
    west, east = (
        sum(jnp.sum(x, axis=0, keepdims=True) for (_, c), x in lines.items() if c == col) for col in (0, sz.cols - 1)
    )
    between = jnp.zeros((sz.cols - 2, sz.lat), F32)
    mine = mine + jnp.concatenate([west, between, east], axis=0)
    s_sum = jnp.sum(s_total, axis=0, keepdims=True)
    sums = jnp.concatenate([mine, s_sum, jnp.zeros((VREG - sz.cols - 1, sz.lat), F32)], axis=0)
    part[...] = sums
    fix[...] = jnp.zeros_like(fix)
    fix[pl.ds(sz.sum_row, 3 * VREG), :] = jnp.concatenate(split3(sums), axis=0)
    start = sz.bands - reach - far_band(sz)
    for k in range(reach):
        band_row = pl.multiple_of((start + k) * sz.ring, VREG)
        at = k * sz.far_band
        for first, count in west_half(sz):
            fix[pl.ds(at, count), :] = adv[pl.ds(band_row + first * sz.cols, count, stride=sz.cols), :]
            at += count
        last = band_row + (sz.quarter + 1) * sz.cols - 1
        fix[pl.ds(at, sz.half), :] = adv[pl.ds(last, sz.half, stride=sz.cols), :]
        s_row = pl.multiple_of((start + k) * sz.side, VREG)
        fix[pl.ds(k * sz.far_band + sz.rim_band, sz.angles), :] = side[pl.ds(s_row, sz.angles), :]
    msg_a[...] = fix[...].astype(BF16)


def nest_kernel(sz, nest, moves, out):
    def band(k, inverse):
        base = pl.multiple_of(k * sz.ring, VREG)
        for v in range(sz.vregs):
            moved = transported(sz, nest, base, v, moves, nest_speedup * speed_coef * inverse)
            out[pl.ds(base + v * VREG, VREG), :] = moved

    over_bands(sz.bands, band_ratio(sz, 0, True), band, True)


def nest_edge_kernel(sz, inner, from_w, from_e, moves, out, wide_w, wide_e):
    grid_rank = lax.axis_index("grid")
    quarter = sz.grid // 4
    keep_w = jnp.where((grid_rank != quarter) & (grid_rank != 3 * quarter), 1.0, 0.0).astype(F32)
    keep_e = jnp.where((grid_rank != quarter - 1) & (grid_rank != 3 * quarter - 1), 1.0, 0.0).astype(F32)
    wide_w[...] = from_w[...].astype(F32)
    wide_e[...] = from_e[...].astype(F32)
    for k in range(sz.bands):
        speed = nest_speedup * speed_coef * band_ratio(sz, k, True)
        at_w, at_e = sz.thin + k * sz.half, sz.thick_nest + k * sz.half
        for first, count, col, moved in edge_parts(sz, moves, wide_w, at_w, wide_e, at_e):
            rows = pl.ds(k * sz.ring + first * sz.cols + col, count, stride=sz.cols)
            out[rows, :] = out[rows, :] + moved * (speed * (keep_w if col == 0 else keep_e))


def dot_lanes(a, b):
    return lax.dot_general(a, b, (((1,), (1,)), ((), ())), preferred_element_type=F32)


def rim_kernel(sz, cell, dest, target, weight, mix):
    device = lax.broadcasted_iota(jnp.int32, (sz.grid, sz.rim), 0)
    hot = jnp.where(device == dest[...], 1.0, 0.0)
    before = lax.broadcasted_iota(jnp.int32, (sz.rim, sz.rim), 0)
    after = lax.broadcasted_iota(jnp.int32, (sz.rim, sz.rim), 1)
    earlier = jnp.dot(
        hot.astype(BF16), jnp.where(before < after, 1.0, 0.0).astype(BF16), preferred_element_type=F32
    )
    rank = jnp.sum(hot * earlier, axis=0, keepdims=True)
    place = dest[...] * sz.cap + rank.astype(jnp.int32)
    slot = lax.broadcasted_iota(jnp.int32, (sz.slots, sz.rim), 0)
    takes = jnp.where(slot == place, 1.0, 0.0).astype(BF16)
    row = lax.broadcasted_iota(jnp.int32, (sz.lat, sz.rim), 0)
    col = cell[0:1, :] - lax.axis_index("grid") * sz.cols
    south_row = cell[1:2, :]
    ex, ny = weight[0:1, :], weight[1:2, :]
    for c in range(sz.cols + 1):
        share = jnp.where(col == c, 1.0 - ex, 0.0) + jnp.where(col + 1 == c, ex, 0.0)
        south, north = share * (1.0 - ny), share * ny
        corner = jnp.where(row == south_row, south, 0.0) + jnp.where(row == south_row + 1, north, 0.0)
        mix[:, c * sz.lat : (c + 1) * sz.lat] = dot_lanes(takes, corner.astype(BF16)).astype(BF16)
    at = sz.bins - (sz.lanes - 128)
    line = lax.broadcasted_iota(jnp.int32, (128, sz.rim), 0)
    t = target[...]
    t_col = t // sz.lat
    about = jnp.where(line == at, t_col.astype(F32), 0.0)
    about = about + jnp.where(line == at + 1, (t - t_col * sz.lat).astype(F32), 0.0)
    about = about + jnp.where(line == at + 2, weight[2:3, :], 0.0)
    n = (sz.cols + 1) * sz.lat
    mix[:, n : n + 128] = dot_lanes(takes, about.astype(BF16)).astype(BF16)


def low_rows(sz):
    return lax.broadcasted_iota(jnp.int32, (VREG, sz.lat), 0) < VREG // 2


def put(sz, plain, turned, slot, vals):
    nv, low = sz.vregs, low_rows(sz)
    for v in range(nv):
        if plain is not None:
            plain[slot, pl.ds(v * VREG, VREG), :] = vals[v]
        nxt = pltpu.roll(jnp.where(low, vals[(v + 1) % nv], vals[v]), VREG // 2, 0)
        turned[slot, pl.ds((v + 2) * VREG, VREG), :] = nxt
        if v >= nv - 2:
            turned[slot, pl.ds((v + 2 - nv) * VREG, VREG), :] = nxt
        if v == 0:
            turned[slot, pl.ds((nv + 2) * VREG, VREG), :] = nxt


def close(sz, ref, slot):
    ref[slot, pl.ds(VREG - 3, 3), :] = ref[slot, pl.ds(VREG + sz.angles - 3, 3), :]
    ref[slot, pl.ds(VREG + sz.angles, 3), :] = ref[slot, pl.ds(VREG, 3), :]


def s_put(sz, s_plain, slot, load):
    for v in range(sz.side // VREG):
        s_plain[slot, pl.ds((v + 1) * VREG, VREG), :] = load(v)
    close(sz, s_plain, slot)


def exchange(sc, c, up, down):
    return sc * (c * (up + down) - 2.0 * (up * down))


def strengths(sz, ratio, n, plain, turned, plus, minus, s_plain, s_plus, s_minus):
    nv = sz.vregs
    strength = nonlin_coef * ratio
    for v in range(nv):
        c = plain[n + 3, pl.ds(v * VREG, VREG), :]
        sc = strength * c
        for ref, up_row, down_row in ((plus, v + 3, v + 1), (minus, v, v + 2)):
            up = turned[n + 5, pl.ds(up_row * VREG, VREG), :]
            down = turned[n, pl.ds(down_row * VREG, VREG), :]
            delta = exchange(sc, c, up, down)
            ref[n, pl.ds((v + 1) * VREG, VREG), :] = delta
            if v == nv - 1:
                ref[n, pl.ds(0, VREG), :] = delta
            if v < 2:
                ref[n, pl.ds((nv + 1 + v) * VREG, VREG), :] = delta
    for v in range(sz.side // VREG):
        row = (v + 1) * VREG
        c = s_plain[n + 3, pl.ds(row, VREG), :]
        sc = strength * c
        for ref, s in ((s_plus, 1), (s_minus, -1)):
            up = s_plain[n + 5, pl.ds(row + 3 * s, VREG), :]
            down = s_plain[n, pl.ds(row - s, VREG), :]
            ref[n, pl.ds(row, VREG), :] = exchange(sc, c, up, down)
    close(sz, s_plus, n)
    close(sz, s_minus, n)


def is_even():
    return lax.rem(lax.axis_index("spec"), 2) == 0


def complete(sz, slot, fix, k, plain, s_plain):
    at = k * sz.far_band
    for start, count in west_half(sz):
        plain[slot, pl.ds(start * sz.cols, count, stride=sz.cols), :] = fix[pl.ds(at, count), :]
        at += count
    last = (sz.quarter + 1) * sz.cols - 1
    plain[slot, pl.ds(last, sz.half, stride=sz.cols), :] = fix[pl.ds(at, sz.half), :]
    at = k * sz.far_band + sz.rim_band
    s_put(sz, s_plain, slot, lambda v: fix[pl.ds(at + v * VREG, VREG), :])


def turn_halo(sz, base, plain, turned, real=None):
    def halo(k, carry):
        vals = [plain[base + k, pl.ds(v * VREG, VREG), :] for v in range(sz.vregs)]
        put(sz, None if real is None else plain, turned, base + k, vals if real is None else [x * real for x in vals])
        return carry

    lax.fori_loop(0, reach, halo, 0)


def inner_kernel(
    sz, adv, side, recv_a, raw_a, raw_b, moves, sea, plain, turned, plus, minus, s_plain, s_plus, s_minus, far_near, wide, fix
):
    base_a = jnp.where(is_even(), sz.bands + reach, 0)
    base_b = sz.bands + reach - base_a
    below, above = band_ratio(sz, -reach, True), band_ratio(sz, sz.bands, True)

    def own(k, carry):
        base = pl.multiple_of(k * sz.ring, VREG)
        put(sz, plain, turned, k + reach, [adv[pl.ds(base + v * VREG, VREG), :] for v in range(sz.vregs)])
        s_base = pl.multiple_of(k * sz.side, VREG)
        s_put(sz, s_plain, k + reach, lambda v: side[pl.ds(s_base + v * VREG, VREG), :])
        return carry

    lax.fori_loop(0, sz.bands, own, 0)

    for raw, first, inverse in (
        (raw_a, base_a, jnp.where(is_even(), above, below)),
        (raw_b, base_b, jnp.where(is_even(), below, above)),
    ):
        wide[...] = raw[...].astype(F32)

        def transport(k, r, first=first):
            base = pl.multiple_of(k * sz.ring, VREG)
            for v in range(sz.vregs):
                moved = transported(sz, wide, base, v, moves, speed_coef * r)
                plain[first + k, pl.ds(v * VREG, VREG), :] = sea[...] * moved

        over_bands(reach, inverse, transport, True)

    far_near[...] = jnp.zeros_like(far_near)
    for k in range(reach):
        for first, count in west_half(sz):
            start = k * sz.ring + first * sz.cols + sz.cols - 1
            far_near[pl.ds(k * sz.side + first, count), :] = wide[pl.ds(start, count, stride=sz.cols), :]
    fix[...] = recv_a[...].astype(F32)
    for k in range(reach):
        complete(sz, base_a + k, fix, k, plain, s_plain)
    turn_halo(sz, base_a, plain, turned)

    arrays = (plain, turned, plus, minus, s_plain, s_plus, s_minus)
    start = jnp.where(is_even(), reach, 0)
    ratio = jnp.where(is_even(), band_ratio(sz, 3), band_ratio(sz, 3 - reach))
    over_bands(sz.bands, ratio, lambda i, r: strengths(sz, r, start + i, *arrays))


def source_kernel(
    sz, adv, side, recv_b, pair, other, gain, moves, s_moves, sea, from_e, mix, far_near,
    plain_in, turned_in, plus_in, minus_in, s_plain_in, s_plus_in, s_minus_in,
    result_hbm, msg, plain, turned, plus, minus, s_plain, s_plus, s_minus, s_out, wide, s_near, out, sems,
):
    spec_rank = lax.axis_index("spec")
    nv, ns = sz.vregs, sz.side // VREG
    low, turn = low_rows(sz), VREG // 2
    base_b = jnp.where(is_even(), 0, sz.bands + reach)
    real_b = jnp.where((spec_rank == 0) | (spec_rank == sz.spec - 1), 0.0, 1.0).astype(F32)
    info = from_e[pl.ds(sz.info // 16 * 16, 32), :].astype(F32)
    at = sz.info % 16
    s_sea = info[at : at + 1] * real_b
    wide[...] = recv_b[...].astype(F32)
    s_near[...] = far_near[...]
    inverse = jnp.where(is_even(), band_ratio(sz, -reach, True), band_ratio(sz, sz.bands, True))
    for k in range(reach):
        speed = inverse * (speed_coef / ratio_step**k)
        slot, row = base_b + k, sz.pass_thick + k * sz.thick
        for start, count, col, moved in edge_parts(sz, moves, wide, k * sz.half, wide, row + sz.quarter):
            rows = pl.ds(start * sz.cols + col, count, stride=sz.cols)
            plain[slot, rows, :] = plain[slot, rows, :] + moved * (speed * sea[col : col + 1, :])
        at_near = k * sz.side
        s_near[pl.ds(at_near + sz.quarter, sz.half), :] = wide[pl.ds(row + sz.angles, sz.half), :]

        def column(v):
            x = wide[pl.ds(row + v * VREG, VREG), :]
            near = s_near[pl.ds(at_near + v * VREG, VREG), :]
            return s_sea * side_transported(sz, x, near, v, s_moves, speed)

        s_put(sz, s_plain, slot, column)
    turn_halo(sz, base_b, plain, turned, real_b)
    arrays = (plain, turned, plus, minus, s_plain, s_plus, s_minus)
    begin = jnp.where(is_even(), 0, sz.bands)
    ratio = jnp.where(is_even(), band_ratio(sz, 3 - reach), band_ratio(sz, sz.bands + 3 - reach))
    over_bands(reach, ratio, lambda i, r: strengths(sz, r, begin + i, *arrays))

    at = at + 1
    s_east = info[at : at + 1] + info[at + 1 : at + 2] + info[at + 2 : at + 3]
    s_north = info[at + 3 : at + 4] + info[at + 4 : at + 5] + info[at + 5 : at + 6]
    total_weight = sz.angles * 0.1 * sum(ratio_step ** (k - sz.freqs // 2) for k in range(sz.freqs))
    means = (pair[...] + other[...]) * (1.0 / total_weight)
    mean = jnp.concatenate([means[0 : sz.cols]] * (VREG // sz.cols), axis=0)
    s_mean = means[sz.cols : sz.cols + 1]

    def result(k, ratio):
        scale = 1.0 / (1.0 + (dissip_coef * ratio * ratio) * mean)
        base = pl.multiple_of(k * sz.ring, VREG)

        def moved_in(v):
            return (
                plus[k, pl.ds(v * VREG, VREG), :]
                + minus[k, pl.ds((v + 3) * VREG, VREG), :]
                + plus[k + 5, pl.ds((v + 2) * VREG, VREG), :]
                + minus[k + 5, pl.ds((v + 1) * VREG, VREG), :]
            )

        before = moved_in(nv - 1)
        for v in range(nv):
            now = moved_in(v)
            moved = pltpu.roll(jnp.where(low, now, before), turn, 0)
            before = now
            here = pl.ds((v + 1) * VREG, VREG)
            transfer = moved - 2.0 * (plus[k + 2, here, :] + minus[k + 2, here, :])
            a = adv[pl.ds(base + v * VREG, VREG), :]
            grown = ratio * gain[pl.ds(v * VREG, VREG), :]
            out[pl.ds(base + v * VREG, VREG), :] = (a + grown * a + transfer) * scale
        write(k).start()

    def write(k):
        band = pl.ds(pl.multiple_of(k * sz.ring, VREG), sz.ring)
        return pltpu.make_async_copy(out.at[band], result_hbm.at[band], sems.at[k])

    over_bands(sz.bands, band_ratio(sz, 0), result)

    s_gain = []
    for v in range(ns):
        here = pl.ds(v * VREG, VREG)
        along = s_moves[3, here, :] * s_east + s_moves[4, here, :] * s_north
        s_gain.append(wind_coef * jnp.maximum(along, 0.0))
    for k in range(sz.bands):
        ratio = band_ratio(sz, k)
        scale = 1.0 / (1.0 + (dissip_coef * ratio * ratio) * s_mean)
        for v in range(ns):
            row = (v + 1) * VREG
            here = pl.ds(row, VREG)
            transfer = (
                s_plus[k, pl.ds(row - 3, VREG), :]
                + s_minus[k, pl.ds(row + 3, VREG), :]
                + s_plus[k + 5, pl.ds(row + 1, VREG), :]
                + s_minus[k + 5, pl.ds(row - 1, VREG), :]
                - 2.0 * (s_plus[k + 2, here, :] + s_minus[k + 2, here, :])
            )
            a = side[pl.ds(k * sz.side + v * VREG, VREG), :]
            s_out[pl.ds(k * sz.angles + v * VREG, VREG), :] = (a + (ratio * s_gain[v]) * a + transfer) * scale

    pad = jnp.zeros((sz.lanes - sz.bins, sz.lat), BF16)
    columns = [out[pl.ds(c, sz.bins, stride=sz.cols), :] for c in range(sz.cols)]
    columns.append(s_out[pl.ds(0, sz.bins), :])
    columns = [jnp.concatenate([c.astype(BF16), pad], axis=0) for c in columns]
    n = (sz.cols + 1) * sz.lat
    spectra = dot_lanes(mix[:, 0:n], jnp.concatenate(columns, axis=1))
    about = mix[:, n : n + 128].astype(F32)
    msg[:, 0 : sz.lanes - 128] = spectra[:, : sz.lanes - 128].astype(BF16)
    msg[:, sz.lanes - 128 : sz.lanes] = (spectra[:, sz.lanes - 128 :] + about).astype(BF16)
    for k in range(sz.bands):
        write(k).wait()


def blend_kernel(sz, recv, nest_adv, result_hbm, out, sems):
    at = sz.bins - (sz.lanes - 128)
    about = recv[:, sz.lanes - 128 :].astype(F32)
    t_col, t_row, rate = about[:, at : at + 1], about[:, at + 1 : at + 2], about[:, at + 2 : at + 3]
    lane = lax.broadcasted_iota(jnp.int32, (sz.slots, sz.lat), 1).astype(F32)
    hit = jnp.where(lane == t_row, rate, 0.0)
    relax = [jnp.where(t_col == float(c), hit, 0.0) for c in range(sz.cols)]
    kept = [1.0 - jnp.sum(r, axis=0, keepdims=True) for r in relax]
    relax = jnp.concatenate(relax, axis=1).astype(BF16)
    writes = []
    for part, start in enumerate(range(0, sz.bins, 128)):
        count = min(128, sz.bins - start)
        added = lax.dot_general(
            recv[:, start : start + 128], relax, (((0,), (0,)), ((), ())), preferred_element_type=F32
        )
        for c in range(sz.cols):
            here = pl.ds(start * sz.cols + c, count, stride=sz.cols)
            out[here, :] = nest_adv[here, :] * kept[c] + added[:count, c * sz.lat : (c + 1) * sz.lat]
        rows = pl.ds(start * sz.cols, count * sz.cols)
        writes.append(pltpu.make_async_copy(out.at[rows], result_hbm.at[rows], sems.at[part]))
        writes[-1].start()
    for write in writes:
        write.wait()


def kernel_call(body, out_shape, n_in, hbm=(), out_hbm=(), scratch=(), aliases=None, flops=0, name=None):
    def specs(count, far):
        return [pl.BlockSpec(memory_space=pltpu.HBM if i in far else pltpu.VMEM) for i in range(count)]

    many = isinstance(out_shape, tuple)
    out_specs = specs(len(out_shape) if many else 1, out_hbm)
    return pl.pallas_call(
        body,
        out_shape=out_shape,
        in_specs=specs(n_in, hbm),
        out_specs=out_specs if many else out_specs[0],
        scratch_shapes=list(scratch),
        input_output_aliases=aliases or {},
        compiler_params=pltpu.CompilerParams(vmem_limit_bytes=20 * 2**20),
        cost_estimate=pl.CostEstimate(flops=flops, bytes_accessed=0, transcendentals=0) if flops else None,
        name=name,
    )


def per_device(
    mesh, energy, nest_energy, ocean_mask, wind_field, rim_cell, rim_dest, rim_target, rim_weight
):
    sz = Sizes(mesh, energy, rim_dest.shape[0])

    def array(*shape, dtype=F32):
        return jax.ShapeDtypeStruct(shape + (sz.lat,), dtype)

    def vmem(*shape):
        return pltpu.VMEM(shape + (sz.lat,), F32)

    def half(rows):
        return array(rows, dtype=BF16)

    field = array(sz.rows)
    table = jnp.asarray(angle_table(sz))
    energy = energy.reshape(sz.rows, sz.lat)
    nest = nest_energy.reshape(sz.rows, sz.lat)
    up = [(i, (i + 1) % sz.grid) for i in range(sz.grid)]
    down = [(j, i) for i, j in up]
    across = [(i, (i + 1 if i % 2 else i - 1) % sz.spec) for i in range(sz.spec)]
    near_rows = [vmem(sz.thin_rows), vmem(sz.thick_rows)]

    stay = functools.partial(pltpu.with_memory_space_constraint, memory_space=pltpu.HBM)
    thin, thick, moves, nest_moves, s_moves, gain, sea = kernel_call(
        functools.partial(pack_kernel, sz),
        (
            half(sz.thin_rows),
            half(sz.thick_rows),
            array(3, sz.ring),
            array(3, sz.ring),
            array(5, sz.side),
            array(sz.ring),
            array(VREG),
        ),
        5,
        hbm=range(5),
        scratch=[
            vmem(*table.shape[:1]),
            vmem(sz.rows),
            vmem(sz.rows),
            pltpu.VMEM(ocean_mask.shape, ocean_mask.dtype),
            pltpu.VMEM(wind_field.shape, F32),
        ]
        + near_rows
        + [pltpu.SemaphoreType.DMA((5,))],
        name="pack",
    )(stay(table), stay(energy), stay(nest), stay(ocean_mask), stay(wind_field))
    from_e = lax.ppermute(thick, "grid", down)
    from_w = lax.ppermute(thin, "grid", up)

    energy, sea = lax.optimization_barrier((energy, sea))
    raw_a, raw_b = kernel_call(
        functools.partial(raw_kernel, sz), (half(sz.edge_rows), half(sz.edge_rows)), 1, name="raw"
    )(energy)
    pairs = [(i, i ^ 1) for i in range(sz.spec)]
    recv_raw_b = lax.ppermute(raw_b, "spec", [(i, j) for i, j in across if abs(i - j) == 1])
    recv_raw_a = lax.ppermute(raw_a, "spec", pairs)
    rim = (rim_cell.T, rim_dest.T, rim_target.reshape(1, sz.rim), rim_weight.T)
    rim, raw_a = lax.optimization_barrier((rim, raw_a))
    mix = kernel_call(
        functools.partial(rim_kernel, sz),
        jax.ShapeDtypeStruct((sz.slots, (sz.cols + 1) * sz.lat + 128), BF16),
        4,
        name="rim",
    )(*rim)
    nest, raw_a = lax.optimization_barrier((nest, raw_a))
    nest_inner = kernel_call(functools.partial(nest_kernel, sz), field, 2, flops=3 * 10**10, name="nest")(nest, nest_moves)
    energy, raw_a = lax.optimization_barrier((energy, raw_a))
    adv, total = kernel_call(
        functools.partial(local_kernel, sz), (field, array(VREG)), 3, flops=3 * 10**10, name="local"
    )(energy, moves, sea)
    from_e, from_w, mix, nest_inner, adv = lax.optimization_barrier((from_e, from_w, mix, nest_inner, adv))

    msg_b = kernel_call(
        functools.partial(pass_kernel, sz),
        half(sz.pass_rows),
        2,
        scratch=near_rows + [vmem(sz.pass_rows)],
        name="pass",
    )(from_w, from_e)
    adv, side, msg_a, part = kernel_call(
        functools.partial(edge_kernel, sz),
        (field, array(sz.bands * sz.side), half(sz.fix_rows), array(VREG)),
        8,
        scratch=near_rows + [vmem(sz.bands * sz.side), vmem(sz.fix_rows)],
        aliases={0: 0},
        flops=3 * 10**10,
        name="edges",
    )(adv, total, energy, from_w, from_e, moves, s_moves, sea)

    msg_a, msg_b, recv_raw_a, recv_raw_b = lax.optimization_barrier((msg_a, msg_b, recv_raw_a, recv_raw_b))
    recv_a = lax.ppermute(msg_a, "spec", pairs)
    recv_b = lax.ppermute(msg_b, "spec", across)
    pieces = recv_a[sz.sum_row : sz.sum_row + 3 * VREG].astype(F32)
    pair = part + pieces.reshape(3, VREG, sz.lat).sum(axis=0)
    other = jnp.zeros_like(pair)
    step = 2
    while step < sz.spec:
        pair = pair + other
        other = lax.ppermute(pair, "spec", [(i, i ^ step) for i in range(sz.spec)])
        step *= 2

    nest_adv = kernel_call(
        functools.partial(nest_edge_kernel, sz),
        field,
        4,
        scratch=near_rows,
        aliases={0: 0},
        name="nest_edge",
    )(nest_inner, from_w, from_e, nest_moves)

    padded, centres, turns = sz.bands + 2 * reach, sz.bands + reach, sz.ring + 3 * VREG
    arrays = (
        array(padded, sz.ring),
        array(padded, turns),
        array(centres, turns),
        array(centres, turns),
        array(padded, sz.frame),
        array(centres, sz.frame),
        array(centres, sz.frame),
    )
    *inner, far_near = kernel_call(
        functools.partial(inner_kernel, sz),
        arrays + (array(reach * sz.side),),
        7,
        scratch=[vmem(sz.edge_rows), vmem(sz.fix_rows)],
        name="inner",
    )(adv, side, recv_a, recv_raw_a, recv_raw_b, moves, sea)
    nest_adv, recv_b = lax.optimization_barrier((nest_adv, recv_b))
    global_next, msg, *_ = kernel_call(
        functools.partial(source_kernel, sz),
        (field, jax.ShapeDtypeStruct((sz.slots, sz.lanes), BF16)) + arrays,
        12 + len(arrays),
        scratch=[vmem(sz.bins + VREG), vmem(sz.pass_rows), vmem(reach * sz.side), vmem(sz.rows), pltpu.SemaphoreType.DMA((sz.bands,))],
        out_hbm=(0,),
        aliases={12 + i: 2 + i for i in range(len(arrays))},
        name="sources",
    )(adv, side, recv_b, pair, other, gain, moves, s_moves, sea, from_e, mix, far_near, *inner)

    recv = lax.all_to_all(msg, "grid", split_axis=0, concat_axis=0, tiled=True)
    nest_next = kernel_call(
        functools.partial(blend_kernel, sz),
        field,
        2,
        out_hbm=(0,),
        scratch=[vmem(sz.rows), pltpu.SemaphoreType.DMA((sz.lanes // 128,))],
        name="blend",
    )(recv, nest_adv)
    full = (sz.bands, sz.angles, sz.cols, sz.lat)
    return global_next.reshape(full), nest_next.reshape(full)


def solution(mesh):
    in_specs = (
        P("spec", None, "grid", None),
        P("spec", None, "grid", None),
        P("grid", None),
        P(None, "grid", None),
        P("grid", None),
        P("grid", None),
        P("grid"),
        P("grid", None),
    )
    out_specs = (P("spec", None, "grid", None), P("spec", None, "grid", None))
    return jax.shard_map(
        functools.partial(per_device, mesh),
        mesh=mesh,
        in_specs=in_specs,
        out_specs=out_specs,
        check_vma=False,
    )
```

```python
import functools

import jax
import jax.numpy as jnp
import numpy as np
from jax import lax
from jax.experimental import pallas as pl
from jax.experimental.pallas import tpu as pltpu
from jax.sharding import PartitionSpec as P

ratio_step = 1.1
speed_coef = 0.054
wind_coef = 0.05
dissip_coef = 0.2
nonlin_coef = 0.12
nest_speedup = 2.0
reach = 5

VREG = 8
BF16 = jnp.bfloat16
F32 = jnp.float32


class Sizes:
    def __init__(self, mesh, energy, rim_rows):
        self.grid = mesh.shape["grid"]
        self.spec = mesh.shape["spec"]
        self.bands, self.angles, self.cols, self.lat = energy.shape
        self.freqs = self.bands * self.spec
        self.bins = self.bands * self.angles
        self.ring = self.angles * self.cols
        self.rows = self.bins * self.cols
        self.vregs = self.ring // VREG
        self.rim = rim_rows
        self.cap = max(2, (2 * rim_rows + self.grid - 1) // self.grid)
        self.slots = self.grid * self.cap
        self.lanes = (self.bins + 3 + 127) // 128 * 128
        self.half = self.angles // 2
        self.quarter = self.angles // 4
        self.side = (self.angles + VREG - 1) // VREG * VREG
        self.frame = self.side + 2 * VREG
        self.thin = self.bands * self.half
        self.thin_rows = (2 * self.thin + 15) // 16 * 16
        self.thick = (self.angles + self.half + VREG - 1) // VREG * VREG
        self.info = self.bands * self.thick
        self.thick_nest = (self.info + 7 + VREG - 1) // VREG * VREG
        self.thick_rows = (self.thick_nest + self.thin + 15) // 16 * 16
        self.edge_rows = reach * self.ring
        self.rim_band = 2 * self.half
        self.far_band = self.rim_band + self.angles
        self.sum_row = (reach * self.far_band + VREG - 1) // VREG * VREG
        self.fix_rows = (self.sum_row + 3 * VREG + 15) // 16 * 16
        self.pass_thick = (reach * self.half + VREG - 1) // VREG * VREG
        self.pass_rows = max(self.fix_rows + 16, (self.pass_thick + reach * self.thick + 15) // 16 * 16)


def band_ratio(sz, band, inverse=False):
    rank = lax.axis_index("spec")
    ratio = F32(0.0)
    for s in range(sz.spec):
        power = ratio_step ** (s * sz.bands + band - sz.freqs // 2)
        ratio = jnp.where(rank == s, F32(1.0 / power if inverse else power), ratio)
    return ratio


def over_bands(count, ratio, body, inverse=False):
    step = F32(1.0 / ratio_step if inverse else ratio_step)

    def turn(i, r):
        body(i, r)
        return r * step

    lax.fori_loop(0, count, turn, ratio)


def angle_table(sz):
    heading = 2.0 * np.pi * np.arange(sz.angles) / sz.angles
    table = np.zeros((sz.ring + VREG + sz.side, sz.lat), np.float32)
    table[sz.ring + VREG :][: sz.angles, 0] = np.cos(heading)
    table[sz.ring + VREG :][: sz.angles, 1] = np.sin(heading)
    table[: sz.ring, 0] = np.repeat(np.cos(heading), sz.cols)
    table[: sz.ring, 1] = np.repeat(np.sin(heading), sz.cols)
    degrees = -60.0 + 120.0 * (np.arange(sz.lat) + 0.5) / sz.lat
    table[sz.ring : sz.ring + VREG] = 1.0 / np.cos(degrees * (np.pi / 180.0))
    return table


def from_west(sz, angle):
    return angle < sz.quarter or angle >= 3 * sz.quarter


def split3(x):
    high = x.astype(BF16).astype(F32)
    middle = (x - high).astype(BF16).astype(F32)
    return [high, middle, x - high - middle]


def upwind(sz, v):
    sub = lax.broadcasted_iota(jnp.int32, (VREG, sz.lat), 0)
    first, per = v * VREG // sz.cols, VREG // sz.cols
    wests = [from_west(sz, first + i) for i in range(per)]
    west = sub < 0
    for i in range(per):
        if wests[i]:
            west = west | ((sub >= i * sz.cols) & (sub < (i + 1) * sz.cols))
    return wests, west, sub % sz.cols


def west_half(sz):
    return ((3 * sz.quarter, sz.angles - 3 * sz.quarter), (0, sz.quarter))


def fetch(pairs, sems):
    copies = [pltpu.make_async_copy(a, b, sems.at[i]) for i, (a, b) in enumerate(pairs)]
    for c in copies:
        c.start()
    return copies


def far_band(sz):
    return jnp.where(lax.rem(lax.axis_index("spec"), 2) == 0, 0, sz.bands - reach)


def pack_kernel(
    sz, table, energy, nest, mask, wind,
    thin, thick, moves, nest_moves, s_moves, gain, sea,
    table_v, field, nest_field, mask_v, wind_v, tmp_thin, tmp_thick, sems,
):
    pairs = [(table, table_v), (mask, mask_v), (wind, wind_v), (energy, field), (nest, nest_field)]
    copies = [pltpu.make_async_copy(a, b, sems.at[i]) for i, (a, b) in enumerate(pairs)]
    for copy in copies:
        copy.start()
    rest = sz.thin_rows - 2 * sz.thin
    if rest:
        tmp_thin[pl.ds(2 * sz.thin, rest), :] = jnp.zeros((rest, sz.lat), F32)
    tmp_thick[...] = jnp.zeros_like(tmp_thick)
    for copy in copies[:3]:
        copy.wait()
    info = [mask_v[0:1, :].astype(F32)] + split3(wind_v[0, 0:1, :]) + split3(wind_v[1, 0:1, :])
    for i, line in enumerate(info):
        tmp_thick[pl.ds(sz.info + i, 1), :] = line
    per = VREG // sz.cols
    sea[...] = jnp.concatenate([mask_v[...].astype(F32)] * per, axis=0)
    east_wind = jnp.concatenate([wind_v[0]] * per, axis=0)
    north_wind = jnp.concatenate([wind_v[1]] * per, axis=0)
    fill_moves(sz, 0, table_v, sz.cols, (moves, nest_moves))
    fill_moves(sz, sz.ring + VREG, table_v, 1, (s_moves, None))
    for v in range(sz.vregs):
        rows = table_v[pl.ds(v * VREG, VREG), :]
        along = rows[:, 0:1] * east_wind + rows[:, 1:2] * north_wind
        gain[pl.ds(v * VREG, VREG), :] = wind_coef * jnp.maximum(along, 0.0)
    for v in range(sz.side // VREG):
        rows = table_v[pl.ds(sz.ring + VREG + v * VREG, VREG), :]
        for i in range(2):
            s_moves[3 + i, pl.ds(v * VREG, VREG), :] = jnp.broadcast_to(rows[:, i : i + 1], (VREG, sz.lat))

    def west(source, row, at):
        for first, count in west_half(sz):
            start = row + first * sz.cols + sz.cols - 1
            tmp_thin[pl.ds(at, count), :] = source[pl.ds(start, count, stride=sz.cols), :]
            at += count

    def east(source, row, at):
        start = row + sz.quarter * sz.cols
        tmp_thick[pl.ds(at, sz.half), :] = source[pl.ds(start, sz.half, stride=sz.cols), :]

    copies[3].wait()
    for k in range(sz.bands):
        row = k * sz.ring
        west(field, row, k * sz.half)
        at = k * sz.thick
        tmp_thick[pl.ds(at, sz.angles), :] = field[pl.ds(row, sz.angles, stride=sz.cols), :]
        east(field, row + 1, at + sz.angles)
    copies[4].wait()
    for k in range(sz.bands):
        row = k * sz.ring
        west(nest_field, row, sz.thin + k * sz.half)
        east(nest_field, row, sz.thick_nest + k * sz.half)
    thin[...] = tmp_thin[...].astype(BF16)
    thick[...] = tmp_thick[...].astype(BF16)


def raw_kernel(sz, energy, raw_a, raw_b):
    for raw, first in ((raw_a, sz.bands - reach - far_band(sz)), (raw_b, far_band(sz))):
        raw[...] = energy[pl.ds(pl.multiple_of(first * sz.ring, VREG), sz.edge_rows), :].astype(BF16)


def pass_kernel(sz, from_w, from_e, msg, wide_w, wide_e, tmp):
    wide_w[...] = from_w[...].astype(F32)
    wide_e[...] = from_e[...].astype(F32)
    tmp[...] = jnp.zeros_like(tmp)
    first = far_band(sz)
    count = reach * sz.half
    tmp[pl.ds(0, count), :] = wide_w[pl.ds(first * sz.half, count), :]
    start = pl.multiple_of(first * sz.thick, VREG)
    tmp[pl.ds(sz.pass_thick, reach * sz.thick), :] = wide_e[pl.ds(start, reach * sz.thick), :]
    msg[...] = tmp[...].astype(BF16)


def fill_moves(sz, rows, table, cols, targets):
    lane = lax.broadcasted_iota(jnp.int32, (VREG, sz.lat), 1)
    sub = lax.broadcasted_iota(jnp.int32, (VREG, sz.lat), 0)
    sec = table[pl.ds(sz.ring, VREG), :]
    for v in range(targets[0].shape[1] // VREG):
        line = table[pl.ds(rows + v * VREG, VREG), :]
        along = jnp.broadcast_to(jnp.abs(line[:, 0:1]), (VREG, sz.lat))
        across = jnp.broadcast_to(jnp.abs(line[:, 1:2]), (VREG, sz.lat))
        edge = lane == jnp.where(sub < sz.half * cols - v * VREG, 0, sz.lat - 1)
        here = pl.ds(v * VREG, VREG)
        for target, by in zip(targets, (along * sec, along)):
            if target is not None:
                target[0, here, :] = by + across
                target[1, here, :] = by
                target[2, here, :] = jnp.where(edge, 0.0, across)


def beside(sz, x, turn):
    if turn >= VREG:
        return pltpu.roll(x, 1, 1)
    if turn <= 0:
        return pltpu.roll(x, sz.lat - 1, 1)
    sub = lax.broadcasted_iota(jnp.int32, (VREG, sz.lat), 0)
    return jnp.where(sub < turn, pltpu.roll(x, 1, 1), pltpu.roll(x, sz.lat - 1, 1))


def transported(sz, field, base, v, moves, speed):
    here = pl.ds(v * VREG, VREG)
    x = field[pl.ds(base + v * VREG, VREG), :]
    wests, west, col = upwind(sz, v)
    if all(wests):
        near, at_edge = pltpu.roll(x, 1, 0), col == 0
    elif not any(wests):
        near, at_edge = pltpu.roll(x, VREG - 1, 0), col == sz.cols - 1
    else:
        near = jnp.where(west, pltpu.roll(x, 1, 0), pltpu.roll(x, VREG - 1, 0))
        at_edge = jnp.where(west, col, sz.cols - 1 - col) == 0
    near = jnp.where(at_edge, 0.0, near)
    south = sz.half * sz.cols - v * VREG
    return x - speed * (moves[0, here, :] * x - moves[1, here, :] * near - moves[2, here, :] * beside(sz, x, south))


def edge_parts(sz, moves, wide_w, at_w, wide_e, at_e):
    parts = []
    for first, count in west_half(sz):
        parts.append((first, count, 0, wide_w[pl.ds(at_w, count), :]))
        at_w += count
    parts.append((sz.quarter, sz.half, sz.cols - 1, wide_e[pl.ds(at_e, sz.half), :]))
    for first, count, col, cells in parts:
        yield first, count, col, moves[1, pl.ds(first * sz.cols, count, stride=sz.cols), :] * cells


def side_transported(sz, x, near, v, s_moves, speed):
    here = pl.ds(v * VREG, VREG)
    move = s_moves[0, here, :] * x - s_moves[1, here, :] * near
    return x - speed * (move - s_moves[2, here, :] * beside(sz, x, sz.half - v * VREG))


def local_kernel(sz, energy, moves, sea, adv, total):
    total[...] = jnp.zeros_like(total)

    def band(k, inverse):
        base = pl.multiple_of(k * sz.ring, VREG)
        line = jnp.zeros((VREG, sz.lat), F32)
        for v in range(sz.vregs):
            out = sea[...] * transported(sz, energy, base, v, moves, speed_coef * inverse)
            adv[pl.ds(base + v * VREG, VREG), :] = out
            line = line + out
        total[...] = total[...] * F32(1.0 / ratio_step) + line

    over_bands(sz.bands, band_ratio(sz, 0, True), band, True)
    total[...] = total[...] * (0.1 * band_ratio(sz, sz.bands - 1))


def edge_kernel(
    sz, adv_in, total, energy, from_w, from_e, moves, s_moves, sea, adv, side, msg_a, part,
    wide_w, wide_e, s_near, fix,
):
    wide_w[...] = from_w[...].astype(F32)
    wide_e[...] = from_e[...].astype(F32)
    s_sea = wide_e[pl.ds(sz.info, 1), :]
    sub = lax.broadcasted_iota(jnp.int32, (VREG, sz.lat), 0)
    s_total = jnp.zeros((VREG, sz.lat), F32)
    lines = {}
    for k in range(sz.bands):
        inverse = band_ratio(sz, k, True)
        weight = 0.1 * band_ratio(sz, k)
        speed = speed_coef * inverse
        at_e = k * sz.thick + sz.quarter
        for first, count, col, moved in edge_parts(sz, moves, wide_w, k * sz.half, wide_e, at_e):
            moved = moved * (speed * sea[col : col + 1, :])
            rows = pl.ds(k * sz.ring + first * sz.cols + col, count, stride=sz.cols)
            adv[rows, :] = adv[rows, :] + moved
            lines[first, col] = lines.get((first, col), 0.0) + moved * weight
        at = k * sz.side
        for first, count in west_half(sz):
            start = k * sz.ring + first * sz.cols + sz.cols - 1
            s_near[pl.ds(at + first, count), :] = energy[pl.ds(start, count, stride=sz.cols), :]
        s_near[pl.ds(at + sz.quarter, sz.half), :] = wide_e[pl.ds(k * sz.thick + sz.angles, sz.half), :]
        if sz.side > sz.angles:
            rest = sz.side - sz.angles
            s_near[pl.ds(at + sz.angles, rest), :] = jnp.zeros((rest, sz.lat), F32)
        s_line = jnp.zeros((VREG, sz.lat), F32)
        for v in range(sz.side // VREG):
            x = wide_e[pl.ds(k * sz.thick + v * VREG, VREG), :]
            near = s_near[pl.ds(at + v * VREG, VREG), :]
            out = s_sea * side_transported(sz, x, near, v, s_moves, speed)
            side[pl.ds(at + v * VREG, VREG), :] = out
            s_line = s_line + (out if (v + 1) * VREG <= sz.angles else jnp.where(sub < sz.angles - v * VREG, out, 0.0))
        s_total = s_total + s_line * weight
    mine = total[0 : sz.cols, :]
    for i in range(1, VREG // sz.cols):
        mine = mine + total[i * sz.cols : (i + 1) * sz.cols, :]
    west, east = (
        sum(jnp.sum(x, axis=0, keepdims=True) for (_, c), x in lines.items() if c == col) for col in (0, sz.cols - 1)
    )
    between = jnp.zeros((sz.cols - 2, sz.lat), F32)
    mine = mine + jnp.concatenate([west, between, east], axis=0)
    s_sum = jnp.sum(s_total, axis=0, keepdims=True)
    sums = jnp.concatenate([mine, s_sum, jnp.zeros((VREG - sz.cols - 1, sz.lat), F32)], axis=0)
    part[...] = sums
    fix[...] = jnp.zeros_like(fix)
    fix[pl.ds(sz.sum_row, 3 * VREG), :] = jnp.concatenate(split3(sums), axis=0)
    start = sz.bands - reach - far_band(sz)
    for k in range(reach):
        band_row = pl.multiple_of((start + k) * sz.ring, VREG)
        at = k * sz.far_band
        for first, count in west_half(sz):
            fix[pl.ds(at, count), :] = adv[pl.ds(band_row + first * sz.cols, count, stride=sz.cols), :]
            at += count
        last = band_row + (sz.quarter + 1) * sz.cols - 1
        fix[pl.ds(at, sz.half), :] = adv[pl.ds(last, sz.half, stride=sz.cols), :]
        s_row = pl.multiple_of((start + k) * sz.side, VREG)
        fix[pl.ds(k * sz.far_band + sz.rim_band, sz.angles), :] = side[pl.ds(s_row, sz.angles), :]
    msg_a[...] = fix[...].astype(BF16)


def nest_kernel(sz, nest, moves, out):
    def band(k, inverse):
        base = pl.multiple_of(k * sz.ring, VREG)
        for v in range(sz.vregs):
            moved = transported(sz, nest, base, v, moves, nest_speedup * speed_coef * inverse)
            out[pl.ds(base + v * VREG, VREG), :] = moved

    over_bands(sz.bands, band_ratio(sz, 0, True), band, True)


def nest_edge_kernel(sz, inner, from_w, from_e, moves, out, wide_w, wide_e):
    grid_rank = lax.axis_index("grid")
    quarter = sz.grid // 4
    keep_w = jnp.where((grid_rank != quarter) & (grid_rank != 3 * quarter), 1.0, 0.0).astype(F32)
    keep_e = jnp.where((grid_rank != quarter - 1) & (grid_rank != 3 * quarter - 1), 1.0, 0.0).astype(F32)
    wide_w[...] = from_w[...].astype(F32)
    wide_e[...] = from_e[...].astype(F32)
    for k in range(sz.bands):
        speed = nest_speedup * speed_coef * band_ratio(sz, k, True)
        at_w, at_e = sz.thin + k * sz.half, sz.thick_nest + k * sz.half
        for first, count, col, moved in edge_parts(sz, moves, wide_w, at_w, wide_e, at_e):
            rows = pl.ds(k * sz.ring + first * sz.cols + col, count, stride=sz.cols)
            out[rows, :] = out[rows, :] + moved * (speed * (keep_w if col == 0 else keep_e))


def dot_lanes(a, b):
    return lax.dot_general(a, b, (((1,), (1,)), ((), ())), preferred_element_type=F32)


def rim_kernel(sz, cell, dest, target, weight, mix):
    device = lax.broadcasted_iota(jnp.int32, (sz.grid, sz.rim), 0)
    hot = jnp.where(device == dest[...], 1.0, 0.0)
    before = lax.broadcasted_iota(jnp.int32, (sz.rim, sz.rim), 0)
    after = lax.broadcasted_iota(jnp.int32, (sz.rim, sz.rim), 1)
    earlier = jnp.dot(
        hot.astype(BF16), jnp.where(before < after, 1.0, 0.0).astype(BF16), preferred_element_type=F32
    )
    rank = jnp.sum(hot * earlier, axis=0, keepdims=True)
    place = dest[...] * sz.cap + rank.astype(jnp.int32)
    slot = lax.broadcasted_iota(jnp.int32, (sz.slots, sz.rim), 0)
    takes = jnp.where(slot == place, 1.0, 0.0).astype(BF16)
    row = lax.broadcasted_iota(jnp.int32, (sz.lat, sz.rim), 0)
    col = cell[0:1, :] - lax.axis_index("grid") * sz.cols
    south_row = cell[1:2, :]
    ex, ny = weight[0:1, :], weight[1:2, :]
    for c in range(sz.cols + 1):
        share = jnp.where(col == c, 1.0 - ex, 0.0) + jnp.where(col + 1 == c, ex, 0.0)
        south, north = share * (1.0 - ny), share * ny
        corner = jnp.where(row == south_row, south, 0.0) + jnp.where(row == south_row + 1, north, 0.0)
        mix[:, c * sz.lat : (c + 1) * sz.lat] = dot_lanes(takes, corner.astype(BF16)).astype(BF16)
    at = sz.bins - (sz.lanes - 128)
    line = lax.broadcasted_iota(jnp.int32, (128, sz.rim), 0)
    t = target[...]
    t_col = t // sz.lat
    about = jnp.where(line == at, t_col.astype(F32), 0.0)
    about = about + jnp.where(line == at + 1, (t - t_col * sz.lat).astype(F32), 0.0)
    about = about + jnp.where(line == at + 2, weight[2:3, :], 0.0)
    n = (sz.cols + 1) * sz.lat
    mix[:, n : n + 128] = dot_lanes(takes, about.astype(BF16)).astype(BF16)


def low_rows(sz):
    return lax.broadcasted_iota(jnp.int32, (VREG, sz.lat), 0) < VREG // 2


def put(sz, plain, turned, slot, vals):
    nv, low = sz.vregs, low_rows(sz)
    for v in range(nv):
        if plain is not None:
            plain[slot, pl.ds(v * VREG, VREG), :] = vals[v]
        nxt = pltpu.roll(jnp.where(low, vals[(v + 1) % nv], vals[v]), VREG // 2, 0)
        turned[slot, pl.ds((v + 2) * VREG, VREG), :] = nxt
        if v >= nv - 2:
            turned[slot, pl.ds((v + 2 - nv) * VREG, VREG), :] = nxt
        if v == 0:
            turned[slot, pl.ds((nv + 2) * VREG, VREG), :] = nxt


def close(sz, ref, slot):
    ref[slot, pl.ds(VREG - 3, 3), :] = ref[slot, pl.ds(VREG + sz.angles - 3, 3), :]
    ref[slot, pl.ds(VREG + sz.angles, 3), :] = ref[slot, pl.ds(VREG, 3), :]


def s_put(sz, s_plain, slot, load):
    for v in range(sz.side // VREG):
        s_plain[slot, pl.ds((v + 1) * VREG, VREG), :] = load(v)
    close(sz, s_plain, slot)


def exchange(sc, c, up, down):
    return sc * (c * (up + down) - 2.0 * (up * down))


def strengths(sz, ratio, n, plain, turned, plus, minus, s_plain, s_plus, s_minus):
    nv = sz.vregs
    strength = nonlin_coef * ratio
    for v in range(nv):
        c = plain[n + 3, pl.ds(v * VREG, VREG), :]
        sc = strength * c
        for ref, up_row, down_row in ((plus, v + 3, v + 1), (minus, v, v + 2)):
            up = turned[n + 5, pl.ds(up_row * VREG, VREG), :]
            down = turned[n, pl.ds(down_row * VREG, VREG), :]
            delta = exchange(sc, c, up, down)
            ref[n, pl.ds((v + 1) * VREG, VREG), :] = delta
            if v == nv - 1:
                ref[n, pl.ds(0, VREG), :] = delta
            if v < 2:
                ref[n, pl.ds((nv + 1 + v) * VREG, VREG), :] = delta
    for v in range(sz.side // VREG):
        row = (v + 1) * VREG
        c = s_plain[n + 3, pl.ds(row, VREG), :]
        sc = strength * c
        for ref, s in ((s_plus, 1), (s_minus, -1)):
            up = s_plain[n + 5, pl.ds(row + 3 * s, VREG), :]
            down = s_plain[n, pl.ds(row - s, VREG), :]
            ref[n, pl.ds(row, VREG), :] = exchange(sc, c, up, down)
    close(sz, s_plus, n)
    close(sz, s_minus, n)


def is_even():
    return lax.rem(lax.axis_index("spec"), 2) == 0


def complete(sz, slot, fix, k, plain, s_plain):
    at = k * sz.far_band
    for start, count in west_half(sz):
        plain[slot, pl.ds(start * sz.cols, count, stride=sz.cols), :] = fix[pl.ds(at, count), :]
        at += count
    last = (sz.quarter + 1) * sz.cols - 1
    plain[slot, pl.ds(last, sz.half, stride=sz.cols), :] = fix[pl.ds(at, sz.half), :]
    at = k * sz.far_band + sz.rim_band
    s_put(sz, s_plain, slot, lambda v: fix[pl.ds(at + v * VREG, VREG), :])


def turn_halo(sz, base, plain, turned, real=None):
    def halo(k, carry):
        vals = [plain[base + k, pl.ds(v * VREG, VREG), :] for v in range(sz.vregs)]
        put(sz, None if real is None else plain, turned, base + k, vals if real is None else [x * real for x in vals])
        return carry

    lax.fori_loop(0, reach, halo, 0)


def inner_kernel(
    sz, adv, side, recv_a, raw_a, raw_b, moves, sea, plain, turned, plus, minus, s_plain, s_plus, s_minus, far_near, wide, fix
):
    base_a = jnp.where(is_even(), sz.bands + reach, 0)
    base_b = sz.bands + reach - base_a
    below, above = band_ratio(sz, -reach, True), band_ratio(sz, sz.bands, True)

    def own(k, carry):
        base = pl.multiple_of(k * sz.ring, VREG)
        put(sz, plain, turned, k + reach, [adv[pl.ds(base + v * VREG, VREG), :] for v in range(sz.vregs)])
        s_base = pl.multiple_of(k * sz.side, VREG)
        s_put(sz, s_plain, k + reach, lambda v: side[pl.ds(s_base + v * VREG, VREG), :])
        return carry

    lax.fori_loop(0, sz.bands, own, 0)

    for raw, first, inverse in (
        (raw_a, base_a, jnp.where(is_even(), above, below)),
        (raw_b, base_b, jnp.where(is_even(), below, above)),
    ):
        wide[...] = raw[...].astype(F32)

        def transport(k, r, first=first):
            base = pl.multiple_of(k * sz.ring, VREG)
            for v in range(sz.vregs):
                moved = transported(sz, wide, base, v, moves, speed_coef * r)
                plain[first + k, pl.ds(v * VREG, VREG), :] = sea[...] * moved

        over_bands(reach, inverse, transport, True)

    far_near[...] = jnp.zeros_like(far_near)
    for k in range(reach):
        for first, count in west_half(sz):
            start = k * sz.ring + first * sz.cols + sz.cols - 1
            far_near[pl.ds(k * sz.side + first, count), :] = wide[pl.ds(start, count, stride=sz.cols), :]
    fix[...] = recv_a[...].astype(F32)
    for k in range(reach):
        complete(sz, base_a + k, fix, k, plain, s_plain)
    turn_halo(sz, base_a, plain, turned)

    arrays = (plain, turned, plus, minus, s_plain, s_plus, s_minus)
    start = jnp.where(is_even(), reach, 0)
    ratio = jnp.where(is_even(), band_ratio(sz, 3), band_ratio(sz, 3 - reach))
    over_bands(sz.bands, ratio, lambda i, r: strengths(sz, r, start + i, *arrays))


def source_kernel(
    sz, adv, side, recv_b, pair, other, gain, moves, s_moves, sea, from_e, mix, far_near,
    plain_in, turned_in, plus_in, minus_in, s_plain_in, s_plus_in, s_minus_in,
    result_hbm, msg, plain, turned, plus, minus, s_plain, s_plus, s_minus, s_out, wide, s_near, out, sems,
):
    spec_rank = lax.axis_index("spec")
    nv, ns = sz.vregs, sz.side // VREG
    low, turn = low_rows(sz), VREG // 2
    base_b = jnp.where(is_even(), 0, sz.bands + reach)
    real_b = jnp.where((spec_rank == 0) | (spec_rank == sz.spec - 1), 0.0, 1.0).astype(F32)
    info = from_e[pl.ds(sz.info // 16 * 16, 32), :].astype(F32)
    at = sz.info % 16
    s_sea = info[at : at + 1] * real_b
    wide[...] = recv_b[...].astype(F32)
    s_near[...] = far_near[...]
    inverse = jnp.where(is_even(), band_ratio(sz, -reach, True), band_ratio(sz, sz.bands, True))
    for k in range(reach):
        speed = inverse * (speed_coef / ratio_step**k)
        slot, row = base_b + k, sz.pass_thick + k * sz.thick
        for start, count, col, moved in edge_parts(sz, moves, wide, k * sz.half, wide, row + sz.quarter):
            rows = pl.ds(start * sz.cols + col, count, stride=sz.cols)
            plain[slot, rows, :] = plain[slot, rows, :] + moved * (speed * sea[col : col + 1, :])
        at_near = k * sz.side
        s_near[pl.ds(at_near + sz.quarter, sz.half), :] = wide[pl.ds(row + sz.angles, sz.half), :]

        def column(v):
            x = wide[pl.ds(row + v * VREG, VREG), :]
            near = s_near[pl.ds(at_near + v * VREG, VREG), :]
            return s_sea * side_transported(sz, x, near, v, s_moves, speed)

        s_put(sz, s_plain, slot, column)
    turn_halo(sz, base_b, plain, turned, real_b)
    arrays = (plain, turned, plus, minus, s_plain, s_plus, s_minus)
    begin = jnp.where(is_even(), 0, sz.bands)
    ratio = jnp.where(is_even(), band_ratio(sz, 3 - reach), band_ratio(sz, sz.bands + 3 - reach))
    over_bands(reach, ratio, lambda i, r: strengths(sz, r, begin + i, *arrays))

    at = at + 1
    s_east = info[at : at + 1] + info[at + 1 : at + 2] + info[at + 2 : at + 3]
    s_north = info[at + 3 : at + 4] + info[at + 4 : at + 5] + info[at + 5 : at + 6]
    total_weight = sz.angles * 0.1 * sum(ratio_step ** (k - sz.freqs // 2) for k in range(sz.freqs))
    means = (pair[...] + other[...]) * (1.0 / total_weight)
    mean = jnp.concatenate([means[0 : sz.cols]] * (VREG // sz.cols), axis=0)
    s_mean = means[sz.cols : sz.cols + 1]

    def result(k, ratio):
        scale = 1.0 / (1.0 + (dissip_coef * ratio * ratio) * mean)
        base = pl.multiple_of(k * sz.ring, VREG)

        def moved_in(v):
            return (
                plus[k, pl.ds(v * VREG, VREG), :]
                + minus[k, pl.ds((v + 3) * VREG, VREG), :]
                + plus[k + 5, pl.ds((v + 2) * VREG, VREG), :]
                + minus[k + 5, pl.ds((v + 1) * VREG, VREG), :]
            )

        before = moved_in(nv - 1)
        for v in range(nv):
            now = moved_in(v)
            moved = pltpu.roll(jnp.where(low, now, before), turn, 0)
            before = now
            here = pl.ds((v + 1) * VREG, VREG)
            transfer = moved - 2.0 * (plus[k + 2, here, :] + minus[k + 2, here, :])
            a = adv[pl.ds(base + v * VREG, VREG), :]
            grown = ratio * gain[pl.ds(v * VREG, VREG), :]
            out[pl.ds(base + v * VREG, VREG), :] = (a + grown * a + transfer) * scale
        write(k).start()

    def write(k):
        band = pl.ds(pl.multiple_of(k * sz.ring, VREG), sz.ring)
        return pltpu.make_async_copy(out.at[band], result_hbm.at[band], sems.at[k])

    over_bands(sz.bands, band_ratio(sz, 0), result)

    s_gain = []
    for v in range(ns):
        here = pl.ds(v * VREG, VREG)
        along = s_moves[3, here, :] * s_east + s_moves[4, here, :] * s_north
        s_gain.append(wind_coef * jnp.maximum(along, 0.0))
    for k in range(sz.bands):
        ratio = band_ratio(sz, k)
        scale = 1.0 / (1.0 + (dissip_coef * ratio * ratio) * s_mean)
        for v in range(ns):
            row = (v + 1) * VREG
            here = pl.ds(row, VREG)
            transfer = (
                s_plus[k, pl.ds(row - 3, VREG), :]
                + s_minus[k, pl.ds(row + 3, VREG), :]
                + s_plus[k + 5, pl.ds(row + 1, VREG), :]
                + s_minus[k + 5, pl.ds(row - 1, VREG), :]
                - 2.0 * (s_plus[k + 2, here, :] + s_minus[k + 2, here, :])
            )
            a = side[pl.ds(k * sz.side + v * VREG, VREG), :]
            s_out[pl.ds(k * sz.angles + v * VREG, VREG), :] = (a + (ratio * s_gain[v]) * a + transfer) * scale

    pad = jnp.zeros((sz.lanes - sz.bins, sz.lat), BF16)
    columns = [out[pl.ds(c, sz.bins, stride=sz.cols), :] for c in range(sz.cols)]
    columns.append(s_out[pl.ds(0, sz.bins), :])
    columns = [jnp.concatenate([c.astype(BF16), pad], axis=0) for c in columns]
    n = (sz.cols + 1) * sz.lat
    spectra = dot_lanes(mix[:, 0:n], jnp.concatenate(columns, axis=1))
    about = mix[:, n : n + 128].astype(F32)
    msg[:, 0 : sz.lanes - 128] = spectra[:, : sz.lanes - 128].astype(BF16)
    msg[:, sz.lanes - 128 : sz.lanes] = (spectra[:, sz.lanes - 128 :] + about).astype(BF16)
    for k in range(sz.bands):
        write(k).wait()


def blend_kernel(sz, recv, nest_adv, result_hbm, out, sems):
    at = sz.bins - (sz.lanes - 128)
    about = recv[:, sz.lanes - 128 :].astype(F32)
    t_col, t_row, rate = about[:, at : at + 1], about[:, at + 1 : at + 2], about[:, at + 2 : at + 3]
    lane = lax.broadcasted_iota(jnp.int32, (sz.slots, sz.lat), 1).astype(F32)
    hit = jnp.where(lane == t_row, rate, 0.0)
    relax = [jnp.where(t_col == float(c), hit, 0.0) for c in range(sz.cols)]
    kept = [1.0 - jnp.sum(r, axis=0, keepdims=True) for r in relax]
    relax = jnp.concatenate(relax, axis=1).astype(BF16)
    writes = []
    for part, start in enumerate(range(0, sz.bins, 128)):
        count = min(128, sz.bins - start)
        added = lax.dot_general(
            recv[:, start : start + 128], relax, (((0,), (0,)), ((), ())), preferred_element_type=F32
        )
        for c in range(sz.cols):
            here = pl.ds(start * sz.cols + c, count, stride=sz.cols)
            out[here, :] = nest_adv[here, :] * kept[c] + added[:count, c * sz.lat : (c + 1) * sz.lat]
        rows = pl.ds(start * sz.cols, count * sz.cols)
        writes.append(pltpu.make_async_copy(out.at[rows], result_hbm.at[rows], sems.at[part]))
        writes[-1].start()
    for write in writes:
        write.wait()


def kernel_call(body, out_shape, n_in, hbm=(), out_hbm=(), scratch=(), aliases=None, flops=0, name=None):
    def specs(count, far):
        return [pl.BlockSpec(memory_space=pltpu.HBM if i in far else pltpu.VMEM) for i in range(count)]

    many = isinstance(out_shape, tuple)
    out_specs = specs(len(out_shape) if many else 1, out_hbm)
    return pl.pallas_call(
        body,
        out_shape=out_shape,
        in_specs=specs(n_in, hbm),
        out_specs=out_specs if many else out_specs[0],
        scratch_shapes=list(scratch),
        input_output_aliases=aliases or {},
        compiler_params=pltpu.CompilerParams(vmem_limit_bytes=20 * 2**20),
        cost_estimate=pl.CostEstimate(flops=flops, bytes_accessed=0, transcendentals=0) if flops else None,
        name=name,
    )


def per_device(
    mesh, energy, nest_energy, ocean_mask, wind_field, rim_cell, rim_dest, rim_target, rim_weight
):
    sz = Sizes(mesh, energy, rim_dest.shape[0])

    def array(*shape, dtype=F32):
        return jax.ShapeDtypeStruct(shape + (sz.lat,), dtype)

    def vmem(*shape):
        return pltpu.VMEM(shape + (sz.lat,), F32)

    def half(rows):
        return array(rows, dtype=BF16)

    field = array(sz.rows)
    table = jnp.asarray(angle_table(sz))
    energy = energy.reshape(sz.rows, sz.lat)
    nest = nest_energy.reshape(sz.rows, sz.lat)
    up = [(i, (i + 1) % sz.grid) for i in range(sz.grid)]
    down = [(j, i) for i, j in up]
    across = []
    for g in range(sz.grid):
        for i in range(sz.spec):
            j = i + 1 if i % 2 else i - 1
            to = (g, j) if 0 <= j < sz.spec else ((g ^ 1) % sz.grid, i)
            across.append((g * sz.spec + i, to[0] * sz.spec + to[1]))
    both = ("grid", "spec")
    near_rows = [vmem(sz.thin_rows), vmem(sz.thick_rows)]

    stay = functools.partial(pltpu.with_memory_space_constraint, memory_space=pltpu.HBM)
    thin, thick, moves, nest_moves, s_moves, gain, sea = kernel_call(
        functools.partial(pack_kernel, sz),
        (
            half(sz.thin_rows),
            half(sz.thick_rows),
            array(3, sz.ring),
            array(3, sz.ring),
            array(5, sz.side),
            array(sz.ring),
            array(VREG),
        ),
        5,
        hbm=range(5),
        scratch=[
            vmem(*table.shape[:1]),
            vmem(sz.rows),
            vmem(sz.rows),
            pltpu.VMEM(ocean_mask.shape, ocean_mask.dtype),
            pltpu.VMEM(wind_field.shape, F32),
        ]
        + near_rows
        + [pltpu.SemaphoreType.DMA((5,))],
        name="pack",
    )(stay(table), stay(energy), stay(nest), stay(ocean_mask), stay(wind_field))
    from_e = lax.ppermute(thick, "grid", down)
    from_w = lax.ppermute(thin, "grid", up)

    energy, sea = lax.optimization_barrier((energy, sea))
    raw_a, raw_b = kernel_call(
        functools.partial(raw_kernel, sz), (half(sz.edge_rows), half(sz.edge_rows)), 1, name="raw"
    )(energy)
    pairs = [(i, i ^ 1) for i in range(sz.spec)]
    recv_raw_b = lax.ppermute(raw_b, "spec", [(i, (i + 1 if i % 2 else i - 1) % sz.spec) for i in range(sz.spec)])
    recv_raw_a = lax.ppermute(raw_a, "spec", pairs)
    rim = (rim_cell.T, rim_dest.T, rim_target.reshape(1, sz.rim), rim_weight.T)
    rim, raw_a = lax.optimization_barrier((rim, raw_a))
    mix = kernel_call(
        functools.partial(rim_kernel, sz),
        jax.ShapeDtypeStruct((sz.slots, (sz.cols + 1) * sz.lat + 128), BF16),
        4,
        name="rim",
    )(*rim)
    nest, raw_a = lax.optimization_barrier((nest, raw_a))
    nest_inner = kernel_call(functools.partial(nest_kernel, sz), field, 2, flops=3 * 10**10, name="nest")(nest, nest_moves)
    energy, raw_a = lax.optimization_barrier((energy, raw_a))
    adv, total = kernel_call(
        functools.partial(local_kernel, sz), (field, array(VREG)), 3, flops=3 * 10**10, name="local"
    )(energy, moves, sea)
    from_e, from_w, mix, nest_inner, adv = lax.optimization_barrier((from_e, from_w, mix, nest_inner, adv))

    msg_b = kernel_call(
        functools.partial(pass_kernel, sz),
        half(sz.pass_rows),
        2,
        scratch=near_rows + [vmem(sz.pass_rows)],
        name="pass",
    )(from_w, from_e)
    adv, side, msg_a, part = kernel_call(
        functools.partial(edge_kernel, sz),
        (field, array(sz.bands * sz.side), half(sz.fix_rows), array(VREG)),
        8,
        scratch=near_rows + [vmem(sz.bands * sz.side), vmem(sz.fix_rows)],
        aliases={0: 0},
        flops=3 * 10**10,
        name="edges",
    )(adv, total, energy, from_w, from_e, moves, s_moves, sea)

    msg_a, msg_b, recv_raw_a, recv_raw_b = lax.optimization_barrier((msg_a, msg_b, recv_raw_a, recv_raw_b))
    recv_a = lax.ppermute(msg_a, "spec", pairs)
    recv_b = lax.ppermute(msg_b, both, across)
    pieces = recv_a[sz.sum_row : sz.sum_row + 3 * VREG].astype(F32)
    pair = part + pieces.reshape(3, VREG, sz.lat).sum(axis=0)
    other = jnp.zeros_like(pair)
    step = 2
    while step < sz.spec:
        pair = pair + other
        other = lax.ppermute(pair, "spec", [(i, i ^ (2 * step - 1)) for i in range(sz.spec)])
        step *= 2

    nest_adv = kernel_call(
        functools.partial(nest_edge_kernel, sz),
        field,
        4,
        scratch=near_rows,
        aliases={0: 0},
        name="nest_edge",
    )(nest_inner, from_w, from_e, nest_moves)

    padded, centres, turns = sz.bands + 2 * reach, sz.bands + reach, sz.ring + 3 * VREG
    arrays = (
        array(padded, sz.ring),
        array(padded, turns),
        array(centres, turns),
        array(centres, turns),
        array(padded, sz.frame),
        array(centres, sz.frame),
        array(centres, sz.frame),
    )
    *inner, far_near = kernel_call(
        functools.partial(inner_kernel, sz),
        arrays + (array(reach * sz.side),),
        7,
        scratch=[vmem(sz.edge_rows), vmem(sz.fix_rows)],
        name="inner",
    )(adv, side, recv_a, recv_raw_a, recv_raw_b, moves, sea)
    nest_adv, recv_b = lax.optimization_barrier((nest_adv, recv_b))
    global_next, msg, *_ = kernel_call(
        functools.partial(source_kernel, sz),
        (field, jax.ShapeDtypeStruct((sz.slots, sz.lanes), BF16)) + arrays,
        12 + len(arrays),
        scratch=[vmem(sz.bins + VREG), vmem(sz.pass_rows), vmem(reach * sz.side), vmem(sz.rows), pltpu.SemaphoreType.DMA((sz.bands,))],
        out_hbm=(0,),
        aliases={12 + i: 2 + i for i in range(len(arrays))},
        name="sources",
    )(adv, side, recv_b, pair, other, gain, moves, s_moves, sea, from_e, mix, far_near, *inner)

    recv = lax.all_to_all(msg, "grid", split_axis=0, concat_axis=0, tiled=True)
    nest_next = kernel_call(
        functools.partial(blend_kernel, sz),
        field,
        2,
        out_hbm=(0,),
        scratch=[vmem(sz.rows), pltpu.SemaphoreType.DMA((sz.lanes // 128,))],
        name="blend",
    )(recv, nest_adv)
    full = (sz.bands, sz.angles, sz.cols, sz.lat)
    return global_next.reshape(full), nest_next.reshape(full)


def solution(mesh):
    in_specs = (
        P("spec", None, "grid", None),
        P("spec", None, "grid", None),
        P("grid", None),
        P(None, "grid", None),
        P("grid", None),
        P("grid", None),
        P("grid"),
        P("grid", None),
    )
    out_specs = (P("spec", None, "grid", None), P("spec", None, "grid", None))
    return jax.shard_map(
        functools.partial(per_device, mesh),
        mesh=mesh,
        in_specs=in_specs,
        out_specs=out_specs,
        check_vma=False,
    )
```

```python
import functools

import jax
import jax.numpy as jnp
import numpy as np
from jax import lax
from jax.experimental import pallas as pl
from jax.experimental.pallas import tpu as pltpu
from jax.sharding import PartitionSpec as P

ratio_step = 1.1
speed_coef = 0.054
wind_coef = 0.05
dissip_coef = 0.2
nonlin_coef = 0.12
nest_speedup = 2.0
reach = 5

VREG = 8
BF16 = jnp.bfloat16
F32 = jnp.float32


class Sizes:
    def __init__(self, mesh, energy, rim_rows):
        self.grid = mesh.shape["grid"]
        self.spec = mesh.shape["spec"]
        self.bands, self.angles, self.cols, self.lat = energy.shape
        self.freqs = self.bands * self.spec
        self.bins = self.bands * self.angles
        self.ring = self.angles * self.cols
        self.rows = self.bins * self.cols
        self.vregs = self.ring // VREG
        self.rim = rim_rows
        self.cap = max(2, (2 * rim_rows + self.grid - 1) // self.grid)
        self.slots = self.grid * self.cap
        self.lanes = (self.bins + 3 + 127) // 128 * 128
        self.half = self.angles // 2
        self.quarter = self.angles // 4
        self.side = (self.angles + VREG - 1) // VREG * VREG
        self.frame = self.side + 2 * VREG
        self.thin = self.bands * self.half
        self.thin_rows = (2 * self.thin + 15) // 16 * 16
        self.thick = self.angles + self.half
        self.info = self.bands * self.thick
        self.thick_nest = (self.info + 7 + VREG - 1) // VREG * VREG
        self.thick_rows = (self.thick_nest + self.thin + 15) // 16 * 16
        self.edge_rows = reach * self.ring
        self.rim_band = 2 * self.half
        self.far_band = self.rim_band + self.angles
        self.sum_row = (reach * self.far_band + VREG - 1) // VREG * VREG
        self.fix_rows = (self.sum_row + 3 * VREG + 15) // 16 * 16
        self.pass_thick = (reach * self.half + VREG - 1) // VREG * VREG
        self.pass_rows = max(self.fix_rows + 16, (self.pass_thick + reach * self.thick + 15) // 16 * 16)


def band_ratio(sz, band, inverse=False):
    rank = lax.axis_index("spec")
    ratio = F32(0.0)
    for s in range(sz.spec):
        power = ratio_step ** (s * sz.bands + band - sz.freqs // 2)
        ratio = jnp.where(rank == s, F32(1.0 / power if inverse else power), ratio)
    return ratio


def over_bands(count, ratio, body, inverse=False):
    step = F32(1.0 / ratio_step if inverse else ratio_step)

    def turn(i, r):
        body(i, r)
        return r * step

    lax.fori_loop(0, count, turn, ratio)


def angle_table(sz):
    heading = 2.0 * np.pi * np.arange(sz.angles) / sz.angles
    table = np.zeros((sz.ring + VREG + sz.side, sz.lat), np.float32)
    table[sz.ring + VREG :][: sz.angles, 0] = np.cos(heading)
    table[sz.ring + VREG :][: sz.angles, 1] = np.sin(heading)
    table[: sz.ring, 0] = np.repeat(np.cos(heading), sz.cols)
    table[: sz.ring, 1] = np.repeat(np.sin(heading), sz.cols)
    degrees = -60.0 + 120.0 * (np.arange(sz.lat) + 0.5) / sz.lat
    table[sz.ring : sz.ring + VREG] = 1.0 / np.cos(degrees * (np.pi / 180.0))
    return table


def from_west(sz, angle):
    return angle < sz.quarter or angle >= 3 * sz.quarter


def split3(x):
    high = x.astype(BF16).astype(F32)
    middle = (x - high).astype(BF16).astype(F32)
    return [high, middle, x - high - middle]


def upwind(sz, v):
    sub = lax.broadcasted_iota(jnp.int32, (VREG, sz.lat), 0)
    first, per = v * VREG // sz.cols, VREG // sz.cols
    wests = [from_west(sz, first + i) for i in range(per)]
    west = sub < 0
    for i in range(per):
        if wests[i]:
            west = west | ((sub >= i * sz.cols) & (sub < (i + 1) * sz.cols))
    return wests, west, sub % sz.cols


def west_half(sz):
    return ((3 * sz.quarter, sz.angles - 3 * sz.quarter), (0, sz.quarter))


def fetch(pairs, sems):
    copies = [pltpu.make_async_copy(a, b, sems.at[i]) for i, (a, b) in enumerate(pairs)]
    for c in copies:
        c.start()
    return copies


def far_band(sz):
    return jnp.where(lax.rem(lax.axis_index("spec"), 2) == 0, 0, sz.bands - reach)


def pack_kernel(
    sz, energy, nest, mask, wind, thin, thick, first, second, first_n, late, early, late_n, early_n,
    mask_v, wind_v, tmp_thin, tmp_thick, sems,
):
    from_east = pl.ds(sz.quarter, sz.half)
    (start, count), (_, rest) = west_half(sz)
    last = sz.cols - 1
    pairs = [
        (mask, mask_v),
        (wind, wind_v),
        (energy.at[:, :, 0], first),
        (energy.at[:, from_east, 1], second),
        (energy.at[:, pl.ds(start, count), last], late),
        (energy.at[:, pl.ds(0, rest), last], early),
        (nest.at[:, from_east, 0], first_n),
        (nest.at[:, pl.ds(start, count), last], late_n),
        (nest.at[:, pl.ds(0, rest), last], early_n),
    ]
    copies = [pltpu.make_async_copy(a, b, sems.at[i]) for i, (a, b) in enumerate(pairs)]
    for copy in copies:
        copy.start()
    spare = sz.thin_rows - 2 * sz.thin
    if spare:
        tmp_thin[pl.ds(2 * sz.thin, spare), :] = jnp.zeros((spare, sz.lat), F32)
    tmp_thick[...] = jnp.zeros_like(tmp_thick)
    for copy in copies[:6]:
        copy.wait()
    info = [mask_v[0:1, :].astype(F32)] + split3(wind_v[0, 0:1, :]) + split3(wind_v[1, 0:1, :])
    for i, line in enumerate(info):
        tmp_thick[pl.ds(sz.info + i, 1), :] = line
    for k in range(sz.bands):
        tmp_thin[pl.ds(k * sz.half, count), :] = late[k]
        tmp_thin[pl.ds(k * sz.half + count, rest), :] = early[k]
        tmp_thick[pl.ds(k * sz.thick, sz.angles), :] = first[k]
        tmp_thick[pl.ds(k * sz.thick + sz.angles, sz.half), :] = second[k]
    for copy in copies[6:]:
        copy.wait()
    for k in range(sz.bands):
        at = sz.thin + k * sz.half
        tmp_thin[pl.ds(at, count), :] = late_n[k]
        tmp_thin[pl.ds(at + count, rest), :] = early_n[k]
        tmp_thick[pl.ds(sz.thick_nest + k * sz.half, sz.half), :] = first_n[k]
    thin[...] = tmp_thin[...].astype(BF16)
    thick[...] = tmp_thick[...].astype(BF16)


def setup_kernel(sz, table, mask, wind, moves, nest_moves, s_moves, gain, sea):
    per = VREG // sz.cols
    sea[...] = jnp.concatenate([mask[...].astype(F32)] * per, axis=0)
    east_wind = jnp.concatenate([wind[0]] * per, axis=0)
    north_wind = jnp.concatenate([wind[1]] * per, axis=0)
    fill_moves(sz, 0, table, sz.cols, (moves, nest_moves))
    fill_moves(sz, sz.ring + VREG, table, 1, (s_moves, None))
    for v in range(sz.vregs):
        rows = table[pl.ds(v * VREG, VREG), :]
        along = rows[:, 0:1] * east_wind + rows[:, 1:2] * north_wind
        gain[pl.ds(v * VREG, VREG), :] = wind_coef * jnp.maximum(along, 0.0)
    for v in range(sz.side // VREG):
        rows = table[pl.ds(sz.ring + VREG + v * VREG, VREG), :]
        for i in range(2):
            s_moves[3 + i, pl.ds(v * VREG, VREG), :] = jnp.broadcast_to(rows[:, i : i + 1], (VREG, sz.lat))


def raw_kernel(sz, energy, raw_a, raw_b):
    for raw, first in ((raw_a, sz.bands - reach - far_band(sz)), (raw_b, far_band(sz))):
        raw[...] = energy[pl.ds(pl.multiple_of(first * sz.ring, VREG), sz.edge_rows), :].astype(BF16)


def pass_kernel(sz, from_w, from_e, msg, wide_w, wide_e, tmp):
    wide_w[...] = from_w[...].astype(F32)
    wide_e[...] = from_e[...].astype(F32)
    tmp[...] = jnp.zeros_like(tmp)
    first = far_band(sz)
    count = reach * sz.half
    tmp[pl.ds(0, count), :] = wide_w[pl.ds(first * sz.half, count), :]
    start = pl.multiple_of(first * sz.thick, VREG)
    tmp[pl.ds(sz.pass_thick, reach * sz.thick), :] = wide_e[pl.ds(start, reach * sz.thick), :]
    msg[...] = tmp[...].astype(BF16)


def fill_moves(sz, rows, table, cols, targets):
    lane = lax.broadcasted_iota(jnp.int32, (VREG, sz.lat), 1)
    sub = lax.broadcasted_iota(jnp.int32, (VREG, sz.lat), 0)
    sec = table[pl.ds(sz.ring, VREG), :]
    for v in range(targets[0].shape[1] // VREG):
        line = table[pl.ds(rows + v * VREG, VREG), :]
        along = jnp.broadcast_to(jnp.abs(line[:, 0:1]), (VREG, sz.lat))
        across = jnp.broadcast_to(jnp.abs(line[:, 1:2]), (VREG, sz.lat))
        edge = lane == jnp.where(sub < sz.half * cols - v * VREG, 0, sz.lat - 1)
        here = pl.ds(v * VREG, VREG)
        for target, by in zip(targets, (along * sec, along)):
            if target is not None:
                target[0, here, :] = by + across
                target[1, here, :] = by
                target[2, here, :] = jnp.where(edge, 0.0, across)


def beside(sz, x, turn):
    if turn >= VREG:
        return pltpu.roll(x, 1, 1)
    if turn <= 0:
        return pltpu.roll(x, sz.lat - 1, 1)
    sub = lax.broadcasted_iota(jnp.int32, (VREG, sz.lat), 0)
    return jnp.where(sub < turn, pltpu.roll(x, 1, 1), pltpu.roll(x, sz.lat - 1, 1))


def transported(sz, field, base, v, moves, speed):
    here = pl.ds(v * VREG, VREG)
    x = field[pl.ds(base + v * VREG, VREG), :]
    wests, west, col = upwind(sz, v)
    if all(wests):
        near, at_edge = pltpu.roll(x, 1, 0), col == 0
    elif not any(wests):
        near, at_edge = pltpu.roll(x, VREG - 1, 0), col == sz.cols - 1
    else:
        near = jnp.where(west, pltpu.roll(x, 1, 0), pltpu.roll(x, VREG - 1, 0))
        at_edge = jnp.where(west, col, sz.cols - 1 - col) == 0
    near = jnp.where(at_edge, 0.0, near)
    south = sz.half * sz.cols - v * VREG
    return x - speed * (moves[0, here, :] * x - moves[1, here, :] * near - moves[2, here, :] * beside(sz, x, south))


def edge_parts(sz, moves, wide_w, at_w, wide_e, at_e):
    parts = []
    for first, count in west_half(sz):
        parts.append((first, count, 0, wide_w[pl.ds(at_w, count), :]))
        at_w += count
    parts.append((sz.quarter, sz.half, sz.cols - 1, wide_e[pl.ds(at_e, sz.half), :]))
    for first, count, col, cells in parts:
        yield first, count, col, moves[1, pl.ds(first * sz.cols, count, stride=sz.cols), :] * cells


def side_transported(sz, x, near, v, s_moves, speed):
    here = pl.ds(v * VREG, VREG)
    move = s_moves[0, here, :] * x - s_moves[1, here, :] * near
    return x - speed * (move - s_moves[2, here, :] * beside(sz, x, sz.half - v * VREG))


def local_kernel(sz, energy, moves, sea, adv, total):
    total[...] = jnp.zeros_like(total)

    def band(k, inverse):
        base = pl.multiple_of(k * sz.ring, VREG)
        line = jnp.zeros((VREG, sz.lat), F32)
        for v in range(sz.vregs):
            out = sea[...] * transported(sz, energy, base, v, moves, speed_coef * inverse)
            adv[pl.ds(base + v * VREG, VREG), :] = out
            line = line + out
        total[...] = total[...] * F32(1.0 / ratio_step) + line

    over_bands(sz.bands, band_ratio(sz, 0, True), band, True)
    total[...] = total[...] * (0.1 * band_ratio(sz, sz.bands - 1))


def edge_kernel(
    sz, adv_in, total, energy, from_w, from_e, moves, s_moves, sea, adv, side, msg_a, part,
    wide_w, wide_e, s_near, fix,
):
    wide_w[...] = from_w[...].astype(F32)
    wide_e[...] = from_e[...].astype(F32)
    s_sea = wide_e[pl.ds(sz.info, 1), :]
    sub = lax.broadcasted_iota(jnp.int32, (VREG, sz.lat), 0)
    s_total = jnp.zeros((VREG, sz.lat), F32)
    lines = {}
    for k in range(sz.bands):
        inverse = band_ratio(sz, k, True)
        weight = 0.1 * band_ratio(sz, k)
        speed = speed_coef * inverse
        at_e = k * sz.thick + sz.quarter
        for first, count, col, moved in edge_parts(sz, moves, wide_w, k * sz.half, wide_e, at_e):
            moved = moved * (speed * sea[col : col + 1, :])
            rows = pl.ds(k * sz.ring + first * sz.cols + col, count, stride=sz.cols)
            adv[rows, :] = adv[rows, :] + moved
            lines[first, col] = lines.get((first, col), 0.0) + moved * weight
        at = k * sz.side
        for first, count in west_half(sz):
            start = k * sz.ring + first * sz.cols + sz.cols - 1
            s_near[pl.ds(at + first, count), :] = energy[pl.ds(start, count, stride=sz.cols), :]
        s_near[pl.ds(at + sz.quarter, sz.half), :] = wide_e[pl.ds(k * sz.thick + sz.angles, sz.half), :]
        if sz.side > sz.angles:
            rest = sz.side - sz.angles
            s_near[pl.ds(at + sz.angles, rest), :] = jnp.zeros((rest, sz.lat), F32)
        s_line = jnp.zeros((VREG, sz.lat), F32)
        for v in range(sz.side // VREG):
            x = wide_e[pl.ds(k * sz.thick + v * VREG, VREG), :]
            near = s_near[pl.ds(at + v * VREG, VREG), :]
            out = s_sea * side_transported(sz, x, near, v, s_moves, speed)
            side[pl.ds(at + v * VREG, VREG), :] = out
            s_line = s_line + (out if (v + 1) * VREG <= sz.angles else jnp.where(sub < sz.angles - v * VREG, out, 0.0))
        s_total = s_total + s_line * weight
    mine = total[0 : sz.cols, :]
    for i in range(1, VREG // sz.cols):
        mine = mine + total[i * sz.cols : (i + 1) * sz.cols, :]
    west, east = (
        sum(jnp.sum(x, axis=0, keepdims=True) for (_, c), x in lines.items() if c == col) for col in (0, sz.cols - 1)
    )
    between = jnp.zeros((sz.cols - 2, sz.lat), F32)
    mine = mine + jnp.concatenate([west, between, east], axis=0)
    s_sum = jnp.sum(s_total, axis=0, keepdims=True)
    sums = jnp.concatenate([mine, s_sum, jnp.zeros((VREG - sz.cols - 1, sz.lat), F32)], axis=0)
    part[...] = sums
    fix[...] = jnp.zeros_like(fix)
    fix[pl.ds(sz.sum_row, 3 * VREG), :] = jnp.concatenate(split3(sums), axis=0)
    start = sz.bands - reach - far_band(sz)
    for k in range(reach):
        band_row = pl.multiple_of((start + k) * sz.ring, VREG)
        at = k * sz.far_band
        for first, count in west_half(sz):
            fix[pl.ds(at, count), :] = adv[pl.ds(band_row + first * sz.cols, count, stride=sz.cols), :]
            at += count
        last = band_row + (sz.quarter + 1) * sz.cols - 1
        fix[pl.ds(at, sz.half), :] = adv[pl.ds(last, sz.half, stride=sz.cols), :]
        s_row = pl.multiple_of((start + k) * sz.side, VREG)
        fix[pl.ds(k * sz.far_band + sz.rim_band, sz.angles), :] = side[pl.ds(s_row, sz.angles), :]
    msg_a[...] = fix[...].astype(BF16)


def nest_kernel(sz, nest, moves, out):
    def band(k, inverse):
        base = pl.multiple_of(k * sz.ring, VREG)
        for v in range(sz.vregs):
            moved = transported(sz, nest, base, v, moves, nest_speedup * speed_coef * inverse)
            out[pl.ds(base + v * VREG, VREG), :] = moved

    over_bands(sz.bands, band_ratio(sz, 0, True), band, True)


def nest_edge_kernel(sz, inner, from_w, from_e, moves, out, columns, wide_w, wide_e):
    grid_rank = lax.axis_index("grid")
    quarter = sz.grid // 4
    keep_w = jnp.where((grid_rank != quarter) & (grid_rank != 3 * quarter), 1.0, 0.0).astype(F32)
    keep_e = jnp.where((grid_rank != quarter - 1) & (grid_rank != 3 * quarter - 1), 1.0, 0.0).astype(F32)
    wide_w[...] = from_w[...].astype(F32)
    wide_e[...] = from_e[...].astype(F32)
    for k in range(sz.bands):
        speed = nest_speedup * speed_coef * band_ratio(sz, k, True)
        at_w, at_e = sz.thin + k * sz.half, sz.thick_nest + k * sz.half
        for first, count, col, moved in edge_parts(sz, moves, wide_w, at_w, wide_e, at_e):
            rows = pl.ds(k * sz.ring + first * sz.cols + col, count, stride=sz.cols)
            out[rows, :] = out[rows, :] + moved * (speed * (keep_w if col == 0 else keep_e))
    for c in range(sz.cols):
        columns[c, pl.ds(0, sz.bins), :] = out[pl.ds(c, sz.bins, stride=sz.cols), :]


def dot_lanes(a, b):
    return lax.dot_general(a, b, (((1,), (1,)), ((), ())), preferred_element_type=F32)


def rim_kernel(sz, cell, dest, target, weight, mix):
    device = lax.broadcasted_iota(jnp.int32, (sz.grid, sz.rim), 0)
    hot = jnp.where(device == dest[...], 1.0, 0.0)
    before = lax.broadcasted_iota(jnp.int32, (sz.rim, sz.rim), 0)
    after = lax.broadcasted_iota(jnp.int32, (sz.rim, sz.rim), 1)
    earlier = jnp.dot(
        hot.astype(BF16), jnp.where(before < after, 1.0, 0.0).astype(BF16), preferred_element_type=F32
    )
    rank = jnp.sum(hot * earlier, axis=0, keepdims=True)
    place = dest[...] * sz.cap + rank.astype(jnp.int32)
    slot = lax.broadcasted_iota(jnp.int32, (sz.slots, sz.rim), 0)
    takes = jnp.where(slot == place, 1.0, 0.0).astype(BF16)
    row = lax.broadcasted_iota(jnp.int32, (sz.lat, sz.rim), 0)
    col = cell[0:1, :] - lax.axis_index("grid") * sz.cols
    south_row = cell[1:2, :]
    ex, ny = weight[0:1, :], weight[1:2, :]
    for c in range(sz.cols + 1):
        share = jnp.where(col == c, 1.0 - ex, 0.0) + jnp.where(col + 1 == c, ex, 0.0)
        south, north = share * (1.0 - ny), share * ny
        corner = jnp.where(row == south_row, south, 0.0) + jnp.where(row == south_row + 1, north, 0.0)
        mix[:, c * sz.lat : (c + 1) * sz.lat] = dot_lanes(takes, corner.astype(BF16)).astype(BF16)
    at = sz.bins - (sz.lanes - 128)
    line = lax.broadcasted_iota(jnp.int32, (128, sz.rim), 0)
    t = target[...]
    t_col = t // sz.lat
    about = jnp.where(line == at, t_col.astype(F32), 0.0)
    about = about + jnp.where(line == at + 1, (t - t_col * sz.lat).astype(F32), 0.0)
    about = about + jnp.where(line == at + 2, weight[2:3, :], 0.0)
    n = (sz.cols + 1) * sz.lat
    mix[:, n : n + 128] = dot_lanes(takes, about.astype(BF16)).astype(BF16)


def low_rows(sz):
    return lax.broadcasted_iota(jnp.int32, (VREG, sz.lat), 0) < VREG // 2


def put(sz, plain, turned, slot, vals):
    nv, low = sz.vregs, low_rows(sz)
    for v in range(nv):
        if plain is not None:
            plain[slot, pl.ds(v * VREG, VREG), :] = vals[v]
        nxt = pltpu.roll(jnp.where(low, vals[(v + 1) % nv], vals[v]), VREG // 2, 0)
        turned[slot, pl.ds((v + 2) * VREG, VREG), :] = nxt
        if v >= nv - 2:
            turned[slot, pl.ds((v + 2 - nv) * VREG, VREG), :] = nxt
        if v == 0:
            turned[slot, pl.ds((nv + 2) * VREG, VREG), :] = nxt


def close(sz, ref, slot):
    ref[slot, pl.ds(VREG - 3, 3), :] = ref[slot, pl.ds(VREG + sz.angles - 3, 3), :]
    ref[slot, pl.ds(VREG + sz.angles, 3), :] = ref[slot, pl.ds(VREG, 3), :]


def s_put(sz, s_plain, slot, load):
    for v in range(sz.side // VREG):
        s_plain[slot, pl.ds((v + 1) * VREG, VREG), :] = load(v)
    close(sz, s_plain, slot)


def exchange(sc, c, up, down):
    return sc * (c * (up + down) - 2.0 * (up * down))


def strengths(sz, ratio, n, plain, turned, plus, minus, s_plain, s_plus, s_minus):
    nv = sz.vregs
    strength = nonlin_coef * ratio
    for v in range(nv):
        c = plain[n + 3, pl.ds(v * VREG, VREG), :]
        sc = strength * c
        for ref, up_row, down_row in ((plus, v + 3, v + 1), (minus, v, v + 2)):
            up = turned[n + 5, pl.ds(up_row * VREG, VREG), :]
            down = turned[n, pl.ds(down_row * VREG, VREG), :]
            delta = exchange(sc, c, up, down)
            ref[n, pl.ds((v + 1) * VREG, VREG), :] = delta
            if v == nv - 1:
                ref[n, pl.ds(0, VREG), :] = delta
            if v < 2:
                ref[n, pl.ds((nv + 1 + v) * VREG, VREG), :] = delta
    for v in range(sz.side // VREG):
        row = (v + 1) * VREG
        c = s_plain[n + 3, pl.ds(row, VREG), :]
        sc = strength * c
        for ref, s in ((s_plus, 1), (s_minus, -1)):
            up = s_plain[n + 5, pl.ds(row + 3 * s, VREG), :]
            down = s_plain[n, pl.ds(row - s, VREG), :]
            ref[n, pl.ds(row, VREG), :] = exchange(sc, c, up, down)
    close(sz, s_plus, n)
    close(sz, s_minus, n)


def is_even():
    return lax.rem(lax.axis_index("spec"), 2) == 0


def complete(sz, slot, fix, k, plain, s_plain):
    at = k * sz.far_band
    for start, count in west_half(sz):
        plain[slot, pl.ds(start * sz.cols, count, stride=sz.cols), :] = fix[pl.ds(at, count), :]
        at += count
    last = (sz.quarter + 1) * sz.cols - 1
    plain[slot, pl.ds(last, sz.half, stride=sz.cols), :] = fix[pl.ds(at, sz.half), :]
    at = k * sz.far_band + sz.rim_band
    s_put(sz, s_plain, slot, lambda v: fix[pl.ds(at + v * VREG, VREG), :])


def turn_halo(sz, base, plain, turned, real=None):
    def halo(k, carry):
        vals = [plain[base + k, pl.ds(v * VREG, VREG), :] for v in range(sz.vregs)]
        put(sz, None if real is None else plain, turned, base + k, vals if real is None else [x * real for x in vals])
        return carry

    lax.fori_loop(0, reach, halo, 0)


def numerators(sz, k, ratio, adv, gain, plus, minus, store):
    nv, low = sz.vregs, low_rows(sz)
    base = pl.multiple_of(k * sz.ring, VREG)

    def moved_in(v):
        return (
            plus[k, pl.ds(v * VREG, VREG), :]
            + minus[k, pl.ds((v + 3) * VREG, VREG), :]
            + plus[k + 5, pl.ds((v + 2) * VREG, VREG), :]
            + minus[k + 5, pl.ds((v + 1) * VREG, VREG), :]
        )

    before = moved_in(nv - 1)
    for v in range(nv):
        now = moved_in(v)
        moved = pltpu.roll(jnp.where(low, now, before), VREG // 2, 0)
        before = now
        here = pl.ds((v + 1) * VREG, VREG)
        transfer = moved - 2.0 * (plus[k + 2, here, :] + minus[k + 2, here, :])
        a = adv[pl.ds(base + v * VREG, VREG), :]
        grown = ratio * gain[pl.ds(v * VREG, VREG), :]
        store(pl.ds(base + v * VREG, VREG), a + grown * a + transfer)


def beyond_kernel(sz, raw_a, raw_b, moves, sea, plain, far_near, wide):
    base_a = jnp.where(is_even(), sz.bands + reach, 0)
    base_b = sz.bands + reach - base_a
    below, above = band_ratio(sz, -reach, True), band_ratio(sz, sz.bands, True)

    for raw, first, inverse in (
        (raw_a, base_a, jnp.where(is_even(), above, below)),
        (raw_b, base_b, jnp.where(is_even(), below, above)),
    ):
        wide[...] = raw[...].astype(F32)

        def transport(k, r, first=first):
            base = pl.multiple_of(k * sz.ring, VREG)
            for v in range(sz.vregs):
                moved = transported(sz, wide, base, v, moves, speed_coef * r)
                plain[first + k, pl.ds(v * VREG, VREG), :] = sea[...] * moved

        over_bands(reach, inverse, transport, True)

    far_near[...] = jnp.zeros_like(far_near)
    for k in range(reach):
        for first, count in west_half(sz):
            start = k * sz.ring + first * sz.cols + sz.cols - 1
            far_near[pl.ds(k * sz.side + first, count), :] = wide[pl.ds(start, count, stride=sz.cols), :]

def inner_kernel(
    sz, adv, side, recv_a, gain, plain_in, plain, turned, plus, minus, s_plain, s_plus, s_minus, num, fix
):
    base_a = jnp.where(is_even(), sz.bands + reach, 0)

    def own(k, carry):
        base = pl.multiple_of(k * sz.ring, VREG)
        put(sz, plain, turned, k + reach, [adv[pl.ds(base + v * VREG, VREG), :] for v in range(sz.vregs)])
        s_base = pl.multiple_of(k * sz.side, VREG)
        s_put(sz, s_plain, k + reach, lambda v: side[pl.ds(s_base + v * VREG, VREG), :])
        return carry

    lax.fori_loop(0, sz.bands, own, 0)

    fix[...] = recv_a[...].astype(F32)
    for k in range(reach):
        complete(sz, base_a + k, fix, k, plain, s_plain)
    turn_halo(sz, base_a, plain, turned)

    arrays = (plain, turned, plus, minus, s_plain, s_plus, s_minus)
    start = jnp.where(is_even(), reach, 0)
    ratio = jnp.where(is_even(), band_ratio(sz, 3), band_ratio(sz, 3 - reach))
    over_bands(sz.bands, ratio, lambda i, r: strengths(sz, r, start + i, *arrays))

    def store(rows, value):
        num[rows, :] = value

    ratio = jnp.where(is_even(), band_ratio(sz, reach), band_ratio(sz, 0))
    over_bands(
        sz.bands - reach, ratio, lambda i, r: numerators(sz, start + i, r, adv, gain, plus, minus, store)
    )


def source_kernel(
    sz, adv, side, recv_b, pair, other, gain, moves, s_moves, sea, from_e, mix, far_near, num,
    plain_in, turned_in, plus_in, minus_in, s_plain_in, s_plus_in, s_minus_in,
    result_hbm, msg, plain, turned, plus, minus, s_plain, s_plus, s_minus, s_out, wide, s_near, out, sems,
):
    spec_rank = lax.axis_index("spec")
    ns = sz.side // VREG
    total_weight = sz.angles * 0.1 * sum(ratio_step ** (k - sz.freqs // 2) for k in range(sz.freqs))
    means = (pair[...] + other[...]) * (1.0 / total_weight)
    mean = jnp.concatenate([means[0 : sz.cols]] * (VREG // sz.cols), axis=0)
    s_mean = means[sz.cols : sz.cols + 1]

    def write(k):
        band = pl.ds(pl.multiple_of(k * sz.ring, VREG), sz.ring)
        return pltpu.make_async_copy(out.at[band], result_hbm.at[band], sems.at[k])

    def scale(ratio):
        return 1.0 / (1.0 + (dissip_coef * ratio * ratio) * mean)

    ready = jnp.where(is_even(), reach, 0)

    def finish(i, ratio):
        factor = scale(ratio)
        base = pl.multiple_of((ready + i) * sz.ring, VREG)
        for v in range(sz.vregs):
            here = pl.ds(base + v * VREG, VREG)
            out[here, :] = num[here, :] * factor
        write(ready + i).start()

    over_bands(sz.bands - reach, jnp.where(is_even(), band_ratio(sz, reach), band_ratio(sz, 0)), finish)

    base_b = jnp.where(is_even(), 0, sz.bands + reach)
    real_b = jnp.where((spec_rank == 0) | (spec_rank == sz.spec - 1), 0.0, 1.0).astype(F32)
    info = from_e[pl.ds(sz.info // 16 * 16, 32), :].astype(F32)
    at = sz.info % 16
    s_sea = info[at : at + 1] * real_b
    wide[...] = recv_b[...].astype(F32)
    s_near[...] = far_near[...]
    inverse = jnp.where(is_even(), band_ratio(sz, -reach, True), band_ratio(sz, sz.bands, True))
    for k in range(reach):
        speed = inverse * (speed_coef / ratio_step**k)
        slot, row = base_b + k, sz.pass_thick + k * sz.thick
        for start, count, col, moved in edge_parts(sz, moves, wide, k * sz.half, wide, row + sz.quarter):
            rows = pl.ds(start * sz.cols + col, count, stride=sz.cols)
            plain[slot, rows, :] = plain[slot, rows, :] + moved * (speed * sea[col : col + 1, :])
        at_near = k * sz.side
        s_near[pl.ds(at_near + sz.quarter, sz.half), :] = wide[pl.ds(row + sz.angles, sz.half), :]

        def column(v):
            x = wide[pl.ds(row + v * VREG, VREG), :]
            near = s_near[pl.ds(at_near + v * VREG, VREG), :]
            return s_sea * side_transported(sz, x, near, v, s_moves, speed)

        s_put(sz, s_plain, slot, column)
    turn_halo(sz, base_b, plain, turned, real_b)
    arrays = (plain, turned, plus, minus, s_plain, s_plus, s_minus)
    begin = jnp.where(is_even(), 0, sz.bands)
    ratio = jnp.where(is_even(), band_ratio(sz, 3 - reach), band_ratio(sz, sz.bands + 3 - reach))
    over_bands(reach, ratio, lambda i, r: strengths(sz, r, begin + i, *arrays))

    at = at + 1
    s_east = info[at : at + 1] + info[at + 1 : at + 2] + info[at + 2 : at + 3]
    s_north = info[at + 3 : at + 4] + info[at + 4 : at + 5] + info[at + 5 : at + 6]
    missing = jnp.where(is_even(), 0, sz.bands - reach)

    def result(i, ratio):
        factor = scale(ratio)

        def store(rows, value):
            out[rows, :] = value * factor

        numerators(sz, missing + i, ratio, adv, gain, plus, minus, store)
        write(missing + i).start()

    over_bands(reach, jnp.where(is_even(), band_ratio(sz, 0), band_ratio(sz, sz.bands - reach)), result)

    s_gain = []
    for v in range(ns):
        here = pl.ds(v * VREG, VREG)
        along = s_moves[3, here, :] * s_east + s_moves[4, here, :] * s_north
        s_gain.append(wind_coef * jnp.maximum(along, 0.0))
    for k in range(sz.bands):
        ratio = band_ratio(sz, k)
        factor = 1.0 / (1.0 + (dissip_coef * ratio * ratio) * s_mean)
        for v in range(ns):
            row = (v + 1) * VREG
            here = pl.ds(row, VREG)
            transfer = (
                s_plus[k, pl.ds(row - 3, VREG), :]
                + s_minus[k, pl.ds(row + 3, VREG), :]
                + s_plus[k + 5, pl.ds(row + 1, VREG), :]
                + s_minus[k + 5, pl.ds(row - 1, VREG), :]
                - 2.0 * (s_plus[k + 2, here, :] + s_minus[k + 2, here, :])
            )
            a = side[pl.ds(k * sz.side + v * VREG, VREG), :]
            s_out[pl.ds(k * sz.angles + v * VREG, VREG), :] = (a + (ratio * s_gain[v]) * a + transfer) * factor

    pad = jnp.zeros((sz.lanes - sz.bins, sz.lat), BF16)
    columns = [out[pl.ds(c, sz.bins, stride=sz.cols), :] for c in range(sz.cols)]
    columns.append(s_out[pl.ds(0, sz.bins), :])
    columns = [jnp.concatenate([c.astype(BF16), pad], axis=0) for c in columns]
    n = (sz.cols + 1) * sz.lat
    spectra = dot_lanes(mix[:, 0:n], jnp.concatenate(columns, axis=1))
    about = mix[:, n : n + 128].astype(F32)
    msg[:, 0 : sz.lanes - 128] = spectra[:, : sz.lanes - 128].astype(BF16)
    msg[:, sz.lanes - 128 : sz.lanes] = (spectra[:, sz.lanes - 128 :] + about).astype(BF16)
    for k in range(sz.bands):
        write(k).wait()


def blend_kernel(sz, recv, nest_adv, result_hbm, out, sems):
    at = sz.bins - (sz.lanes - 128)
    about = recv[:, sz.lanes - 128 :].astype(F32)
    t_col, t_row, rate = about[:, at : at + 1], about[:, at + 1 : at + 2], about[:, at + 2 : at + 3]
    lane = lax.broadcasted_iota(jnp.int32, (sz.slots, sz.lat), 1).astype(F32)
    hit = jnp.where(lane == t_row, rate, 0.0)
    relax = [jnp.where(t_col == float(c), hit, 0.0) for c in range(sz.cols)]
    kept = [1.0 - jnp.sum(r, axis=0, keepdims=True) for r in relax]
    relax = jnp.concatenate(relax, axis=1).astype(BF16)
    writes = []
    for part, start in enumerate(range(0, sz.bins, 128)):
        count = min(128, sz.bins - start)
        added = lax.dot_general(
            recv[:, start : start + 128], relax, (((0,), (0,)), ((), ())), preferred_element_type=F32
        )
        for c in range(sz.cols):
            here = pl.ds(start * sz.cols + c, count, stride=sz.cols)
            own = nest_adv[c, pl.ds(start, count), :]
            out[here, :] = own * kept[c] + added[:count, c * sz.lat : (c + 1) * sz.lat]
        rows = pl.ds(start * sz.cols, count * sz.cols)
        writes.append(pltpu.make_async_copy(out.at[rows], result_hbm.at[rows], sems.at[part]))
        writes[-1].start()
    for write in writes:
        write.wait()


def kernel_call(body, out_shape, n_in, hbm=(), out_hbm=(), scratch=(), aliases=None, flops=0, name=None):
    def specs(count, far):
        return [pl.BlockSpec(memory_space=pltpu.HBM if i in far else pltpu.VMEM) for i in range(count)]

    many = isinstance(out_shape, tuple)
    out_specs = specs(len(out_shape) if many else 1, out_hbm)
    return pl.pallas_call(
        body,
        out_shape=out_shape,
        in_specs=specs(n_in, hbm),
        out_specs=out_specs if many else out_specs[0],
        scratch_shapes=list(scratch),
        input_output_aliases=aliases or {},
        compiler_params=pltpu.CompilerParams(vmem_limit_bytes=20 * 2**20),
        cost_estimate=pl.CostEstimate(flops=flops, bytes_accessed=0, transcendentals=0) if flops else None,
        name=name,
    )


def per_device(
    mesh, energy, nest_energy, ocean_mask, wind_field, rim_cell, rim_dest, rim_target, rim_weight
):
    sz = Sizes(mesh, energy, rim_dest.shape[0])

    def array(*shape, dtype=F32):
        return jax.ShapeDtypeStruct(shape + (sz.lat,), dtype)

    def vmem(*shape):
        return pltpu.VMEM(shape + (sz.lat,), F32)

    def half(rows):
        return array(rows, dtype=BF16)

    field = array(sz.rows)
    table = jnp.asarray(angle_table(sz))
    energy4, energy = energy, energy.reshape(sz.rows, sz.lat)
    nest = nest_energy.reshape(sz.rows, sz.lat)
    up = [(i, (i + 1) % sz.grid) for i in range(sz.grid)]
    down = [(j, i) for i, j in up]
    across = []
    for g in range(sz.grid):
        for i in range(sz.spec):
            j = i + 1 if i % 2 else i - 1
            to = (g, j) if 0 <= j < sz.spec else ((g ^ 2) % sz.grid, i)
            across.append((g * sz.spec + i, to[0] * sz.spec + to[1]))
    both = ("grid", "spec")
    near_rows = [vmem(sz.thin_rows), vmem(sz.thick_rows)]

    stay = functools.partial(pltpu.with_memory_space_constraint, memory_space=pltpu.HBM)
    def column(n):
        return vmem(sz.bands, n)

    thin, thick = kernel_call(
        functools.partial(pack_kernel, sz),
        (half(sz.thin_rows), half(sz.thick_rows)),
        4,
        hbm=range(4),
        scratch=[
            column(sz.angles),
            column(sz.half),
            column(sz.half),
            column(sz.angles - 3 * sz.quarter),
            column(sz.quarter),
            column(sz.angles - 3 * sz.quarter),
            column(sz.quarter),
            pltpu.VMEM(ocean_mask.shape, ocean_mask.dtype),
            pltpu.VMEM(wind_field.shape, F32),
        ]
        + near_rows
        + [pltpu.SemaphoreType.DMA((9,))],
        name="pack",
    )(stay(energy4), stay(nest_energy), stay(ocean_mask), stay(wind_field))
    from_e = lax.ppermute(thick, "grid", down)
    from_w = lax.ppermute(thin, "grid", up)

    table, thin = lax.optimization_barrier((table, thin))
    moves, nest_moves, s_moves, gain, sea = kernel_call(
        functools.partial(setup_kernel, sz),
        (array(3, sz.ring), array(3, sz.ring), array(5, sz.side), array(sz.ring), array(VREG)),
        3,
        name="setup",
    )(table, ocean_mask, wind_field)
    energy, table = lax.optimization_barrier((energy, table))
    raw_a, raw_b = kernel_call(
        functools.partial(raw_kernel, sz), (half(sz.edge_rows), half(sz.edge_rows)), 1, name="raw"
    )(energy)
    pairs = [(i, i ^ 1) for i in range(sz.spec)]
    recv_raw_b = lax.ppermute(raw_b, "spec", [(i, (i + 1 if i % 2 else i - 1) % sz.spec) for i in range(sz.spec)])
    recv_raw_a = lax.ppermute(raw_a, "spec", pairs)
    rim = (rim_cell.T, rim_dest.T, rim_target.reshape(1, sz.rim), rim_weight.T)
    rim, raw_a = lax.optimization_barrier((rim, raw_a))
    mix = kernel_call(
        functools.partial(rim_kernel, sz),
        jax.ShapeDtypeStruct((sz.slots, (sz.cols + 1) * sz.lat + 128), BF16),
        4,
        name="rim",
    )(*rim)
    nest, raw_a = lax.optimization_barrier((nest, raw_a))
    nest_inner = kernel_call(functools.partial(nest_kernel, sz), field, 2, flops=3 * 10**10, name="nest")(nest, nest_moves)
    energy, raw_a = lax.optimization_barrier((energy, raw_a))
    adv, total = kernel_call(
        functools.partial(local_kernel, sz), (field, array(VREG)), 3, flops=3 * 10**10, name="local"
    )(energy, moves, sea)
    from_e, from_w, mix, nest_inner, adv = lax.optimization_barrier((from_e, from_w, mix, nest_inner, adv))

    msg_b = kernel_call(
        functools.partial(pass_kernel, sz),
        half(sz.pass_rows),
        2,
        scratch=near_rows + [vmem(sz.pass_rows)],
        name="pass",
    )(from_w, from_e)
    adv, side, msg_a, part = kernel_call(
        functools.partial(edge_kernel, sz),
        (field, array(sz.bands * sz.side), half(sz.fix_rows), array(VREG)),
        8,
        scratch=near_rows + [vmem(sz.bands * sz.side), vmem(sz.fix_rows)],
        aliases={0: 0},
        flops=3 * 10**10,
        name="edges",
    )(adv, total, energy, from_w, from_e, moves, s_moves, sea)

    msg_a, msg_b = lax.optimization_barrier((msg_a, msg_b))
    recv_a = lax.ppermute(msg_a, "spec", pairs)
    recv_b = lax.ppermute(msg_b, both, across)
    recv_a, recv_raw_a, recv_raw_b = lax.optimization_barrier((recv_a, recv_raw_a, recv_raw_b))
    plain, far_near = kernel_call(
        functools.partial(beyond_kernel, sz),
        (array(sz.bands + 2 * reach, sz.ring), array(reach * sz.side)),
        4,
        scratch=[vmem(sz.edge_rows)],
        flops=3 * 10**10,
        name="beyond",
    )(recv_raw_a, recv_raw_b, moves, sea)
    pieces = recv_a[sz.sum_row : sz.sum_row + 3 * VREG].astype(F32)
    pair = part + pieces.reshape(3, VREG, sz.lat).sum(axis=0)
    other = jnp.zeros_like(pair)
    step = 2
    while step < sz.spec:
        pair = pair + other
        other = lax.ppermute(pair, "spec", [(i, i ^ (2 * step - 1)) for i in range(sz.spec)])
        step *= 2

    _, nest_adv = kernel_call(
        functools.partial(nest_edge_kernel, sz),
        (field, array(sz.cols, sz.bins + VREG)),
        4,
        scratch=near_rows,
        aliases={0: 0},
        name="nest_edge",
    )(nest_inner, from_w, from_e, nest_moves)

    padded, centres, turns = sz.bands + 2 * reach, sz.bands + reach, sz.ring + 3 * VREG
    arrays = (
        array(padded, sz.ring),
        array(padded, turns),
        array(centres, turns),
        array(centres, turns),
        array(padded, sz.frame),
        array(centres, sz.frame),
        array(centres, sz.frame),
    )
    *inner, num = kernel_call(
        functools.partial(inner_kernel, sz),
        arrays + (field,),
        5,
        scratch=[vmem(sz.fix_rows)],
        aliases={4: 0},
        name="inner",
    )(adv, side, recv_a, gain, plain)
    nest_adv, recv_b = lax.optimization_barrier((nest_adv, recv_b))
    global_next, msg, *_ = kernel_call(
        functools.partial(source_kernel, sz),
        (field, jax.ShapeDtypeStruct((sz.slots, sz.lanes), BF16)) + arrays,
        13 + len(arrays),
        scratch=[vmem(sz.bins + VREG), vmem(sz.pass_rows), vmem(reach * sz.side), vmem(sz.rows), pltpu.SemaphoreType.DMA((sz.bands,))],
        out_hbm=(0,),
        aliases={13 + i: 2 + i for i in range(len(arrays))},
        name="sources",
    )(adv, side, recv_b, pair, other, gain, moves, s_moves, sea, from_e, mix, far_near, num, *inner)

    recv = lax.all_to_all(msg, "grid", split_axis=0, concat_axis=0, tiled=True)
    nest_next = kernel_call(
        functools.partial(blend_kernel, sz),
        field,
        2,
        out_hbm=(0,),
        scratch=[vmem(sz.rows), pltpu.SemaphoreType.DMA((sz.lanes // 128,))],
        name="blend",
    )(recv, nest_adv)
    full = (sz.bands, sz.angles, sz.cols, sz.lat)
    return global_next.reshape(full), nest_next.reshape(full)


def solution(mesh):
    in_specs = (
        P("spec", None, "grid", None),
        P("spec", None, "grid", None),
        P("grid", None),
        P(None, "grid", None),
        P("grid", None),
        P("grid", None),
        P("grid"),
        P("grid", None),
    )
    out_specs = (P("spec", None, "grid", None), P("spec", None, "grid", None))
    return jax.shard_map(
        functools.partial(per_device, mesh),
        mesh=mesh,
        in_specs=in_specs,
        out_specs=out_specs,
        check_vma=False,
    )
```

```python
import functools

import jax
import jax.numpy as jnp
import numpy as np
from jax import lax
from jax.experimental import pallas as pl
from jax.experimental.pallas import tpu as pltpu
from jax.sharding import PartitionSpec as P

ratio_step = 1.1
speed_coef = 0.054
wind_coef = 0.05
dissip_coef = 0.2
nonlin_coef = 0.12
nest_speedup = 2.0
reach = 5

VREG = 8
BF16 = jnp.bfloat16
F32 = jnp.float32


class Sizes:
    def __init__(self, mesh, energy, rim_rows):
        self.grid = mesh.shape["grid"]
        self.spec = mesh.shape["spec"]
        self.bands, self.angles, self.cols, self.lat = energy.shape
        self.freqs = self.bands * self.spec
        self.bins = self.bands * self.angles
        self.ring = self.angles * self.cols
        self.rows = self.bins * self.cols
        self.vregs = self.ring // VREG
        self.rim = rim_rows
        self.cap = max(2, (2 * rim_rows + self.grid - 1) // self.grid)
        self.slots = self.grid * self.cap
        self.lanes = (self.bins + 3 + 127) // 128 * 128
        self.half = self.angles // 2
        self.quarter = self.angles // 4
        self.side = (self.angles + VREG - 1) // VREG * VREG
        self.frame = self.side + 2 * VREG
        self.thin = self.bands * self.half
        self.thin_rows = (2 * self.thin + 15) // 16 * 16
        self.thick = self.angles + self.half
        self.info = self.bands * self.thick
        self.thick_nest = (self.info + 7 + VREG - 1) // VREG * VREG
        self.thick_rows = (self.thick_nest + self.thin + 15) // 16 * 16
        self.edge_rows = reach * self.ring
        self.rim_band = 2 * self.half
        self.far_band = self.rim_band + self.angles
        self.sum_row = (reach * self.far_band + VREG - 1) // VREG * VREG
        self.fix_rows = (self.sum_row + 3 * VREG + 15) // 16 * 16
        self.pass_thick = (reach * self.half + VREG - 1) // VREG * VREG
        self.pass_rows = max(self.fix_rows + 16, (self.pass_thick + reach * self.thick + 15) // 16 * 16)


def band_ratio(sz, band, inverse=False):
    rank = lax.axis_index("spec")
    ratio = F32(0.0)
    for s in range(sz.spec):
        power = ratio_step ** (s * sz.bands + band - sz.freqs // 2)
        ratio = jnp.where(rank == s, F32(1.0 / power if inverse else power), ratio)
    return ratio


def over_bands(count, ratio, body, inverse=False):
    step = F32(1.0 / ratio_step if inverse else ratio_step)

    def turn(i, r):
        body(i, r)
        return r * step

    lax.fori_loop(0, count, turn, ratio)


def angle_table(sz):
    heading = 2.0 * np.pi * np.arange(sz.angles) / sz.angles
    table = np.zeros((sz.ring + VREG + sz.side, sz.lat), np.float32)
    table[sz.ring + VREG :][: sz.angles, 0] = np.cos(heading)
    table[sz.ring + VREG :][: sz.angles, 1] = np.sin(heading)
    table[: sz.ring, 0] = np.repeat(np.cos(heading), sz.cols)
    table[: sz.ring, 1] = np.repeat(np.sin(heading), sz.cols)
    degrees = -60.0 + 120.0 * (np.arange(sz.lat) + 0.5) / sz.lat
    table[sz.ring : sz.ring + VREG] = 1.0 / np.cos(degrees * (np.pi / 180.0))
    return table


def from_west(sz, angle):
    return angle < sz.quarter or angle >= 3 * sz.quarter


def split3(x):
    high = x.astype(BF16).astype(F32)
    middle = (x - high).astype(BF16).astype(F32)
    return [high, middle, x - high - middle]


def upwind(sz, v):
    sub = lax.broadcasted_iota(jnp.int32, (VREG, sz.lat), 0)
    first, per = v * VREG // sz.cols, VREG // sz.cols
    wests = [from_west(sz, first + i) for i in range(per)]
    west = sub < 0
    for i in range(per):
        if wests[i]:
            west = west | ((sub >= i * sz.cols) & (sub < (i + 1) * sz.cols))
    return wests, west, sub % sz.cols


def west_half(sz):
    return ((3 * sz.quarter, sz.angles - 3 * sz.quarter), (0, sz.quarter))


def fetch(pairs, sems):
    copies = [pltpu.make_async_copy(a, b, sems.at[i]) for i, (a, b) in enumerate(pairs)]
    for c in copies:
        c.start()
    return copies


def far_band(sz):
    return jnp.where(lax.rem(lax.axis_index("spec"), 2) == 0, 0, sz.bands - reach)


def pack_kernel(
    sz, energy, nest, mask, wind, thin, thick, first, second, first_n, late, early, late_n, early_n,
    mask_v, wind_v, tmp_thin, tmp_thick, sems,
):
    from_east = pl.ds(sz.quarter, sz.half)
    (start, count), (_, rest) = west_half(sz)
    last = sz.cols - 1
    pairs = [
        (mask, mask_v),
        (wind, wind_v),
        (energy.at[:, :, 0], first),
        (energy.at[:, from_east, 1], second),
        (energy.at[:, pl.ds(start, count), last], late),
        (energy.at[:, pl.ds(0, rest), last], early),
        (nest.at[:, from_east, 0], first_n),
        (nest.at[:, pl.ds(start, count), last], late_n),
        (nest.at[:, pl.ds(0, rest), last], early_n),
    ]
    copies = [pltpu.make_async_copy(a, b, sems.at[i]) for i, (a, b) in enumerate(pairs)]
    for copy in copies:
        copy.start()
    spare = sz.thin_rows - 2 * sz.thin
    if spare:
        tmp_thin[pl.ds(2 * sz.thin, spare), :] = jnp.zeros((spare, sz.lat), F32)
    tmp_thick[...] = jnp.zeros_like(tmp_thick)
    for copy in copies[:6]:
        copy.wait()
    info = [mask_v[0:1, :].astype(F32)] + split3(wind_v[0, 0:1, :]) + split3(wind_v[1, 0:1, :])
    for i, line in enumerate(info):
        tmp_thick[pl.ds(sz.info + i, 1), :] = line
    for k in range(sz.bands):
        tmp_thin[pl.ds(k * sz.half, count), :] = late[k]
        tmp_thin[pl.ds(k * sz.half + count, rest), :] = early[k]
        tmp_thick[pl.ds(k * sz.thick, sz.angles), :] = first[k]
        tmp_thick[pl.ds(k * sz.thick + sz.angles, sz.half), :] = second[k]
    for copy in copies[6:]:
        copy.wait()
    for k in range(sz.bands):
        at = sz.thin + k * sz.half
        tmp_thin[pl.ds(at, count), :] = late_n[k]
        tmp_thin[pl.ds(at + count, rest), :] = early_n[k]
        tmp_thick[pl.ds(sz.thick_nest + k * sz.half, sz.half), :] = first_n[k]
    thin[...] = tmp_thin[...].astype(BF16)
    thick[...] = tmp_thick[...].astype(BF16)


def setup_kernel(sz, table, mask, wind, moves, nest_moves, s_moves, gain, sea):
    per = VREG // sz.cols
    sea[...] = jnp.concatenate([mask[...].astype(F32)] * per, axis=0)
    east_wind = jnp.concatenate([wind[0]] * per, axis=0)
    north_wind = jnp.concatenate([wind[1]] * per, axis=0)
    fill_moves(sz, 0, table, sz.cols, (moves, nest_moves))
    fill_moves(sz, sz.ring + VREG, table, 1, (s_moves, None))
    for v in range(sz.vregs):
        rows = table[pl.ds(v * VREG, VREG), :]
        along = rows[:, 0:1] * east_wind + rows[:, 1:2] * north_wind
        gain[pl.ds(v * VREG, VREG), :] = wind_coef * jnp.maximum(along, 0.0)
    for v in range(sz.side // VREG):
        rows = table[pl.ds(sz.ring + VREG + v * VREG, VREG), :]
        for i in range(2):
            s_moves[3 + i, pl.ds(v * VREG, VREG), :] = jnp.broadcast_to(rows[:, i : i + 1], (VREG, sz.lat))


def raw_kernel(sz, energy, raw_a, raw_b):
    for raw, first in ((raw_a, sz.bands - reach - far_band(sz)), (raw_b, far_band(sz))):
        raw[...] = energy[pl.ds(pl.multiple_of(first * sz.ring, VREG), sz.edge_rows), :].astype(BF16)


def pass_kernel(sz, from_w, from_e, msg, wide_w, wide_e, tmp):
    wide_w[...] = from_w[...].astype(F32)
    wide_e[...] = from_e[...].astype(F32)
    tmp[...] = jnp.zeros_like(tmp)
    first = far_band(sz)
    count = reach * sz.half
    tmp[pl.ds(0, count), :] = wide_w[pl.ds(first * sz.half, count), :]
    start = pl.multiple_of(first * sz.thick, VREG)
    tmp[pl.ds(sz.pass_thick, reach * sz.thick), :] = wide_e[pl.ds(start, reach * sz.thick), :]
    msg[...] = tmp[...].astype(BF16)


def fill_moves(sz, rows, table, cols, targets):
    lane = lax.broadcasted_iota(jnp.int32, (VREG, sz.lat), 1)
    sub = lax.broadcasted_iota(jnp.int32, (VREG, sz.lat), 0)
    sec = table[pl.ds(sz.ring, VREG), :]
    for v in range(targets[0].shape[1] // VREG):
        line = table[pl.ds(rows + v * VREG, VREG), :]
        along = jnp.broadcast_to(jnp.abs(line[:, 0:1]), (VREG, sz.lat))
        across = jnp.broadcast_to(jnp.abs(line[:, 1:2]), (VREG, sz.lat))
        edge = lane == jnp.where(sub < sz.half * cols - v * VREG, 0, sz.lat - 1)
        here = pl.ds(v * VREG, VREG)
        for target, by in zip(targets, (along * sec, along)):
            if target is not None:
                target[0, here, :] = by + across
                target[1, here, :] = by
                target[2, here, :] = jnp.where(edge, 0.0, across)


def beside(sz, x, turn):
    if turn >= VREG:
        return pltpu.roll(x, 1, 1)
    if turn <= 0:
        return pltpu.roll(x, sz.lat - 1, 1)
    sub = lax.broadcasted_iota(jnp.int32, (VREG, sz.lat), 0)
    return jnp.where(sub < turn, pltpu.roll(x, 1, 1), pltpu.roll(x, sz.lat - 1, 1))


def transported(sz, field, base, v, moves, speed):
    here = pl.ds(v * VREG, VREG)
    x = field[pl.ds(base + v * VREG, VREG), :]
    wests, west, col = upwind(sz, v)
    if all(wests):
        near, at_edge = pltpu.roll(x, 1, 0), col == 0
    elif not any(wests):
        near, at_edge = pltpu.roll(x, VREG - 1, 0), col == sz.cols - 1
    else:
        near = jnp.where(west, pltpu.roll(x, 1, 0), pltpu.roll(x, VREG - 1, 0))
        at_edge = jnp.where(west, col, sz.cols - 1 - col) == 0
    near = jnp.where(at_edge, 0.0, near)
    south = sz.half * sz.cols - v * VREG
    return x - speed * (moves[0, here, :] * x - moves[1, here, :] * near - moves[2, here, :] * beside(sz, x, south))


def edge_parts(sz, moves, wide_w, at_w, wide_e, at_e):
    parts = []
    for first, count in west_half(sz):
        parts.append((first, count, 0, wide_w[pl.ds(at_w, count), :]))
        at_w += count
    parts.append((sz.quarter, sz.half, sz.cols - 1, wide_e[pl.ds(at_e, sz.half), :]))
    for first, count, col, cells in parts:
        yield first, count, col, moves[1, pl.ds(first * sz.cols, count, stride=sz.cols), :] * cells


def side_transported(sz, x, near, v, s_moves, speed):
    here = pl.ds(v * VREG, VREG)
    move = s_moves[0, here, :] * x - s_moves[1, here, :] * near
    return x - speed * (move - s_moves[2, here, :] * beside(sz, x, sz.half - v * VREG))


def local_kernel(sz, energy, moves, sea, adv, total):
    total[...] = jnp.zeros_like(total)

    def band(k, inverse):
        base = pl.multiple_of(k * sz.ring, VREG)
        line = jnp.zeros((VREG, sz.lat), F32)
        for v in range(sz.vregs):
            out = sea[...] * transported(sz, energy, base, v, moves, speed_coef * inverse)
            adv[pl.ds(base + v * VREG, VREG), :] = out
            line = line + out
        total[...] = total[...] * F32(1.0 / ratio_step) + line

    over_bands(sz.bands, band_ratio(sz, 0, True), band, True)
    total[...] = total[...] * (0.1 * band_ratio(sz, sz.bands - 1))


def edge_kernel(
    sz, adv_in, total, energy, from_w, from_e, moves, s_moves, sea, adv, side, msg_a, part,
    wide_w, wide_e, s_near, fix,
):
    wide_w[...] = from_w[...].astype(F32)
    wide_e[...] = from_e[...].astype(F32)
    s_sea = wide_e[pl.ds(sz.info, 1), :]
    sub = lax.broadcasted_iota(jnp.int32, (VREG, sz.lat), 0)
    s_total = jnp.zeros((VREG, sz.lat), F32)
    lines = {}
    for k in range(sz.bands):
        inverse = band_ratio(sz, k, True)
        weight = 0.1 * band_ratio(sz, k)
        speed = speed_coef * inverse
        at_e = k * sz.thick + sz.quarter
        for first, count, col, moved in edge_parts(sz, moves, wide_w, k * sz.half, wide_e, at_e):
            moved = moved * (speed * sea[col : col + 1, :])
            rows = pl.ds(k * sz.ring + first * sz.cols + col, count, stride=sz.cols)
            adv[rows, :] = adv[rows, :] + moved
            lines[first, col] = lines.get((first, col), 0.0) + moved * weight
        at = k * sz.side
        for first, count in west_half(sz):
            start = k * sz.ring + first * sz.cols + sz.cols - 1
            s_near[pl.ds(at + first, count), :] = energy[pl.ds(start, count, stride=sz.cols), :]
        s_near[pl.ds(at + sz.quarter, sz.half), :] = wide_e[pl.ds(k * sz.thick + sz.angles, sz.half), :]
        if sz.side > sz.angles:
            rest = sz.side - sz.angles
            s_near[pl.ds(at + sz.angles, rest), :] = jnp.zeros((rest, sz.lat), F32)
        s_line = jnp.zeros((VREG, sz.lat), F32)
        for v in range(sz.side // VREG):
            x = wide_e[pl.ds(k * sz.thick + v * VREG, VREG), :]
            near = s_near[pl.ds(at + v * VREG, VREG), :]
            out = s_sea * side_transported(sz, x, near, v, s_moves, speed)
            side[pl.ds(at + v * VREG, VREG), :] = out
            s_line = s_line + (out if (v + 1) * VREG <= sz.angles else jnp.where(sub < sz.angles - v * VREG, out, 0.0))
        s_total = s_total + s_line * weight
    mine = total[0 : sz.cols, :]
    for i in range(1, VREG // sz.cols):
        mine = mine + total[i * sz.cols : (i + 1) * sz.cols, :]
    west, east = (
        sum(jnp.sum(x, axis=0, keepdims=True) for (_, c), x in lines.items() if c == col) for col in (0, sz.cols - 1)
    )
    between = jnp.zeros((sz.cols - 2, sz.lat), F32)
    mine = mine + jnp.concatenate([west, between, east], axis=0)
    s_sum = jnp.sum(s_total, axis=0, keepdims=True)
    sums = jnp.concatenate([mine, s_sum, jnp.zeros((VREG - sz.cols - 1, sz.lat), F32)], axis=0)
    part[...] = sums
    fix[...] = jnp.zeros_like(fix)
    fix[pl.ds(sz.sum_row, 3 * VREG), :] = jnp.concatenate(split3(sums), axis=0)
    start = sz.bands - reach - far_band(sz)
    for k in range(reach):
        band_row = pl.multiple_of((start + k) * sz.ring, VREG)
        at = k * sz.far_band
        for first, count in west_half(sz):
            fix[pl.ds(at, count), :] = adv[pl.ds(band_row + first * sz.cols, count, stride=sz.cols), :]
            at += count
        last = band_row + (sz.quarter + 1) * sz.cols - 1
        fix[pl.ds(at, sz.half), :] = adv[pl.ds(last, sz.half, stride=sz.cols), :]
        s_row = pl.multiple_of((start + k) * sz.side, VREG)
        fix[pl.ds(k * sz.far_band + sz.rim_band, sz.angles), :] = side[pl.ds(s_row, sz.angles), :]
    msg_a[...] = fix[...].astype(BF16)


def nest_kernel(sz, nest, moves, out):
    def band(k, inverse):
        base = pl.multiple_of(k * sz.ring, VREG)
        for v in range(sz.vregs):
            moved = transported(sz, nest, base, v, moves, nest_speedup * speed_coef * inverse)
            out[pl.ds(base + v * VREG, VREG), :] = moved

    over_bands(sz.bands, band_ratio(sz, 0, True), band, True)


def nest_edge_kernel(sz, inner, from_w, from_e, moves, out, columns, wide_w, wide_e):
    grid_rank = lax.axis_index("grid")
    quarter = sz.grid // 4
    keep_w = jnp.where((grid_rank != quarter) & (grid_rank != 3 * quarter), 1.0, 0.0).astype(F32)
    keep_e = jnp.where((grid_rank != quarter - 1) & (grid_rank != 3 * quarter - 1), 1.0, 0.0).astype(F32)
    wide_w[...] = from_w[...].astype(F32)
    wide_e[...] = from_e[...].astype(F32)
    for k in range(sz.bands):
        speed = nest_speedup * speed_coef * band_ratio(sz, k, True)
        at_w, at_e = sz.thin + k * sz.half, sz.thick_nest + k * sz.half
        for first, count, col, moved in edge_parts(sz, moves, wide_w, at_w, wide_e, at_e):
            rows = pl.ds(k * sz.ring + first * sz.cols + col, count, stride=sz.cols)
            out[rows, :] = out[rows, :] + moved * (speed * (keep_w if col == 0 else keep_e))
    for c in range(sz.cols):
        columns[c, pl.ds(0, sz.bins), :] = out[pl.ds(c, sz.bins, stride=sz.cols), :]


def dot_lanes(a, b):
    return lax.dot_general(a, b, (((1,), (1,)), ((), ())), preferred_element_type=F32)


def rim_kernel(sz, cell, dest, target, weight, mix):
    device = lax.broadcasted_iota(jnp.int32, (sz.grid, sz.rim), 0)
    hot = jnp.where(device == dest[...], 1.0, 0.0)
    before = lax.broadcasted_iota(jnp.int32, (sz.rim, sz.rim), 0)
    after = lax.broadcasted_iota(jnp.int32, (sz.rim, sz.rim), 1)
    earlier = jnp.dot(
        hot.astype(BF16), jnp.where(before < after, 1.0, 0.0).astype(BF16), preferred_element_type=F32
    )
    rank = jnp.sum(hot * earlier, axis=0, keepdims=True)
    place = dest[...] * sz.cap + rank.astype(jnp.int32)
    slot = lax.broadcasted_iota(jnp.int32, (sz.slots, sz.rim), 0)
    takes = jnp.where(slot == place, 1.0, 0.0).astype(BF16)
    row = lax.broadcasted_iota(jnp.int32, (sz.lat, sz.rim), 0)
    col = cell[0:1, :] - lax.axis_index("grid") * sz.cols
    south_row = cell[1:2, :]
    ex, ny = weight[0:1, :], weight[1:2, :]
    for c in range(sz.cols + 1):
        share = jnp.where(col == c, 1.0 - ex, 0.0) + jnp.where(col + 1 == c, ex, 0.0)
        south, north = share * (1.0 - ny), share * ny
        corner = jnp.where(row == south_row, south, 0.0) + jnp.where(row == south_row + 1, north, 0.0)
        mix[:, c * sz.lat : (c + 1) * sz.lat] = dot_lanes(takes, corner.astype(BF16)).astype(BF16)
    at = sz.bins - (sz.lanes - 128)
    line = lax.broadcasted_iota(jnp.int32, (128, sz.rim), 0)
    t = target[...]
    t_col = t // sz.lat
    about = jnp.where(line == at, t_col.astype(F32), 0.0)
    about = about + jnp.where(line == at + 1, (t - t_col * sz.lat).astype(F32), 0.0)
    about = about + jnp.where(line == at + 2, weight[2:3, :], 0.0)
    n = (sz.cols + 1) * sz.lat
    mix[:, n : n + 128] = dot_lanes(takes, about.astype(BF16)).astype(BF16)


def low_rows(sz):
    return lax.broadcasted_iota(jnp.int32, (VREG, sz.lat), 0) < VREG // 2


def put(sz, plain, turned, slot, vals):
    nv, low = sz.vregs, low_rows(sz)
    for v in range(nv):
        if plain is not None:
            plain[slot, pl.ds(v * VREG, VREG), :] = vals[v]
        nxt = pltpu.roll(jnp.where(low, vals[(v + 1) % nv], vals[v]), VREG // 2, 0)
        turned[slot, pl.ds((v + 2) * VREG, VREG), :] = nxt
        if v >= nv - 2:
            turned[slot, pl.ds((v + 2 - nv) * VREG, VREG), :] = nxt
        if v == 0:
            turned[slot, pl.ds((nv + 2) * VREG, VREG), :] = nxt


def close(sz, ref, slot):
    ref[slot, pl.ds(VREG - 3, 3), :] = ref[slot, pl.ds(VREG + sz.angles - 3, 3), :]
    ref[slot, pl.ds(VREG + sz.angles, 3), :] = ref[slot, pl.ds(VREG, 3), :]


def s_put(sz, s_plain, slot, load):
    for v in range(sz.side // VREG):
        s_plain[slot, pl.ds((v + 1) * VREG, VREG), :] = load(v)
    close(sz, s_plain, slot)


def exchange(sc, c, up, down):
    return sc * (c * (up + down) - 2.0 * (up * down))


def strengths(sz, ratio, n, plain, turned, plus, minus, s_plain, s_plus, s_minus):
    nv = sz.vregs
    strength = nonlin_coef * ratio
    for v in range(nv):
        c = plain[n + 3, pl.ds(v * VREG, VREG), :]
        sc = strength * c
        for ref, up_row, down_row in ((plus, v + 3, v + 1), (minus, v, v + 2)):
            up = turned[n + 5, pl.ds(up_row * VREG, VREG), :]
            down = turned[n, pl.ds(down_row * VREG, VREG), :]
            delta = exchange(sc, c, up, down)
            ref[n, pl.ds((v + 1) * VREG, VREG), :] = delta
            if v == nv - 1:
                ref[n, pl.ds(0, VREG), :] = delta
            if v < 2:
                ref[n, pl.ds((nv + 1 + v) * VREG, VREG), :] = delta
    for v in range(sz.side // VREG):
        row = (v + 1) * VREG
        c = s_plain[n + 3, pl.ds(row, VREG), :]
        sc = strength * c
        for ref, s in ((s_plus, 1), (s_minus, -1)):
            up = s_plain[n + 5, pl.ds(row + 3 * s, VREG), :]
            down = s_plain[n, pl.ds(row - s, VREG), :]
            ref[n, pl.ds(row, VREG), :] = exchange(sc, c, up, down)
    close(sz, s_plus, n)
    close(sz, s_minus, n)


def is_even():
    return lax.rem(lax.axis_index("spec"), 2) == 0


def complete(sz, slot, fix, k, plain, s_plain):
    at = k * sz.far_band
    for start, count in west_half(sz):
        plain[slot, pl.ds(start * sz.cols, count, stride=sz.cols), :] = fix[pl.ds(at, count), :]
        at += count
    last = (sz.quarter + 1) * sz.cols - 1
    plain[slot, pl.ds(last, sz.half, stride=sz.cols), :] = fix[pl.ds(at, sz.half), :]
    at = k * sz.far_band + sz.rim_band
    s_put(sz, s_plain, slot, lambda v: fix[pl.ds(at + v * VREG, VREG), :])


def turn_halo(sz, base, plain, turned, real=None):
    def halo(k, carry):
        vals = [plain[base + k, pl.ds(v * VREG, VREG), :] for v in range(sz.vregs)]
        put(sz, None if real is None else plain, turned, base + k, vals if real is None else [x * real for x in vals])
        return carry

    lax.fori_loop(0, reach, halo, 0)


def numerators(sz, k, ratio, adv, gain, plus, minus, store):
    nv, low = sz.vregs, low_rows(sz)
    base = pl.multiple_of(k * sz.ring, VREG)

    def moved_in(v):
        return (
            plus[k, pl.ds(v * VREG, VREG), :]
            + minus[k, pl.ds((v + 3) * VREG, VREG), :]
            + plus[k + 5, pl.ds((v + 2) * VREG, VREG), :]
            + minus[k + 5, pl.ds((v + 1) * VREG, VREG), :]
        )

    before = moved_in(nv - 1)
    for v in range(nv):
        now = moved_in(v)
        moved = pltpu.roll(jnp.where(low, now, before), VREG // 2, 0)
        before = now
        here = pl.ds((v + 1) * VREG, VREG)
        transfer = moved - 2.0 * (plus[k + 2, here, :] + minus[k + 2, here, :])
        a = adv[pl.ds(base + v * VREG, VREG), :]
        grown = ratio * gain[pl.ds(v * VREG, VREG), :]
        store(pl.ds(base + v * VREG, VREG), a + grown * a + transfer)


def beyond_kernel(sz, raw_a, raw_b, moves, sea, plain, far_near, wide):
    base_a = jnp.where(is_even(), sz.bands + reach, 0)
    base_b = sz.bands + reach - base_a
    below, above = band_ratio(sz, -reach, True), band_ratio(sz, sz.bands, True)

    for raw, first, inverse in (
        (raw_a, base_a, jnp.where(is_even(), above, below)),
        (raw_b, base_b, jnp.where(is_even(), below, above)),
    ):
        wide[...] = raw[...].astype(F32)

        def transport(k, r, first=first):
            base = pl.multiple_of(k * sz.ring, VREG)
            for v in range(sz.vregs):
                moved = transported(sz, wide, base, v, moves, speed_coef * r)
                plain[first + k, pl.ds(v * VREG, VREG), :] = sea[...] * moved

        over_bands(reach, inverse, transport, True)

    far_near[...] = jnp.zeros_like(far_near)
    for k in range(reach):
        for first, count in west_half(sz):
            start = k * sz.ring + first * sz.cols + sz.cols - 1
            far_near[pl.ds(k * sz.side + first, count), :] = wide[pl.ds(start, count, stride=sz.cols), :]

def inner_kernel(
    sz, adv, side, recv_a, gain, plain_in, plain, turned, plus, minus, s_plain, s_plus, s_minus, num, fix
):
    base_a = jnp.where(is_even(), sz.bands + reach, 0)

    def own(k, carry):
        base = pl.multiple_of(k * sz.ring, VREG)
        put(sz, plain, turned, k + reach, [adv[pl.ds(base + v * VREG, VREG), :] for v in range(sz.vregs)])
        s_base = pl.multiple_of(k * sz.side, VREG)
        s_put(sz, s_plain, k + reach, lambda v: side[pl.ds(s_base + v * VREG, VREG), :])
        return carry

    lax.fori_loop(0, sz.bands, own, 0)

    fix[...] = recv_a[...].astype(F32)
    for k in range(reach):
        complete(sz, base_a + k, fix, k, plain, s_plain)
    turn_halo(sz, base_a, plain, turned)

    arrays = (plain, turned, plus, minus, s_plain, s_plus, s_minus)
    start = jnp.where(is_even(), reach, 0)
    ratio = jnp.where(is_even(), band_ratio(sz, 3), band_ratio(sz, 3 - reach))
    over_bands(sz.bands, ratio, lambda i, r: strengths(sz, r, start + i, *arrays))

    def store(rows, value):
        num[rows, :] = value

    ratio = jnp.where(is_even(), band_ratio(sz, reach), band_ratio(sz, 0))
    over_bands(
        sz.bands - reach, ratio, lambda i, r: numerators(sz, start + i, r, adv, gain, plus, minus, store)
    )


def source_kernel(
    sz, adv, side, recv_b, pair, other, gain, moves, s_moves, sea, from_e, mix, far_near, num,
    plain_in, turned_in, plus_in, minus_in, s_plain_in, s_plus_in, s_minus_in,
    result_hbm, msg, plain, turned, plus, minus, s_plain, s_plus, s_minus, s_out, wide, s_near, out, sems,
):
    spec_rank = lax.axis_index("spec")
    ns = sz.side // VREG
    total_weight = sz.angles * 0.1 * sum(ratio_step ** (k - sz.freqs // 2) for k in range(sz.freqs))
    means = (pair[...] + other[...]) * (1.0 / total_weight)
    mean = jnp.concatenate([means[0 : sz.cols]] * (VREG // sz.cols), axis=0)
    s_mean = means[sz.cols : sz.cols + 1]

    def write(k):
        band = pl.ds(pl.multiple_of(k * sz.ring, VREG), sz.ring)
        return pltpu.make_async_copy(out.at[band], result_hbm.at[band], sems.at[k])

    def scale(ratio):
        return 1.0 / (1.0 + (dissip_coef * ratio * ratio) * mean)

    ready = jnp.where(is_even(), reach, 0)

    def finish(i, ratio):
        factor = scale(ratio)
        base = pl.multiple_of((ready + i) * sz.ring, VREG)
        for v in range(sz.vregs):
            here = pl.ds(base + v * VREG, VREG)
            out[here, :] = num[here, :] * factor
        write(ready + i).start()

    over_bands(sz.bands - reach, jnp.where(is_even(), band_ratio(sz, reach), band_ratio(sz, 0)), finish)

    base_b = jnp.where(is_even(), 0, sz.bands + reach)
    real_b = jnp.where((spec_rank == 0) | (spec_rank == sz.spec - 1), 0.0, 1.0).astype(F32)
    info = from_e[pl.ds(sz.info // 16 * 16, 32), :].astype(F32)
    at = sz.info % 16
    s_sea = info[at : at + 1] * real_b
    wide[...] = recv_b[...].astype(F32)
    s_near[...] = far_near[...]
    inverse = jnp.where(is_even(), band_ratio(sz, -reach, True), band_ratio(sz, sz.bands, True))
    for k in range(reach):
        speed = inverse * (speed_coef / ratio_step**k)
        slot, row = base_b + k, sz.pass_thick + k * sz.thick
        for start, count, col, moved in edge_parts(sz, moves, wide, k * sz.half, wide, row + sz.quarter):
            rows = pl.ds(start * sz.cols + col, count, stride=sz.cols)
            plain[slot, rows, :] = plain[slot, rows, :] + moved * (speed * sea[col : col + 1, :])
        at_near = k * sz.side
        s_near[pl.ds(at_near + sz.quarter, sz.half), :] = wide[pl.ds(row + sz.angles, sz.half), :]

        def column(v):
            x = wide[pl.ds(row + v * VREG, VREG), :]
            near = s_near[pl.ds(at_near + v * VREG, VREG), :]
            return s_sea * side_transported(sz, x, near, v, s_moves, speed)

        s_put(sz, s_plain, slot, column)
    turn_halo(sz, base_b, plain, turned, real_b)
    arrays = (plain, turned, plus, minus, s_plain, s_plus, s_minus)
    begin = jnp.where(is_even(), 0, sz.bands)
    ratio = jnp.where(is_even(), band_ratio(sz, 3 - reach), band_ratio(sz, sz.bands + 3 - reach))
    over_bands(reach, ratio, lambda i, r: strengths(sz, r, begin + i, *arrays))

    at = at + 1
    s_east = info[at : at + 1] + info[at + 1 : at + 2] + info[at + 2 : at + 3]
    s_north = info[at + 3 : at + 4] + info[at + 4 : at + 5] + info[at + 5 : at + 6]
    missing = jnp.where(is_even(), 0, sz.bands - reach)

    def result(i, ratio):
        factor = scale(ratio)

        def store(rows, value):
            out[rows, :] = value * factor

        numerators(sz, missing + i, ratio, adv, gain, plus, minus, store)
        write(missing + i).start()

    over_bands(reach, jnp.where(is_even(), band_ratio(sz, 0), band_ratio(sz, sz.bands - reach)), result)

    s_gain = []
    for v in range(ns):
        here = pl.ds(v * VREG, VREG)
        along = s_moves[3, here, :] * s_east + s_moves[4, here, :] * s_north
        s_gain.append(wind_coef * jnp.maximum(along, 0.0))
    for k in range(sz.bands):
        ratio = band_ratio(sz, k)
        factor = 1.0 / (1.0 + (dissip_coef * ratio * ratio) * s_mean)
        for v in range(ns):
            row = (v + 1) * VREG
            here = pl.ds(row, VREG)
            transfer = (
                s_plus[k, pl.ds(row - 3, VREG), :]
                + s_minus[k, pl.ds(row + 3, VREG), :]
                + s_plus[k + 5, pl.ds(row + 1, VREG), :]
                + s_minus[k + 5, pl.ds(row - 1, VREG), :]
                - 2.0 * (s_plus[k + 2, here, :] + s_minus[k + 2, here, :])
            )
            a = side[pl.ds(k * sz.side + v * VREG, VREG), :]
            s_out[pl.ds(k * sz.angles + v * VREG, VREG), :] = (a + (ratio * s_gain[v]) * a + transfer) * factor

    pad = jnp.zeros((sz.lanes - sz.bins, sz.lat), BF16)
    columns = [out[pl.ds(c, sz.bins, stride=sz.cols), :] for c in range(sz.cols)]
    columns.append(s_out[pl.ds(0, sz.bins), :])
    columns = [jnp.concatenate([c.astype(BF16), pad], axis=0) for c in columns]
    n = (sz.cols + 1) * sz.lat
    spectra = dot_lanes(mix[:, 0:n], jnp.concatenate(columns, axis=1))
    about = mix[:, n : n + 128].astype(F32)
    msg[:, 0 : sz.lanes - 128] = spectra[:, : sz.lanes - 128].astype(BF16)
    msg[:, sz.lanes - 128 : sz.lanes] = (spectra[:, sz.lanes - 128 :] + about).astype(BF16)
    for k in range(sz.bands):
        write(k).wait()


def blend_kernel(sz, recv, nest_adv, result_hbm, out, sems):
    at = sz.bins - (sz.lanes - 128)
    about = recv[:, sz.lanes - 128 :].astype(F32)
    t_col, t_row, rate = about[:, at : at + 1], about[:, at + 1 : at + 2], about[:, at + 2 : at + 3]
    lane = lax.broadcasted_iota(jnp.int32, (sz.slots, sz.lat), 1).astype(F32)
    hit = jnp.where(lane == t_row, rate, 0.0)
    relax = [jnp.where(t_col == float(c), hit, 0.0) for c in range(sz.cols)]
    kept = [1.0 - jnp.sum(r, axis=0, keepdims=True) for r in relax]
    relax = jnp.concatenate(relax, axis=1).astype(BF16)
    writes = []
    for part, start in enumerate(range(0, sz.bins, 128)):
        count = min(128, sz.bins - start)
        added = lax.dot_general(
            recv[:, start : start + 128], relax, (((0,), (0,)), ((), ())), preferred_element_type=F32
        )
        for c in range(sz.cols):
            here = pl.ds(start * sz.cols + c, count, stride=sz.cols)
            own = nest_adv[c, pl.ds(start, count), :]
            out[here, :] = own * kept[c] + added[:count, c * sz.lat : (c + 1) * sz.lat]
        rows = pl.ds(start * sz.cols, count * sz.cols)
        writes.append(pltpu.make_async_copy(out.at[rows], result_hbm.at[rows], sems.at[part]))
        writes[-1].start()
    for write in writes:
        write.wait()


def kernel_call(body, out_shape, n_in, hbm=(), out_hbm=(), scratch=(), aliases=None, flops=0, name=None):
    def specs(count, far):
        return [pl.BlockSpec(memory_space=pltpu.HBM if i in far else pltpu.VMEM) for i in range(count)]

    many = isinstance(out_shape, tuple)
    out_specs = specs(len(out_shape) if many else 1, out_hbm)
    call = pl.pallas_call(
        body,
        out_shape=out_shape,
        in_specs=specs(n_in, hbm),
        out_specs=out_specs if many else out_specs[0],
        scratch_shapes=list(scratch),
        input_output_aliases=aliases or {},
        compiler_params=pltpu.CompilerParams(vmem_limit_bytes=20 * 2**20),
        cost_estimate=pl.CostEstimate(flops=flops, bytes_accessed=0, transcendentals=0) if flops else None,
        name=name,
    )
    if not aliases:
        return call

    def in_place(*args):
        pin = functools.partial(pltpu.with_memory_space_constraint, memory_space=pltpu.VMEM)
        return call(*[pin(a) if i in aliases else a for i, a in enumerate(args)])

    return in_place


def per_device(
    mesh, energy, nest_energy, ocean_mask, wind_field, rim_cell, rim_dest, rim_target, rim_weight
):
    sz = Sizes(mesh, energy, rim_dest.shape[0])

    def array(*shape, dtype=F32):
        return jax.ShapeDtypeStruct(shape + (sz.lat,), dtype)

    def vmem(*shape):
        return pltpu.VMEM(shape + (sz.lat,), F32)

    def half(rows):
        return array(rows, dtype=BF16)

    field = array(sz.rows)
    table = jnp.asarray(angle_table(sz))
    energy4, energy = energy, energy.reshape(sz.rows, sz.lat)
    nest = nest_energy.reshape(sz.rows, sz.lat)
    up = [(i, (i + 1) % sz.grid) for i in range(sz.grid)]
    down = [(j, i) for i, j in up]
    across = []
    for g in range(sz.grid):
        for i in range(sz.spec):
            j = i + 1 if i % 2 else i - 1
            to = (g, j) if 0 <= j < sz.spec else ((g ^ 2) % sz.grid, i)
            across.append((g * sz.spec + i, to[0] * sz.spec + to[1]))
    both = ("grid", "spec")
    near_rows = [vmem(sz.thin_rows), vmem(sz.thick_rows)]

    stay = functools.partial(pltpu.with_memory_space_constraint, memory_space=pltpu.HBM)
    def column(n):
        return vmem(sz.bands, n)

    thin, thick = kernel_call(
        functools.partial(pack_kernel, sz),
        (half(sz.thin_rows), half(sz.thick_rows)),
        4,
        hbm=range(4),
        scratch=[
            column(sz.angles),
            column(sz.half),
            column(sz.half),
            column(sz.angles - 3 * sz.quarter),
            column(sz.quarter),
            column(sz.angles - 3 * sz.quarter),
            column(sz.quarter),
            pltpu.VMEM(ocean_mask.shape, ocean_mask.dtype),
            pltpu.VMEM(wind_field.shape, F32),
        ]
        + near_rows
        + [pltpu.SemaphoreType.DMA((9,))],
        name="pack",
    )(stay(energy4), stay(nest_energy), stay(ocean_mask), stay(wind_field))
    from_e = lax.ppermute(thick, "grid", down)
    from_w = lax.ppermute(thin, "grid", up)

    table, thin = lax.optimization_barrier((table, thin))
    moves, nest_moves, s_moves, gain, sea = kernel_call(
        functools.partial(setup_kernel, sz),
        (array(3, sz.ring), array(3, sz.ring), array(5, sz.side), array(sz.ring), array(VREG)),
        3,
        name="setup",
    )(table, ocean_mask, wind_field)
    energy, table = lax.optimization_barrier((energy, table))
    raw_a, raw_b = kernel_call(
        functools.partial(raw_kernel, sz), (half(sz.edge_rows), half(sz.edge_rows)), 1, name="raw"
    )(energy)
    pairs = [(i, i ^ 1) for i in range(sz.spec)]
    recv_raw_b = lax.ppermute(raw_b, "spec", [(i, (i + 1 if i % 2 else i - 1) % sz.spec) for i in range(sz.spec)])
    recv_raw_a = lax.ppermute(raw_a, "spec", pairs)
    rim = (rim_cell.T, rim_dest.T, rim_target.reshape(1, sz.rim), rim_weight.T)
    rim, raw_a = lax.optimization_barrier((rim, raw_a))
    mix = kernel_call(
        functools.partial(rim_kernel, sz),
        jax.ShapeDtypeStruct((sz.slots, (sz.cols + 1) * sz.lat + 128), BF16),
        4,
        name="rim",
    )(*rim)
    nest, raw_a = lax.optimization_barrier((nest, raw_a))
    nest_inner = kernel_call(functools.partial(nest_kernel, sz), field, 2, flops=3 * 10**10, name="nest")(nest, nest_moves)
    energy, raw_a = lax.optimization_barrier((energy, raw_a))
    adv, total = kernel_call(
        functools.partial(local_kernel, sz), (field, array(VREG)), 3, flops=3 * 10**10, name="local"
    )(energy, moves, sea)
    from_e, from_w, mix, nest_inner, adv = lax.optimization_barrier((from_e, from_w, mix, nest_inner, adv))

    msg_b = kernel_call(
        functools.partial(pass_kernel, sz),
        half(sz.pass_rows),
        2,
        scratch=near_rows + [vmem(sz.pass_rows)],
        name="pass",
    )(from_w, from_e)
    adv, side, msg_a, part = kernel_call(
        functools.partial(edge_kernel, sz),
        (field, array(sz.bands * sz.side), half(sz.fix_rows), array(VREG)),
        8,
        scratch=near_rows + [vmem(sz.bands * sz.side), vmem(sz.fix_rows)],
        aliases={0: 0},
        flops=3 * 10**10,
        name="edges",
    )(adv, total, energy, from_w, from_e, moves, s_moves, sea)

    msg_a, msg_b = lax.optimization_barrier((msg_a, msg_b))
    recv_a = lax.ppermute(msg_a, "spec", pairs)
    recv_b = lax.ppermute(msg_b, both, across)
    recv_a, recv_raw_a, recv_raw_b = lax.optimization_barrier((recv_a, recv_raw_a, recv_raw_b))
    plain, far_near = kernel_call(
        functools.partial(beyond_kernel, sz),
        (array(sz.bands + 2 * reach, sz.ring), array(reach * sz.side)),
        4,
        scratch=[vmem(sz.edge_rows)],
        flops=3 * 10**10,
        name="beyond",
    )(recv_raw_a, recv_raw_b, moves, sea)
    pieces = recv_a[sz.sum_row : sz.sum_row + 3 * VREG].astype(F32)
    pair = part + pieces.reshape(3, VREG, sz.lat).sum(axis=0)
    other = jnp.zeros_like(pair)
    step = 2
    while step < sz.spec:
        pair = pair + other
        other = lax.ppermute(pair, "spec", [(i, i ^ (2 * step - 1)) for i in range(sz.spec)])
        step *= 2

    _, nest_adv = kernel_call(
        functools.partial(nest_edge_kernel, sz),
        (field, array(sz.cols, sz.bins + VREG)),
        4,
        scratch=near_rows,
        aliases={0: 0},
        name="nest_edge",
    )(nest_inner, from_w, from_e, nest_moves)

    padded, centres, turns = sz.bands + 2 * reach, sz.bands + reach, sz.ring + 3 * VREG
    arrays = (
        array(padded, sz.ring),
        array(padded, turns),
        array(centres, turns),
        array(centres, turns),
        array(padded, sz.frame),
        array(centres, sz.frame),
        array(centres, sz.frame),
    )
    *inner, num = kernel_call(
        functools.partial(inner_kernel, sz),
        arrays + (field,),
        5,
        scratch=[vmem(sz.fix_rows)],
        aliases={4: 0},
        name="inner",
    )(adv, side, recv_a, gain, plain)
    nest_adv, recv_b = lax.optimization_barrier((nest_adv, recv_b))
    global_next, msg, *_ = kernel_call(
        functools.partial(source_kernel, sz),
        (field, jax.ShapeDtypeStruct((sz.slots, sz.lanes), BF16)) + arrays,
        13 + len(arrays),
        scratch=[vmem(sz.bins + VREG), vmem(sz.pass_rows), vmem(reach * sz.side), vmem(sz.rows), pltpu.SemaphoreType.DMA((sz.bands,))],
        out_hbm=(0,),
        aliases={13 + i: 2 + i for i in range(len(arrays))},
        name="sources",
    )(adv, side, recv_b, pair, other, gain, moves, s_moves, sea, from_e, mix, far_near, num, *inner)

    recv = lax.all_to_all(msg, "grid", split_axis=0, concat_axis=0, tiled=True)
    nest_next = kernel_call(
        functools.partial(blend_kernel, sz),
        field,
        2,
        out_hbm=(0,),
        scratch=[vmem(sz.rows), pltpu.SemaphoreType.DMA((sz.lanes // 128,))],
        name="blend",
    )(recv, nest_adv)
    full = (sz.bands, sz.angles, sz.cols, sz.lat)
    return global_next.reshape(full), nest_next.reshape(full)


def solution(mesh):
    in_specs = (
        P("spec", None, "grid", None),
        P("spec", None, "grid", None),
        P("grid", None),
        P(None, "grid", None),
        P("grid", None),
        P("grid", None),
        P("grid"),
        P("grid", None),
    )
    out_specs = (P("spec", None, "grid", None), P("spec", None, "grid", None))
    return jax.shard_map(
        functools.partial(per_device, mesh),
        mesh=mesh,
        in_specs=in_specs,
        out_specs=out_specs,
        check_vma=False,
    )
```

```python
import functools

import jax
import jax.numpy as jnp
import numpy as np
from jax import lax
from jax.experimental import pallas as pl
from jax.experimental.pallas import tpu as pltpu
from jax.sharding import PartitionSpec as P

ratio_step = 1.1
speed_coef = 0.054
wind_coef = 0.05
dissip_coef = 0.2
nonlin_coef = 0.12
nest_speedup = 2.0
reach = 5

VREG = 8
BF16 = jnp.bfloat16
F32 = jnp.float32


class Sizes:
    def __init__(self, mesh, energy, rim_rows):
        self.grid = mesh.shape["grid"]
        self.spec = mesh.shape["spec"]
        self.bands, self.angles, self.cols, self.lat = energy.shape
        self.freqs = self.bands * self.spec
        self.bins = self.bands * self.angles
        self.ring = self.angles * self.cols
        self.rows = self.bins * self.cols
        self.vregs = self.ring // VREG
        self.rim = rim_rows
        self.cap = max(2, (2 * rim_rows + self.grid - 1) // self.grid)
        self.slots = self.grid * self.cap
        self.lanes = (self.bins + 3 + 127) // 128 * 128
        self.half = self.angles // 2
        self.quarter = self.angles // 4
        self.side = (self.angles + VREG - 1) // VREG * VREG
        self.frame = self.side + 2 * VREG
        self.thin = self.bands * self.half
        self.thin_rows = (2 * self.thin + 15) // 16 * 16
        self.thick = self.angles + self.half
        self.info = self.bands * self.thick
        self.thick_nest = (self.info + 7 + VREG - 1) // VREG * VREG
        self.thick_rows = (self.thick_nest + self.thin + 15) // 16 * 16
        self.edge_rows = reach * self.ring
        self.rim_band = 2 * self.half
        self.far_band = self.rim_band + self.angles
        self.sum_row = (reach * self.far_band + VREG - 1) // VREG * VREG
        self.fix_rows = (self.sum_row + 3 * VREG + 15) // 16 * 16
        self.pass_thick = (reach * self.half + VREG - 1) // VREG * VREG
        self.pass_rows = max(self.fix_rows + 16, (self.pass_thick + reach * self.thick + 15) // 16 * 16)


def band_ratio(sz, band, inverse=False):
    rank = lax.axis_index("spec")
    ratio = F32(0.0)
    for s in range(sz.spec):
        power = ratio_step ** (s * sz.bands + band - sz.freqs // 2)
        ratio = jnp.where(rank == s, F32(1.0 / power if inverse else power), ratio)
    return ratio


def over_bands(count, ratio, body, inverse=False):
    step = F32(1.0 / ratio_step if inverse else ratio_step)

    def turn(i, r):
        body(i, r)
        return r * step

    lax.fori_loop(0, count, turn, ratio)


def angle_table(sz):
    heading = 2.0 * np.pi * np.arange(sz.angles) / sz.angles
    table = np.zeros((sz.ring + VREG + sz.side, sz.lat), np.float32)
    table[sz.ring + VREG :][: sz.angles, 0] = np.cos(heading)
    table[sz.ring + VREG :][: sz.angles, 1] = np.sin(heading)
    table[: sz.ring, 0] = np.repeat(np.cos(heading), sz.cols)
    table[: sz.ring, 1] = np.repeat(np.sin(heading), sz.cols)
    degrees = -60.0 + 120.0 * (np.arange(sz.lat) + 0.5) / sz.lat
    table[sz.ring : sz.ring + VREG] = 1.0 / np.cos(degrees * (np.pi / 180.0))
    return table


def from_west(sz, angle):
    return angle < sz.quarter or angle >= 3 * sz.quarter


def split3(x):
    high = x.astype(BF16).astype(F32)
    middle = (x - high).astype(BF16).astype(F32)
    return [high, middle, x - high - middle]


def upwind(sz, v):
    sub = lax.broadcasted_iota(jnp.int32, (VREG, sz.lat), 0)
    first, per = v * VREG // sz.cols, VREG // sz.cols
    wests = [from_west(sz, first + i) for i in range(per)]
    west = sub < 0
    for i in range(per):
        if wests[i]:
            west = west | ((sub >= i * sz.cols) & (sub < (i + 1) * sz.cols))
    return wests, west, sub % sz.cols


def west_half(sz):
    return ((3 * sz.quarter, sz.angles - 3 * sz.quarter), (0, sz.quarter))


def fetch(pairs, sems):
    copies = [pltpu.make_async_copy(a, b, sems.at[i]) for i, (a, b) in enumerate(pairs)]
    for c in copies:
        c.start()
    return copies


def far_band(sz):
    return jnp.where(lax.rem(lax.axis_index("spec"), 2) == 0, 0, sz.bands - reach)


def pack_kernel(
    sz, energy, nest, mask, wind, thin, thick, first, second, first_n, late, early, late_n, early_n,
    mask_v, wind_v, tmp_thin, tmp_thick, sems,
):
    from_east = pl.ds(sz.quarter, sz.half)
    (start, count), (_, rest) = west_half(sz)
    last = sz.cols - 1
    pairs = [
        (mask, mask_v),
        (wind, wind_v),
        (energy.at[:, :, 0], first),
        (energy.at[:, from_east, 1], second),
        (energy.at[:, pl.ds(start, count), last], late),
        (energy.at[:, pl.ds(0, rest), last], early),
        (nest.at[:, from_east, 0], first_n),
        (nest.at[:, pl.ds(start, count), last], late_n),
        (nest.at[:, pl.ds(0, rest), last], early_n),
    ]
    copies = [pltpu.make_async_copy(a, b, sems.at[i]) for i, (a, b) in enumerate(pairs)]
    for copy in copies:
        copy.start()
    spare = sz.thin_rows - 2 * sz.thin
    if spare:
        tmp_thin[pl.ds(2 * sz.thin, spare), :] = jnp.zeros((spare, sz.lat), F32)
    tmp_thick[...] = jnp.zeros_like(tmp_thick)
    for copy in copies[:6]:
        copy.wait()
    info = [mask_v[0:1, :].astype(F32)] + split3(wind_v[0, 0:1, :]) + split3(wind_v[1, 0:1, :])
    for i, line in enumerate(info):
        tmp_thick[pl.ds(sz.info + i, 1), :] = line
    for k in range(sz.bands):
        tmp_thin[pl.ds(k * sz.half, count), :] = late[k]
        tmp_thin[pl.ds(k * sz.half + count, rest), :] = early[k]
        tmp_thick[pl.ds(k * sz.thick, sz.angles), :] = first[k]
        tmp_thick[pl.ds(k * sz.thick + sz.angles, sz.half), :] = second[k]
    for copy in copies[6:]:
        copy.wait()
    for k in range(sz.bands):
        at = sz.thin + k * sz.half
        tmp_thin[pl.ds(at, count), :] = late_n[k]
        tmp_thin[pl.ds(at + count, rest), :] = early_n[k]
        tmp_thick[pl.ds(sz.thick_nest + k * sz.half, sz.half), :] = first_n[k]
    thin[...] = tmp_thin[...].astype(BF16)
    thick[...] = tmp_thick[...].astype(BF16)


def setup_kernel(sz, table, mask, wind, moves, nest_moves, s_moves, gain, sea):
    per = VREG // sz.cols
    sea[...] = jnp.concatenate([mask[...].astype(F32)] * per, axis=0)
    east_wind = jnp.concatenate([wind[0]] * per, axis=0)
    north_wind = jnp.concatenate([wind[1]] * per, axis=0)
    fill_moves(sz, 0, table, sz.cols, (moves, nest_moves))
    fill_moves(sz, sz.ring + VREG, table, 1, (s_moves, None))
    for v in range(sz.vregs):
        rows = table[pl.ds(v * VREG, VREG), :]
        along = rows[:, 0:1] * east_wind + rows[:, 1:2] * north_wind
        gain[pl.ds(v * VREG, VREG), :] = wind_coef * jnp.maximum(along, 0.0)
    for v in range(sz.side // VREG):
        rows = table[pl.ds(sz.ring + VREG + v * VREG, VREG), :]
        for i in range(2):
            s_moves[3 + i, pl.ds(v * VREG, VREG), :] = jnp.broadcast_to(rows[:, i : i + 1], (VREG, sz.lat))


def raw_kernel(sz, energy, raw_a, raw_b):
    for raw, first in ((raw_a, sz.bands - reach - far_band(sz)), (raw_b, far_band(sz))):
        raw[...] = energy[pl.ds(pl.multiple_of(first * sz.ring, VREG), sz.edge_rows), :].astype(BF16)


def pass_kernel(sz, from_w, from_e, msg, wide_w, wide_e, tmp):
    wide_w[...] = from_w[...].astype(F32)
    wide_e[...] = from_e[...].astype(F32)
    tmp[...] = jnp.zeros_like(tmp)
    first = far_band(sz)
    count = reach * sz.half
    tmp[pl.ds(0, count), :] = wide_w[pl.ds(first * sz.half, count), :]
    start = pl.multiple_of(first * sz.thick, VREG)
    tmp[pl.ds(sz.pass_thick, reach * sz.thick), :] = wide_e[pl.ds(start, reach * sz.thick), :]
    msg[...] = tmp[...].astype(BF16)


def fill_moves(sz, rows, table, cols, targets):
    lane = lax.broadcasted_iota(jnp.int32, (VREG, sz.lat), 1)
    sub = lax.broadcasted_iota(jnp.int32, (VREG, sz.lat), 0)
    sec = table[pl.ds(sz.ring, VREG), :]
    for v in range(targets[0].shape[1] // VREG):
        line = table[pl.ds(rows + v * VREG, VREG), :]
        along = jnp.broadcast_to(jnp.abs(line[:, 0:1]), (VREG, sz.lat))
        across = jnp.broadcast_to(jnp.abs(line[:, 1:2]), (VREG, sz.lat))
        edge = lane == jnp.where(sub < sz.half * cols - v * VREG, 0, sz.lat - 1)
        here = pl.ds(v * VREG, VREG)
        for target, by in zip(targets, (along * sec, along)):
            if target is not None:
                target[0, here, :] = by + across
                target[1, here, :] = by
                target[2, here, :] = jnp.where(edge, 0.0, across)


def beside(sz, x, turn):
    if turn >= VREG:
        return pltpu.roll(x, 1, 1)
    if turn <= 0:
        return pltpu.roll(x, sz.lat - 1, 1)
    sub = lax.broadcasted_iota(jnp.int32, (VREG, sz.lat), 0)
    return jnp.where(sub < turn, pltpu.roll(x, 1, 1), pltpu.roll(x, sz.lat - 1, 1))


def transported(sz, field, base, v, moves, speed):
    here = pl.ds(v * VREG, VREG)
    x = field[pl.ds(base + v * VREG, VREG), :]
    wests, west, col = upwind(sz, v)
    if all(wests):
        near, at_edge = pltpu.roll(x, 1, 0), col == 0
    elif not any(wests):
        near, at_edge = pltpu.roll(x, VREG - 1, 0), col == sz.cols - 1
    else:
        near = jnp.where(west, pltpu.roll(x, 1, 0), pltpu.roll(x, VREG - 1, 0))
        at_edge = jnp.where(west, col, sz.cols - 1 - col) == 0
    near = jnp.where(at_edge, 0.0, near)
    south = sz.half * sz.cols - v * VREG
    return x - speed * (moves[0, here, :] * x - moves[1, here, :] * near - moves[2, here, :] * beside(sz, x, south))


def edge_parts(sz, moves, wide_w, at_w, wide_e, at_e):
    parts = []
    for first, count in west_half(sz):
        parts.append((first, count, 0, wide_w[pl.ds(at_w, count), :]))
        at_w += count
    parts.append((sz.quarter, sz.half, sz.cols - 1, wide_e[pl.ds(at_e, sz.half), :]))
    for first, count, col, cells in parts:
        yield first, count, col, moves[1, pl.ds(first * sz.cols, count, stride=sz.cols), :] * cells


def side_transported(sz, x, near, v, s_moves, speed):
    here = pl.ds(v * VREG, VREG)
    move = s_moves[0, here, :] * x - s_moves[1, here, :] * near
    return x - speed * (move - s_moves[2, here, :] * beside(sz, x, sz.half - v * VREG))


def local_kernel(sz, energy, moves, sea, adv, total):
    total[...] = jnp.zeros_like(total)

    def band(k, inverse):
        base = pl.multiple_of(k * sz.ring, VREG)
        line = jnp.zeros((VREG, sz.lat), F32)
        for v in range(sz.vregs):
            out = sea[...] * transported(sz, energy, base, v, moves, speed_coef * inverse)
            adv[pl.ds(base + v * VREG, VREG), :] = out
            line = line + out
        total[...] = total[...] * F32(1.0 / ratio_step) + line

    over_bands(sz.bands, band_ratio(sz, 0, True), band, True)
    total[...] = total[...] * (0.1 * band_ratio(sz, sz.bands - 1))


def edge_kernel(
    sz, adv_in, total, energy, from_w, from_e, moves, s_moves, sea, adv, side, msg_a, part,
    wide_w, wide_e, s_near, fix,
):
    wide_w[...] = from_w[...].astype(F32)
    wide_e[...] = from_e[...].astype(F32)
    s_sea = wide_e[pl.ds(sz.info, 1), :]
    sub = lax.broadcasted_iota(jnp.int32, (VREG, sz.lat), 0)
    s_total = jnp.zeros((VREG, sz.lat), F32)
    lines = {}
    for k in range(sz.bands):
        inverse = band_ratio(sz, k, True)
        weight = 0.1 * band_ratio(sz, k)
        speed = speed_coef * inverse
        at_e = k * sz.thick + sz.quarter
        for first, count, col, moved in edge_parts(sz, moves, wide_w, k * sz.half, wide_e, at_e):
            moved = moved * (speed * sea[col : col + 1, :])
            rows = pl.ds(k * sz.ring + first * sz.cols + col, count, stride=sz.cols)
            adv[rows, :] = adv[rows, :] + moved
            lines[first, col] = lines.get((first, col), 0.0) + moved * weight
        at = k * sz.side
        for first, count in west_half(sz):
            start = k * sz.ring + first * sz.cols + sz.cols - 1
            s_near[pl.ds(at + first, count), :] = energy[pl.ds(start, count, stride=sz.cols), :]
        s_near[pl.ds(at + sz.quarter, sz.half), :] = wide_e[pl.ds(k * sz.thick + sz.angles, sz.half), :]
        if sz.side > sz.angles:
            rest = sz.side - sz.angles
            s_near[pl.ds(at + sz.angles, rest), :] = jnp.zeros((rest, sz.lat), F32)
        s_line = jnp.zeros((VREG, sz.lat), F32)
        for v in range(sz.side // VREG):
            x = wide_e[pl.ds(k * sz.thick + v * VREG, VREG), :]
            near = s_near[pl.ds(at + v * VREG, VREG), :]
            out = s_sea * side_transported(sz, x, near, v, s_moves, speed)
            side[pl.ds(at + v * VREG, VREG), :] = out
            s_line = s_line + (out if (v + 1) * VREG <= sz.angles else jnp.where(sub < sz.angles - v * VREG, out, 0.0))
        s_total = s_total + s_line * weight
    mine = total[0 : sz.cols, :]
    for i in range(1, VREG // sz.cols):
        mine = mine + total[i * sz.cols : (i + 1) * sz.cols, :]
    west, east = (
        sum(jnp.sum(x, axis=0, keepdims=True) for (_, c), x in lines.items() if c == col) for col in (0, sz.cols - 1)
    )
    between = jnp.zeros((sz.cols - 2, sz.lat), F32)
    mine = mine + jnp.concatenate([west, between, east], axis=0)
    s_sum = jnp.sum(s_total, axis=0, keepdims=True)
    sums = jnp.concatenate([mine, s_sum, jnp.zeros((VREG - sz.cols - 1, sz.lat), F32)], axis=0)
    part[...] = sums
    fix[...] = jnp.zeros_like(fix)
    fix[pl.ds(sz.sum_row, 3 * VREG), :] = jnp.concatenate(split3(sums), axis=0)
    start = sz.bands - reach - far_band(sz)
    for k in range(reach):
        band_row = pl.multiple_of((start + k) * sz.ring, VREG)
        at = k * sz.far_band
        for first, count in west_half(sz):
            fix[pl.ds(at, count), :] = adv[pl.ds(band_row + first * sz.cols, count, stride=sz.cols), :]
            at += count
        last = band_row + (sz.quarter + 1) * sz.cols - 1
        fix[pl.ds(at, sz.half), :] = adv[pl.ds(last, sz.half, stride=sz.cols), :]
        s_row = pl.multiple_of((start + k) * sz.side, VREG)
        fix[pl.ds(k * sz.far_band + sz.rim_band, sz.angles), :] = side[pl.ds(s_row, sz.angles), :]
    msg_a[...] = fix[...].astype(BF16)


def nest_kernel(sz, nest, moves, out):
    def band(k, inverse):
        base = pl.multiple_of(k * sz.ring, VREG)
        for v in range(sz.vregs):
            moved = transported(sz, nest, base, v, moves, nest_speedup * speed_coef * inverse)
            out[pl.ds(base + v * VREG, VREG), :] = moved

    over_bands(sz.bands, band_ratio(sz, 0, True), band, True)


def nest_edge_kernel(sz, inner, from_w, from_e, moves, out, columns, wide_w, wide_e):
    grid_rank = lax.axis_index("grid")
    quarter = sz.grid // 4
    keep_w = jnp.where((grid_rank != quarter) & (grid_rank != 3 * quarter), 1.0, 0.0).astype(F32)
    keep_e = jnp.where((grid_rank != quarter - 1) & (grid_rank != 3 * quarter - 1), 1.0, 0.0).astype(F32)
    wide_w[...] = from_w[...].astype(F32)
    wide_e[...] = from_e[...].astype(F32)
    for k in range(sz.bands):
        speed = nest_speedup * speed_coef * band_ratio(sz, k, True)
        at_w, at_e = sz.thin + k * sz.half, sz.thick_nest + k * sz.half
        for first, count, col, moved in edge_parts(sz, moves, wide_w, at_w, wide_e, at_e):
            rows = pl.ds(k * sz.ring + first * sz.cols + col, count, stride=sz.cols)
            out[rows, :] = out[rows, :] + moved * (speed * (keep_w if col == 0 else keep_e))
    for c in range(sz.cols):
        columns[c, pl.ds(0, sz.bins), :] = out[pl.ds(c, sz.bins, stride=sz.cols), :]


def dot_lanes(a, b):
    return lax.dot_general(a, b, (((1,), (1,)), ((), ())), preferred_element_type=F32)


def rim_kernel(sz, cell, dest, target, weight, mix):
    device = lax.broadcasted_iota(jnp.int32, (sz.grid, sz.rim), 0)
    hot = jnp.where(device == dest[...], 1.0, 0.0)
    before = lax.broadcasted_iota(jnp.int32, (sz.rim, sz.rim), 0)
    after = lax.broadcasted_iota(jnp.int32, (sz.rim, sz.rim), 1)
    earlier = jnp.dot(
        hot.astype(BF16), jnp.where(before < after, 1.0, 0.0).astype(BF16), preferred_element_type=F32
    )
    rank = jnp.sum(hot * earlier, axis=0, keepdims=True)
    place = dest[...] * sz.cap + rank.astype(jnp.int32)
    slot = lax.broadcasted_iota(jnp.int32, (sz.slots, sz.rim), 0)
    takes = jnp.where(slot == place, 1.0, 0.0).astype(BF16)
    row = lax.broadcasted_iota(jnp.int32, (sz.lat, sz.rim), 0)
    col = cell[0:1, :] - lax.axis_index("grid") * sz.cols
    south_row = cell[1:2, :]
    ex, ny = weight[0:1, :], weight[1:2, :]
    for c in range(sz.cols + 1):
        share = jnp.where(col == c, 1.0 - ex, 0.0) + jnp.where(col + 1 == c, ex, 0.0)
        south, north = share * (1.0 - ny), share * ny
        corner = jnp.where(row == south_row, south, 0.0) + jnp.where(row == south_row + 1, north, 0.0)
        mix[:, c * sz.lat : (c + 1) * sz.lat] = dot_lanes(takes, corner.astype(BF16)).astype(BF16)
    at = sz.bins - (sz.lanes - 128)
    line = lax.broadcasted_iota(jnp.int32, (128, sz.rim), 0)
    t = target[...]
    t_col = t // sz.lat
    about = jnp.where(line == at, t_col.astype(F32), 0.0)
    about = about + jnp.where(line == at + 1, (t - t_col * sz.lat).astype(F32), 0.0)
    about = about + jnp.where(line == at + 2, weight[2:3, :], 0.0)
    n = (sz.cols + 1) * sz.lat
    mix[:, n : n + 128] = dot_lanes(takes, about.astype(BF16)).astype(BF16)


def low_rows(sz):
    return lax.broadcasted_iota(jnp.int32, (VREG, sz.lat), 0) < VREG // 2


def put(sz, plain, turned, slot, vals):
    nv, low = sz.vregs, low_rows(sz)
    for v in range(nv):
        if plain is not None:
            plain[slot, pl.ds(v * VREG, VREG), :] = vals[v]
        nxt = pltpu.roll(jnp.where(low, vals[(v + 1) % nv], vals[v]), VREG // 2, 0)
        turned[slot, pl.ds((v + 2) * VREG, VREG), :] = nxt
        if v >= nv - 2:
            turned[slot, pl.ds((v + 2 - nv) * VREG, VREG), :] = nxt
        if v == 0:
            turned[slot, pl.ds((nv + 2) * VREG, VREG), :] = nxt


def close(sz, ref, slot):
    ref[slot, pl.ds(VREG - 3, 3), :] = ref[slot, pl.ds(VREG + sz.angles - 3, 3), :]
    ref[slot, pl.ds(VREG + sz.angles, 3), :] = ref[slot, pl.ds(VREG, 3), :]


def s_put(sz, s_plain, slot, load):
    for v in range(sz.side // VREG):
        s_plain[slot, pl.ds((v + 1) * VREG, VREG), :] = load(v)
    close(sz, s_plain, slot)


def exchange(sc, c, up, down):
    return sc * (c * (up + down) - 2.0 * (up * down))


def strengths(sz, ratio, n, plain, turned, plus, minus, s_plain, s_plus, s_minus):
    nv = sz.vregs
    strength = nonlin_coef * ratio
    for v in range(nv):
        c = plain[n + 3, pl.ds(v * VREG, VREG), :]
        sc = strength * c
        for ref, up_row, down_row in ((plus, v + 3, v + 1), (minus, v, v + 2)):
            up = turned[n + 5, pl.ds(up_row * VREG, VREG), :]
            down = turned[n, pl.ds(down_row * VREG, VREG), :]
            delta = exchange(sc, c, up, down)
            ref[n, pl.ds((v + 1) * VREG, VREG), :] = delta
            if v == nv - 1:
                ref[n, pl.ds(0, VREG), :] = delta
            if v < 2:
                ref[n, pl.ds((nv + 1 + v) * VREG, VREG), :] = delta
    for v in range(sz.side // VREG):
        row = (v + 1) * VREG
        c = s_plain[n + 3, pl.ds(row, VREG), :]
        sc = strength * c
        for ref, s in ((s_plus, 1), (s_minus, -1)):
            up = s_plain[n + 5, pl.ds(row + 3 * s, VREG), :]
            down = s_plain[n, pl.ds(row - s, VREG), :]
            ref[n, pl.ds(row, VREG), :] = exchange(sc, c, up, down)
    close(sz, s_plus, n)
    close(sz, s_minus, n)


def is_even():
    return lax.rem(lax.axis_index("spec"), 2) == 0


def complete(sz, slot, fix, k, plain, s_plain):
    at = k * sz.far_band
    for start, count in west_half(sz):
        plain[slot, pl.ds(start * sz.cols, count, stride=sz.cols), :] = fix[pl.ds(at, count), :]
        at += count
    last = (sz.quarter + 1) * sz.cols - 1
    plain[slot, pl.ds(last, sz.half, stride=sz.cols), :] = fix[pl.ds(at, sz.half), :]
    at = k * sz.far_band + sz.rim_band
    s_put(sz, s_plain, slot, lambda v: fix[pl.ds(at + v * VREG, VREG), :])


def turn_halo(sz, base, plain, turned, real=None):
    def halo(k, carry):
        vals = [plain[base + k, pl.ds(v * VREG, VREG), :] for v in range(sz.vregs)]
        put(sz, None if real is None else plain, turned, base + k, vals if real is None else [x * real for x in vals])
        return carry

    lax.fori_loop(0, reach, halo, 0)


def numerators(sz, k, ratio, adv, gain, plus, minus, store):
    nv, low = sz.vregs, low_rows(sz)
    base = pl.multiple_of(k * sz.ring, VREG)

    def moved_in(v):
        return (
            plus[k, pl.ds(v * VREG, VREG), :]
            + minus[k, pl.ds((v + 3) * VREG, VREG), :]
            + plus[k + 5, pl.ds((v + 2) * VREG, VREG), :]
            + minus[k + 5, pl.ds((v + 1) * VREG, VREG), :]
        )

    before = moved_in(nv - 1)
    for v in range(nv):
        now = moved_in(v)
        moved = pltpu.roll(jnp.where(low, now, before), VREG // 2, 0)
        before = now
        here = pl.ds((v + 1) * VREG, VREG)
        transfer = moved - 2.0 * (plus[k + 2, here, :] + minus[k + 2, here, :])
        a = adv[pl.ds(base + v * VREG, VREG), :]
        grown = ratio * gain[pl.ds(v * VREG, VREG), :]
        store(pl.ds(base + v * VREG, VREG), a + grown * a + transfer)


def transport_raw(sz, raw, moves, sea, plain, wide, upper):
    base = jnp.where(upper, sz.bands + reach, 0)
    inverse = jnp.where(upper, band_ratio(sz, sz.bands, True), band_ratio(sz, -reach, True))
    wide[...] = raw[...].astype(F32)

    def transport(k, r):
        start = pl.multiple_of(k * sz.ring, VREG)
        for v in range(sz.vregs):
            moved = transported(sz, wide, start, v, moves, speed_coef * r)
            plain[base + k, pl.ds(v * VREG, VREG), :] = sea[...] * moved

    over_bands(reach, inverse, transport, True)


def beside_kernel(sz, raw_a, moves, sea, plain, wide):
    transport_raw(sz, raw_a, moves, sea, plain, wide, is_even())


def beyond_kernel(sz, raw_b, moves, sea, plain_in, plain, far_near, wide):
    transport_raw(sz, raw_b, moves, sea, plain, wide, jnp.logical_not(is_even()))
    far_near[...] = jnp.zeros_like(far_near)
    for k in range(reach):
        for first, count in west_half(sz):
            start = k * sz.ring + first * sz.cols + sz.cols - 1
            far_near[pl.ds(k * sz.side + first, count), :] = wide[pl.ds(start, count, stride=sz.cols), :]


def inner_kernel(
    sz, adv, side, recv_a, gain, plain_in, plain, turned, plus, minus, s_plain, s_plus, s_minus, num, fix
):
    base_a = jnp.where(is_even(), sz.bands + reach, 0)

    def own(k, carry):
        base = pl.multiple_of(k * sz.ring, VREG)
        put(sz, plain, turned, k + reach, [adv[pl.ds(base + v * VREG, VREG), :] for v in range(sz.vregs)])
        s_base = pl.multiple_of(k * sz.side, VREG)
        s_put(sz, s_plain, k + reach, lambda v: side[pl.ds(s_base + v * VREG, VREG), :])
        return carry

    lax.fori_loop(0, sz.bands, own, 0)

    fix[...] = recv_a[...].astype(F32)
    for k in range(reach):
        complete(sz, base_a + k, fix, k, plain, s_plain)
    turn_halo(sz, base_a, plain, turned)

    arrays = (plain, turned, plus, minus, s_plain, s_plus, s_minus)
    start = jnp.where(is_even(), reach, 0)
    ratio = jnp.where(is_even(), band_ratio(sz, 3), band_ratio(sz, 3 - reach))
    over_bands(sz.bands, ratio, lambda i, r: strengths(sz, r, start + i, *arrays))

    def store(rows, value):
        num[rows, :] = value

    ratio = jnp.where(is_even(), band_ratio(sz, reach), band_ratio(sz, 0))
    over_bands(
        sz.bands - reach, ratio, lambda i, r: numerators(sz, start + i, r, adv, gain, plus, minus, store)
    )


def outer_kernel(
    sz, adv, side, recv_b, gain, moves, s_moves, sea, from_e, far_near, num_in,
    plain_in, turned_in, plus_in, minus_in, s_plain_in, s_plus_in, s_minus_in,
    num, plain, turned, plus, minus, s_plain, s_plus, s_minus, s_num, wide, s_near,
):
    spec_rank = lax.axis_index("spec")
    ns = sz.side // VREG
    base_b = jnp.where(is_even(), 0, sz.bands + reach)
    real_b = jnp.where((spec_rank == 0) | (spec_rank == sz.spec - 1), 0.0, 1.0).astype(F32)
    info = from_e[pl.ds(sz.info // 16 * 16, 32), :].astype(F32)
    at = sz.info % 16
    s_sea = info[at : at + 1] * real_b
    wide[...] = recv_b[...].astype(F32)
    s_near[...] = far_near[...]
    inverse = jnp.where(is_even(), band_ratio(sz, -reach, True), band_ratio(sz, sz.bands, True))
    for k in range(reach):
        speed = inverse * (speed_coef / ratio_step**k)
        slot, row = base_b + k, sz.pass_thick + k * sz.thick
        for start, count, col, moved in edge_parts(sz, moves, wide, k * sz.half, wide, row + sz.quarter):
            rows = pl.ds(start * sz.cols + col, count, stride=sz.cols)
            plain[slot, rows, :] = plain[slot, rows, :] + moved * (speed * sea[col : col + 1, :])
        at_near = k * sz.side
        s_near[pl.ds(at_near + sz.quarter, sz.half), :] = wide[pl.ds(row + sz.angles, sz.half), :]

        def column(v):
            x = wide[pl.ds(row + v * VREG, VREG), :]
            near = s_near[pl.ds(at_near + v * VREG, VREG), :]
            return s_sea * side_transported(sz, x, near, v, s_moves, speed)

        s_put(sz, s_plain, slot, column)
    turn_halo(sz, base_b, plain, turned, real_b)
    arrays = (plain, turned, plus, minus, s_plain, s_plus, s_minus)
    begin = jnp.where(is_even(), 0, sz.bands)
    ratio = jnp.where(is_even(), band_ratio(sz, 3 - reach), band_ratio(sz, sz.bands + 3 - reach))
    over_bands(reach, ratio, lambda i, r: strengths(sz, r, begin + i, *arrays))

    at = at + 1
    s_east = info[at : at + 1] + info[at + 1 : at + 2] + info[at + 2 : at + 3]
    s_north = info[at + 3 : at + 4] + info[at + 4 : at + 5] + info[at + 5 : at + 6]
    missing = jnp.where(is_even(), 0, sz.bands - reach)

    def store(rows, value):
        num[rows, :] = value

    over_bands(
        reach,
        jnp.where(is_even(), band_ratio(sz, 0), band_ratio(sz, sz.bands - reach)),
        lambda i, r: numerators(sz, missing + i, r, adv, gain, plus, minus, store),
    )

    s_gain = []
    for v in range(ns):
        here = pl.ds(v * VREG, VREG)
        along = s_moves[3, here, :] * s_east + s_moves[4, here, :] * s_north
        s_gain.append(wind_coef * jnp.maximum(along, 0.0))
    for k in range(sz.bands):
        ratio = band_ratio(sz, k)
        for v in range(ns):
            row = (v + 1) * VREG
            here = pl.ds(row, VREG)
            transfer = (
                s_plus[k, pl.ds(row - 3, VREG), :]
                + s_minus[k, pl.ds(row + 3, VREG), :]
                + s_plus[k + 5, pl.ds(row + 1, VREG), :]
                + s_minus[k + 5, pl.ds(row - 1, VREG), :]
                - 2.0 * (s_plus[k + 2, here, :] + s_minus[k + 2, here, :])
            )
            a = side[pl.ds(k * sz.side + v * VREG, VREG), :]
            s_num[pl.ds(k * sz.side + v * VREG, VREG), :] = a + (ratio * s_gain[v]) * a + transfer


def source_kernel(sz, num, s_num, pair, other, mix, out, msg, s_out):
    total_weight = sz.angles * 0.1 * sum(ratio_step ** (k - sz.freqs // 2) for k in range(sz.freqs))
    means = (pair[...] + other[...]) * (1.0 / total_weight)
    mean = jnp.concatenate([means[0 : sz.cols]] * (VREG // sz.cols), axis=0)
    s_mean = means[sz.cols : sz.cols + 1]

    def finish(k, ratio):
        factor = 1.0 / (1.0 + (dissip_coef * ratio * ratio) * mean)
        base = pl.multiple_of(k * sz.ring, VREG)
        for v in range(sz.vregs):
            here = pl.ds(base + v * VREG, VREG)
            out[here, :] = num[here, :] * factor

    over_bands(sz.bands, band_ratio(sz, 0), finish)
    for k in range(sz.bands):
        ratio = band_ratio(sz, k)
        factor = 1.0 / (1.0 + (dissip_coef * ratio * ratio) * s_mean)
        for v in range(sz.side // VREG):
            here = pl.ds(k * sz.angles + v * VREG, VREG)
            s_out[here, :] = s_num[pl.ds(k * sz.side + v * VREG, VREG), :] * factor

    pad = jnp.zeros((sz.lanes - sz.bins, sz.lat), BF16)
    columns = [out[pl.ds(c, sz.bins, stride=sz.cols), :] for c in range(sz.cols)]
    columns.append(s_out[pl.ds(0, sz.bins), :])
    columns = [jnp.concatenate([c.astype(BF16), pad], axis=0) for c in columns]
    n = (sz.cols + 1) * sz.lat
    spectra = dot_lanes(mix[:, 0:n], jnp.concatenate(columns, axis=1))
    about = mix[:, n : n + 128].astype(F32)
    msg[:, 0 : sz.lanes - 128] = spectra[:, : sz.lanes - 128].astype(BF16)
    msg[:, sz.lanes - 128 : sz.lanes] = (spectra[:, sz.lanes - 128 :] + about).astype(BF16)


def blend_kernel(sz, recv, nest_adv, spectra, global_hbm, result_hbm, out, sems):
    writes = [pltpu.make_async_copy(spectra, global_hbm, sems.at[sz.lanes // 128])]
    writes[0].start()
    at = sz.bins - (sz.lanes - 128)
    about = recv[:, sz.lanes - 128 :].astype(F32)
    t_col, t_row, rate = about[:, at : at + 1], about[:, at + 1 : at + 2], about[:, at + 2 : at + 3]
    lane = lax.broadcasted_iota(jnp.int32, (sz.slots, sz.lat), 1).astype(F32)
    hit = jnp.where(lane == t_row, rate, 0.0)
    relax = [jnp.where(t_col == float(c), hit, 0.0) for c in range(sz.cols)]
    kept = [1.0 - jnp.sum(r, axis=0, keepdims=True) for r in relax]
    relax = jnp.concatenate(relax, axis=1).astype(BF16)
    for part, start in enumerate(range(0, sz.bins, 128)):
        count = min(128, sz.bins - start)
        added = lax.dot_general(
            recv[:, start : start + 128], relax, (((0,), (0,)), ((), ())), preferred_element_type=F32
        )
        for c in range(sz.cols):
            here = pl.ds(start * sz.cols + c, count, stride=sz.cols)
            own = nest_adv[c, pl.ds(start, count), :]
            out[here, :] = own * kept[c] + added[:count, c * sz.lat : (c + 1) * sz.lat]
        rows = pl.ds(start * sz.cols, count * sz.cols)
        writes.append(pltpu.make_async_copy(out.at[rows], result_hbm.at[rows], sems.at[part]))
        writes[-1].start()
    for write in writes:
        write.wait()


def kernel_call(body, out_shape, n_in, hbm=(), out_hbm=(), scratch=(), aliases=None, flops=0, name=None):
    def specs(count, far):
        return [pl.BlockSpec(memory_space=pltpu.HBM if i in far else pltpu.VMEM) for i in range(count)]

    many = isinstance(out_shape, tuple)
    out_specs = specs(len(out_shape) if many else 1, out_hbm)
    call = pl.pallas_call(
        body,
        out_shape=out_shape,
        in_specs=specs(n_in, hbm),
        out_specs=out_specs if many else out_specs[0],
        scratch_shapes=list(scratch),
        input_output_aliases=aliases or {},
        compiler_params=pltpu.CompilerParams(vmem_limit_bytes=20 * 2**20),
        cost_estimate=pl.CostEstimate(flops=flops, bytes_accessed=0, transcendentals=0) if flops else None,
        name=name,
    )
    if not aliases:
        return call

    def in_place(*args):
        pin = functools.partial(pltpu.with_memory_space_constraint, memory_space=pltpu.VMEM)
        return call(*[pin(a) if i in aliases else a for i, a in enumerate(args)])

    return in_place


def per_device(
    mesh, energy, nest_energy, ocean_mask, wind_field, rim_cell, rim_dest, rim_target, rim_weight
):
    sz = Sizes(mesh, energy, rim_dest.shape[0])

    def array(*shape, dtype=F32):
        return jax.ShapeDtypeStruct(shape + (sz.lat,), dtype)

    def vmem(*shape):
        return pltpu.VMEM(shape + (sz.lat,), F32)

    def half(rows):
        return array(rows, dtype=BF16)

    field = array(sz.rows)
    table = jnp.asarray(angle_table(sz))
    energy4, energy = energy, energy.reshape(sz.rows, sz.lat)
    nest = nest_energy.reshape(sz.rows, sz.lat)
    up = [(i, (i + 1) % sz.grid) for i in range(sz.grid)]
    down = [(j, i) for i, j in up]
    across = []
    for g in range(sz.grid):
        for i in range(sz.spec):
            j = i + 1 if i % 2 else i - 1
            to = (g, j) if 0 <= j < sz.spec else ((g ^ 1) % sz.grid, i)
            across.append((g * sz.spec + i, to[0] * sz.spec + to[1]))
    both = ("grid", "spec")
    near_rows = [vmem(sz.thin_rows), vmem(sz.thick_rows)]

    stay = functools.partial(pltpu.with_memory_space_constraint, memory_space=pltpu.HBM)
    def column(n):
        return vmem(sz.bands, n)

    thin, thick = kernel_call(
        functools.partial(pack_kernel, sz),
        (half(sz.thin_rows), half(sz.thick_rows)),
        4,
        hbm=range(4),
        scratch=[
            column(sz.angles),
            column(sz.half),
            column(sz.half),
            column(sz.angles - 3 * sz.quarter),
            column(sz.quarter),
            column(sz.angles - 3 * sz.quarter),
            column(sz.quarter),
            pltpu.VMEM(ocean_mask.shape, ocean_mask.dtype),
            pltpu.VMEM(wind_field.shape, F32),
        ]
        + near_rows
        + [pltpu.SemaphoreType.DMA((9,))],
        name="pack",
    )(stay(energy4), stay(nest_energy), stay(ocean_mask), stay(wind_field))
    from_e = lax.ppermute(thick, "grid", down)
    from_w = lax.ppermute(thin, "grid", up)

    table, thin = lax.optimization_barrier((table, thin))
    moves, nest_moves, s_moves, gain, sea = kernel_call(
        functools.partial(setup_kernel, sz),
        (array(3, sz.ring), array(3, sz.ring), array(5, sz.side), array(sz.ring), array(VREG)),
        3,
        name="setup",
    )(table, ocean_mask, wind_field)
    energy, table = lax.optimization_barrier((energy, table))
    raw_a, raw_b = kernel_call(
        functools.partial(raw_kernel, sz), (half(sz.edge_rows), half(sz.edge_rows)), 1, name="raw"
    )(energy)
    pairs = [(i, i ^ 1) for i in range(sz.spec)]
    recv_raw_b = lax.ppermute(raw_b, "spec", [(i, (i + 1 if i % 2 else i - 1) % sz.spec) for i in range(sz.spec)])
    recv_raw_a = lax.ppermute(raw_a, "spec", pairs)
    rim = (rim_cell.T, rim_dest.T, rim_target.reshape(1, sz.rim), rim_weight.T)
    rim, raw_a = lax.optimization_barrier((rim, raw_a))
    mix = kernel_call(
        functools.partial(rim_kernel, sz),
        jax.ShapeDtypeStruct((sz.slots, (sz.cols + 1) * sz.lat + 128), BF16),
        4,
        name="rim",
    )(*rim)
    nest, raw_a = lax.optimization_barrier((nest, raw_a))
    nest_inner = kernel_call(functools.partial(nest_kernel, sz), field, 2, flops=3 * 10**10, name="nest")(nest, nest_moves)
    energy, raw_a = lax.optimization_barrier((energy, raw_a))
    adv, total = kernel_call(
        functools.partial(local_kernel, sz), (field, array(VREG)), 3, flops=3 * 10**10, name="local"
    )(energy, moves, sea)
    band_fields = array(sz.bands + 2 * reach, sz.ring)
    plain = kernel_call(
        functools.partial(beside_kernel, sz), band_fields, 3, scratch=[vmem(sz.edge_rows)], flops=10**10, name="beside"
    )(recv_raw_a, moves, sea)
    from_e, from_w, mix, nest_inner, adv, plain = lax.optimization_barrier(
        (from_e, from_w, mix, nest_inner, adv, plain)
    )

    msg_b = kernel_call(
        functools.partial(pass_kernel, sz),
        half(sz.pass_rows),
        2,
        scratch=near_rows + [vmem(sz.pass_rows)],
        name="pass",
    )(from_w, from_e)
    adv, side, msg_a, part = kernel_call(
        functools.partial(edge_kernel, sz),
        (field, array(sz.bands * sz.side), half(sz.fix_rows), array(VREG)),
        8,
        scratch=near_rows + [vmem(sz.bands * sz.side), vmem(sz.fix_rows)],
        aliases={0: 0},
        flops=3 * 10**10,
        name="edges",
    )(adv, total, energy, from_w, from_e, moves, s_moves, sea)

    recv_a = lax.ppermute(msg_a, "spec", pairs)
    recv_b = lax.ppermute(msg_b, both, across)
    recv_a, recv_raw_b = lax.optimization_barrier((recv_a, recv_raw_b))
    plain, far_near = kernel_call(
        functools.partial(beyond_kernel, sz),
        (band_fields, array(reach * sz.side)),
        4,
        scratch=[vmem(sz.edge_rows)],
        aliases={3: 0},
        flops=3 * 10**10,
        name="beyond",
    )(recv_raw_b, moves, sea, plain)
    pieces = recv_a[sz.sum_row : sz.sum_row + 3 * VREG].astype(F32)
    pair = part + pieces.reshape(3, VREG, sz.lat).sum(axis=0)
    other = jnp.zeros_like(pair)
    step = 2
    while step < sz.spec:
        pair = pair + other
        other = lax.ppermute(pair, "spec", [(i, i ^ (2 * step - 1)) for i in range(sz.spec)])
        step *= 2

    _, nest_adv = kernel_call(
        functools.partial(nest_edge_kernel, sz),
        (field, array(sz.cols, sz.bins + VREG)),
        4,
        scratch=near_rows,
        aliases={0: 0},
        name="nest_edge",
    )(nest_inner, from_w, from_e, nest_moves)

    padded, centres, turns = sz.bands + 2 * reach, sz.bands + reach, sz.ring + 3 * VREG
    arrays = (
        array(padded, sz.ring),
        array(padded, turns),
        array(centres, turns),
        array(centres, turns),
        array(padded, sz.frame),
        array(centres, sz.frame),
        array(centres, sz.frame),
    )
    *inner, num = kernel_call(
        functools.partial(inner_kernel, sz),
        arrays + (field,),
        5,
        scratch=[vmem(sz.fix_rows)],
        aliases={4: 0},
        name="inner",
    )(adv, side, recv_a, gain, plain)
    nest_adv, recv_b = lax.optimization_barrier((nest_adv, recv_b))
    num, *_, s_num = kernel_call(
        functools.partial(outer_kernel, sz),
        (field,) + arrays + (array(sz.bands * sz.side),),
        10 + len(arrays),
        scratch=[vmem(sz.pass_rows), vmem(reach * sz.side)],
        aliases={9 + i: i for i in range(1 + len(arrays))},
        name="outer",
    )(adv, side, recv_b, gain, moves, s_moves, sea, from_e, far_near, num, *inner)
    spectra, msg = kernel_call(
        functools.partial(source_kernel, sz),
        (field, jax.ShapeDtypeStruct((sz.slots, sz.lanes), BF16)),
        5,
        scratch=[vmem(sz.bins + VREG)],
        name="sources",
    )(num, s_num, pair, other, mix)

    recv = lax.all_to_all(msg, "grid", split_axis=0, concat_axis=0, tiled=True)
    global_next, nest_next = kernel_call(
        functools.partial(blend_kernel, sz),
        (field, field),
        3,
        out_hbm=(0, 1),
        scratch=[vmem(sz.rows), pltpu.SemaphoreType.DMA((sz.lanes // 128 + 1,))],
        name="blend",
    )(recv, nest_adv, pltpu.with_memory_space_constraint(spectra, pltpu.VMEM))
    full = (sz.bands, sz.angles, sz.cols, sz.lat)
    return global_next.reshape(full), nest_next.reshape(full)


def solution(mesh):
    in_specs = (
        P("spec", None, "grid", None),
        P("spec", None, "grid", None),
        P("grid", None),
        P(None, "grid", None),
        P("grid", None),
        P("grid", None),
        P("grid"),
        P("grid", None),
    )
    out_specs = (P("spec", None, "grid", None), P("spec", None, "grid", None))
    return jax.shard_map(
        functools.partial(per_device, mesh),
        mesh=mesh,
        in_specs=in_specs,
        out_specs=out_specs,
        check_vma=False,
    )
```

```python
import functools

import jax
import jax.numpy as jnp
import numpy as np
from jax import lax
from jax.experimental import pallas as pl
from jax.experimental.pallas import tpu as pltpu
from jax.sharding import PartitionSpec as P

ratio_step = 1.1
speed_coef = 0.054
wind_coef = 0.05
dissip_coef = 0.2
nonlin_coef = 0.12
nest_speedup = 2.0
reach = 5

VREG = 8
BF16 = jnp.bfloat16
F32 = jnp.float32


class Sizes:
    def __init__(self, mesh, energy, rim_rows):
        self.grid = mesh.shape["grid"]
        self.spec = mesh.shape["spec"]
        self.bands, self.angles, self.cols, self.lat = energy.shape
        self.freqs = self.bands * self.spec
        self.bins = self.bands * self.angles
        self.ring = self.angles * self.cols
        self.rows = self.bins * self.cols
        self.vregs = self.ring // VREG
        self.rim = rim_rows
        self.cap = max(2, (2 * rim_rows + self.grid - 1) // self.grid)
        self.slots = self.grid * self.cap
        self.lanes = (self.bins + 3 + 127) // 128 * 128
        self.half = self.angles // 2
        self.quarter = self.angles // 4
        self.side = (self.angles + VREG - 1) // VREG * VREG
        self.frame = self.side + 2 * VREG
        self.thin = self.bands * self.half
        self.thin_rows = (2 * self.thin + 15) // 16 * 16
        self.thick = self.angles + self.half
        self.info = self.bands * self.thick
        self.thick_nest = (self.info + 7 + VREG - 1) // VREG * VREG
        self.thick_rows = (self.thick_nest + self.thin + 15) // 16 * 16
        self.edge_rows = reach * self.ring
        self.rim_band = 2 * self.half
        self.far_band = self.rim_band + self.angles
        self.sum_row = (reach * self.far_band + VREG - 1) // VREG * VREG
        self.fix_rows = (self.sum_row + 3 * VREG + 15) // 16 * 16
        self.pass_thick = (reach * self.half + VREG - 1) // VREG * VREG
        self.pass_rows = max(self.fix_rows + 16, (self.pass_thick + reach * self.thick + 15) // 16 * 16)


def band_ratio(sz, band, inverse=False):
    rank = lax.axis_index("spec")
    ratio = F32(0.0)
    for s in range(sz.spec):
        power = ratio_step ** (s * sz.bands + band - sz.freqs // 2)
        ratio = jnp.where(rank == s, F32(1.0 / power if inverse else power), ratio)
    return ratio


def over_bands(count, ratio, body, inverse=False):
    step = F32(1.0 / ratio_step if inverse else ratio_step)

    def turn(i, r):
        body(i, r)
        return r * step

    lax.fori_loop(0, count, turn, ratio)


def angle_table(sz):
    heading = 2.0 * np.pi * np.arange(sz.angles) / sz.angles
    table = np.zeros((sz.ring + VREG + sz.side, sz.lat), np.float32)
    table[sz.ring + VREG :][: sz.angles, 0] = np.cos(heading)
    table[sz.ring + VREG :][: sz.angles, 1] = np.sin(heading)
    table[: sz.ring, 0] = np.repeat(np.cos(heading), sz.cols)
    table[: sz.ring, 1] = np.repeat(np.sin(heading), sz.cols)
    degrees = -60.0 + 120.0 * (np.arange(sz.lat) + 0.5) / sz.lat
    table[sz.ring : sz.ring + VREG] = 1.0 / np.cos(degrees * (np.pi / 180.0))
    return table


def from_west(sz, angle):
    return angle < sz.quarter or angle >= 3 * sz.quarter


def split3(x):
    high = x.astype(BF16).astype(F32)
    middle = (x - high).astype(BF16).astype(F32)
    return [high, middle, x - high - middle]


def upwind(sz, v):
    sub = lax.broadcasted_iota(jnp.int32, (VREG, sz.lat), 0)
    first, per = v * VREG // sz.cols, VREG // sz.cols
    wests = [from_west(sz, first + i) for i in range(per)]
    west = sub < 0
    for i in range(per):
        if wests[i]:
            west = west | ((sub >= i * sz.cols) & (sub < (i + 1) * sz.cols))
    return wests, west, sub % sz.cols


def west_half(sz):
    return ((3 * sz.quarter, sz.angles - 3 * sz.quarter), (0, sz.quarter))


def fetch(pairs, sems):
    copies = [pltpu.make_async_copy(a, b, sems.at[i]) for i, (a, b) in enumerate(pairs)]
    for c in copies:
        c.start()
    return copies


def far_band(sz):
    return jnp.where(lax.rem(lax.axis_index("spec"), 2) == 0, 0, sz.bands - reach)


def pack_kernel(
    sz, energy, nest, mask, wind, thin, thick, first, second, first_n, late, early, late_n, early_n,
    mask_v, wind_v, tmp_thin, tmp_thick, sems,
):
    from_east = pl.ds(sz.quarter, sz.half)
    (start, count), (_, rest) = west_half(sz)
    last = sz.cols - 1
    pairs = [
        (mask, mask_v),
        (wind, wind_v),
        (energy.at[:, :, 0], first),
        (energy.at[:, from_east, 1], second),
        (energy.at[:, pl.ds(start, count), last], late),
        (energy.at[:, pl.ds(0, rest), last], early),
        (nest.at[:, from_east, 0], first_n),
        (nest.at[:, pl.ds(start, count), last], late_n),
        (nest.at[:, pl.ds(0, rest), last], early_n),
    ]
    copies = [pltpu.make_async_copy(a, b, sems.at[i]) for i, (a, b) in enumerate(pairs)]
    for copy in copies:
        copy.start()
    spare = sz.thin_rows - 2 * sz.thin
    if spare:
        tmp_thin[pl.ds(2 * sz.thin, spare), :] = jnp.zeros((spare, sz.lat), F32)
    tmp_thick[...] = jnp.zeros_like(tmp_thick)
    for copy in copies[:6]:
        copy.wait()
    info = [mask_v[0:1, :].astype(F32)] + split3(wind_v[0, 0:1, :]) + split3(wind_v[1, 0:1, :])
    for i, line in enumerate(info):
        tmp_thick[pl.ds(sz.info + i, 1), :] = line
    for k in range(sz.bands):
        tmp_thin[pl.ds(k * sz.half, count), :] = late[k]
        tmp_thin[pl.ds(k * sz.half + count, rest), :] = early[k]
        tmp_thick[pl.ds(k * sz.thick, sz.angles), :] = first[k]
        tmp_thick[pl.ds(k * sz.thick + sz.angles, sz.half), :] = second[k]
    for copy in copies[6:]:
        copy.wait()
    for k in range(sz.bands):
        at = sz.thin + k * sz.half
        tmp_thin[pl.ds(at, count), :] = late_n[k]
        tmp_thin[pl.ds(at + count, rest), :] = early_n[k]
        tmp_thick[pl.ds(sz.thick_nest + k * sz.half, sz.half), :] = first_n[k]
    thin[...] = tmp_thin[...].astype(BF16)
    thick[...] = tmp_thick[...].astype(BF16)


def setup_kernel(sz, table, mask, wind, moves, nest_moves, s_moves, gain, sea):
    per = VREG // sz.cols
    sea[...] = jnp.concatenate([mask[...].astype(F32)] * per, axis=0)
    east_wind = jnp.concatenate([wind[0]] * per, axis=0)
    north_wind = jnp.concatenate([wind[1]] * per, axis=0)
    fill_moves(sz, 0, table, sz.cols, (moves, nest_moves))
    fill_moves(sz, sz.ring + VREG, table, 1, (s_moves, None))
    for v in range(sz.vregs):
        rows = table[pl.ds(v * VREG, VREG), :]
        along = rows[:, 0:1] * east_wind + rows[:, 1:2] * north_wind
        gain[pl.ds(v * VREG, VREG), :] = wind_coef * jnp.maximum(along, 0.0)
    for v in range(sz.side // VREG):
        rows = table[pl.ds(sz.ring + VREG + v * VREG, VREG), :]
        for i in range(2):
            s_moves[3 + i, pl.ds(v * VREG, VREG), :] = jnp.broadcast_to(rows[:, i : i + 1], (VREG, sz.lat))


def raw_kernel(sz, energy, raw_a, raw_b):
    for raw, first in ((raw_a, sz.bands - reach - far_band(sz)), (raw_b, far_band(sz))):
        raw[...] = energy[pl.ds(pl.multiple_of(first * sz.ring, VREG), sz.edge_rows), :].astype(BF16)


def pass_kernel(sz, from_w, from_e, msg, wide_w, wide_e, tmp):
    wide_w[...] = from_w[...].astype(F32)
    wide_e[...] = from_e[...].astype(F32)
    tmp[...] = jnp.zeros_like(tmp)
    first = far_band(sz)
    count = reach * sz.half
    tmp[pl.ds(0, count), :] = wide_w[pl.ds(first * sz.half, count), :]
    start = pl.multiple_of(first * sz.thick, VREG)
    tmp[pl.ds(sz.pass_thick, reach * sz.thick), :] = wide_e[pl.ds(start, reach * sz.thick), :]
    msg[...] = tmp[...].astype(BF16)


def fill_moves(sz, rows, table, cols, targets):
    lane = lax.broadcasted_iota(jnp.int32, (VREG, sz.lat), 1)
    sub = lax.broadcasted_iota(jnp.int32, (VREG, sz.lat), 0)
    sec = table[pl.ds(sz.ring, VREG), :]
    for v in range(targets[0].shape[1] // VREG):
        line = table[pl.ds(rows + v * VREG, VREG), :]
        along = jnp.broadcast_to(jnp.abs(line[:, 0:1]), (VREG, sz.lat))
        across = jnp.broadcast_to(jnp.abs(line[:, 1:2]), (VREG, sz.lat))
        edge = lane == jnp.where(sub < sz.half * cols - v * VREG, 0, sz.lat - 1)
        here = pl.ds(v * VREG, VREG)
        for target, by in zip(targets, (along * sec, along)):
            if target is not None:
                target[0, here, :] = by + across
                target[1, here, :] = by
                target[2, here, :] = jnp.where(edge, 0.0, across)


def beside(sz, x, turn):
    if turn >= VREG:
        return pltpu.roll(x, 1, 1)
    if turn <= 0:
        return pltpu.roll(x, sz.lat - 1, 1)
    sub = lax.broadcasted_iota(jnp.int32, (VREG, sz.lat), 0)
    return jnp.where(sub < turn, pltpu.roll(x, 1, 1), pltpu.roll(x, sz.lat - 1, 1))


def transported(sz, field, base, v, moves, speed):
    here = pl.ds(v * VREG, VREG)
    x = field[pl.ds(base + v * VREG, VREG), :]
    wests, west, col = upwind(sz, v)
    if all(wests):
        near, at_edge = pltpu.roll(x, 1, 0), col == 0
    elif not any(wests):
        near, at_edge = pltpu.roll(x, VREG - 1, 0), col == sz.cols - 1
    else:
        near = jnp.where(west, pltpu.roll(x, 1, 0), pltpu.roll(x, VREG - 1, 0))
        at_edge = jnp.where(west, col, sz.cols - 1 - col) == 0
    near = jnp.where(at_edge, 0.0, near)
    south = sz.half * sz.cols - v * VREG
    return x - speed * (moves[0, here, :] * x - moves[1, here, :] * near - moves[2, here, :] * beside(sz, x, south))


def edge_parts(sz, moves, wide_w, at_w, wide_e, at_e):
    parts = []
    for first, count in west_half(sz):
        parts.append((first, count, 0, wide_w[pl.ds(at_w, count), :]))
        at_w += count
    parts.append((sz.quarter, sz.half, sz.cols - 1, wide_e[pl.ds(at_e, sz.half), :]))
    for first, count, col, cells in parts:
        yield first, count, col, moves[1, pl.ds(first * sz.cols, count, stride=sz.cols), :] * cells


def side_transported(sz, x, near, v, s_moves, speed):
    here = pl.ds(v * VREG, VREG)
    move = s_moves[0, here, :] * x - s_moves[1, here, :] * near
    return x - speed * (move - s_moves[2, here, :] * beside(sz, x, sz.half - v * VREG))


def local_kernel(sz, energy, moves, sea, adv, total):
    total[...] = jnp.zeros_like(total)

    def band(k, inverse):
        base = pl.multiple_of(k * sz.ring, VREG)
        line = jnp.zeros((VREG, sz.lat), F32)
        for v in range(sz.vregs):
            out = sea[...] * transported(sz, energy, base, v, moves, speed_coef * inverse)
            adv[pl.ds(base + v * VREG, VREG), :] = out
            line = line + out
        total[...] = total[...] * F32(1.0 / ratio_step) + line

    over_bands(sz.bands, band_ratio(sz, 0, True), band, True)
    total[...] = total[...] * (0.1 * band_ratio(sz, sz.bands - 1))


def edge_kernel(
    sz, adv_in, total, energy, from_w, from_e, moves, s_moves, sea, adv, side, msg_a, part,
    wide_w, wide_e, s_near, fix,
):
    wide_w[...] = from_w[...].astype(F32)
    wide_e[...] = from_e[...].astype(F32)
    s_sea = wide_e[pl.ds(sz.info, 1), :]
    sub = lax.broadcasted_iota(jnp.int32, (VREG, sz.lat), 0)
    s_total = jnp.zeros((VREG, sz.lat), F32)
    lines = {}
    for k in range(sz.bands):
        inverse = band_ratio(sz, k, True)
        weight = 0.1 * band_ratio(sz, k)
        speed = speed_coef * inverse
        at_e = k * sz.thick + sz.quarter
        for first, count, col, moved in edge_parts(sz, moves, wide_w, k * sz.half, wide_e, at_e):
            moved = moved * (speed * sea[col : col + 1, :])
            rows = pl.ds(k * sz.ring + first * sz.cols + col, count, stride=sz.cols)
            adv[rows, :] = adv[rows, :] + moved
            lines[first, col] = lines.get((first, col), 0.0) + moved * weight
        at = k * sz.side
        for first, count in west_half(sz):
            start = k * sz.ring + first * sz.cols + sz.cols - 1
            s_near[pl.ds(at + first, count), :] = energy[pl.ds(start, count, stride=sz.cols), :]
        s_near[pl.ds(at + sz.quarter, sz.half), :] = wide_e[pl.ds(k * sz.thick + sz.angles, sz.half), :]
        if sz.side > sz.angles:
            rest = sz.side - sz.angles
            s_near[pl.ds(at + sz.angles, rest), :] = jnp.zeros((rest, sz.lat), F32)
        s_line = jnp.zeros((VREG, sz.lat), F32)
        for v in range(sz.side // VREG):
            x = wide_e[pl.ds(k * sz.thick + v * VREG, VREG), :]
            near = s_near[pl.ds(at + v * VREG, VREG), :]
            out = s_sea * side_transported(sz, x, near, v, s_moves, speed)
            side[pl.ds(at + v * VREG, VREG), :] = out
            s_line = s_line + (out if (v + 1) * VREG <= sz.angles else jnp.where(sub < sz.angles - v * VREG, out, 0.0))
        s_total = s_total + s_line * weight
    mine = total[0 : sz.cols, :]
    for i in range(1, VREG // sz.cols):
        mine = mine + total[i * sz.cols : (i + 1) * sz.cols, :]
    west, east = (
        sum(jnp.sum(x, axis=0, keepdims=True) for (_, c), x in lines.items() if c == col) for col in (0, sz.cols - 1)
    )
    between = jnp.zeros((sz.cols - 2, sz.lat), F32)
    mine = mine + jnp.concatenate([west, between, east], axis=0)
    s_sum = jnp.sum(s_total, axis=0, keepdims=True)
    sums = jnp.concatenate([mine, s_sum, jnp.zeros((VREG - sz.cols - 1, sz.lat), F32)], axis=0)
    part[...] = sums
    fix[...] = jnp.zeros_like(fix)
    fix[pl.ds(sz.sum_row, 3 * VREG), :] = jnp.concatenate(split3(sums), axis=0)
    start = sz.bands - reach - far_band(sz)
    for k in range(reach):
        band_row = pl.multiple_of((start + k) * sz.ring, VREG)
        at = k * sz.far_band
        for first, count in west_half(sz):
            fix[pl.ds(at, count), :] = adv[pl.ds(band_row + first * sz.cols, count, stride=sz.cols), :]
            at += count
        last = band_row + (sz.quarter + 1) * sz.cols - 1
        fix[pl.ds(at, sz.half), :] = adv[pl.ds(last, sz.half, stride=sz.cols), :]
        s_row = pl.multiple_of((start + k) * sz.side, VREG)
        fix[pl.ds(k * sz.far_band + sz.rim_band, sz.angles), :] = side[pl.ds(s_row, sz.angles), :]
    msg_a[...] = fix[...].astype(BF16)


def nest_kernel(sz, nest, moves, out):
    def band(k, inverse):
        base = pl.multiple_of(k * sz.ring, VREG)
        for v in range(sz.vregs):
            moved = transported(sz, nest, base, v, moves, nest_speedup * speed_coef * inverse)
            out[pl.ds(base + v * VREG, VREG), :] = moved

    over_bands(sz.bands, band_ratio(sz, 0, True), band, True)


def nest_edge_kernel(sz, inner, from_w, from_e, moves, out, columns, wide_w, wide_e):
    grid_rank = lax.axis_index("grid")
    quarter = sz.grid // 4
    keep_w = jnp.where((grid_rank != quarter) & (grid_rank != 3 * quarter), 1.0, 0.0).astype(F32)
    keep_e = jnp.where((grid_rank != quarter - 1) & (grid_rank != 3 * quarter - 1), 1.0, 0.0).astype(F32)
    wide_w[...] = from_w[...].astype(F32)
    wide_e[...] = from_e[...].astype(F32)
    for k in range(sz.bands):
        speed = nest_speedup * speed_coef * band_ratio(sz, k, True)
        at_w, at_e = sz.thin + k * sz.half, sz.thick_nest + k * sz.half
        for first, count, col, moved in edge_parts(sz, moves, wide_w, at_w, wide_e, at_e):
            rows = pl.ds(k * sz.ring + first * sz.cols + col, count, stride=sz.cols)
            out[rows, :] = out[rows, :] + moved * (speed * (keep_w if col == 0 else keep_e))
    for c in range(sz.cols):
        columns[c, pl.ds(0, sz.bins), :] = out[pl.ds(c, sz.bins, stride=sz.cols), :]


def dot_lanes(a, b):
    return lax.dot_general(a, b, (((1,), (1,)), ((), ())), preferred_element_type=F32)


def rim_kernel(sz, cell, dest, target, weight, mix):
    device = lax.broadcasted_iota(jnp.int32, (sz.grid, sz.rim), 0)
    hot = jnp.where(device == dest[...], 1.0, 0.0)
    before = lax.broadcasted_iota(jnp.int32, (sz.rim, sz.rim), 0)
    after = lax.broadcasted_iota(jnp.int32, (sz.rim, sz.rim), 1)
    earlier = jnp.dot(
        hot.astype(BF16), jnp.where(before < after, 1.0, 0.0).astype(BF16), preferred_element_type=F32
    )
    rank = jnp.sum(hot * earlier, axis=0, keepdims=True)
    place = dest[...] * sz.cap + rank.astype(jnp.int32)
    slot = lax.broadcasted_iota(jnp.int32, (sz.slots, sz.rim), 0)
    takes = jnp.where(slot == place, 1.0, 0.0).astype(BF16)
    row = lax.broadcasted_iota(jnp.int32, (sz.lat, sz.rim), 0)
    col = cell[0:1, :] - lax.axis_index("grid") * sz.cols
    south_row = cell[1:2, :]
    ex, ny = weight[0:1, :], weight[1:2, :]
    for c in range(sz.cols + 1):
        share = jnp.where(col == c, 1.0 - ex, 0.0) + jnp.where(col + 1 == c, ex, 0.0)
        south, north = share * (1.0 - ny), share * ny
        corner = jnp.where(row == south_row, south, 0.0) + jnp.where(row == south_row + 1, north, 0.0)
        mix[:, c * sz.lat : (c + 1) * sz.lat] = dot_lanes(takes, corner.astype(BF16)).astype(BF16)
    at = sz.bins - (sz.lanes - 128)
    line = lax.broadcasted_iota(jnp.int32, (128, sz.rim), 0)
    t = target[...]
    t_col = t // sz.lat
    about = jnp.where(line == at, t_col.astype(F32), 0.0)
    about = about + jnp.where(line == at + 1, (t - t_col * sz.lat).astype(F32), 0.0)
    about = about + jnp.where(line == at + 2, weight[2:3, :], 0.0)
    n = (sz.cols + 1) * sz.lat
    mix[:, n : n + 128] = dot_lanes(takes, about.astype(BF16)).astype(BF16)


def low_rows(sz):
    return lax.broadcasted_iota(jnp.int32, (VREG, sz.lat), 0) < VREG // 2


def put(sz, plain, turned, slot, vals):
    nv, low = sz.vregs, low_rows(sz)
    for v in range(nv):
        if plain is not None:
            plain[slot, pl.ds(v * VREG, VREG), :] = vals[v]
        nxt = pltpu.roll(jnp.where(low, vals[(v + 1) % nv], vals[v]), VREG // 2, 0)
        turned[slot, pl.ds((v + 2) * VREG, VREG), :] = nxt
        if v >= nv - 2:
            turned[slot, pl.ds((v + 2 - nv) * VREG, VREG), :] = nxt
        if v == 0:
            turned[slot, pl.ds((nv + 2) * VREG, VREG), :] = nxt


def close(sz, ref, slot):
    ref[slot, pl.ds(VREG - 3, 3), :] = ref[slot, pl.ds(VREG + sz.angles - 3, 3), :]
    ref[slot, pl.ds(VREG + sz.angles, 3), :] = ref[slot, pl.ds(VREG, 3), :]


def s_put(sz, s_plain, slot, load):
    for v in range(sz.side // VREG):
        s_plain[slot, pl.ds((v + 1) * VREG, VREG), :] = load(v)
    close(sz, s_plain, slot)


def exchange(sc, c, up, down):
    return sc * (c * (up + down) - 2.0 * (up * down))


def strengths(sz, ratio, n, plain, turned, plus, minus, s_plain, s_plus, s_minus):
    nv = sz.vregs
    strength = nonlin_coef * ratio
    for v in range(nv):
        c = plain[n + 3, pl.ds(v * VREG, VREG), :]
        sc = strength * c
        for ref, up_row, down_row in ((plus, v + 3, v + 1), (minus, v, v + 2)):
            up = turned[n + 5, pl.ds(up_row * VREG, VREG), :]
            down = turned[n, pl.ds(down_row * VREG, VREG), :]
            delta = exchange(sc, c, up, down)
            ref[n, pl.ds((v + 1) * VREG, VREG), :] = delta
            if v == nv - 1:
                ref[n, pl.ds(0, VREG), :] = delta
            if v < 2:
                ref[n, pl.ds((nv + 1 + v) * VREG, VREG), :] = delta
    for v in range(sz.side // VREG):
        row = (v + 1) * VREG
        c = s_plain[n + 3, pl.ds(row, VREG), :]
        sc = strength * c
        for ref, s in ((s_plus, 1), (s_minus, -1)):
            up = s_plain[n + 5, pl.ds(row + 3 * s, VREG), :]
            down = s_plain[n, pl.ds(row - s, VREG), :]
            ref[n, pl.ds(row, VREG), :] = exchange(sc, c, up, down)
    close(sz, s_plus, n)
    close(sz, s_minus, n)


def is_even():
    return lax.rem(lax.axis_index("spec"), 2) == 0


def complete(sz, slot, fix, k, plain, s_plain):
    at = k * sz.far_band
    for start, count in west_half(sz):
        plain[slot, pl.ds(start * sz.cols, count, stride=sz.cols), :] = fix[pl.ds(at, count), :]
        at += count
    last = (sz.quarter + 1) * sz.cols - 1
    plain[slot, pl.ds(last, sz.half, stride=sz.cols), :] = fix[pl.ds(at, sz.half), :]
    at = k * sz.far_band + sz.rim_band
    s_put(sz, s_plain, slot, lambda v: fix[pl.ds(at + v * VREG, VREG), :])


def turn_halo(sz, base, plain, turned, real=None):
    def halo(k, carry):
        vals = [plain[base + k, pl.ds(v * VREG, VREG), :] for v in range(sz.vregs)]
        put(sz, None if real is None else plain, turned, base + k, vals if real is None else [x * real for x in vals])
        return carry

    lax.fori_loop(0, reach, halo, 0)


def numerators(sz, k, ratio, adv, gain, plus, minus, store):
    nv, low = sz.vregs, low_rows(sz)
    base = pl.multiple_of(k * sz.ring, VREG)

    def moved_in(v):
        return (
            plus[k, pl.ds(v * VREG, VREG), :]
            + minus[k, pl.ds((v + 3) * VREG, VREG), :]
            + plus[k + 5, pl.ds((v + 2) * VREG, VREG), :]
            + minus[k + 5, pl.ds((v + 1) * VREG, VREG), :]
        )

    before = moved_in(nv - 1)
    for v in range(nv):
        now = moved_in(v)
        moved = pltpu.roll(jnp.where(low, now, before), VREG // 2, 0)
        before = now
        here = pl.ds((v + 1) * VREG, VREG)
        transfer = moved - 2.0 * (plus[k + 2, here, :] + minus[k + 2, here, :])
        a = adv[pl.ds(base + v * VREG, VREG), :]
        grown = ratio * gain[pl.ds(v * VREG, VREG), :]
        store(pl.ds(base + v * VREG, VREG), a + grown * a + transfer)


def transport_raw(sz, raw, moves, sea, plain, wide, upper):
    base = jnp.where(upper, sz.bands + reach, 0)
    inverse = jnp.where(upper, band_ratio(sz, sz.bands, True), band_ratio(sz, -reach, True))
    wide[...] = raw[...].astype(F32)

    def transport(k, r):
        start = pl.multiple_of(k * sz.ring, VREG)
        for v in range(sz.vregs):
            moved = transported(sz, wide, start, v, moves, speed_coef * r)
            plain[base + k, pl.ds(v * VREG, VREG), :] = sea[...] * moved

    over_bands(reach, inverse, transport, True)


def beside_kernel(sz, raw_a, moves, sea, plain, wide):
    transport_raw(sz, raw_a, moves, sea, plain, wide, is_even())


def beyond_kernel(sz, raw_b, moves, sea, plain_in, plain, far_near, wide):
    transport_raw(sz, raw_b, moves, sea, plain, wide, jnp.logical_not(is_even()))
    far_near[...] = jnp.zeros_like(far_near)
    for k in range(reach):
        for first, count in west_half(sz):
            start = k * sz.ring + first * sz.cols + sz.cols - 1
            far_near[pl.ds(k * sz.side + first, count), :] = wide[pl.ds(start, count, stride=sz.cols), :]


def inner_kernel(
    sz, adv, side, recv_a, gain, plain_in, plain, turned, plus, minus, s_plain, s_plus, s_minus, num, fix
):
    base_a = jnp.where(is_even(), sz.bands + reach, 0)

    def own(k, carry):
        base = pl.multiple_of(k * sz.ring, VREG)
        put(sz, plain, turned, k + reach, [adv[pl.ds(base + v * VREG, VREG), :] for v in range(sz.vregs)])
        s_base = pl.multiple_of(k * sz.side, VREG)
        s_put(sz, s_plain, k + reach, lambda v: side[pl.ds(s_base + v * VREG, VREG), :])
        return carry

    lax.fori_loop(0, sz.bands, own, 0)

    fix[...] = recv_a[...].astype(F32)
    for k in range(reach):
        complete(sz, base_a + k, fix, k, plain, s_plain)
    turn_halo(sz, base_a, plain, turned)

    arrays = (plain, turned, plus, minus, s_plain, s_plus, s_minus)
    start = jnp.where(is_even(), reach, 0)
    ratio = jnp.where(is_even(), band_ratio(sz, 3), band_ratio(sz, 3 - reach))
    over_bands(sz.bands, ratio, lambda i, r: strengths(sz, r, start + i, *arrays))

    def store(rows, value):
        num[rows, :] = value

    ratio = jnp.where(is_even(), band_ratio(sz, reach), band_ratio(sz, 0))
    over_bands(
        sz.bands - reach, ratio, lambda i, r: numerators(sz, start + i, r, adv, gain, plus, minus, store)
    )


def outer_kernel(
    sz, adv, side, recv_b, gain, moves, s_moves, sea, from_e, far_near, num_in,
    plain_in, turned_in, plus_in, minus_in, s_plain_in, s_plus_in, s_minus_in,
    num, plain, turned, plus, minus, s_plain, s_plus, s_minus, s_num, wide, s_near,
):
    spec_rank = lax.axis_index("spec")
    ns = sz.side // VREG
    base_b = jnp.where(is_even(), 0, sz.bands + reach)
    real_b = jnp.where((spec_rank == 0) | (spec_rank == sz.spec - 1), 0.0, 1.0).astype(F32)
    info = from_e[pl.ds(sz.info // 16 * 16, 32), :].astype(F32)
    at = sz.info % 16
    s_sea = info[at : at + 1] * real_b
    wide[...] = recv_b[...].astype(F32)
    s_near[...] = far_near[...]
    inverse = jnp.where(is_even(), band_ratio(sz, -reach, True), band_ratio(sz, sz.bands, True))
    for k in range(reach):
        speed = inverse * (speed_coef / ratio_step**k)
        slot, row = base_b + k, sz.pass_thick + k * sz.thick
        for start, count, col, moved in edge_parts(sz, moves, wide, k * sz.half, wide, row + sz.quarter):
            rows = pl.ds(start * sz.cols + col, count, stride=sz.cols)
            plain[slot, rows, :] = plain[slot, rows, :] + moved * (speed * sea[col : col + 1, :])
        at_near = k * sz.side
        s_near[pl.ds(at_near + sz.quarter, sz.half), :] = wide[pl.ds(row + sz.angles, sz.half), :]

        def column(v):
            x = wide[pl.ds(row + v * VREG, VREG), :]
            near = s_near[pl.ds(at_near + v * VREG, VREG), :]
            return s_sea * side_transported(sz, x, near, v, s_moves, speed)

        s_put(sz, s_plain, slot, column)
    turn_halo(sz, base_b, plain, turned, real_b)
    arrays = (plain, turned, plus, minus, s_plain, s_plus, s_minus)
    begin = jnp.where(is_even(), 0, sz.bands)
    ratio = jnp.where(is_even(), band_ratio(sz, 3 - reach), band_ratio(sz, sz.bands + 3 - reach))
    over_bands(reach, ratio, lambda i, r: strengths(sz, r, begin + i, *arrays))

    at = at + 1
    s_east = info[at : at + 1] + info[at + 1 : at + 2] + info[at + 2 : at + 3]
    s_north = info[at + 3 : at + 4] + info[at + 4 : at + 5] + info[at + 5 : at + 6]
    missing = jnp.where(is_even(), 0, sz.bands - reach)

    def store(rows, value):
        num[rows, :] = value

    over_bands(
        reach,
        jnp.where(is_even(), band_ratio(sz, 0), band_ratio(sz, sz.bands - reach)),
        lambda i, r: numerators(sz, missing + i, r, adv, gain, plus, minus, store),
    )

    s_gain = []
    for v in range(ns):
        here = pl.ds(v * VREG, VREG)
        along = s_moves[3, here, :] * s_east + s_moves[4, here, :] * s_north
        s_gain.append(wind_coef * jnp.maximum(along, 0.0))
    for k in range(sz.bands):
        ratio = band_ratio(sz, k)
        for v in range(ns):
            row = (v + 1) * VREG
            here = pl.ds(row, VREG)
            transfer = (
                s_plus[k, pl.ds(row - 3, VREG), :]
                + s_minus[k, pl.ds(row + 3, VREG), :]
                + s_plus[k + 5, pl.ds(row + 1, VREG), :]
                + s_minus[k + 5, pl.ds(row - 1, VREG), :]
                - 2.0 * (s_plus[k + 2, here, :] + s_minus[k + 2, here, :])
            )
            a = side[pl.ds(k * sz.side + v * VREG, VREG), :]
            s_num[pl.ds(k * sz.side + v * VREG, VREG), :] = a + (ratio * s_gain[v]) * a + transfer


def source_kernel(sz, num, s_num, pair, other, mix, out, msg, s_out):
    total_weight = sz.angles * 0.1 * sum(ratio_step ** (k - sz.freqs // 2) for k in range(sz.freqs))
    means = (pair[...] + other[...]) * (1.0 / total_weight)
    mean = jnp.concatenate([means[0 : sz.cols]] * (VREG // sz.cols), axis=0)
    s_mean = means[sz.cols : sz.cols + 1]

    def finish(k, ratio):
        factor = 1.0 / (1.0 + (dissip_coef * ratio * ratio) * mean)
        base = pl.multiple_of(k * sz.ring, VREG)
        for v in range(sz.vregs):
            here = pl.ds(base + v * VREG, VREG)
            out[here, :] = num[here, :] * factor

    over_bands(sz.bands, band_ratio(sz, 0), finish)
    for k in range(sz.bands):
        ratio = band_ratio(sz, k)
        factor = 1.0 / (1.0 + (dissip_coef * ratio * ratio) * s_mean)
        for v in range(sz.side // VREG):
            here = pl.ds(k * sz.angles + v * VREG, VREG)
            s_out[here, :] = s_num[pl.ds(k * sz.side + v * VREG, VREG), :] * factor

    pad = jnp.zeros((sz.lanes - sz.bins, sz.lat), BF16)
    columns = [out[pl.ds(c, sz.bins, stride=sz.cols), :] for c in range(sz.cols)]
    columns.append(s_out[pl.ds(0, sz.bins), :])
    columns = [jnp.concatenate([c.astype(BF16), pad], axis=0) for c in columns]
    n = (sz.cols + 1) * sz.lat
    spectra = dot_lanes(mix[:, 0:n], jnp.concatenate(columns, axis=1))
    about = mix[:, n : n + 128].astype(F32)
    msg[:, 0 : sz.lanes - 128] = spectra[:, : sz.lanes - 128].astype(BF16)
    msg[:, sz.lanes - 128 : sz.lanes] = (spectra[:, sz.lanes - 128 :] + about).astype(BF16)


def blend_kernel(sz, recv, nest_adv, spectra, global_hbm, result_hbm, out, sems):
    writes = [pltpu.make_async_copy(spectra, global_hbm, sems.at[sz.lanes // 128])]
    writes[0].start()
    at = sz.bins - (sz.lanes - 128)
    about = recv[:, sz.lanes - 128 :].astype(F32)
    t_col, t_row, rate = about[:, at : at + 1], about[:, at + 1 : at + 2], about[:, at + 2 : at + 3]
    lane = lax.broadcasted_iota(jnp.int32, (sz.slots, sz.lat), 1).astype(F32)
    hit = jnp.where(lane == t_row, rate, 0.0)
    relax = [jnp.where(t_col == float(c), hit, 0.0) for c in range(sz.cols)]
    kept = [1.0 - jnp.sum(r, axis=0, keepdims=True) for r in relax]
    relax = jnp.concatenate(relax, axis=1).astype(BF16)
    for part, start in enumerate(range(0, sz.bins, 128)):
        count = min(128, sz.bins - start)
        added = lax.dot_general(
            recv[:, start : start + 128], relax, (((0,), (0,)), ((), ())), preferred_element_type=F32
        )
        for c in range(sz.cols):
            here = pl.ds(start * sz.cols + c, count, stride=sz.cols)
            own = nest_adv[c, pl.ds(start, count), :]
            out[here, :] = own * kept[c] + added[:count, c * sz.lat : (c + 1) * sz.lat]
        rows = pl.ds(start * sz.cols, count * sz.cols)
        writes.append(pltpu.make_async_copy(out.at[rows], result_hbm.at[rows], sems.at[part]))
        writes[-1].start()
    for write in writes:
        write.wait()


def kernel_call(body, out_shape, n_in, hbm=(), out_hbm=(), scratch=(), aliases=None, flops=0, name=None):
    def specs(count, far):
        return [pl.BlockSpec(memory_space=pltpu.HBM if i in far else pltpu.VMEM) for i in range(count)]

    many = isinstance(out_shape, tuple)
    out_specs = specs(len(out_shape) if many else 1, out_hbm)
    call = pl.pallas_call(
        body,
        out_shape=out_shape,
        in_specs=specs(n_in, hbm),
        out_specs=out_specs if many else out_specs[0],
        scratch_shapes=list(scratch),
        input_output_aliases=aliases or {},
        compiler_params=pltpu.CompilerParams(vmem_limit_bytes=20 * 2**20),
        cost_estimate=pl.CostEstimate(flops=flops, bytes_accessed=0, transcendentals=0) if flops else None,
        name=name,
    )
    if not aliases:
        return call

    def in_place(*args):
        pin = functools.partial(pltpu.with_memory_space_constraint, memory_space=pltpu.VMEM)
        return call(*[pin(a) if i in aliases else a for i, a in enumerate(args)])

    return in_place


def per_device(
    mesh, energy, nest_energy, ocean_mask, wind_field, rim_cell, rim_dest, rim_target, rim_weight
):
    sz = Sizes(mesh, energy, rim_dest.shape[0])

    def array(*shape, dtype=F32):
        return jax.ShapeDtypeStruct(shape + (sz.lat,), dtype)

    def vmem(*shape):
        return pltpu.VMEM(shape + (sz.lat,), F32)

    def half(rows):
        return array(rows, dtype=BF16)

    field = array(sz.rows)
    table = jnp.asarray(angle_table(sz))
    energy4, energy = energy, energy.reshape(sz.rows, sz.lat)
    nest = nest_energy.reshape(sz.rows, sz.lat)
    up = [(i, (i + 1) % sz.grid) for i in range(sz.grid)]
    down = [(j, i) for i, j in up]
    across = []
    for g in range(sz.grid):
        for i in range(sz.spec):
            j = i + 1 if i % 2 else i - 1
            to = (g, j) if 0 <= j < sz.spec else ((g ^ 1) % sz.grid, i)
            across.append((g * sz.spec + i, to[0] * sz.spec + to[1]))
    both = ("grid", "spec")
    near_rows = [vmem(sz.thin_rows), vmem(sz.thick_rows)]

    stay = functools.partial(pltpu.with_memory_space_constraint, memory_space=pltpu.HBM)
    def column(n):
        return vmem(sz.bands, n)

    thin, thick = kernel_call(
        functools.partial(pack_kernel, sz),
        (half(sz.thin_rows), half(sz.thick_rows)),
        4,
        hbm=range(4),
        scratch=[
            column(sz.angles),
            column(sz.half),
            column(sz.half),
            column(sz.angles - 3 * sz.quarter),
            column(sz.quarter),
            column(sz.angles - 3 * sz.quarter),
            column(sz.quarter),
            pltpu.VMEM(ocean_mask.shape, ocean_mask.dtype),
            pltpu.VMEM(wind_field.shape, F32),
        ]
        + near_rows
        + [pltpu.SemaphoreType.DMA((9,))],
        name="pack",
    )(stay(energy4), stay(nest_energy), stay(ocean_mask), stay(wind_field))
    from_e = lax.ppermute(thick, "grid", down)
    from_w = lax.ppermute(thin, "grid", up)

    table, thin = lax.optimization_barrier((table, thin))
    moves, nest_moves, s_moves, gain, sea = kernel_call(
        functools.partial(setup_kernel, sz),
        (array(3, sz.ring), array(3, sz.ring), array(5, sz.side), array(sz.ring), array(VREG)),
        3,
        name="setup",
    )(table, ocean_mask, wind_field)
    energy, table = lax.optimization_barrier((energy, table))
    raw_a, raw_b = kernel_call(
        functools.partial(raw_kernel, sz), (half(sz.edge_rows), half(sz.edge_rows)), 1, name="raw"
    )(energy)
    pairs = [(i, i ^ 1) for i in range(sz.spec)]
    recv_raw_b = lax.ppermute(raw_b, "spec", [(i, (i + 1 if i % 2 else i - 1) % sz.spec) for i in range(sz.spec)])
    recv_raw_a = lax.ppermute(raw_a, "spec", pairs)
    rim = (rim_cell.T, rim_dest.T, rim_target.reshape(1, sz.rim), rim_weight.T)
    rim, raw_a = lax.optimization_barrier((rim, raw_a))
    mix = kernel_call(
        functools.partial(rim_kernel, sz),
        jax.ShapeDtypeStruct((sz.slots, (sz.cols + 1) * sz.lat + 128), BF16),
        4,
        name="rim",
    )(*rim)
    nest, raw_a = lax.optimization_barrier((nest, raw_a))
    nest_inner = kernel_call(functools.partial(nest_kernel, sz), field, 2, flops=3 * 10**10, name="nest")(nest, nest_moves)
    energy, raw_a = lax.optimization_barrier((energy, raw_a))
    adv, total = kernel_call(
        functools.partial(local_kernel, sz), (field, array(VREG)), 3, flops=3 * 10**10, name="local"
    )(energy, moves, sea)
    band_fields = array(sz.bands + 2 * reach, sz.ring)
    plain = kernel_call(
        functools.partial(beside_kernel, sz), band_fields, 3, scratch=[vmem(sz.edge_rows)], flops=10**10, name="beside"
    )(recv_raw_a, moves, sea)
    from_e, from_w, mix, nest_inner, adv, plain = lax.optimization_barrier(
        (from_e, from_w, mix, nest_inner, adv, plain)
    )

    msg_b = kernel_call(
        functools.partial(pass_kernel, sz),
        half(sz.pass_rows),
        2,
        scratch=near_rows + [vmem(sz.pass_rows)],
        name="pass",
    )(from_w, from_e)
    adv, side, msg_a, part = kernel_call(
        functools.partial(edge_kernel, sz),
        (field, array(sz.bands * sz.side), half(sz.fix_rows), array(VREG)),
        8,
        scratch=near_rows + [vmem(sz.bands * sz.side), vmem(sz.fix_rows)],
        aliases={0: 0},
        flops=3 * 10**10,
        name="edges",
    )(adv, total, energy, from_w, from_e, moves, s_moves, sea)

    recv_a = lax.ppermute(msg_a, "spec", pairs)
    recv_b = lax.ppermute(msg_b, both, across)
    recv_a, recv_raw_b = lax.optimization_barrier((recv_a, recv_raw_b))
    plain, far_near = kernel_call(
        functools.partial(beyond_kernel, sz),
        (band_fields, array(reach * sz.side)),
        4,
        scratch=[vmem(sz.edge_rows)],
        aliases={3: 0},
        flops=3 * 10**10,
        name="beyond",
    )(recv_raw_b, moves, sea, plain)
    pieces = recv_a[sz.sum_row : sz.sum_row + 3 * VREG].astype(F32)
    pair = part + pieces.reshape(3, VREG, sz.lat).sum(axis=0)
    other = jnp.zeros_like(pair)
    step = 2
    while step < sz.spec:
        pair = pair + other
        other = lax.ppermute(pair, "spec", [(i, i ^ (2 * step - 1)) for i in range(sz.spec)])
        step *= 2

    padded, centres, turns = sz.bands + 2 * reach, sz.bands + reach, sz.ring + 3 * VREG
    arrays = (
        array(padded, sz.ring),
        array(padded, turns),
        array(centres, turns),
        array(centres, turns),
        array(padded, sz.frame),
        array(centres, sz.frame),
        array(centres, sz.frame),
    )
    *inner, num = kernel_call(
        functools.partial(inner_kernel, sz),
        arrays + (field,),
        5,
        scratch=[vmem(sz.fix_rows)],
        aliases={4: 0},
        name="inner",
    )(adv, side, recv_a, gain, plain)
    nest_inner, num = lax.optimization_barrier((nest_inner, num))
    _, nest_adv = kernel_call(
        functools.partial(nest_edge_kernel, sz),
        (field, array(sz.cols, sz.bins + VREG)),
        4,
        scratch=near_rows,
        aliases={0: 0},
        name="nest_edge",
    )(nest_inner, from_w, from_e, nest_moves)
    nest_adv, recv_b = lax.optimization_barrier((nest_adv, recv_b))
    num, *_, s_num = kernel_call(
        functools.partial(outer_kernel, sz),
        (field,) + arrays + (array(sz.bands * sz.side),),
        10 + len(arrays),
        scratch=[vmem(sz.pass_rows), vmem(reach * sz.side)],
        aliases={9 + i: i for i in range(1 + len(arrays))},
        name="outer",
    )(adv, side, recv_b, gain, moves, s_moves, sea, from_e, far_near, num, *inner)
    spectra, msg = kernel_call(
        functools.partial(source_kernel, sz),
        (field, jax.ShapeDtypeStruct((sz.slots, sz.lanes), BF16)),
        5,
        scratch=[vmem(sz.bins + VREG)],
        name="sources",
    )(num, s_num, pair, other, mix)

    recv = lax.all_to_all(msg, "grid", split_axis=0, concat_axis=0, tiled=True)
    global_next, nest_next = kernel_call(
        functools.partial(blend_kernel, sz),
        (field, field),
        3,
        out_hbm=(0, 1),
        scratch=[vmem(sz.rows), pltpu.SemaphoreType.DMA((sz.lanes // 128 + 1,))],
        name="blend",
    )(recv, nest_adv, pltpu.with_memory_space_constraint(spectra, pltpu.VMEM))
    full = (sz.bands, sz.angles, sz.cols, sz.lat)
    return global_next.reshape(full), nest_next.reshape(full)


def solution(mesh):
    in_specs = (
        P("spec", None, "grid", None),
        P("spec", None, "grid", None),
        P("grid", None),
        P(None, "grid", None),
        P("grid", None),
        P("grid", None),
        P("grid"),
        P("grid", None),
    )
    out_specs = (P("spec", None, "grid", None), P("spec", None, "grid", None))
    return jax.shard_map(
        functools.partial(per_device, mesh),
        mesh=mesh,
        in_specs=in_specs,
        out_specs=out_specs,
        check_vma=False,
    )
```

```python
import functools

import jax
import jax.numpy as jnp
import numpy as np
from jax import lax
from jax.experimental import pallas as pl
from jax.experimental.pallas import tpu as pltpu
from jax.sharding import PartitionSpec as P

ratio_step = 1.1
speed_coef = 0.054
wind_coef = 0.05
dissip_coef = 0.2
nonlin_coef = 0.12
nest_speedup = 2.0
reach = 5

VREG = 8
BF16 = jnp.bfloat16
F32 = jnp.float32


class Sizes:
    def __init__(self, mesh, energy, rim_rows):
        self.grid = mesh.shape["grid"]
        self.spec = mesh.shape["spec"]
        self.bands, self.angles, self.cols, self.lat = energy.shape
        self.freqs = self.bands * self.spec
        self.bins = self.bands * self.angles
        self.ring = self.angles * self.cols
        self.rows = self.bins * self.cols
        self.vregs = self.ring // VREG
        self.rim = rim_rows
        self.cap = max(2, (2 * rim_rows + self.grid - 1) // self.grid)
        self.slots = self.grid * self.cap
        self.lanes = (self.bins + 3 + 127) // 128 * 128
        self.half = self.angles // 2
        self.quarter = self.angles // 4
        self.side = (self.angles + VREG - 1) // VREG * VREG
        self.frame = self.side + 2 * VREG
        self.thin = self.bands * self.half
        self.thin_rows = (2 * self.thin + 15) // 16 * 16
        self.thick = self.angles + self.half
        self.info = self.bands * self.thick
        self.thick_nest = (self.info + 7 + VREG - 1) // VREG * VREG
        self.thick_rows = (self.thick_nest + self.thin + 15) // 16 * 16
        self.edge_rows = reach * self.ring
        self.rim_band = 2 * self.half
        self.far_band = self.rim_band + self.angles
        self.sum_row = (reach * self.far_band + VREG - 1) // VREG * VREG
        self.fix_rows = (self.sum_row + 3 * VREG + 15) // 16 * 16
        self.pass_thick = (reach * self.half + VREG - 1) // VREG * VREG
        self.pass_rows = max(self.fix_rows + 16, (self.pass_thick + reach * self.thick + 15) // 16 * 16)


def band_ratio(sz, band, inverse=False):
    rank = lax.axis_index("spec")
    ratio = F32(0.0)
    for s in range(sz.spec):
        power = ratio_step ** (s * sz.bands + band - sz.freqs // 2)
        ratio = jnp.where(rank == s, F32(1.0 / power if inverse else power), ratio)
    return ratio


def over_bands(count, ratio, body, inverse=False):
    step = F32(1.0 / ratio_step if inverse else ratio_step)

    def turn(i, r):
        body(i, r)
        return r * step

    lax.fori_loop(0, count, turn, ratio)


def angle_table(sz):
    heading = 2.0 * np.pi * np.arange(sz.angles) / sz.angles
    table = np.zeros((sz.ring + VREG + sz.side, sz.lat), np.float32)
    table[sz.ring + VREG :][: sz.angles, 0] = np.cos(heading)
    table[sz.ring + VREG :][: sz.angles, 1] = np.sin(heading)
    table[: sz.ring, 0] = np.repeat(np.cos(heading), sz.cols)
    table[: sz.ring, 1] = np.repeat(np.sin(heading), sz.cols)
    degrees = -60.0 + 120.0 * (np.arange(sz.lat) + 0.5) / sz.lat
    table[sz.ring : sz.ring + VREG] = 1.0 / np.cos(degrees * (np.pi / 180.0))
    return table


def from_west(sz, angle):
    return angle < sz.quarter or angle >= 3 * sz.quarter


def split3(x):
    high = x.astype(BF16).astype(F32)
    middle = (x - high).astype(BF16).astype(F32)
    return [high, middle, x - high - middle]


def upwind(sz, v):
    sub = lax.broadcasted_iota(jnp.int32, (VREG, sz.lat), 0)
    first, per = v * VREG // sz.cols, VREG // sz.cols
    wests = [from_west(sz, first + i) for i in range(per)]
    west = sub < 0
    for i in range(per):
        if wests[i]:
            west = west | ((sub >= i * sz.cols) & (sub < (i + 1) * sz.cols))
    return wests, west, sub % sz.cols


def west_half(sz):
    return ((3 * sz.quarter, sz.angles - 3 * sz.quarter), (0, sz.quarter))


def fetch(pairs, sems):
    copies = [pltpu.make_async_copy(a, b, sems.at[i]) for i, (a, b) in enumerate(pairs)]
    for c in copies:
        c.start()
    return copies


def far_band(sz):
    return jnp.where(lax.rem(lax.axis_index("spec"), 2) == 0, 0, sz.bands - reach)


def pack_kernel(
    sz, energy, nest, mask, wind, thin, thick, first, second, first_n, late, early, late_n, early_n,
    mask_v, wind_v, tmp_thin, tmp_thick, sems,
):
    from_east = pl.ds(sz.quarter, sz.half)
    (start, count), (_, rest) = west_half(sz)
    last = sz.cols - 1
    pairs = [
        (mask, mask_v),
        (wind, wind_v),
        (energy.at[:, :, 0], first),
        (energy.at[:, from_east, 1], second),
        (energy.at[:, pl.ds(start, count), last], late),
        (energy.at[:, pl.ds(0, rest), last], early),
        (nest.at[:, from_east, 0], first_n),
        (nest.at[:, pl.ds(start, count), last], late_n),
        (nest.at[:, pl.ds(0, rest), last], early_n),
    ]
    copies = [pltpu.make_async_copy(a, b, sems.at[i]) for i, (a, b) in enumerate(pairs)]
    for copy in copies:
        copy.start()
    spare = sz.thin_rows - 2 * sz.thin
    if spare:
        tmp_thin[pl.ds(2 * sz.thin, spare), :] = jnp.zeros((spare, sz.lat), F32)
    tmp_thick[...] = jnp.zeros_like(tmp_thick)
    for copy in copies[:6]:
        copy.wait()
    info = [mask_v[0:1, :].astype(F32)] + split3(wind_v[0, 0:1, :]) + split3(wind_v[1, 0:1, :])
    for i, line in enumerate(info):
        tmp_thick[pl.ds(sz.info + i, 1), :] = line
    for k in range(sz.bands):
        tmp_thin[pl.ds(k * sz.half, count), :] = late[k]
        tmp_thin[pl.ds(k * sz.half + count, rest), :] = early[k]
        tmp_thick[pl.ds(k * sz.thick, sz.angles), :] = first[k]
        tmp_thick[pl.ds(k * sz.thick + sz.angles, sz.half), :] = second[k]
    for copy in copies[6:]:
        copy.wait()
    for k in range(sz.bands):
        at = sz.thin + k * sz.half
        tmp_thin[pl.ds(at, count), :] = late_n[k]
        tmp_thin[pl.ds(at + count, rest), :] = early_n[k]
        tmp_thick[pl.ds(sz.thick_nest + k * sz.half, sz.half), :] = first_n[k]
    thin[...] = tmp_thin[...].astype(BF16)
    thick[...] = tmp_thick[...].astype(BF16)


def setup_kernel(sz, table, mask, wind, moves, nest_moves, s_moves, gain, sea):
    per = VREG // sz.cols
    sea[...] = jnp.concatenate([mask[...].astype(F32)] * per, axis=0)
    east_wind = jnp.concatenate([wind[0]] * per, axis=0)
    north_wind = jnp.concatenate([wind[1]] * per, axis=0)
    fill_moves(sz, 0, table, sz.cols, (moves, nest_moves))
    fill_moves(sz, sz.ring + VREG, table, 1, (s_moves, None))
    for v in range(sz.vregs):
        rows = table[pl.ds(v * VREG, VREG), :]
        along = rows[:, 0:1] * east_wind + rows[:, 1:2] * north_wind
        gain[pl.ds(v * VREG, VREG), :] = wind_coef * jnp.maximum(along, 0.0)
    for v in range(sz.side // VREG):
        rows = table[pl.ds(sz.ring + VREG + v * VREG, VREG), :]
        for i in range(2):
            s_moves[3 + i, pl.ds(v * VREG, VREG), :] = jnp.broadcast_to(rows[:, i : i + 1], (VREG, sz.lat))


def raw_kernel(sz, energy, raw_a, raw_b):
    for raw, first in ((raw_a, sz.bands - reach - far_band(sz)), (raw_b, far_band(sz))):
        raw[...] = energy[pl.ds(pl.multiple_of(first * sz.ring, VREG), sz.edge_rows), :].astype(BF16)


def pass_kernel(sz, from_w, from_e, msg, wide_w, wide_e, tmp):
    wide_w[...] = from_w[...].astype(F32)
    wide_e[...] = from_e[...].astype(F32)
    tmp[...] = jnp.zeros_like(tmp)
    first = far_band(sz)
    count = reach * sz.half
    tmp[pl.ds(0, count), :] = wide_w[pl.ds(first * sz.half, count), :]
    start = pl.multiple_of(first * sz.thick, VREG)
    tmp[pl.ds(sz.pass_thick, reach * sz.thick), :] = wide_e[pl.ds(start, reach * sz.thick), :]
    msg[...] = tmp[...].astype(BF16)


def fill_moves(sz, rows, table, cols, targets):
    lane = lax.broadcasted_iota(jnp.int32, (VREG, sz.lat), 1)
    sub = lax.broadcasted_iota(jnp.int32, (VREG, sz.lat), 0)
    sec = table[pl.ds(sz.ring, VREG), :]
    for v in range(targets[0].shape[1] // VREG):
        line = table[pl.ds(rows + v * VREG, VREG), :]
        along = jnp.broadcast_to(jnp.abs(line[:, 0:1]), (VREG, sz.lat))
        across = jnp.broadcast_to(jnp.abs(line[:, 1:2]), (VREG, sz.lat))
        edge = lane == jnp.where(sub < sz.half * cols - v * VREG, 0, sz.lat - 1)
        here = pl.ds(v * VREG, VREG)
        for target, by in zip(targets, (along * sec, along)):
            if target is not None:
                target[0, here, :] = by + across
                target[1, here, :] = by
                target[2, here, :] = jnp.where(edge, 0.0, across)


def beside(sz, x, turn):
    if turn >= VREG:
        return pltpu.roll(x, 1, 1)
    if turn <= 0:
        return pltpu.roll(x, sz.lat - 1, 1)
    sub = lax.broadcasted_iota(jnp.int32, (VREG, sz.lat), 0)
    return jnp.where(sub < turn, pltpu.roll(x, 1, 1), pltpu.roll(x, sz.lat - 1, 1))


def transported(sz, field, base, v, moves, speed):
    here = pl.ds(v * VREG, VREG)
    x = field[pl.ds(base + v * VREG, VREG), :]
    wests, west, col = upwind(sz, v)
    if all(wests):
        near, at_edge = pltpu.roll(x, 1, 0), col == 0
    elif not any(wests):
        near, at_edge = pltpu.roll(x, VREG - 1, 0), col == sz.cols - 1
    else:
        near = jnp.where(west, pltpu.roll(x, 1, 0), pltpu.roll(x, VREG - 1, 0))
        at_edge = jnp.where(west, col, sz.cols - 1 - col) == 0
    near = jnp.where(at_edge, 0.0, near)
    south = sz.half * sz.cols - v * VREG
    return x - speed * (moves[0, here, :] * x - moves[1, here, :] * near - moves[2, here, :] * beside(sz, x, south))


def edge_parts(sz, moves, wide_w, at_w, wide_e, at_e):
    parts = []
    for first, count in west_half(sz):
        parts.append((first, count, 0, wide_w[pl.ds(at_w, count), :]))
        at_w += count
    parts.append((sz.quarter, sz.half, sz.cols - 1, wide_e[pl.ds(at_e, sz.half), :]))
    for first, count, col, cells in parts:
        yield first, count, col, moves[1, pl.ds(first * sz.cols, count, stride=sz.cols), :] * cells


def side_transported(sz, x, near, v, s_moves, speed):
    here = pl.ds(v * VREG, VREG)
    move = s_moves[0, here, :] * x - s_moves[1, here, :] * near
    return x - speed * (move - s_moves[2, here, :] * beside(sz, x, sz.half - v * VREG))


def local_kernel(sz, energy, moves, sea, adv, total):
    total[...] = jnp.zeros_like(total)

    def band(k, inverse):
        base = pl.multiple_of(k * sz.ring, VREG)
        line = jnp.zeros((VREG, sz.lat), F32)
        for v in range(sz.vregs):
            out = sea[...] * transported(sz, energy, base, v, moves, speed_coef * inverse)
            adv[pl.ds(base + v * VREG, VREG), :] = out
            line = line + out
        total[...] = total[...] * F32(1.0 / ratio_step) + line

    over_bands(sz.bands, band_ratio(sz, 0, True), band, True)
    total[...] = total[...] * (0.1 * band_ratio(sz, sz.bands - 1))


def edge_kernel(
    sz, adv_in, total, energy, from_w, from_e, moves, s_moves, sea, adv, side, msg_a, part,
    wide_w, wide_e, s_near, fix,
):
    wide_w[...] = from_w[...].astype(F32)
    wide_e[...] = from_e[...].astype(F32)
    s_sea = wide_e[pl.ds(sz.info, 1), :]
    sub = lax.broadcasted_iota(jnp.int32, (VREG, sz.lat), 0)
    s_total = jnp.zeros((VREG, sz.lat), F32)
    lines = {}
    for k in range(sz.bands):
        inverse = band_ratio(sz, k, True)
        weight = 0.1 * band_ratio(sz, k)
        speed = speed_coef * inverse
        at_e = k * sz.thick + sz.quarter
        for first, count, col, moved in edge_parts(sz, moves, wide_w, k * sz.half, wide_e, at_e):
            moved = moved * (speed * sea[col : col + 1, :])
            rows = pl.ds(k * sz.ring + first * sz.cols + col, count, stride=sz.cols)
            adv[rows, :] = adv[rows, :] + moved
            lines[first, col] = lines.get((first, col), 0.0) + moved * weight
        at = k * sz.side
        for first, count in west_half(sz):
            start = k * sz.ring + first * sz.cols + sz.cols - 1
            s_near[pl.ds(at + first, count), :] = energy[pl.ds(start, count, stride=sz.cols), :]
        s_near[pl.ds(at + sz.quarter, sz.half), :] = wide_e[pl.ds(k * sz.thick + sz.angles, sz.half), :]
        if sz.side > sz.angles:
            rest = sz.side - sz.angles
            s_near[pl.ds(at + sz.angles, rest), :] = jnp.zeros((rest, sz.lat), F32)
        s_line = jnp.zeros((VREG, sz.lat), F32)
        for v in range(sz.side // VREG):
            x = wide_e[pl.ds(k * sz.thick + v * VREG, VREG), :]
            near = s_near[pl.ds(at + v * VREG, VREG), :]
            out = s_sea * side_transported(sz, x, near, v, s_moves, speed)
            side[pl.ds(at + v * VREG, VREG), :] = out
            s_line = s_line + (out if (v + 1) * VREG <= sz.angles else jnp.where(sub < sz.angles - v * VREG, out, 0.0))
        s_total = s_total + s_line * weight
    mine = total[0 : sz.cols, :]
    for i in range(1, VREG // sz.cols):
        mine = mine + total[i * sz.cols : (i + 1) * sz.cols, :]
    west, east = (
        sum(jnp.sum(x, axis=0, keepdims=True) for (_, c), x in lines.items() if c == col) for col in (0, sz.cols - 1)
    )
    between = jnp.zeros((sz.cols - 2, sz.lat), F32)
    mine = mine + jnp.concatenate([west, between, east], axis=0)
    s_sum = jnp.sum(s_total, axis=0, keepdims=True)
    sums = jnp.concatenate([mine, s_sum, jnp.zeros((VREG - sz.cols - 1, sz.lat), F32)], axis=0)
    part[...] = sums
    fix[...] = jnp.zeros_like(fix)
    fix[pl.ds(sz.sum_row, 3 * VREG), :] = jnp.concatenate(split3(sums), axis=0)
    start = sz.bands - reach - far_band(sz)
    for k in range(reach):
        band_row = pl.multiple_of((start + k) * sz.ring, VREG)
        at = k * sz.far_band
        for first, count in west_half(sz):
            fix[pl.ds(at, count), :] = adv[pl.ds(band_row + first * sz.cols, count, stride=sz.cols), :]
            at += count
        last = band_row + (sz.quarter + 1) * sz.cols - 1
        fix[pl.ds(at, sz.half), :] = adv[pl.ds(last, sz.half, stride=sz.cols), :]
        s_row = pl.multiple_of((start + k) * sz.side, VREG)
        fix[pl.ds(k * sz.far_band + sz.rim_band, sz.angles), :] = side[pl.ds(s_row, sz.angles), :]
    msg_a[...] = fix[...].astype(BF16)


def nest_kernel(sz, nest, moves, out):
    def band(k, inverse):
        base = pl.multiple_of(k * sz.ring, VREG)
        for v in range(sz.vregs):
            moved = transported(sz, nest, base, v, moves, nest_speedup * speed_coef * inverse)
            out[pl.ds(base + v * VREG, VREG), :] = moved

    over_bands(sz.bands, band_ratio(sz, 0, True), band, True)


def nest_edge_kernel(sz, inner, from_w, from_e, moves, out, columns, wide_w, wide_e):
    grid_rank = lax.axis_index("grid")
    quarter = sz.grid // 4
    keep_w = jnp.where((grid_rank != quarter) & (grid_rank != 3 * quarter), 1.0, 0.0).astype(F32)
    keep_e = jnp.where((grid_rank != quarter - 1) & (grid_rank != 3 * quarter - 1), 1.0, 0.0).astype(F32)
    wide_w[...] = from_w[...].astype(F32)
    wide_e[...] = from_e[...].astype(F32)
    for k in range(sz.bands):
        speed = nest_speedup * speed_coef * band_ratio(sz, k, True)
        at_w, at_e = sz.thin + k * sz.half, sz.thick_nest + k * sz.half
        for first, count, col, moved in edge_parts(sz, moves, wide_w, at_w, wide_e, at_e):
            rows = pl.ds(k * sz.ring + first * sz.cols + col, count, stride=sz.cols)
            out[rows, :] = out[rows, :] + moved * (speed * (keep_w if col == 0 else keep_e))
    for c in range(sz.cols):
        columns[c, pl.ds(0, sz.bins), :] = out[pl.ds(c, sz.bins, stride=sz.cols), :]


def dot_lanes(a, b):
    return lax.dot_general(a, b, (((1,), (1,)), ((), ())), preferred_element_type=F32)


def rim_kernel(sz, cell, dest, target, weight, mix):
    device = lax.broadcasted_iota(jnp.int32, (sz.grid, sz.rim), 0)
    hot = jnp.where(device == dest[...], 1.0, 0.0)
    before = lax.broadcasted_iota(jnp.int32, (sz.rim, sz.rim), 0)
    after = lax.broadcasted_iota(jnp.int32, (sz.rim, sz.rim), 1)
    earlier = jnp.dot(
        hot.astype(BF16), jnp.where(before < after, 1.0, 0.0).astype(BF16), preferred_element_type=F32
    )
    rank = jnp.sum(hot * earlier, axis=0, keepdims=True)
    place = dest[...] * sz.cap + rank.astype(jnp.int32)
    slot = lax.broadcasted_iota(jnp.int32, (sz.slots, sz.rim), 0)
    takes = jnp.where(slot == place, 1.0, 0.0).astype(BF16)
    row = lax.broadcasted_iota(jnp.int32, (sz.lat, sz.rim), 0)
    col = cell[0:1, :] - lax.axis_index("grid") * sz.cols
    south_row = cell[1:2, :]
    ex, ny = weight[0:1, :], weight[1:2, :]
    for c in range(sz.cols + 1):
        share = jnp.where(col == c, 1.0 - ex, 0.0) + jnp.where(col + 1 == c, ex, 0.0)
        south, north = share * (1.0 - ny), share * ny
        corner = jnp.where(row == south_row, south, 0.0) + jnp.where(row == south_row + 1, north, 0.0)
        mix[:, c * sz.lat : (c + 1) * sz.lat] = dot_lanes(takes, corner.astype(BF16)).astype(BF16)
    at = sz.bins - (sz.lanes - 128)
    line = lax.broadcasted_iota(jnp.int32, (128, sz.rim), 0)
    t = target[...]
    t_col = t // sz.lat
    about = jnp.where(line == at, t_col.astype(F32), 0.0)
    about = about + jnp.where(line == at + 1, (t - t_col * sz.lat).astype(F32), 0.0)
    about = about + jnp.where(line == at + 2, weight[2:3, :], 0.0)
    n = (sz.cols + 1) * sz.lat
    mix[:, n : n + 128] = dot_lanes(takes, about.astype(BF16)).astype(BF16)


def low_rows(sz):
    return lax.broadcasted_iota(jnp.int32, (VREG, sz.lat), 0) < VREG // 2


def put(sz, plain, turned, slot, vals):
    nv, low = sz.vregs, low_rows(sz)
    for v in range(nv):
        if plain is not None:
            plain[slot, pl.ds(v * VREG, VREG), :] = vals[v]
        nxt = pltpu.roll(jnp.where(low, vals[(v + 1) % nv], vals[v]), VREG // 2, 0)
        turned[slot, pl.ds((v + 2) * VREG, VREG), :] = nxt
        if v >= nv - 2:
            turned[slot, pl.ds((v + 2 - nv) * VREG, VREG), :] = nxt
        if v == 0:
            turned[slot, pl.ds((nv + 2) * VREG, VREG), :] = nxt


def close(sz, ref, slot):
    ref[slot, pl.ds(VREG - 3, 3), :] = ref[slot, pl.ds(VREG + sz.angles - 3, 3), :]
    ref[slot, pl.ds(VREG + sz.angles, 3), :] = ref[slot, pl.ds(VREG, 3), :]


def s_put(sz, s_plain, slot, load):
    for v in range(sz.side // VREG):
        s_plain[slot, pl.ds((v + 1) * VREG, VREG), :] = load(v)
    close(sz, s_plain, slot)


def exchange(sc, c, up, down):
    return sc * (c * (up + down) - 2.0 * (up * down))


def strengths(sz, ratio, n, plain, turned, plus, minus, s_plain, s_plus, s_minus):
    nv = sz.vregs
    strength = nonlin_coef * ratio
    for v in range(nv):
        c = plain[n + 3, pl.ds(v * VREG, VREG), :]
        sc = strength * c
        for ref, up_row, down_row in ((plus, v + 3, v + 1), (minus, v, v + 2)):
            up = turned[n + 5, pl.ds(up_row * VREG, VREG), :]
            down = turned[n, pl.ds(down_row * VREG, VREG), :]
            delta = exchange(sc, c, up, down)
            ref[n, pl.ds((v + 1) * VREG, VREG), :] = delta
            if v == nv - 1:
                ref[n, pl.ds(0, VREG), :] = delta
            if v < 2:
                ref[n, pl.ds((nv + 1 + v) * VREG, VREG), :] = delta
    for v in range(sz.side // VREG):
        row = (v + 1) * VREG
        c = s_plain[n + 3, pl.ds(row, VREG), :]
        sc = strength * c
        for ref, s in ((s_plus, 1), (s_minus, -1)):
            up = s_plain[n + 5, pl.ds(row + 3 * s, VREG), :]
            down = s_plain[n, pl.ds(row - s, VREG), :]
            ref[n, pl.ds(row, VREG), :] = exchange(sc, c, up, down)
    close(sz, s_plus, n)
    close(sz, s_minus, n)


def is_even():
    return lax.rem(lax.axis_index("spec"), 2) == 0


def complete(sz, slot, fix, k, plain, s_plain):
    at = k * sz.far_band
    for start, count in west_half(sz):
        plain[slot, pl.ds(start * sz.cols, count, stride=sz.cols), :] = fix[pl.ds(at, count), :]
        at += count
    last = (sz.quarter + 1) * sz.cols - 1
    plain[slot, pl.ds(last, sz.half, stride=sz.cols), :] = fix[pl.ds(at, sz.half), :]
    at = k * sz.far_band + sz.rim_band
    s_put(sz, s_plain, slot, lambda v: fix[pl.ds(at + v * VREG, VREG), :])


def turn_halo(sz, base, plain, turned, real=None):
    def halo(k, carry):
        vals = [plain[base + k, pl.ds(v * VREG, VREG), :] for v in range(sz.vregs)]
        put(sz, None if real is None else plain, turned, base + k, vals if real is None else [x * real for x in vals])
        return carry

    lax.fori_loop(0, reach, halo, 0)


def numerators(sz, k, ratio, adv, gain, plus, minus, store):
    nv, low = sz.vregs, low_rows(sz)
    base = pl.multiple_of(k * sz.ring, VREG)

    def moved_in(v):
        return (
            plus[k, pl.ds(v * VREG, VREG), :]
            + minus[k, pl.ds((v + 3) * VREG, VREG), :]
            + plus[k + 5, pl.ds((v + 2) * VREG, VREG), :]
            + minus[k + 5, pl.ds((v + 1) * VREG, VREG), :]
        )

    before = moved_in(nv - 1)
    for v in range(nv):
        now = moved_in(v)
        moved = pltpu.roll(jnp.where(low, now, before), VREG // 2, 0)
        before = now
        here = pl.ds((v + 1) * VREG, VREG)
        transfer = moved - 2.0 * (plus[k + 2, here, :] + minus[k + 2, here, :])
        a = adv[pl.ds(base + v * VREG, VREG), :]
        grown = ratio * gain[pl.ds(v * VREG, VREG), :]
        store(pl.ds(base + v * VREG, VREG), a + grown * a + transfer)


def has_across(sz):
    rank = lax.axis_index("spec")
    return jnp.where((rank == 0) | (rank == sz.spec - 1), 0.0, 1.0).astype(F32)


def transport_raw(sz, raw, moves, sea, plain, wide, upper):
    base = jnp.where(upper, sz.bands + reach, 0)
    inverse = jnp.where(upper, band_ratio(sz, sz.bands, True), band_ratio(sz, -reach, True))
    wide[...] = raw[...].astype(F32)

    def transport(k, r):
        start = pl.multiple_of(k * sz.ring, VREG)
        for v in range(sz.vregs):
            moved = transported(sz, wide, start, v, moves, speed_coef * r)
            plain[base + k, pl.ds(v * VREG, VREG), :] = sea * moved

    over_bands(reach, inverse, transport, True)


def beside_kernel(sz, raw_a, moves, sea, plain, wide):
    transport_raw(sz, raw_a, moves, sea[...], plain, wide, is_even())


def beyond_kernel(sz, raw_b, moves, sea, plain_in, plain, far_near, wide):
    transport_raw(sz, raw_b, moves, sea[...] * has_across(sz), plain, wide, jnp.logical_not(is_even()))
    far_near[...] = jnp.zeros_like(far_near)
    for k in range(reach):
        for first, count in west_half(sz):
            start = k * sz.ring + first * sz.cols + sz.cols - 1
            far_near[pl.ds(k * sz.side + first, count), :] = wide[pl.ds(start, count, stride=sz.cols), :]


def inner_kernel(
    sz, adv, side, recv_a, gain, plain_in, plain, turned, plus, minus, s_plain, s_plus, s_minus, num, fix
):
    base_a = jnp.where(is_even(), sz.bands + reach, 0)

    def own(k, carry):
        base = pl.multiple_of(k * sz.ring, VREG)
        put(sz, plain, turned, k + reach, [adv[pl.ds(base + v * VREG, VREG), :] for v in range(sz.vregs)])
        s_base = pl.multiple_of(k * sz.side, VREG)
        s_put(sz, s_plain, k + reach, lambda v: side[pl.ds(s_base + v * VREG, VREG), :])
        return carry

    lax.fori_loop(0, sz.bands, own, 0)

    fix[...] = recv_a[...].astype(F32)
    for k in range(reach):
        complete(sz, base_a + k, fix, k, plain, s_plain)
    turn_halo(sz, base_a, plain, turned)

    arrays = (plain, turned, plus, minus, s_plain, s_plus, s_minus)
    start = jnp.where(is_even(), reach, 0)
    ratio = jnp.where(is_even(), band_ratio(sz, 3), band_ratio(sz, 3 - reach))
    over_bands(sz.bands, ratio, lambda i, r: strengths(sz, r, start + i, *arrays))

    def store(rows, value):
        num[rows, :] = value

    ratio = jnp.where(is_even(), band_ratio(sz, reach), band_ratio(sz, 0))
    over_bands(
        sz.bands - reach, ratio, lambda i, r: numerators(sz, start + i, r, adv, gain, plus, minus, store)
    )


def outer_kernel(
    sz, adv, side, recv_b, gain, moves, s_moves, sea, from_e, far_near, num_in,
    plain_in, turned_in, plus_in, minus_in, s_plain_in, s_plus_in, s_minus_in,
    num, plain, turned, plus, minus, s_plain, s_plus, s_minus, s_num, wide, s_near,
):
    spec_rank = lax.axis_index("spec")
    ns = sz.side // VREG
    base_b = jnp.where(is_even(), 0, sz.bands + reach)
    real_b = has_across(sz)
    info = from_e[pl.ds(sz.info // 16 * 16, 32), :].astype(F32)
    at = sz.info % 16
    s_sea = info[at : at + 1] * real_b
    wide[...] = recv_b[...].astype(F32)
    s_near[...] = far_near[...]
    inverse = jnp.where(is_even(), band_ratio(sz, -reach, True), band_ratio(sz, sz.bands, True))
    for k in range(reach):
        speed = inverse * (speed_coef / ratio_step**k)
        slot, row = base_b + k, sz.pass_thick + k * sz.thick
        for start, count, col, moved in edge_parts(sz, moves, wide, k * sz.half, wide, row + sz.quarter):
            rows = pl.ds(start * sz.cols + col, count, stride=sz.cols)
            plain[slot, rows, :] = plain[slot, rows, :] + moved * (speed * real_b * sea[col : col + 1, :])
        at_near = k * sz.side
        s_near[pl.ds(at_near + sz.quarter, sz.half), :] = wide[pl.ds(row + sz.angles, sz.half), :]

        def column(v):
            x = wide[pl.ds(row + v * VREG, VREG), :]
            near = s_near[pl.ds(at_near + v * VREG, VREG), :]
            return s_sea * side_transported(sz, x, near, v, s_moves, speed)

        s_put(sz, s_plain, slot, column)
    turn_halo(sz, base_b, plain, turned)
    arrays = (plain, turned, plus, minus, s_plain, s_plus, s_minus)
    begin = jnp.where(is_even(), 0, sz.bands)
    ratio = jnp.where(is_even(), band_ratio(sz, 3 - reach), band_ratio(sz, sz.bands + 3 - reach))
    over_bands(reach, ratio, lambda i, r: strengths(sz, r, begin + i, *arrays))

    at = at + 1
    s_east = info[at : at + 1] + info[at + 1 : at + 2] + info[at + 2 : at + 3]
    s_north = info[at + 3 : at + 4] + info[at + 4 : at + 5] + info[at + 5 : at + 6]
    missing = jnp.where(is_even(), 0, sz.bands - reach)

    def store(rows, value):
        num[rows, :] = value

    over_bands(
        reach,
        jnp.where(is_even(), band_ratio(sz, 0), band_ratio(sz, sz.bands - reach)),
        lambda i, r: numerators(sz, missing + i, r, adv, gain, plus, minus, store),
    )

    s_gain = []
    for v in range(ns):
        here = pl.ds(v * VREG, VREG)
        along = s_moves[3, here, :] * s_east + s_moves[4, here, :] * s_north
        s_gain.append(wind_coef * jnp.maximum(along, 0.0))
    for k in range(sz.bands):
        ratio = band_ratio(sz, k)
        for v in range(ns):
            row = (v + 1) * VREG
            here = pl.ds(row, VREG)
            transfer = (
                s_plus[k, pl.ds(row - 3, VREG), :]
                + s_minus[k, pl.ds(row + 3, VREG), :]
                + s_plus[k + 5, pl.ds(row + 1, VREG), :]
                + s_minus[k + 5, pl.ds(row - 1, VREG), :]
                - 2.0 * (s_plus[k + 2, here, :] + s_minus[k + 2, here, :])
            )
            a = side[pl.ds(k * sz.side + v * VREG, VREG), :]
            s_num[pl.ds(k * sz.side + v * VREG, VREG), :] = a + (ratio * s_gain[v]) * a + transfer


def source_kernel(sz, num, s_num, pair, other, mix, out, msg, s_out):
    total_weight = sz.angles * 0.1 * sum(ratio_step ** (k - sz.freqs // 2) for k in range(sz.freqs))
    means = (pair[...] + other[...]) * (1.0 / total_weight)
    mean = jnp.concatenate([means[0 : sz.cols]] * (VREG // sz.cols), axis=0)
    s_mean = means[sz.cols : sz.cols + 1]

    def finish(k, ratio):
        factor = 1.0 / (1.0 + (dissip_coef * ratio * ratio) * mean)
        base = pl.multiple_of(k * sz.ring, VREG)
        for v in range(sz.vregs):
            here = pl.ds(base + v * VREG, VREG)
            out[here, :] = num[here, :] * factor

    over_bands(sz.bands, band_ratio(sz, 0), finish)
    for k in range(sz.bands):
        ratio = band_ratio(sz, k)
        factor = 1.0 / (1.0 + (dissip_coef * ratio * ratio) * s_mean)
        for v in range(sz.side // VREG):
            here = pl.ds(k * sz.angles + v * VREG, VREG)
            s_out[here, :] = s_num[pl.ds(k * sz.side + v * VREG, VREG), :] * factor

    pad = jnp.zeros((sz.lanes - sz.bins, sz.lat), BF16)
    columns = [out[pl.ds(c, sz.bins, stride=sz.cols), :] for c in range(sz.cols)]
    columns.append(s_out[pl.ds(0, sz.bins), :])
    columns = [jnp.concatenate([c.astype(BF16), pad], axis=0) for c in columns]
    n = (sz.cols + 1) * sz.lat
    spectra = dot_lanes(mix[:, 0:n], jnp.concatenate(columns, axis=1))
    about = mix[:, n : n + 128].astype(F32)
    msg[:, 0 : sz.lanes - 128] = spectra[:, : sz.lanes - 128].astype(BF16)
    msg[:, sz.lanes - 128 : sz.lanes] = (spectra[:, sz.lanes - 128 :] + about).astype(BF16)


def blend_kernel(sz, recv, nest_adv, spectra, global_hbm, result_hbm, out, sems):
    writes = [pltpu.make_async_copy(spectra, global_hbm, sems.at[sz.lanes // 128])]
    writes[0].start()
    at = sz.bins - (sz.lanes - 128)
    about = recv[:, sz.lanes - 128 :].astype(F32)
    t_col, t_row, rate = about[:, at : at + 1], about[:, at + 1 : at + 2], about[:, at + 2 : at + 3]
    lane = lax.broadcasted_iota(jnp.int32, (sz.slots, sz.lat), 1).astype(F32)
    hit = jnp.where(lane == t_row, rate, 0.0)
    relax = [jnp.where(t_col == float(c), hit, 0.0) for c in range(sz.cols)]
    kept = [1.0 - jnp.sum(r, axis=0, keepdims=True) for r in relax]
    relax = jnp.concatenate(relax, axis=1).astype(BF16)
    for part, start in enumerate(range(0, sz.bins, 128)):
        count = min(128, sz.bins - start)
        added = lax.dot_general(
            recv[:, start : start + 128], relax, (((0,), (0,)), ((), ())), preferred_element_type=F32
        )
        for c in range(sz.cols):
            here = pl.ds(start * sz.cols + c, count, stride=sz.cols)
            own = nest_adv[c, pl.ds(start, count), :]
            out[here, :] = own * kept[c] + added[:count, c * sz.lat : (c + 1) * sz.lat]
        rows = pl.ds(start * sz.cols, count * sz.cols)
        writes.append(pltpu.make_async_copy(out.at[rows], result_hbm.at[rows], sems.at[part]))
        writes[-1].start()
    for write in writes:
        write.wait()


def kernel_call(body, out_shape, n_in, hbm=(), out_hbm=(), scratch=(), aliases=None, flops=0, name=None):
    def specs(count, far):
        return [pl.BlockSpec(memory_space=pltpu.HBM if i in far else pltpu.VMEM) for i in range(count)]

    many = isinstance(out_shape, tuple)
    out_specs = specs(len(out_shape) if many else 1, out_hbm)
    call = pl.pallas_call(
        body,
        out_shape=out_shape,
        in_specs=specs(n_in, hbm),
        out_specs=out_specs if many else out_specs[0],
        scratch_shapes=list(scratch),
        input_output_aliases=aliases or {},
        compiler_params=pltpu.CompilerParams(vmem_limit_bytes=20 * 2**20),
        cost_estimate=pl.CostEstimate(flops=flops, bytes_accessed=0, transcendentals=0) if flops else None,
        name=name,
    )
    if not aliases:
        return call

    def in_place(*args):
        pin = functools.partial(pltpu.with_memory_space_constraint, memory_space=pltpu.VMEM)
        return call(*[pin(a) if i in aliases else a for i, a in enumerate(args)])

    return in_place


def per_device(
    mesh, energy, nest_energy, ocean_mask, wind_field, rim_cell, rim_dest, rim_target, rim_weight
):
    sz = Sizes(mesh, energy, rim_dest.shape[0])

    def array(*shape, dtype=F32):
        return jax.ShapeDtypeStruct(shape + (sz.lat,), dtype)

    def vmem(*shape):
        return pltpu.VMEM(shape + (sz.lat,), F32)

    def half(rows):
        return array(rows, dtype=BF16)

    field = array(sz.rows)
    table = jnp.asarray(angle_table(sz))
    energy4, energy = energy, energy.reshape(sz.rows, sz.lat)
    nest = nest_energy.reshape(sz.rows, sz.lat)
    up = [(i, (i + 1) % sz.grid) for i in range(sz.grid)]
    down = [(j, i) for i, j in up]
    across = []
    for g in range(sz.grid):
        for i in range(sz.spec):
            j = i + 1 if i % 2 else i - 1
            to = (g, j) if 0 <= j < sz.spec else ((g ^ 1) % sz.grid, i)
            across.append((g * sz.spec + i, to[0] * sz.spec + to[1]))
    both = ("grid", "spec")
    near_rows = [vmem(sz.thin_rows), vmem(sz.thick_rows)]

    stay = functools.partial(pltpu.with_memory_space_constraint, memory_space=pltpu.HBM)
    def column(n):
        return vmem(sz.bands, n)

    thin, thick = kernel_call(
        functools.partial(pack_kernel, sz),
        (half(sz.thin_rows), half(sz.thick_rows)),
        4,
        hbm=range(4),
        scratch=[
            column(sz.angles),
            column(sz.half),
            column(sz.half),
            column(sz.angles - 3 * sz.quarter),
            column(sz.quarter),
            column(sz.angles - 3 * sz.quarter),
            column(sz.quarter),
            pltpu.VMEM(ocean_mask.shape, ocean_mask.dtype),
            pltpu.VMEM(wind_field.shape, F32),
        ]
        + near_rows
        + [pltpu.SemaphoreType.DMA((9,))],
        name="pack",
    )(stay(energy4), stay(nest_energy), stay(ocean_mask), stay(wind_field))
    from_e = lax.ppermute(thick, "grid", down)
    from_w = lax.ppermute(thin, "grid", up)

    table, thin = lax.optimization_barrier((table, thin))
    moves, nest_moves, s_moves, gain, sea = kernel_call(
        functools.partial(setup_kernel, sz),
        (array(3, sz.ring), array(3, sz.ring), array(5, sz.side), array(sz.ring), array(VREG)),
        3,
        name="setup",
    )(table, ocean_mask, wind_field)
    energy, table = lax.optimization_barrier((energy, table))
    raw_a, raw_b = kernel_call(
        functools.partial(raw_kernel, sz), (half(sz.edge_rows), half(sz.edge_rows)), 1, name="raw"
    )(energy)
    pairs = [(i, i ^ 1) for i in range(sz.spec)]
    recv_raw_b = lax.ppermute(raw_b, "spec", [(i, (i + 1 if i % 2 else i - 1) % sz.spec) for i in range(sz.spec)])
    recv_raw_a = lax.ppermute(raw_a, "spec", pairs)
    rim = (rim_cell.T, rim_dest.T, rim_target.reshape(1, sz.rim), rim_weight.T)
    rim, raw_a = lax.optimization_barrier((rim, raw_a))
    mix = kernel_call(
        functools.partial(rim_kernel, sz),
        jax.ShapeDtypeStruct((sz.slots, (sz.cols + 1) * sz.lat + 128), BF16),
        4,
        name="rim",
    )(*rim)
    nest, raw_a = lax.optimization_barrier((nest, raw_a))
    nest_inner = kernel_call(functools.partial(nest_kernel, sz), field, 2, flops=3 * 10**10, name="nest")(nest, nest_moves)
    energy, raw_a = lax.optimization_barrier((energy, raw_a))
    adv, total = kernel_call(
        functools.partial(local_kernel, sz), (field, array(VREG)), 3, flops=3 * 10**10, name="local"
    )(energy, moves, sea)
    band_fields = array(sz.bands + 2 * reach, sz.ring)
    plain = kernel_call(
        functools.partial(beside_kernel, sz), band_fields, 3, scratch=[vmem(sz.edge_rows)], flops=10**10, name="beside"
    )(recv_raw_a, moves, sea)
    from_e, from_w, mix, nest_inner, adv, plain = lax.optimization_barrier(
        (from_e, from_w, mix, nest_inner, adv, plain)
    )

    msg_b = kernel_call(
        functools.partial(pass_kernel, sz),
        half(sz.pass_rows),
        2,
        scratch=near_rows + [vmem(sz.pass_rows)],
        name="pass",
    )(from_w, from_e)
    adv, side, msg_a, part = kernel_call(
        functools.partial(edge_kernel, sz),
        (field, array(sz.bands * sz.side), half(sz.fix_rows), array(VREG)),
        8,
        scratch=near_rows + [vmem(sz.bands * sz.side), vmem(sz.fix_rows)],
        aliases={0: 0},
        flops=3 * 10**10,
        name="edges",
    )(adv, total, energy, from_w, from_e, moves, s_moves, sea)

    recv_a = lax.ppermute(msg_a, "spec", pairs)
    recv_b = lax.ppermute(msg_b, both, across)
    recv_a, recv_raw_b = lax.optimization_barrier((recv_a, recv_raw_b))
    plain, far_near = kernel_call(
        functools.partial(beyond_kernel, sz),
        (band_fields, array(reach * sz.side)),
        4,
        scratch=[vmem(sz.edge_rows)],
        aliases={3: 0},
        flops=3 * 10**10,
        name="beyond",
    )(recv_raw_b, moves, sea, plain)
    pieces = recv_a[sz.sum_row : sz.sum_row + 3 * VREG].astype(F32)
    pair = part + pieces.reshape(3, VREG, sz.lat).sum(axis=0)
    other = jnp.zeros_like(pair)
    step = 2
    while step < sz.spec:
        pair = pair + other
        other = lax.ppermute(pair, "spec", [(i, i ^ (2 * step - 1)) for i in range(sz.spec)])
        step *= 2

    padded, centres, turns = sz.bands + 2 * reach, sz.bands + reach, sz.ring + 3 * VREG
    arrays = (
        array(padded, sz.ring),
        array(padded, turns),
        array(centres, turns),
        array(centres, turns),
        array(padded, sz.frame),
        array(centres, sz.frame),
        array(centres, sz.frame),
    )
    *inner, num = kernel_call(
        functools.partial(inner_kernel, sz),
        arrays + (field,),
        5,
        scratch=[vmem(sz.fix_rows)],
        aliases={4: 0},
        name="inner",
    )(adv, side, recv_a, gain, plain)
    nest_inner, num = lax.optimization_barrier((nest_inner, num))
    _, nest_adv = kernel_call(
        functools.partial(nest_edge_kernel, sz),
        (field, array(sz.cols, sz.bins + VREG)),
        4,
        scratch=near_rows,
        aliases={0: 0},
        name="nest_edge",
    )(nest_inner, from_w, from_e, nest_moves)
    nest_adv, recv_b = lax.optimization_barrier((nest_adv, recv_b))
    num, *_, s_num = kernel_call(
        functools.partial(outer_kernel, sz),
        (field,) + arrays + (array(sz.bands * sz.side),),
        10 + len(arrays),
        scratch=[vmem(sz.pass_rows), vmem(reach * sz.side)],
        aliases={9 + i: i for i in range(1 + len(arrays))},
        name="outer",
    )(adv, side, recv_b, gain, moves, s_moves, sea, from_e, far_near, num, *inner)
    spectra, msg = kernel_call(
        functools.partial(source_kernel, sz),
        (field, jax.ShapeDtypeStruct((sz.slots, sz.lanes), BF16)),
        5,
        scratch=[vmem(sz.bins + VREG)],
        name="sources",
    )(num, s_num, pair, other, mix)

    recv = lax.all_to_all(msg, "grid", split_axis=0, concat_axis=0, tiled=True)
    global_next, nest_next = kernel_call(
        functools.partial(blend_kernel, sz),
        (field, field),
        3,
        out_hbm=(0, 1),
        scratch=[vmem(sz.rows), pltpu.SemaphoreType.DMA((sz.lanes // 128 + 1,))],
        name="blend",
    )(recv, nest_adv, pltpu.with_memory_space_constraint(spectra, pltpu.VMEM))
    full = (sz.bands, sz.angles, sz.cols, sz.lat)
    return global_next.reshape(full), nest_next.reshape(full)


def solution(mesh):
    in_specs = (
        P("spec", None, "grid", None),
        P("spec", None, "grid", None),
        P("grid", None),
        P(None, "grid", None),
        P("grid", None),
        P("grid", None),
        P("grid"),
        P("grid", None),
    )
    out_specs = (P("spec", None, "grid", None), P("spec", None, "grid", None))
    return jax.shard_map(
        functools.partial(per_device, mesh),
        mesh=mesh,
        in_specs=in_specs,
        out_specs=out_specs,
        check_vma=False,
    )
```

```python
import functools

import jax
import jax.numpy as jnp
import numpy as np
from jax import lax
from jax.experimental import pallas as pl
from jax.experimental.pallas import tpu as pltpu
from jax.sharding import PartitionSpec as P

ratio_step = 1.1
speed_coef = 0.054
wind_coef = 0.05
dissip_coef = 0.2
nonlin_coef = 0.12
nest_speedup = 2.0
reach = 5

VREG = 8
BF16 = jnp.bfloat16
F32 = jnp.float32


class Sizes:
    def __init__(self, mesh, energy, rim_rows):
        self.grid = mesh.shape["grid"]
        self.spec = mesh.shape["spec"]
        self.bands, self.angles, self.cols, self.lat = energy.shape
        self.freqs = self.bands * self.spec
        self.bins = self.bands * self.angles
        self.ring = self.angles * self.cols
        self.rows = self.bins * self.cols
        self.vregs = self.ring // VREG
        self.rim = rim_rows
        self.cap = max(2, (2 * rim_rows + self.grid - 1) // self.grid)
        self.slots = self.grid * self.cap
        self.lanes = (self.bins + 3 + 127) // 128 * 128
        self.half = self.angles // 2
        self.quarter = self.angles // 4
        self.side = (self.angles + VREG - 1) // VREG * VREG
        self.frame = self.side + 2 * VREG
        self.thin = self.bands * self.half
        self.thin_rows = (2 * self.thin + 15) // 16 * 16
        self.thick = self.angles + self.half
        self.info = self.bands * self.thick
        self.thick_nest = (self.info + 7 + VREG - 1) // VREG * VREG
        self.thick_rows = (self.thick_nest + self.thin + 15) // 16 * 16
        self.edge_rows = reach * self.ring
        self.rim_band = 2 * self.half
        self.far_band = self.rim_band + self.angles
        self.sum_row = (reach * self.far_band + VREG - 1) // VREG * VREG
        self.fix_rows = (self.sum_row + 3 * VREG + 15) // 16 * 16
        self.pass_thick = (reach * self.half + VREG - 1) // VREG * VREG
        self.pass_rows = max(self.fix_rows + 16, (self.pass_thick + reach * self.thick + 15) // 16 * 16)


def band_ratio(sz, band, inverse=False):
    rank = lax.axis_index("spec")
    ratio = F32(0.0)
    for s in range(sz.spec):
        power = ratio_step ** (s * sz.bands + band - sz.freqs // 2)
        ratio = jnp.where(rank == s, F32(1.0 / power if inverse else power), ratio)
    return ratio


def over_bands(count, ratio, body, inverse=False):
    step = F32(1.0 / ratio_step if inverse else ratio_step)

    def turn(i, r):
        body(i, r)
        return r * step

    lax.fori_loop(0, count, turn, ratio)


def angle_table(sz):
    heading = 2.0 * np.pi * np.arange(sz.angles) / sz.angles
    table = np.zeros((sz.ring + VREG + sz.side, sz.lat), np.float32)
    table[sz.ring + VREG :][: sz.angles, 0] = np.cos(heading)
    table[sz.ring + VREG :][: sz.angles, 1] = np.sin(heading)
    table[: sz.ring, 0] = np.repeat(np.cos(heading), sz.cols)
    table[: sz.ring, 1] = np.repeat(np.sin(heading), sz.cols)
    degrees = -60.0 + 120.0 * (np.arange(sz.lat) + 0.5) / sz.lat
    table[sz.ring : sz.ring + VREG] = 1.0 / np.cos(degrees * (np.pi / 180.0))
    return table


def from_west(sz, angle):
    return angle < sz.quarter or angle >= 3 * sz.quarter


def split3(x):
    high = x.astype(BF16).astype(F32)
    middle = (x - high).astype(BF16).astype(F32)
    return [high, middle, x - high - middle]


def upwind(sz, v):
    sub = lax.broadcasted_iota(jnp.int32, (VREG, sz.lat), 0)
    first, per = v * VREG // sz.cols, VREG // sz.cols
    wests = [from_west(sz, first + i) for i in range(per)]
    west = sub < 0
    for i in range(per):
        if wests[i]:
            west = west | ((sub >= i * sz.cols) & (sub < (i + 1) * sz.cols))
    return wests, west, sub % sz.cols


def west_half(sz):
    return ((3 * sz.quarter, sz.angles - 3 * sz.quarter), (0, sz.quarter))


def fetch(pairs, sems):
    copies = [pltpu.make_async_copy(a, b, sems.at[i]) for i, (a, b) in enumerate(pairs)]
    for c in copies:
        c.start()
    return copies


def far_band(sz):
    return jnp.where(lax.rem(lax.axis_index("spec"), 2) == 0, 0, sz.bands - reach)


def pack_kernel(
    sz, energy, nest, mask, wind, thin, thick, first, second, first_n, late, early, late_n, early_n,
    mask_v, wind_v, tmp_thin, tmp_thick, sems,
):
    from_east = pl.ds(sz.quarter, sz.half)
    (start, count), (_, rest) = west_half(sz)
    last = sz.cols - 1
    pairs = [
        (mask, mask_v),
        (wind, wind_v),
        (energy.at[:, :, 0], first),
        (energy.at[:, from_east, 1], second),
        (energy.at[:, pl.ds(start, count), last], late),
        (energy.at[:, pl.ds(0, rest), last], early),
        (nest.at[:, from_east, 0], first_n),
        (nest.at[:, pl.ds(start, count), last], late_n),
        (nest.at[:, pl.ds(0, rest), last], early_n),
    ]
    copies = [pltpu.make_async_copy(a, b, sems.at[i]) for i, (a, b) in enumerate(pairs)]
    for copy in copies:
        copy.start()
    spare = sz.thin_rows - 2 * sz.thin
    if spare:
        tmp_thin[pl.ds(2 * sz.thin, spare), :] = jnp.zeros((spare, sz.lat), F32)
    tmp_thick[...] = jnp.zeros_like(tmp_thick)
    for copy in copies[:6]:
        copy.wait()
    info = [mask_v[0:1, :].astype(F32)] + split3(wind_v[0, 0:1, :]) + split3(wind_v[1, 0:1, :])
    for i, line in enumerate(info):
        tmp_thick[pl.ds(sz.info + i, 1), :] = line
    for k in range(sz.bands):
        tmp_thin[pl.ds(k * sz.half, count), :] = late[k]
        tmp_thin[pl.ds(k * sz.half + count, rest), :] = early[k]
        tmp_thick[pl.ds(k * sz.thick, sz.angles), :] = first[k]
        tmp_thick[pl.ds(k * sz.thick + sz.angles, sz.half), :] = second[k]
    for copy in copies[6:]:
        copy.wait()
    for k in range(sz.bands):
        at = sz.thin + k * sz.half
        tmp_thin[pl.ds(at, count), :] = late_n[k]
        tmp_thin[pl.ds(at + count, rest), :] = early_n[k]
        tmp_thick[pl.ds(sz.thick_nest + k * sz.half, sz.half), :] = first_n[k]
    thin[...] = tmp_thin[...].astype(BF16)
    thick[...] = tmp_thick[...].astype(BF16)


def setup_kernel(sz, table, mask, wind, moves, nest_moves, s_moves, gain, sea):
    per = VREG // sz.cols
    sea[...] = jnp.concatenate([mask[...].astype(F32)] * per, axis=0)
    east_wind = jnp.concatenate([wind[0]] * per, axis=0)
    north_wind = jnp.concatenate([wind[1]] * per, axis=0)
    fill_moves(sz, 0, table, sz.cols, (moves, nest_moves))
    fill_moves(sz, sz.ring + VREG, table, 1, (s_moves, None))
    for v in range(sz.vregs):
        rows = table[pl.ds(v * VREG, VREG), :]
        along = rows[:, 0:1] * east_wind + rows[:, 1:2] * north_wind
        gain[pl.ds(v * VREG, VREG), :] = wind_coef * jnp.maximum(along, 0.0)
    for v in range(sz.side // VREG):
        rows = table[pl.ds(sz.ring + VREG + v * VREG, VREG), :]
        for i in range(2):
            s_moves[3 + i, pl.ds(v * VREG, VREG), :] = jnp.broadcast_to(rows[:, i : i + 1], (VREG, sz.lat))


def raw_kernel(sz, energy, raw_a, raw_b):
    for raw, first in ((raw_a, sz.bands - reach - far_band(sz)), (raw_b, far_band(sz))):
        raw[...] = energy[pl.ds(pl.multiple_of(first * sz.ring, VREG), sz.edge_rows), :].astype(BF16)


def pass_kernel(sz, from_w, from_e, msg, wide_w, wide_e, tmp):
    wide_w[...] = from_w[...].astype(F32)
    wide_e[...] = from_e[...].astype(F32)
    for row, end in ((reach * sz.half, sz.pass_thick), (sz.pass_thick + reach * sz.thick, sz.pass_rows)):
        row = row // VREG * VREG
        if end > row:
            tmp[pl.ds(row, end - row), :] = jnp.zeros((end - row, sz.lat), F32)
    first = far_band(sz)
    count = reach * sz.half
    tmp[pl.ds(0, count), :] = wide_w[pl.ds(first * sz.half, count), :]
    start = pl.multiple_of(first * sz.thick, VREG)
    tmp[pl.ds(sz.pass_thick, reach * sz.thick), :] = wide_e[pl.ds(start, reach * sz.thick), :]
    msg[...] = tmp[...].astype(BF16)


def fill_moves(sz, rows, table, cols, targets):
    lane = lax.broadcasted_iota(jnp.int32, (VREG, sz.lat), 1)
    sub = lax.broadcasted_iota(jnp.int32, (VREG, sz.lat), 0)
    sec = table[pl.ds(sz.ring, VREG), :]
    for v in range(targets[0].shape[1] // VREG):
        line = table[pl.ds(rows + v * VREG, VREG), :]
        along = jnp.broadcast_to(jnp.abs(line[:, 0:1]), (VREG, sz.lat))
        across = jnp.broadcast_to(jnp.abs(line[:, 1:2]), (VREG, sz.lat))
        edge = lane == jnp.where(sub < sz.half * cols - v * VREG, 0, sz.lat - 1)
        here = pl.ds(v * VREG, VREG)
        for target, by in zip(targets, (along * sec, along)):
            if target is not None:
                target[0, here, :] = by + across
                target[1, here, :] = by
                target[2, here, :] = jnp.where(edge, 0.0, across)


def beside(sz, x, turn):
    if turn >= VREG:
        return pltpu.roll(x, 1, 1)
    if turn <= 0:
        return pltpu.roll(x, sz.lat - 1, 1)
    sub = lax.broadcasted_iota(jnp.int32, (VREG, sz.lat), 0)
    return jnp.where(sub < turn, pltpu.roll(x, 1, 1), pltpu.roll(x, sz.lat - 1, 1))


def transported(sz, field, base, v, moves, speed):
    here = pl.ds(v * VREG, VREG)
    x = field[pl.ds(base + v * VREG, VREG), :]
    wests, west, col = upwind(sz, v)
    if all(wests):
        near, at_edge = pltpu.roll(x, 1, 0), col == 0
    elif not any(wests):
        near, at_edge = pltpu.roll(x, VREG - 1, 0), col == sz.cols - 1
    else:
        near = jnp.where(west, pltpu.roll(x, 1, 0), pltpu.roll(x, VREG - 1, 0))
        at_edge = jnp.where(west, col, sz.cols - 1 - col) == 0
    near = jnp.where(at_edge, 0.0, near)
    south = sz.half * sz.cols - v * VREG
    return x - speed * (moves[0, here, :] * x - moves[1, here, :] * near - moves[2, here, :] * beside(sz, x, south))


def edge_parts(sz, moves, wide_w, at_w, wide_e, at_e):
    parts = []
    for first, count in west_half(sz):
        parts.append((first, count, 0, wide_w[pl.ds(at_w, count), :]))
        at_w += count
    parts.append((sz.quarter, sz.half, sz.cols - 1, wide_e[pl.ds(at_e, sz.half), :]))
    for first, count, col, cells in parts:
        yield first, count, col, moves[1, pl.ds(first * sz.cols, count, stride=sz.cols), :] * cells


def side_transported(sz, x, near, v, s_moves, speed):
    here = pl.ds(v * VREG, VREG)
    move = s_moves[0, here, :] * x - s_moves[1, here, :] * near
    return x - speed * (move - s_moves[2, here, :] * beside(sz, x, sz.half - v * VREG))


def local_kernel(sz, energy, moves, sea, adv, total):
    total[...] = jnp.zeros_like(total)

    def band(k, inverse):
        base = pl.multiple_of(k * sz.ring, VREG)
        line = jnp.zeros((VREG, sz.lat), F32)
        for v in range(sz.vregs):
            out = sea[...] * transported(sz, energy, base, v, moves, speed_coef * inverse)
            adv[pl.ds(base + v * VREG, VREG), :] = out
            line = line + out
        total[...] = total[...] * F32(1.0 / ratio_step) + line

    over_bands(sz.bands, band_ratio(sz, 0, True), band, True)
    total[...] = total[...] * (0.1 * band_ratio(sz, sz.bands - 1))


def edge_kernel(
    sz, adv_in, total, energy, from_w, from_e, moves, s_moves, sea, adv, side, msg_a, part,
    wide_w, wide_e, s_near, fix,
):
    wide_w[...] = from_w[...].astype(F32)
    wide_e[...] = from_e[...].astype(F32)
    s_sea = wide_e[pl.ds(sz.info, 1), :]
    sub = lax.broadcasted_iota(jnp.int32, (VREG, sz.lat), 0)
    s_total = jnp.zeros((VREG, sz.lat), F32)
    lines = {}
    for k in range(sz.bands):
        inverse = band_ratio(sz, k, True)
        weight = 0.1 * band_ratio(sz, k)
        speed = speed_coef * inverse
        at_e = k * sz.thick + sz.quarter
        for first, count, col, moved in edge_parts(sz, moves, wide_w, k * sz.half, wide_e, at_e):
            moved = moved * (speed * sea[col : col + 1, :])
            rows = pl.ds(k * sz.ring + first * sz.cols + col, count, stride=sz.cols)
            adv[rows, :] = adv[rows, :] + moved
            lines[first, col] = lines.get((first, col), 0.0) + moved * weight
        at = k * sz.side
        for first, count in west_half(sz):
            start = k * sz.ring + first * sz.cols + sz.cols - 1
            s_near[pl.ds(at + first, count), :] = energy[pl.ds(start, count, stride=sz.cols), :]
        s_near[pl.ds(at + sz.quarter, sz.half), :] = wide_e[pl.ds(k * sz.thick + sz.angles, sz.half), :]
        if sz.side > sz.angles:
            rest = sz.side - sz.angles
            s_near[pl.ds(at + sz.angles, rest), :] = jnp.zeros((rest, sz.lat), F32)
        s_line = jnp.zeros((VREG, sz.lat), F32)
        for v in range(sz.side // VREG):
            x = wide_e[pl.ds(k * sz.thick + v * VREG, VREG), :]
            near = s_near[pl.ds(at + v * VREG, VREG), :]
            out = s_sea * side_transported(sz, x, near, v, s_moves, speed)
            side[pl.ds(at + v * VREG, VREG), :] = out
            s_line = s_line + (out if (v + 1) * VREG <= sz.angles else jnp.where(sub < sz.angles - v * VREG, out, 0.0))
        s_total = s_total + s_line * weight
    mine = total[0 : sz.cols, :]
    for i in range(1, VREG // sz.cols):
        mine = mine + total[i * sz.cols : (i + 1) * sz.cols, :]
    west, east = (
        sum(jnp.sum(x, axis=0, keepdims=True) for (_, c), x in lines.items() if c == col) for col in (0, sz.cols - 1)
    )
    between = jnp.zeros((sz.cols - 2, sz.lat), F32)
    mine = mine + jnp.concatenate([west, between, east], axis=0)
    s_sum = jnp.sum(s_total, axis=0, keepdims=True)
    sums = jnp.concatenate([mine, s_sum, jnp.zeros((VREG - sz.cols - 1, sz.lat), F32)], axis=0)
    part[...] = sums
    fix[...] = jnp.zeros_like(fix)
    fix[pl.ds(sz.sum_row, 3 * VREG), :] = jnp.concatenate(split3(sums), axis=0)
    start = sz.bands - reach - far_band(sz)
    for k in range(reach):
        band_row = pl.multiple_of((start + k) * sz.ring, VREG)
        at = k * sz.far_band
        for first, count in west_half(sz):
            fix[pl.ds(at, count), :] = adv[pl.ds(band_row + first * sz.cols, count, stride=sz.cols), :]
            at += count
        last = band_row + (sz.quarter + 1) * sz.cols - 1
        fix[pl.ds(at, sz.half), :] = adv[pl.ds(last, sz.half, stride=sz.cols), :]
        s_row = pl.multiple_of((start + k) * sz.side, VREG)
        fix[pl.ds(k * sz.far_band + sz.rim_band, sz.angles), :] = side[pl.ds(s_row, sz.angles), :]
    msg_a[...] = fix[...].astype(BF16)


def nest_kernel(sz, nest, moves, out):
    def band(k, inverse):
        base = pl.multiple_of(k * sz.ring, VREG)
        for v in range(sz.vregs):
            moved = transported(sz, nest, base, v, moves, nest_speedup * speed_coef * inverse)
            out[pl.ds(base + v * VREG, VREG), :] = moved

    over_bands(sz.bands, band_ratio(sz, 0, True), band, True)


def nest_edge_kernel(sz, inner, from_w, from_e, moves, out, columns, wide_w, wide_e):
    grid_rank = lax.axis_index("grid")
    quarter = sz.grid // 4
    keep_w = jnp.where((grid_rank != quarter) & (grid_rank != 3 * quarter), 1.0, 0.0).astype(F32)
    keep_e = jnp.where((grid_rank != quarter - 1) & (grid_rank != 3 * quarter - 1), 1.0, 0.0).astype(F32)
    wide_w[...] = from_w[...].astype(F32)
    wide_e[...] = from_e[...].astype(F32)
    for k in range(sz.bands):
        speed = nest_speedup * speed_coef * band_ratio(sz, k, True)
        at_w, at_e = sz.thin + k * sz.half, sz.thick_nest + k * sz.half
        for first, count, col, moved in edge_parts(sz, moves, wide_w, at_w, wide_e, at_e):
            rows = pl.ds(k * sz.ring + first * sz.cols + col, count, stride=sz.cols)
            out[rows, :] = out[rows, :] + moved * (speed * (keep_w if col == 0 else keep_e))
    for c in range(sz.cols):
        columns[c, pl.ds(0, sz.bins), :] = out[pl.ds(c, sz.bins, stride=sz.cols), :]


def dot_lanes(a, b):
    return lax.dot_general(a, b, (((1,), (1,)), ((), ())), preferred_element_type=F32)


def rim_kernel(sz, cell, dest, target, weight, mix):
    device = lax.broadcasted_iota(jnp.int32, (sz.grid, sz.rim), 0)
    hot = jnp.where(device == dest[...], 1.0, 0.0)
    before = lax.broadcasted_iota(jnp.int32, (sz.rim, sz.rim), 0)
    after = lax.broadcasted_iota(jnp.int32, (sz.rim, sz.rim), 1)
    earlier = jnp.dot(
        hot.astype(BF16), jnp.where(before < after, 1.0, 0.0).astype(BF16), preferred_element_type=F32
    )
    rank = jnp.sum(hot * earlier, axis=0, keepdims=True)
    place = dest[...] * sz.cap + rank.astype(jnp.int32)
    slot = lax.broadcasted_iota(jnp.int32, (sz.slots, sz.rim), 0)
    takes = jnp.where(slot == place, 1.0, 0.0).astype(BF16)
    row = lax.broadcasted_iota(jnp.int32, (sz.lat, sz.rim), 0)
    col = cell[0:1, :] - lax.axis_index("grid") * sz.cols
    south_row = cell[1:2, :]
    ex, ny = weight[0:1, :], weight[1:2, :]
    for c in range(sz.cols + 1):
        share = jnp.where(col == c, 1.0 - ex, 0.0) + jnp.where(col + 1 == c, ex, 0.0)
        south, north = share * (1.0 - ny), share * ny
        corner = jnp.where(row == south_row, south, 0.0) + jnp.where(row == south_row + 1, north, 0.0)
        mix[:, c * sz.lat : (c + 1) * sz.lat] = dot_lanes(takes, corner.astype(BF16)).astype(BF16)
    at = sz.bins - (sz.lanes - 128)
    line = lax.broadcasted_iota(jnp.int32, (128, sz.rim), 0)
    t = target[...]
    t_col = t // sz.lat
    about = jnp.where(line == at, t_col.astype(F32), 0.0)
    about = about + jnp.where(line == at + 1, (t - t_col * sz.lat).astype(F32), 0.0)
    about = about + jnp.where(line == at + 2, weight[2:3, :], 0.0)
    n = (sz.cols + 1) * sz.lat
    mix[:, n : n + 128] = dot_lanes(takes, about.astype(BF16)).astype(BF16)


def low_rows(sz):
    return lax.broadcasted_iota(jnp.int32, (VREG, sz.lat), 0) < VREG // 2


def put(sz, plain, turned, slot, vals):
    nv, low = sz.vregs, low_rows(sz)
    for v in range(nv):
        if plain is not None:
            plain[slot, pl.ds(v * VREG, VREG), :] = vals[v]
        nxt = pltpu.roll(jnp.where(low, vals[(v + 1) % nv], vals[v]), VREG // 2, 0)
        turned[slot, pl.ds((v + 2) * VREG, VREG), :] = nxt
        if v >= nv - 2:
            turned[slot, pl.ds((v + 2 - nv) * VREG, VREG), :] = nxt
        if v == 0:
            turned[slot, pl.ds((nv + 2) * VREG, VREG), :] = nxt


def close(sz, ref, slot):
    ref[slot, pl.ds(VREG - 3, 3), :] = ref[slot, pl.ds(VREG + sz.angles - 3, 3), :]
    ref[slot, pl.ds(VREG + sz.angles, 3), :] = ref[slot, pl.ds(VREG, 3), :]


def s_put(sz, s_plain, slot, load):
    for v in range(sz.side // VREG):
        s_plain[slot, pl.ds((v + 1) * VREG, VREG), :] = load(v)
    close(sz, s_plain, slot)


def exchange(sc, c, up, down):
    return sc * (c * (up + down) - 2.0 * (up * down))


def strengths(sz, ratio, n, plain, turned, plus, minus, s_plain, s_plus, s_minus):
    nv = sz.vregs
    strength = nonlin_coef * ratio
    for v in range(nv):
        c = plain[n + 3, pl.ds(v * VREG, VREG), :]
        sc = strength * c
        for ref, up_row, down_row in ((plus, v + 3, v + 1), (minus, v, v + 2)):
            up = turned[n + 5, pl.ds(up_row * VREG, VREG), :]
            down = turned[n, pl.ds(down_row * VREG, VREG), :]
            delta = exchange(sc, c, up, down)
            ref[n, pl.ds((v + 1) * VREG, VREG), :] = delta
            if v == nv - 1:
                ref[n, pl.ds(0, VREG), :] = delta
            if v < 2:
                ref[n, pl.ds((nv + 1 + v) * VREG, VREG), :] = delta
    for v in range(sz.side // VREG):
        row = (v + 1) * VREG
        c = s_plain[n + 3, pl.ds(row, VREG), :]
        sc = strength * c
        for ref, s in ((s_plus, 1), (s_minus, -1)):
            up = s_plain[n + 5, pl.ds(row + 3 * s, VREG), :]
            down = s_plain[n, pl.ds(row - s, VREG), :]
            ref[n, pl.ds(row, VREG), :] = exchange(sc, c, up, down)
    close(sz, s_plus, n)
    close(sz, s_minus, n)


def is_even():
    return lax.rem(lax.axis_index("spec"), 2) == 0


def complete(sz, slot, fix, k, plain, s_plain):
    at = k * sz.far_band
    for start, count in west_half(sz):
        plain[slot, pl.ds(start * sz.cols, count, stride=sz.cols), :] = fix[pl.ds(at, count), :]
        at += count
    last = (sz.quarter + 1) * sz.cols - 1
    plain[slot, pl.ds(last, sz.half, stride=sz.cols), :] = fix[pl.ds(at, sz.half), :]
    at = k * sz.far_band + sz.rim_band
    s_put(sz, s_plain, slot, lambda v: fix[pl.ds(at + v * VREG, VREG), :])


def turn_halo(sz, base, plain, turned, real=None):
    def halo(k, carry):
        vals = [plain[base + k, pl.ds(v * VREG, VREG), :] for v in range(sz.vregs)]
        put(sz, None if real is None else plain, turned, base + k, vals if real is None else [x * real for x in vals])
        return carry

    lax.fori_loop(0, reach, halo, 0)


def numerators(sz, k, ratio, adv, gain, plus, minus, store):
    nv, low = sz.vregs, low_rows(sz)
    base = pl.multiple_of(k * sz.ring, VREG)

    def moved_in(v):
        return (
            plus[k, pl.ds(v * VREG, VREG), :]
            + minus[k, pl.ds((v + 3) * VREG, VREG), :]
            + plus[k + 5, pl.ds((v + 2) * VREG, VREG), :]
            + minus[k + 5, pl.ds((v + 1) * VREG, VREG), :]
        )

    before = moved_in(nv - 1)
    for v in range(nv):
        now = moved_in(v)
        moved = pltpu.roll(jnp.where(low, now, before), VREG // 2, 0)
        before = now
        here = pl.ds((v + 1) * VREG, VREG)
        transfer = moved - 2.0 * (plus[k + 2, here, :] + minus[k + 2, here, :])
        a = adv[pl.ds(base + v * VREG, VREG), :]
        grown = ratio * gain[pl.ds(v * VREG, VREG), :]
        store(pl.ds(base + v * VREG, VREG), a + grown * a + transfer)


def has_across(sz):
    rank = lax.axis_index("spec")
    return jnp.where((rank == 0) | (rank == sz.spec - 1), 0.0, 1.0).astype(F32)


def transport_raw(sz, raw, moves, sea, plain, wide, upper):
    base = jnp.where(upper, sz.bands + reach, 0)
    inverse = jnp.where(upper, band_ratio(sz, sz.bands, True), band_ratio(sz, -reach, True))
    wide[...] = raw[...].astype(F32)

    def transport(k, r):
        start = pl.multiple_of(k * sz.ring, VREG)
        for v in range(sz.vregs):
            moved = transported(sz, wide, start, v, moves, speed_coef * r)
            plain[base + k, pl.ds(v * VREG, VREG), :] = sea * moved

    over_bands(reach, inverse, transport, True)


def beside_kernel(sz, raw_a, moves, sea, plain, wide):
    transport_raw(sz, raw_a, moves, sea[...], plain, wide, is_even())


def beyond_kernel(sz, raw_b, moves, sea, plain_in, plain, far_near, wide):
    transport_raw(sz, raw_b, moves, sea[...] * has_across(sz), plain, wide, jnp.logical_not(is_even()))
    far_near[...] = jnp.zeros_like(far_near)
    for k in range(reach):
        for first, count in west_half(sz):
            start = k * sz.ring + first * sz.cols + sz.cols - 1
            far_near[pl.ds(k * sz.side + first, count), :] = wide[pl.ds(start, count, stride=sz.cols), :]


def inner_kernel(
    sz, adv, side, recv_a, gain, plain_in, plain, turned, plus, minus, s_plain, s_plus, s_minus, num, fix
):
    base_a = jnp.where(is_even(), sz.bands + reach, 0)

    def own(k, carry):
        base = pl.multiple_of(k * sz.ring, VREG)
        put(sz, plain, turned, k + reach, [adv[pl.ds(base + v * VREG, VREG), :] for v in range(sz.vregs)])
        s_base = pl.multiple_of(k * sz.side, VREG)
        s_put(sz, s_plain, k + reach, lambda v: side[pl.ds(s_base + v * VREG, VREG), :])
        return carry

    lax.fori_loop(0, sz.bands, own, 0)

    fix[...] = recv_a[...].astype(F32)
    for k in range(reach):
        complete(sz, base_a + k, fix, k, plain, s_plain)
    turn_halo(sz, base_a, plain, turned)

    arrays = (plain, turned, plus, minus, s_plain, s_plus, s_minus)
    start = jnp.where(is_even(), reach, 0)
    ratio = jnp.where(is_even(), band_ratio(sz, 3), band_ratio(sz, 3 - reach))
    over_bands(sz.bands, ratio, lambda i, r: strengths(sz, r, start + i, *arrays))

    def store(rows, value):
        num[rows, :] = value

    ratio = jnp.where(is_even(), band_ratio(sz, reach), band_ratio(sz, 0))
    over_bands(
        sz.bands - reach, ratio, lambda i, r: numerators(sz, start + i, r, adv, gain, plus, minus, store)
    )


def outer_kernel(
    sz, adv, side, recv_b, gain, moves, s_moves, sea, from_e, far_near, num_in,
    plain_in, turned_in, plus_in, minus_in, s_plain_in, s_plus_in, s_minus_in,
    num, plain, turned, plus, minus, s_plain, s_plus, s_minus, s_num, wide, s_near,
):
    spec_rank = lax.axis_index("spec")
    ns = sz.side // VREG
    base_b = jnp.where(is_even(), 0, sz.bands + reach)
    real_b = has_across(sz)
    info = from_e[pl.ds(sz.info // 16 * 16, 32), :].astype(F32)
    at = sz.info % 16
    s_sea = info[at : at + 1] * real_b
    wide[...] = recv_b[...].astype(F32)
    s_near[...] = far_near[...]
    inverse = jnp.where(is_even(), band_ratio(sz, -reach, True), band_ratio(sz, sz.bands, True))
    for k in range(reach):
        speed = inverse * (speed_coef / ratio_step**k)
        slot, row = base_b + k, sz.pass_thick + k * sz.thick
        for start, count, col, moved in edge_parts(sz, moves, wide, k * sz.half, wide, row + sz.quarter):
            rows = pl.ds(start * sz.cols + col, count, stride=sz.cols)
            plain[slot, rows, :] = plain[slot, rows, :] + moved * (speed * real_b * sea[col : col + 1, :])
        at_near = k * sz.side
        s_near[pl.ds(at_near + sz.quarter, sz.half), :] = wide[pl.ds(row + sz.angles, sz.half), :]

        def column(v):
            x = wide[pl.ds(row + v * VREG, VREG), :]
            near = s_near[pl.ds(at_near + v * VREG, VREG), :]
            return s_sea * side_transported(sz, x, near, v, s_moves, speed)

        s_put(sz, s_plain, slot, column)
    turn_halo(sz, base_b, plain, turned)
    arrays = (plain, turned, plus, minus, s_plain, s_plus, s_minus)
    begin = jnp.where(is_even(), 0, sz.bands)
    ratio = jnp.where(is_even(), band_ratio(sz, 3 - reach), band_ratio(sz, sz.bands + 3 - reach))
    over_bands(reach, ratio, lambda i, r: strengths(sz, r, begin + i, *arrays))

    at = at + 1
    s_east = info[at : at + 1] + info[at + 1 : at + 2] + info[at + 2 : at + 3]
    s_north = info[at + 3 : at + 4] + info[at + 4 : at + 5] + info[at + 5 : at + 6]
    missing = jnp.where(is_even(), 0, sz.bands - reach)

    def store(rows, value):
        num[rows, :] = value

    over_bands(
        reach,
        jnp.where(is_even(), band_ratio(sz, 0), band_ratio(sz, sz.bands - reach)),
        lambda i, r: numerators(sz, missing + i, r, adv, gain, plus, minus, store),
    )

    s_gain = []
    for v in range(ns):
        here = pl.ds(v * VREG, VREG)
        along = s_moves[3, here, :] * s_east + s_moves[4, here, :] * s_north
        s_gain.append(wind_coef * jnp.maximum(along, 0.0))
    for k in range(sz.bands):
        ratio = band_ratio(sz, k)
        for v in range(ns):
            row = (v + 1) * VREG
            here = pl.ds(row, VREG)
            transfer = (
                s_plus[k, pl.ds(row - 3, VREG), :]
                + s_minus[k, pl.ds(row + 3, VREG), :]
                + s_plus[k + 5, pl.ds(row + 1, VREG), :]
                + s_minus[k + 5, pl.ds(row - 1, VREG), :]
                - 2.0 * (s_plus[k + 2, here, :] + s_minus[k + 2, here, :])
            )
            a = side[pl.ds(k * sz.side + v * VREG, VREG), :]
            s_num[pl.ds(k * sz.side + v * VREG, VREG), :] = a + (ratio * s_gain[v]) * a + transfer


def source_kernel(sz, num, s_num, pair, other, mix, out, msg, s_out):
    total_weight = sz.angles * 0.1 * sum(ratio_step ** (k - sz.freqs // 2) for k in range(sz.freqs))
    means = (pair[...] + other[...]) * (1.0 / total_weight)
    mean = jnp.concatenate([means[0 : sz.cols]] * (VREG // sz.cols), axis=0)
    s_mean = means[sz.cols : sz.cols + 1]

    def finish(k, ratio):
        factor = 1.0 / (1.0 + (dissip_coef * ratio * ratio) * mean)
        base = pl.multiple_of(k * sz.ring, VREG)
        for v in range(sz.vregs):
            here = pl.ds(base + v * VREG, VREG)
            out[here, :] = num[here, :] * factor

    over_bands(sz.bands, band_ratio(sz, 0), finish)
    for k in range(sz.bands):
        ratio = band_ratio(sz, k)
        factor = 1.0 / (1.0 + (dissip_coef * ratio * ratio) * s_mean)
        for v in range(sz.side // VREG):
            here = pl.ds(k * sz.angles + v * VREG, VREG)
            s_out[here, :] = s_num[pl.ds(k * sz.side + v * VREG, VREG), :] * factor

    pad = jnp.zeros((sz.lanes - sz.bins, sz.lat), BF16)
    columns = [out[pl.ds(c, sz.bins, stride=sz.cols), :] for c in range(sz.cols)]
    columns.append(s_out[pl.ds(0, sz.bins), :])
    columns = [jnp.concatenate([c.astype(BF16), pad], axis=0) for c in columns]
    n = (sz.cols + 1) * sz.lat
    spectra = dot_lanes(mix[:, 0:n], jnp.concatenate(columns, axis=1))
    about = mix[:, n : n + 128].astype(F32)
    msg[:, 0 : sz.lanes - 128] = spectra[:, : sz.lanes - 128].astype(BF16)
    msg[:, sz.lanes - 128 : sz.lanes] = (spectra[:, sz.lanes - 128 :] + about).astype(BF16)


def blend_kernel(sz, recv, nest_adv, spectra, global_hbm, result_hbm, out, sems):
    writes = [pltpu.make_async_copy(spectra, global_hbm, sems.at[sz.lanes // 128])]
    writes[0].start()
    at = sz.bins - (sz.lanes - 128)
    about = recv[:, sz.lanes - 128 :].astype(F32)
    t_col, t_row, rate = about[:, at : at + 1], about[:, at + 1 : at + 2], about[:, at + 2 : at + 3]
    lane = lax.broadcasted_iota(jnp.int32, (sz.slots, sz.lat), 1).astype(F32)
    hit = jnp.where(lane == t_row, rate, 0.0)
    relax = [jnp.where(t_col == float(c), hit, 0.0) for c in range(sz.cols)]
    kept = [1.0 - jnp.sum(r, axis=0, keepdims=True) for r in relax]
    relax = jnp.concatenate(relax, axis=1).astype(BF16)
    for part, start in enumerate(range(0, sz.bins, 128)):
        count = min(128, sz.bins - start)
        added = lax.dot_general(
            recv[:, start : start + 128], relax, (((0,), (0,)), ((), ())), preferred_element_type=F32
        )
        for c in range(sz.cols):
            here = pl.ds(start * sz.cols + c, count, stride=sz.cols)
            own = nest_adv[c, pl.ds(start, count), :]
            out[here, :] = own * kept[c] + added[:count, c * sz.lat : (c + 1) * sz.lat]
        rows = pl.ds(start * sz.cols, count * sz.cols)
        writes.append(pltpu.make_async_copy(out.at[rows], result_hbm.at[rows], sems.at[part]))
        writes[-1].start()
    for write in writes:
        write.wait()


def kernel_call(body, out_shape, n_in, hbm=(), out_hbm=(), scratch=(), aliases=None, flops=0, name=None):
    def specs(count, far):
        return [pl.BlockSpec(memory_space=pltpu.HBM if i in far else pltpu.VMEM) for i in range(count)]

    many = isinstance(out_shape, tuple)
    out_specs = specs(len(out_shape) if many else 1, out_hbm)
    call = pl.pallas_call(
        body,
        out_shape=out_shape,
        in_specs=specs(n_in, hbm),
        out_specs=out_specs if many else out_specs[0],
        scratch_shapes=list(scratch),
        input_output_aliases=aliases or {},
        compiler_params=pltpu.CompilerParams(vmem_limit_bytes=20 * 2**20),
        cost_estimate=pl.CostEstimate(flops=flops, bytes_accessed=0, transcendentals=0) if flops else None,
        name=name,
    )
    if not aliases:
        return call

    def in_place(*args):
        pin = functools.partial(pltpu.with_memory_space_constraint, memory_space=pltpu.VMEM)
        return call(*[pin(a) if i in aliases else a for i, a in enumerate(args)])

    return in_place


def per_device(
    mesh, energy, nest_energy, ocean_mask, wind_field, rim_cell, rim_dest, rim_target, rim_weight
):
    sz = Sizes(mesh, energy, rim_dest.shape[0])

    def array(*shape, dtype=F32):
        return jax.ShapeDtypeStruct(shape + (sz.lat,), dtype)

    def vmem(*shape):
        return pltpu.VMEM(shape + (sz.lat,), F32)

    def half(rows):
        return array(rows, dtype=BF16)

    field = array(sz.rows)
    table = jnp.asarray(angle_table(sz))
    energy4, energy = energy, energy.reshape(sz.rows, sz.lat)
    nest = nest_energy.reshape(sz.rows, sz.lat)
    up = [(i, (i + 1) % sz.grid) for i in range(sz.grid)]
    down = [(j, i) for i, j in up]
    across = []
    for g in range(sz.grid):
        for i in range(sz.spec):
            j = i + 1 if i % 2 else i - 1
            to = (g, j) if 0 <= j < sz.spec else ((g ^ 1) % sz.grid, i)
            across.append((g * sz.spec + i, to[0] * sz.spec + to[1]))
    both = ("grid", "spec")
    near_rows = [vmem(sz.thin_rows), vmem(sz.thick_rows)]

    stay = functools.partial(pltpu.with_memory_space_constraint, memory_space=pltpu.HBM)
    def column(n):
        return vmem(sz.bands, n)

    thin, thick = kernel_call(
        functools.partial(pack_kernel, sz),
        (half(sz.thin_rows), half(sz.thick_rows)),
        4,
        hbm=range(4),
        scratch=[
            column(sz.angles),
            column(sz.half),
            column(sz.half),
            column(sz.angles - 3 * sz.quarter),
            column(sz.quarter),
            column(sz.angles - 3 * sz.quarter),
            column(sz.quarter),
            pltpu.VMEM(ocean_mask.shape, ocean_mask.dtype),
            pltpu.VMEM(wind_field.shape, F32),
        ]
        + near_rows
        + [pltpu.SemaphoreType.DMA((9,))],
        name="pack",
    )(stay(energy4), stay(nest_energy), stay(ocean_mask), stay(wind_field))
    from_e = lax.ppermute(thick, "grid", down)
    from_w = lax.ppermute(thin, "grid", up)

    table, thin = lax.optimization_barrier((table, thin))
    moves, nest_moves, s_moves, gain, sea = kernel_call(
        functools.partial(setup_kernel, sz),
        (array(3, sz.ring), array(3, sz.ring), array(5, sz.side), array(sz.ring), array(VREG)),
        3,
        name="setup",
    )(table, ocean_mask, wind_field)
    energy, table = lax.optimization_barrier((energy, table))
    raw_a, raw_b = kernel_call(
        functools.partial(raw_kernel, sz), (half(sz.edge_rows), half(sz.edge_rows)), 1, name="raw"
    )(energy)
    pairs = [(i, i ^ 1) for i in range(sz.spec)]
    recv_raw_b = lax.ppermute(raw_b, "spec", [(i, (i + 1 if i % 2 else i - 1) % sz.spec) for i in range(sz.spec)])
    recv_raw_a = lax.ppermute(raw_a, "spec", pairs)
    rim = (rim_cell.T, rim_dest.T, rim_target.reshape(1, sz.rim), rim_weight.T)
    rim, raw_a = lax.optimization_barrier((rim, raw_a))
    mix = kernel_call(
        functools.partial(rim_kernel, sz),
        jax.ShapeDtypeStruct((sz.slots, (sz.cols + 1) * sz.lat + 128), BF16),
        4,
        name="rim",
    )(*rim)
    nest, raw_a = lax.optimization_barrier((nest, raw_a))
    nest_inner = kernel_call(functools.partial(nest_kernel, sz), field, 2, flops=3 * 10**10, name="nest")(nest, nest_moves)
    energy, raw_a = lax.optimization_barrier((energy, raw_a))
    adv, total = kernel_call(
        functools.partial(local_kernel, sz), (field, array(VREG)), 3, flops=3 * 10**10, name="local"
    )(energy, moves, sea)
    band_fields = array(sz.bands + 2 * reach, sz.ring)
    plain = kernel_call(
        functools.partial(beside_kernel, sz), band_fields, 3, scratch=[vmem(sz.edge_rows)], flops=10**10, name="beside"
    )(recv_raw_a, moves, sea)
    from_e, from_w, mix, nest_inner, adv, plain = lax.optimization_barrier(
        (from_e, from_w, mix, nest_inner, adv, plain)
    )

    msg_b = kernel_call(
        functools.partial(pass_kernel, sz),
        half(sz.pass_rows),
        2,
        scratch=near_rows + [vmem(sz.pass_rows)],
        name="pass",
    )(from_w, from_e)
    adv, side, msg_a, part = kernel_call(
        functools.partial(edge_kernel, sz),
        (field, array(sz.bands * sz.side), half(sz.fix_rows), array(VREG)),
        8,
        scratch=near_rows + [vmem(sz.bands * sz.side), vmem(sz.fix_rows)],
        aliases={0: 0},
        flops=3 * 10**10,
        name="edges",
    )(adv, total, energy, from_w, from_e, moves, s_moves, sea)

    recv_a = lax.ppermute(msg_a, "spec", pairs)
    recv_b = lax.ppermute(msg_b, both, across)
    recv_a, recv_raw_b = lax.optimization_barrier((recv_a, recv_raw_b))
    plain, far_near = kernel_call(
        functools.partial(beyond_kernel, sz),
        (band_fields, array(reach * sz.side)),
        4,
        scratch=[vmem(sz.edge_rows)],
        aliases={3: 0},
        flops=3 * 10**10,
        name="beyond",
    )(recv_raw_b, moves, sea, plain)
    pieces = recv_a[sz.sum_row : sz.sum_row + 3 * VREG].astype(F32)
    pair = part + pieces.reshape(3, VREG, sz.lat).sum(axis=0)
    other = jnp.zeros_like(pair)
    step = 2
    while step < sz.spec:
        pair = pair + other
        other = lax.ppermute(pair, "spec", [(i, i ^ (2 * step - 1)) for i in range(sz.spec)])
        step *= 2

    padded, centres, turns = sz.bands + 2 * reach, sz.bands + reach, sz.ring + 3 * VREG
    arrays = (
        array(padded, sz.ring),
        array(padded, turns),
        array(centres, turns),
        array(centres, turns),
        array(padded, sz.frame),
        array(centres, sz.frame),
        array(centres, sz.frame),
    )
    *inner, num = kernel_call(
        functools.partial(inner_kernel, sz),
        arrays + (field,),
        5,
        scratch=[vmem(sz.fix_rows)],
        aliases={4: 0},
        name="inner",
    )(adv, side, recv_a, gain, plain)
    nest_inner, num = lax.optimization_barrier((nest_inner, num))
    _, nest_adv = kernel_call(
        functools.partial(nest_edge_kernel, sz),
        (field, array(sz.cols, sz.bins + VREG)),
        4,
        scratch=near_rows,
        aliases={0: 0},
        name="nest_edge",
    )(nest_inner, from_w, from_e, nest_moves)
    nest_adv, recv_b = lax.optimization_barrier((nest_adv, recv_b))
    num, *_, s_num = kernel_call(
        functools.partial(outer_kernel, sz),
        (field,) + arrays + (array(sz.bands * sz.side),),
        10 + len(arrays),
        scratch=[vmem(sz.pass_rows), vmem(reach * sz.side)],
        aliases={9 + i: i for i in range(1 + len(arrays))},
        name="outer",
    )(adv, side, recv_b, gain, moves, s_moves, sea, from_e, far_near, num, *inner)
    spectra, msg = kernel_call(
        functools.partial(source_kernel, sz),
        (field, jax.ShapeDtypeStruct((sz.slots, sz.lanes), BF16)),
        5,
        scratch=[vmem(sz.bins + VREG)],
        name="sources",
    )(num, s_num, pair, other, mix)

    recv = lax.all_to_all(msg, "grid", split_axis=0, concat_axis=0, tiled=True)
    global_next, nest_next = kernel_call(
        functools.partial(blend_kernel, sz),
        (field, field),
        3,
        out_hbm=(0, 1),
        scratch=[vmem(sz.rows), pltpu.SemaphoreType.DMA((sz.lanes // 128 + 1,))],
        name="blend",
    )(recv, nest_adv, pltpu.with_memory_space_constraint(spectra, pltpu.VMEM))
    full = (sz.bands, sz.angles, sz.cols, sz.lat)
    return global_next.reshape(full), nest_next.reshape(full)


def solution(mesh):
    in_specs = (
        P("spec", None, "grid", None),
        P("spec", None, "grid", None),
        P("grid", None),
        P(None, "grid", None),
        P("grid", None),
        P("grid", None),
        P("grid"),
        P("grid", None),
    )
    out_specs = (P("spec", None, "grid", None), P("spec", None, "grid", None))
    return jax.shard_map(
        functools.partial(per_device, mesh),
        mesh=mesh,
        in_specs=in_specs,
        out_specs=out_specs,
        check_vma=False,
    )
```
